32 devices in a mesh: morton: 8 (over z, x), sib: 4 (over y, core).
Axes of the slice: x: 2, y: 2, z: 4, core: 2. Of those that a mesh axis runs over, the one named last changes fastest.
Arguments:
- velocity: bfloat16 [4096, 3, 512], P(('morton', 'sib')), may hold values from -6 to 6
- pressure: bfloat16 [4096, 512], P(('morton', 'sib')), may hold values from -96 to 96
- viscosity: float32 [4096, 512], P(('morton', 'sib')), may hold values from 0.25 to 8
- levels: int32 [4096], P(('morton', 'sib')), may hold values from 3 to 7
- morton_keys: int32 [4096], P(('morton', 'sib')), may hold values from 0 to 2097151, as said below
- counts: int32 [32], replicated, may hold values from 32 to 128, as said below
- neighbors: int32 [4096, 6], P(('morton', 'sib')), may hold values from -1 to 4095, as said below
Outputs:
- stokes_force: float32 [4096, 3, 512], P(('morton', 'sib'))
- continuity: float32 [4096, 512], P(('morton', 'sib'))
- box_multipoles: float32 [8, 3, 216], P('morton')
- root_multipole: float32 [8, 3, 216], P('morton')
The draws below stay inside these ranges and needn't reach their ends.
Inputs may be any that keep to these rules, and one draw needn't show every extreme that they name: counts[r] live leaves occupy slots 0 to counts[r] - 1 of range r; some range is full in every draw. `morton_keys`: the key of a leaf of range r lies in that range's key block. `neighbors`: -1 marks the domain's boundary and every face of a padded slot. Otherwise the entry is a live leaf of the same Morton index m (any range), or one of the last 32 live leaves of a range of Morton index m - 1, or one of the first 32 leaves of a range of Morton index m + 1; in every draw the outermost leaf of both bands is referenced for every m that has such a neighbour.
All inputs are finite; a program needn't handle non-finite values.
Results may differ from the reference program's by a relative error of at most 0.0068.
Values may be sent and summed in bfloat16 or wider, within the bound.
No kernel may reach another device: no remote copies, remote signals or barrier semaphores. Data moves between devices by JAX's collectives and lax.ppermute only.
A program may use at most 64 MiB of HBM per device.

```python
import math
import jax
import jax.numpy as jnp
import numpy as np
from jax import lax

LEAF_DEV = 128
NODES = 512
DEG = 5
LMAX = 7
LMIN = 3
MOMENTS = 216
TOTAL = 4096
N_MORTON = 8
N_SIB = 4


def range_loads(key):
    ranges = TOTAL // LEAF_DEV
    quarter = LEAF_DEV // 4
    draw_ticks = jax.random.randint(key, (ranges,), 0, 65)
    leaf_loads = quarter + 3 * quarter * draw_ticks * draw_ticks // 4096
    fullest = jax.random.randint(jax.random.fold_in(key, 99), (), 0, ranges)
    return jnp.where(jnp.arange(ranges) == fullest, LEAF_DEV, leaf_loads).astype(jnp.int32)


def draw_counts(key, part):
    leaf_loads = range_loads(key)
    return leaf_loads


def draw_morton_keys(key, part):
    key = jax.random.fold_in(key, 7)
    ranges = TOTAL // LEAF_DEV
    key_range = (1 << 3 * LMAX) // ranges
    leaf_ids = jnp.arange(TOTAL, dtype=jnp.int32)
    offsets = jax.random.randint(key, (TOTAL,), 0, key_range)
    return (leaf_ids // LEAF_DEV * key_range + offsets).astype(jnp.int32)


def draw_neighbors(key, part):
    leaf_loads = range_loads(key)
    key = jax.random.fold_in(key, 5)
    ranges = TOTAL // LEAF_DEV
    mortons = ranges // N_SIB
    edge_rows = LEAF_DEV // 4
    leaf_ids = jnp.arange(TOTAL, dtype=jnp.int32)
    own_range = leaf_ids // LEAF_DEV
    slot_ids = leaf_ids % LEAF_DEV
    live_leaf = slot_ids < leaf_loads[own_range]
    keys_split = jax.random.split(key, 3)
    face_kinds = jax.random.randint(keys_split[0], (TOTAL, 6), 0, 6)
    target_sib = jax.random.randint(keys_split[1], (TOTAL, 6), 0, N_SIB)
    raw_slot = jax.random.randint(keys_split[2], (TOTAL, 6), 0, 1 << 20)
    morton_col = (own_range // N_SIB)[:, None]
    lower_ok = morton_col >= 1
    upper_ok = morton_col <= mortons - 2
    go_lower = (face_kinds == 3) & lower_ok
    go_upper = (face_kinds == 4) & upper_ok
    go_same = face_kinds <= 2
    target_morton = jnp.where(go_lower, morton_col - 1, jnp.where(go_upper, morton_col + 1, morton_col))
    target_range = target_morton * N_SIB + target_sib
    target_load = leaf_loads[target_range]
    target_slot = jnp.where(go_lower, target_load - edge_rows + raw_slot % edge_rows, jnp.where(go_upper, raw_slot % edge_rows, raw_slot % target_load))
    chosen = jnp.where(go_same | go_lower | go_upper, target_range * LEAF_DEV + target_slot, -1)
    first_leaf = (slot_ids == 0) & (own_range % N_SIB == 0)
    face_ids = jnp.arange(6)[None, :]
    force_low = first_leaf[:, None] & (face_ids == 0) & lower_ok
    force_up = first_leaf[:, None] & (face_ids == 1) & upper_ok
    low_range = jnp.clip((morton_col - 1) * N_SIB + (N_SIB - 1), 0, ranges - 1)
    low_target = low_range * LEAF_DEV + leaf_loads[low_range] - edge_rows
    up_target = (morton_col + 1) * N_SIB * LEAF_DEV + edge_rows - 1
    chosen = jnp.where(force_low, low_target, jnp.where(force_up, up_target, chosen))
    return jnp.where(live_leaf[:, None], chosen, -1).astype(jnp.int32)


def set_ends(entries, stream_key, smallest, top_value):
    dims = entries.shape
    spot = [jax.random.randint(jax.random.fold_in(stream_key, axis), (), 0, dims[axis]) for axis in range(len(dims))]
    entries = entries.at[tuple(spot)].set(smallest)
    longest = dims.index(max(dims))
    spot[longest] = (spot[longest] + 1) % dims[longest]
    return entries.at[tuple(spot)].set(top_value)


def shard_levels(key, dims, cuts, least, largest):
    def one(axis_at, blocks):
        steps = jax.random.uniform(jax.random.fold_in(jax.random.fold_in(key, 6), axis_at), (blocks,), jnp.float32, least / len(cuts), largest / len(cuts))
        return jnp.repeat(jnp.exp(steps), dims[axis_at] // blocks).reshape((-1,) + (1,) * (len(dims) - axis_at - 1))

    gain = one(*cuts[0])
    for cut in cuts[1:]:
        gain = gain * one(*cut)
    return gain


def gaussian(rng, dims, deviation, limit, cuts=(), held_as=jnp.bfloat16):
    factor_of = shard_levels(rng, dims, cuts, -0.22, 0.18) if cuts else 1.0
    values = jax.random.normal(rng, dims, jnp.float32) * deviation * factor_of
    return jnp.minimum(jnp.maximum(values, -limit), limit).astype(held_as)


def setup_inputs(seed: int = 0) -> dict:
    keys = jax.random.split(jax.random.key(seed), 8)
    return {
        "velocity": gaussian(keys[0], (TOTAL, 3, NODES), 1.0, 6.0, ((0, 32),)),
        "pressure": gaussian(keys[1], (TOTAL, NODES), 16.0, 96.0, ((0, 32),)),
        "viscosity": jnp.clip(jnp.exp(math.log(8.0) - 3.465736 * jax.random.uniform(keys[2], (TOTAL, NODES), jnp.float32) ** shard_levels(keys[2], (TOTAL, NODES), ((0, 32),), -0.2, 0.2)), 0.25, 8.0),
        "levels": set_ends(jax.random.randint(keys[3], (TOTAL,), LMIN, LMAX + 1), jax.random.fold_in(keys[3], 1), LMIN, LMAX).astype(jnp.int32),
        "morton_keys": draw_morton_keys(jax.random.fold_in(keys[7], 71), 0),
        "counts": draw_counts(jax.random.fold_in(keys[7], 71), 0),
        "neighbors": draw_neighbors(jax.random.fold_in(keys[7], 71), 0),
    }


penalty = 256.0
out_scale = 1.0 / 1024.0
mass_scale = 1.0 / 32.0
highest = lax.Precision.HIGHEST


def cheb_matrix():
    points = -np.cos(np.pi * np.arange(8) / 7.0)
    bary_weights = np.array([(-1.0) ** node_idx for node_idx in range(8)])
    bary_weights[0] = bary_weights[0] * 0.5
    bary_weights[7] = bary_weights[7] * 0.5
    derivative = np.zeros((8, 8))
    for row_idx in range(8):
        for col_idx in range(8):
            if row_idx != col_idx:
                derivative[row_idx, col_idx] = (bary_weights[col_idx] / bary_weights[row_idx]) / (points[row_idx] - points[col_idx])
        derivative[row_idx, row_idx] = -np.sum(derivative[row_idx])
    return points, derivative


def face_nodes():
    node_list = []
    for face_idx in range(6):
        face_dim = face_idx // 2
        face_side = face_idx % 2
        for first_idx in range(8):
            for second_idx in range(8):
                coords = [first_idx, second_idx]
                coords.insert(face_dim, 7 * face_side)
                node_list.append(64 * coords[0] + 8 * coords[1] + coords[2])
    return np.array(node_list, dtype=np.int32)


def derivative_along(nodal_field, diff_matrix, dim_idx):
    forms = ['...abc,Aa->...Abc', '...abc,Bb->...aBc', '...abc,Cc->...abC']
    return jnp.einsum(forms[dim_idx], nodal_field, diff_matrix, precision=highest)


def power_table(values):
    power_terms = [jnp.ones_like(values)]
    for power_idx in range(DEG):
        power_terms.append(power_terms[-1] * values)
    return jnp.stack(power_terms, axis=-1)


def leaf_geometry(morton_keys, levels):
    shift_bits = 3 * (LMAX - levels)
    anchor = jnp.left_shift(jnp.right_shift(morton_keys, shift_bits), shift_bits)
    leaf_span = jnp.left_shift(jnp.ones_like(levels), LMAX - levels).astype(jnp.float32)
    finest = 1.0 / float(2 ** LMAX)
    cell_coords = []
    for offset in (2, 1, 0):
        coordinate = jnp.zeros_like(anchor)
        for bit_idx in range(LMAX):
            coordinate = coordinate + jnp.left_shift(jnp.bitwise_and(jnp.right_shift(anchor, 3 * bit_idx + offset), 1), bit_idx)
        cell_coords.append((coordinate.astype(jnp.float32) + 0.5 * leaf_span) * finest)
    return jnp.stack(cell_coords, axis=-1), 0.5 * leaf_span * finest


def box_geometry(base_key, key_bits):
    finest = 1.0 / float(2 ** LMAX)
    centers = []
    side_lengths = []
    for offset in (2, 1, 0):
        free_bits = max(0, min(LMAX, (key_bits - offset + 2) // 3))
        coordinate = jnp.zeros_like(base_key)
        for bit_idx in range(LMAX):
            coordinate = coordinate + jnp.left_shift(jnp.bitwise_and(jnp.right_shift(base_key, 3 * bit_idx + offset), 1), bit_idx)
        side_len = float(2 ** free_bits) * finest
        centers.append(coordinate.astype(jnp.float32) * finest + 0.5 * side_len)
        side_lengths.append(side_len)
    return jnp.stack(centers), 0.5 * max(side_lengths)


def moments(forces, centers, radius, box_center, box_scale, points):
    leaf_count = forces.shape[0]
    nodal_field = forces.reshape(leaf_count, 3, 8, 8, 8)
    tables = []
    for dim_idx in range(3):
        position = centers[:, dim_idx][:, None] + radius[:, None] * points[None, :]
        tables.append(power_table((position - box_center[dim_idx]) / box_scale))
    step_one = jnp.einsum('liabc,lcz->liabz', nodal_field, tables[2], precision=highest)
    step_two = jnp.einsum('liabz,lby->liayz', step_one, tables[1], precision=highest)
    moment_sum = jnp.einsum('liayz,lax->ixyz', step_two, tables[0], precision=highest)
    return (moment_sum / 512.0).reshape(3, MOMENTS)


def leaf_forces(vel_rows, press_rows, visc_rows, nbr_faces, live_rows, diff_matrix, node_list):
    leaf_count = vel_rows.shape[0]
    nodal_field = vel_rows.astype(jnp.float32).reshape(leaf_count, 3, 8, 8, 8)
    gradient = jnp.stack([derivative_along(nodal_field, diff_matrix, dim_idx) for dim_idx in range(3)], axis=2).reshape(leaf_count, 3, 3, 512)
    press_field = press_rows.astype(jnp.float32).reshape(leaf_count, 8, 8, 8)
    press_grad = jnp.stack([derivative_along(press_field, diff_matrix, dim_idx) for dim_idx in range(3)], axis=1).reshape(leaf_count, 3, 512)
    stress = (visc_rows[:, None, None, :] * (gradient + jnp.swapaxes(gradient, 1, 2))).astype(jnp.bfloat16)
    stress_field = stress.astype(jnp.float32).reshape(leaf_count, 3, 3, 8, 8, 8)
    divergence = derivative_along(stress_field[:, :, 0], diff_matrix, 0) + derivative_along(stress_field[:, :, 1], diff_matrix, 1) + derivative_along(stress_field[:, :, 2], diff_matrix, 2)
    divergence = divergence.reshape(leaf_count, 3, 512)
    own_faces = vel_rows.astype(jnp.float32)[:, :, node_list]
    face_jump = jnp.zeros((leaf_count, 3, 512), jnp.float32).at[:, :, node_list].add(own_faces - nbr_faces)
    momentum = (penalty * visc_rows[:, None, :] * face_jump - divergence + press_grad) * out_scale
    mass_rows = -(gradient[:, 0, 0] + gradient[:, 1, 1] + gradient[:, 2, 2]) * mass_scale
    return jnp.where(live_rows[:, None, None], momentum, 0.0), jnp.where(live_rows[:, None], mass_rows, 0.0)


def reference(velocity, pressure, viscosity, levels, morton_keys, counts, neighbors):
    points_np, derivative_np = cheb_matrix()
    points = jnp.asarray(points_np.astype(np.float32)).astype(jnp.float32)
    rounded = lax.optimization_barrier(jnp.asarray(derivative_np.astype(np.float32)).astype(jnp.bfloat16))
    diff_matrix = rounded.astype(jnp.float32)
    node_list = face_nodes()
    opposite = velocity[:, :, node_list].reshape(TOTAL, 3, 6, 64).transpose(2, 0, 1, 3)
    key_range = 2 ** (3 * LMAX) // (N_MORTON * N_SIB)
    box_bits = 3 * LMAX - (N_MORTON.bit_length() - 1)
    group_leaves = N_SIB * LEAF_DEV
    root_center = jnp.full((3,), 0.5, jnp.float32)

    def per_box(morton_idx):
        first_leaf = morton_idx * group_leaves
        vel_rows = lax.dynamic_slice_in_dim(velocity, first_leaf, group_leaves, 0)
        press_rows = lax.dynamic_slice_in_dim(pressure, first_leaf, group_leaves, 0)
        visc_rows = lax.dynamic_slice_in_dim(viscosity, first_leaf, group_leaves, 0)
        level_rows = lax.dynamic_slice_in_dim(levels, first_leaf, group_leaves, 0)
        key_rows = lax.dynamic_slice_in_dim(morton_keys, first_leaf, group_leaves, 0)
        nbr_rows = lax.dynamic_slice_in_dim(neighbors, first_leaf, group_leaves, 0)
        leaf_ids = first_leaf + jnp.arange(group_leaves, dtype=jnp.int32)
        live_rows = (leaf_ids % LEAF_DEV) < jnp.take(counts, leaf_ids // LEAF_DEV)
        fetched = []
        for face_idx in range(6):
            target = nbr_rows[:, face_idx]
            rows_got = jnp.take(opposite[face_idx ^ 1], jnp.clip(target, 0, TOTAL - 1), axis=0)
            fetched.append(jnp.where((target >= 0)[:, None, None], rows_got, jnp.zeros_like(rows_got)))
        nbr_faces = jnp.stack(fetched, axis=2).reshape(group_leaves, 3, 384).astype(jnp.float32)
        forces, masses = leaf_forces(vel_rows, press_rows, visc_rows, nbr_faces, live_rows, diff_matrix, node_list)
        centers, radius = leaf_geometry(key_rows, level_rows)
        box_center, box_scale = box_geometry(morton_idx * (N_SIB * key_range), box_bits)
        box_part = moments(forces, centers, radius, box_center, box_scale, points)
        root_part = moments(forces, centers, radius, root_center, 0.5, points)
        return forces, masses, box_part, root_part

    forces, masses, box_parts, root_parts = lax.map(per_box, jnp.arange(N_MORTON, dtype=jnp.int32))
    root_total = jnp.sum(root_parts, axis=0)
    root_copies = jnp.broadcast_to(root_total[None], (N_MORTON, 3, MOMENTS))
    return forces.reshape(TOTAL, 3, NODES), masses.reshape(TOTAL, NODES), box_parts, root_copies
```

```python
import functools

import jax
import jax.numpy as jnp
import numpy as np
from jax import lax
from jax.experimental import pallas as pl
from jax.experimental.pallas import tpu as pltpu
from jax.sharding import PartitionSpec as P

DEG = 5
LMAX = 7
MOMENTS = 216
BAND = 32
NODES = 512
FACES = 384
ROWS = 288
LANES = 128

penalty = 256.0
out_scale = 1.0 / 1024.0
mass_scale = 1.0 / 32.0
highest = lax.Precision.HIGHEST
f32 = jnp.float32
bf16 = jnp.bfloat16


def cheb_matrix():
    points = -np.cos(np.pi * np.arange(8) / 7.0)
    weights = np.array([(-1.0) ** node for node in range(8)])
    weights[0] *= 0.5
    weights[7] *= 0.5
    derivative = np.zeros((8, 8))
    for row in range(8):
        for col in range(8):
            if row != col:
                derivative[row, col] = weights[col] / weights[row] / (points[row] - points[col])
        derivative[row, row] = -np.sum(derivative[row])
    return points, derivative


def operator_tables():
    _, derivative = cheb_matrix()
    along_x = np.kron(derivative, np.eye(64)).T
    along_y = np.kron(np.eye(4), np.kron(derivative, np.eye(8))).T
    along_z = np.kron(np.eye(32), derivative).T
    return along_x, np.concatenate([along_y, along_z], axis=1)


def face_table():
    pick = np.zeros((NODES, FACES))
    for face in range(6):
        for first in range(8):
            for second in range(8):
                coords = [first, second]
                coords.insert(face // 2, 7 * (face % 2))
                node = 64 * coords[0] + 8 * coords[1] + coords[2]
                pick[node, face * 64 + first * 8 + second] = 1.0
    return pick


def spread_table():
    pick = face_table()
    order = np.concatenate([np.arange(64) + 64 * (face ^ 1) for face in range(6)])
    return pick[:, order].T


def basis_tables():
    points, _ = cheb_matrix()
    powers = np.stack([points**power for power in range(DEG + 1)])
    basis = np.zeros((6, 6, 8, 8, 8, 8))
    basis[:, :, :6] = np.einsum("xa,yb,zc->xyzabc", powers, powers, powers)
    basis = basis.reshape(ROWS, NODES).astype(np.float32)
    top = np.asarray(basis.astype(jnp.bfloat16))
    rest = np.asarray((basis - top.astype(np.float32)).astype(jnp.bfloat16))
    return top, rest


def compact_table():
    table = np.zeros((ROWS, 256), np.float32)
    for group in range(36):
        for power in range(6):
            table[group * 8 + power, group * 6 + power] = 1.0 / 512.0
    return table


def box_table(morton_count):
    bits = morton_count.bit_length() - 1
    key_bits = 3 * LMAX - bits
    table = np.zeros((morton_count, 8, LANES), np.float32)
    for morton in range(morton_count):
        base = morton << key_bits
        lows, sides = [], []
        for offset in (2, 1, 0):
            free = max(0, min(LMAX, (key_bits - offset + 2) // 3))
            cell = sum(((base >> (3 * bit + offset)) & 1) << bit for bit in range(LMAX))
            sides.append(2.0**free / 2.0**LMAX)
            lows.append(cell / 2.0**LMAX)
        scale = 0.5 * max(sides)
        for dim in range(3):
            center = lows[dim] + 0.5 * sides[dim]
            table[morton, dim, 3:6] = (center - 0.5) / 0.5
            table[morton, 4 + dim] = center
        table[morton, 3] = 1.0
        table[morton, 3, 3:6] = scale / 0.5
        table[morton, 7] = 1.0 / scale
    return table.reshape(morton_count * 8, LANES)


def doubling(count):
    order = [0]
    for bit in reversed(range(count.bit_length() - 1)):
        order += [other ^ 1 << bit for other in order]
    return order


def swap(block, axis, apart):
    return lax.ppermute(block, axis, [(at, at ^ apart) for at in range(lax.axis_size(axis))])


def dot(left, right):
    return jnp.dot(left, right, preferred_element_type=f32)


def dot_nt(left, right, precision=None):
    return lax.dot_general(
        left, right, (((1,), (1,)), ((), ())), preferred_element_type=f32, precision=precision
    )


def pack_kernel(counts_ref, vel_ref, pick_ref, faces_ref, low_ref, high_ref):
    sib_count = lax.axis_size("sib")
    own = lax.axis_index("morton") * sib_count + lax.axis_index("sib")
    for comp in range(3):
        picked = dot(vel_ref[comp], pick_ref[...]).astype(bf16)
        for dim in range(3):
            lane = (dim * 3 + comp) * LANES
            faces_ref[:, lane : lane + LANES] = picked[:, dim * LANES : (dim + 1) * LANES]
    low_ref[...] = faces_ref[:BAND, :]
    first = counts_ref[own] - BAND
    leaf_count = faces_ref.shape[0]
    row = lax.broadcasted_iota(jnp.int32, (BAND, leaf_count), 0)
    col = lax.broadcasted_iota(jnp.int32, (BAND, leaf_count), 1)
    pick_rows = jnp.where(col == row + first, 1.0, 0.0).astype(bf16)
    high_ref[...] = dot(pick_rows, faces_ref[...]).astype(bf16)


def pre_kernel(
    counts_ref, vel_ref, press_ref, visc_ref, levels_ref, keys_ref, nbrs_ref, dx_ref, dyz_ref, box_ref,
    part_ref, mass_ref, spots_ref, geom_ref,
):
    sib_count = lax.axis_size("sib")
    morton_count = lax.axis_size("morton")
    morton = lax.axis_index("morton")
    own = morton * sib_count + lax.axis_index("sib")
    leaf_count = mass_ref.shape[0]
    live = lax.broadcasted_iota(jnp.int32, (leaf_count, NODES), 0) < counts_ref[own]
    node = lax.broadcasted_iota(jnp.int32, (1, NODES), 1)
    touching = jnp.zeros((1, NODES), f32)
    for shift in (6, 3, 0):
        idx = jnp.bitwise_and(jnp.right_shift(node, shift), 7)
        touching = touching + jnp.where((idx == 0) | (idx == 7), 1.0, 0.0)

    def gradient(field):
        halves = [dot(field[:, at : at + 256], dyz_ref[...]) for at in (0, 256)]
        return (
            dot(field, dx_ref[...]),
            jnp.concatenate([half[:, :256] for half in halves], axis=1),
            jnp.concatenate([half[:, 256:] for half in halves], axis=1),
        )

    visc = visc_ref[...]
    grads = [gradient(vel_ref[comp]) for comp in range(3)]
    mass = -(grads[0][0] + grads[1][1] + grads[2][2]) * mass_scale
    mass_ref[...] = jnp.where(live, mass, 0.0)
    press_grad = gradient(press_ref[...])
    stress = {}
    for first in range(3):
        for second in range(first, 3):
            value = (visc * (grads[first][second] + grads[second][first])).astype(bf16)
            stress[first, second] = stress[second, first] = value
    for comp in range(3):
        div = dot(stress[comp, 0], dx_ref[...])
        rest = [
            dot(stress[comp, 1][:, at : at + 256], dyz_ref[:, :256])
            + dot(stress[comp, 2][:, at : at + 256], dyz_ref[:, 256:])
            for at in (0, 256)
        ]
        div = div + jnp.concatenate(rest, axis=1)
        jump = touching * vel_ref[comp].astype(f32)
        part = (penalty * visc * jump - div + press_grad[comp]) * out_scale
        part_ref[comp] = jnp.where(live, part, 0.0)

    nbrs = nbrs_ref[...]
    target = jnp.maximum(nbrs, 0)
    owner = target // leaf_count
    slot = target - owner * leaf_count
    owner_morton = owner // sib_count
    owner_sib = owner - owner_morton * sib_count
    apart = jnp.bitwise_xor(owner_sib, lax.axis_index("sib"))
    piece = jnp.zeros_like(apart)
    for at, other in enumerate(doubling(sib_count)):
        piece = jnp.where(apart == other, at, piece)
    step = owner_morton - morton
    below = jnp.maximum(morton - 1, 0) * sib_count
    band_start = jnp.zeros_like(slot)
    for sib in range(sib_count):
        band_start = jnp.where(owner_sib == sib, counts_ref[below + sib] - BAND, band_start)
    base = sib_count * leaf_count
    spot = jnp.where(
        step == 0,
        piece * leaf_count + slot,
        base + piece * (2 * BAND) + jnp.where(step < 0, slot - band_start, BAND + slot),
    )
    spot = jnp.where(nbrs >= 0, spot, -1).astype(f32)
    padded = jnp.concatenate([spot, jnp.full((LANES - spot.shape[0], leaf_count), -1.0, f32)], axis=0)
    spots_ref[...] = padded.T

    box = box_ref[pl.ds(pl.multiple_of(morton * 8, 8), 8), :]
    shift_bits = 3 * (LMAX - levels_ref[...])
    anchor = jnp.left_shift(jnp.right_shift(keys_ref[...], shift_bits), shift_bits)
    span = jnp.left_shift(jnp.ones_like(shift_bits), LMAX - levels_ref[...]).astype(f32)
    finest = 1.0 / float(2**LMAX)
    rows = []
    for dim, offset in enumerate((2, 1, 0)):
        cell = jnp.zeros_like(anchor)
        for bit in range(LMAX):
            picked = jnp.bitwise_and(jnp.right_shift(anchor, 3 * bit + offset), 1)
            cell = cell + jnp.left_shift(picked, bit)
        center = (cell.astype(f32) + 0.5 * span) * finest
        rows.append((center - box[4 + dim : 5 + dim, :]) * box[7:8, :])
    rows.append(0.5 * span * finest * box[7:8, :])
    rows.append(jnp.zeros((4, leaf_count), f32))
    geom_ref[...] = jnp.concatenate(rows, axis=0)


def shifted(tiles, geom):
    width = tiles[0].shape
    scale = jnp.broadcast_to(geom[3:4, :], width)
    level = lax.broadcasted_iota(jnp.int32, width, 0)
    depth = jnp.ones(width, f32)
    for power in range(1, DEG + 1):
        depth = depth * jnp.where(level >= power, scale, 1.0)
    scales = [depth]
    for _ in range(2 * DEG):
        scales.append(scales[-1] * scale)
    tiles = [tile * scales[at // 6 + at % 6] for at, tile in enumerate(tiles)]
    along = [jnp.broadcast_to(geom[dim : dim + 1, :], width) for dim in range(3)]
    for low in range(1, DEG + 1):
        for power in range(DEG, low - 1, -1):
            for other in range(6):
                at = power * 6 + other
                tiles[at] = tiles[at] + along[0] * tiles[at - 6]
            for other in range(6):
                at = other * 6 + power
                tiles[at] = tiles[at] + along[1] * tiles[at - 1]
    steps = [jnp.where(level >= low, along[2], 0.0) for low in range(1, DEG + 1)]
    for step in steps:
        tiles = [tile + step * pltpu.roll(tile, 1, 0) for tile in tiles]
    return tiles


def post_kernel(
    part_ref, visc_ref, spots_ref, geom_ref, box_ref, spread_ref, top_ref, rest_ref, compact_ref, *refs
):
    window_refs, (force_ref, sums_ref, raw_ref) = refs[:-3], refs[-3:]
    morton = lax.axis_index("morton")
    leaf_count = visc_ref.shape[0]
    spots = spots_ref[...].astype(jnp.int32)
    lane = lax.broadcasted_iota(jnp.int32, (leaf_count, FACES), 1)
    upper = jnp.bitwise_and(lane, 64) > 0
    window_rows = sum(window_ref.shape[0] for window_ref in window_refs)
    cols = lax.broadcasted_iota(jnp.int32, (leaf_count, window_rows), 1)
    chosen = []
    for dim in range(3):
        at = dim * FACES
        window = jnp.concatenate([ref[:, at : at + FACES] for ref in window_refs], axis=0)
        sides = []
        for side in range(2):
            face = 2 * dim + side
            place = jnp.broadcast_to(spots[:, face : face + 1], (leaf_count, 1))
            onehot = jnp.where(cols == place, 1.0, 0.0).astype(bf16)
            sides.append(dot(onehot, window))
        chosen.append(jnp.where(upper, sides[0], sides[1]).astype(bf16))
    weight = visc_ref[...] * (penalty * out_scale)
    highs, lows = [], []
    for comp in range(3):
        at = comp * LANES
        picked = jnp.concatenate([block[:, at : at + LANES] for block in chosen], axis=1)
        force = part_ref[comp] - weight * dot(picked, spread_ref[...])
        force_ref[comp] = force
        high = force.astype(bf16)
        highs.append(high)
        lows.append((force - high.astype(f32)).astype(bf16))
    high = jnp.concatenate(highs, axis=0)
    low = jnp.concatenate(lows, axis=0)
    raw_ref[...] = dot_nt(top_ref[...], high) + dot_nt(top_ref[...], low) + dot_nt(rest_ref[...], high)
    geom = jnp.concatenate([geom_ref[...]] * 3, axis=1)
    tiles = shifted([raw_ref[8 * at : 8 * at + 8, :] for at in range(36)], geom)
    moved = jnp.concatenate(tiles, axis=0)
    group = lax.broadcasted_iota(jnp.int32, (3 * leaf_count, LANES), 0) // leaf_count
    column = lax.broadcasted_iota(jnp.int32, (3 * leaf_count, LANES), 1)
    gather = jnp.where((group == column) | (group + 3 == column), 1.0, 0.0)
    summed = jnp.dot(moved, gather, precision=highest, preferred_element_type=f32)
    box = box_ref[pl.ds(pl.multiple_of(morton * 8, 8), 8), :]
    both = shifted([summed[8 * at : 8 * at + 8, :] for at in range(36)], box)
    flat = jnp.concatenate(both, axis=0).T
    sums = jnp.dot(flat[:8], compact_ref[...], precision=highest, preferred_element_type=f32)
    for other in range(sums_ref.shape[0]):
        sums_ref[other] = sums


def final_kernel(sums_ref, box_ref, root_ref):
    sib_count = lax.axis_size("sib")
    first = lax.axis_index("morton") * sib_count
    box = sums_ref[first]
    for sib in range(1, sib_count):
        box = box + sums_ref[first + sib]
    root = jnp.sum(sums_ref[...], axis=0)
    for comp in range(3):
        box_ref[comp] = box[comp : comp + 1, :MOMENTS]
        root_ref[comp] = root[3 + comp : 4 + comp, :MOMENTS]


def call(kernel, shapes, flops, scalars, operands, scratch=(), limit=32):
    specs = [pl.BlockSpec(memory_space=pltpu.SMEM)] * len(scalars)
    specs += [pl.BlockSpec(memory_space=pltpu.VMEM)] * len(operands)
    moved = sum(array.size * array.dtype.itemsize for array in operands)
    return pl.pallas_call(
        kernel,
        out_shape=[jax.ShapeDtypeStruct(shape, dtype) for shape, dtype in shapes],
        in_specs=specs,
        out_specs=[pl.BlockSpec(memory_space=pltpu.VMEM)] * len(shapes),
        scratch_shapes=list(scratch),
        compiler_params=pltpu.CompilerParams(vmem_limit_bytes=limit * 2**20),
        cost_estimate=pl.CostEstimate(flops=flops, bytes_accessed=moved, transcendentals=0),
    )(*scalars, *operands)


def on_device(velocity, pressure, viscosity, levels, morton_keys, counts, neighbors):
    leaf_count = velocity.shape[0]
    morton_count = lax.axis_size("morton")
    along_x, along_yz = operator_tables()
    dx_table = jnp.asarray(along_x.astype(np.float32)).astype(bf16)
    dyz_table = jnp.asarray(along_yz.astype(np.float32)).astype(bf16)
    pick = jnp.asarray(face_table().astype(np.float32)).astype(bf16)
    spread = jnp.asarray(spread_table().astype(np.float32)).astype(bf16)
    top, rest = basis_tables()
    boxes = jnp.asarray(box_table(morton_count))
    vel = jnp.transpose(velocity, (1, 0, 2))
    nbrs = jnp.transpose(neighbors, (1, 0))

    width = 3 * FACES
    faces, low, high = call(
        pack_kernel,
        [((leaf_count, width), bf16), ((BAND, width), bf16), ((BAND, width), bf16)],
        4 * 10**8,
        [counts],
        [vel, pick],
        limit=60,
    )
    ahead = [(at, at + 1) for at in range(morton_count - 1)]
    back = [(target, source) for source, target in ahead]
    sib_count = lax.axis_size("sib")
    part, continuity, spots, geom = call(
        pre_kernel,
        [
            ((3, leaf_count, NODES), f32),
            ((leaf_count, NODES), f32),
            ((leaf_count, LANES), f32),
            ((8, leaf_count), f32),
        ],
        2 * 10**9,
        [counts],
        [
            vel, pressure, viscosity, levels.reshape(1, -1), morton_keys.reshape(1, -1), nbrs,
            dx_table, dyz_table, boxes,
        ],
    )
    window = [faces]
    bands = [jnp.concatenate([lax.ppermute(high, "morton", ahead), lax.ppermute(low, "morton", back)], axis=0)]
    bands[0], part = lax.optimization_barrier((bands[0], part))
    for bit in reversed(range(sib_count.bit_length() - 1)):
        window += [swap(piece, "sib", 1 << bit) for piece in window]
        held = jnp.concatenate(bands, axis=0)
        bands = [held, swap(held, "sib", 1 << bit)]

    force, sums = call(
        post_kernel,
        [((3, leaf_count, NODES), f32), ((morton_count * sib_count, 8, 256), f32)],
        10**9,
        [],
        [
            part, viscosity, spots, geom, boxes, spread, jnp.asarray(top), jnp.asarray(rest),
            jnp.asarray(compact_table()), *window, *bands,
        ],
        [pltpu.VMEM((ROWS, 3 * leaf_count), f32)],
    )
    every = lax.all_to_all(sums, ("morton", "sib"), 0, 0, tiled=True)
    box, root = call(
        final_kernel,
        [((3, 1, MOMENTS), f32), ((3, 1, MOMENTS), f32)],
        10**5,
        [],
        [every],
    )
    return (
        jnp.transpose(force, (1, 0, 2)),
        continuity,
        jnp.transpose(box, (1, 0, 2)),
        jnp.transpose(root, (1, 0, 2)),
    )


def solution(mesh):
    spread_all = ("morton", "sib")
    in_specs = (
        P(spread_all, None, None),
        P(spread_all, None),
        P(spread_all, None),
        P(spread_all),
        P(spread_all),
        P(),
        P(spread_all, None),
    )
    out_specs = (
        P(spread_all, None, None),
        P(spread_all, None),
        P("morton", None, None),
        P("morton", None, None),
    )
    return jax.shard_map(
        on_device, mesh=mesh, in_specs=in_specs, out_specs=out_specs, check_vma=False
    )
```

```python
import math

import jax
import jax.numpy as jnp
import numpy as np
from jax import lax
from jax.experimental import pallas as pl
from jax.experimental.pallas import tpu as pltpu
from jax.sharding import PartitionSpec as P

DEG = 5
LMAX = 7
MOMENTS = 216
BAND = 32
NODES = 512
FACES = 384
ROWS = 288
LANES = 128

penalty = 256.0
out_scale = 1.0 / 1024.0
mass_scale = 1.0 / 32.0
highest = lax.Precision.HIGHEST
f32 = jnp.float32
bf16 = jnp.bfloat16


def cheb_matrix():
    points = -np.cos(np.pi * np.arange(8) / 7.0)
    weights = np.array([(-1.0) ** node for node in range(8)])
    weights[0] *= 0.5
    weights[7] *= 0.5
    derivative = np.zeros((8, 8))
    for row in range(8):
        for col in range(8):
            if row != col:
                derivative[row, col] = weights[col] / weights[row] / (points[row] - points[col])
        derivative[row, row] = -np.sum(derivative[row])
    return points, derivative


def operator_tables():
    _, derivative = cheb_matrix()
    along_x = np.kron(derivative, np.eye(64)).T
    along_y = np.kron(np.eye(4), np.kron(derivative, np.eye(8))).T
    along_z = np.kron(np.eye(32), derivative).T
    return along_x, np.concatenate([along_y, along_z], axis=1)


def face_table():
    pick = np.zeros((NODES, FACES))
    for face in range(6):
        for first in range(8):
            for second in range(8):
                coords = [first, second]
                coords.insert(face // 2, 7 * (face % 2))
                node = 64 * coords[0] + 8 * coords[1] + coords[2]
                pick[node, face * 64 + first * 8 + second] = 1.0
    return pick


def spread_table():
    pick = face_table()
    order = np.concatenate([np.arange(64) + 64 * (face ^ 1) for face in range(6)])
    return pick[:, order].T


def basis_tables():
    points, _ = cheb_matrix()
    powers = np.stack([points**power for power in range(DEG + 1)])
    basis = np.zeros((6, 6, 8, 8, 8, 8))
    basis[:, :, :6] = np.einsum("xa,yb,zc->xyzabc", powers, powers, powers)
    basis = basis.reshape(ROWS, NODES).astype(np.float32)
    top = np.asarray(basis.astype(jnp.bfloat16))
    rest = np.asarray((basis - top.astype(np.float32)).astype(jnp.bfloat16))
    return top, rest


def compact_table():
    table = np.zeros((ROWS, 256), np.float32)
    for group in range(36):
        for power in range(6):
            table[group * 8 + power, group * 6 + power] = 1.0 / 512.0
    return table


def box_table(morton_count):
    bits = morton_count.bit_length() - 1
    key_bits = 3 * LMAX - bits
    table = np.zeros((morton_count, 8, LANES), np.float32)
    for morton in range(morton_count):
        base = morton << key_bits
        lows, sides = [], []
        for offset in (2, 1, 0):
            free = max(0, min(LMAX, (key_bits - offset + 2) // 3))
            cell = sum(((base >> (3 * bit + offset)) & 1) << bit for bit in range(LMAX))
            sides.append(2.0**free / 2.0**LMAX)
            lows.append(cell / 2.0**LMAX)
        scale = 0.5 * max(sides)
        for dim in range(3):
            center = lows[dim] + 0.5 * sides[dim]
            table[morton, dim, 3:6] = (center - 0.5) / 0.5
            table[morton, 4 + dim] = center
        table[morton, 3] = 1.0
        table[morton, 3, 3:6] = scale / 0.5
        table[morton, 7] = 1.0 / scale
    return table.reshape(morton_count * 8, LANES)


def doubling(count):
    order = [0]
    for bit in reversed(range(count.bit_length() - 1)):
        order += [other ^ 1 << bit for other in order]
    return order


def swap(block, axis, apart):
    return lax.ppermute(block, axis, [(at, at ^ apart) for at in range(lax.axis_size(axis))])


def move_tables(morton_count):
    bits = 3 * LMAX - (morton_count.bit_length() - 1)
    ratio = 2.0 ** max(max(0, min(LMAX, (bits - offset + 2) // 3)) for offset in range(3)) / 2.0**LMAX
    shift = np.zeros((256, 256), np.float32)
    powers = np.zeros((256, 256), np.int32)
    triples = list(np.ndindex(6, 6, 6))
    for row, beta in enumerate(triples):
        for col, alpha in enumerate(triples):
            if all(b <= a for a, b in zip(alpha, beta)):
                shift[row, col] = math.prod(math.comb(a, b) for a, b in zip(alpha, beta)) * ratio ** sum(beta)
                powers[row, col] = sum((a - b) << 3 * dim for dim, (a, b) in enumerate(zip(alpha, beta)))
    return shift, powers


def pairs(block, first):
    route = []
    for low in range(first, lax.axis_size("morton") - 1, 2):
        route += [(low, low + 1), (low + 1, low)]
    return lax.ppermute(block, "morton", route)


def dot(left, right):
    return jnp.dot(left, right, preferred_element_type=f32)


def dot_nt(left, right, precision=None):
    return lax.dot_general(
        left, right, (((1,), (1,)), ((), ())), preferred_element_type=f32, precision=precision
    )


def pack_kernel(
    counts_ref, vel_hbm, pick_hbm, faces_hbm, even_hbm, odd_hbm, vel_ref, pick_ref, faces_ref, bands_ref, sems
):
    sib_count = lax.axis_size("sib")
    morton = lax.axis_index("morton")
    own = morton * sib_count + lax.axis_index("sib")
    loads = [
        pltpu.make_async_copy(vel_hbm, vel_ref, sems.at[0]),
        pltpu.make_async_copy(pick_hbm, pick_ref, sems.at[1]),
    ]
    for load in loads:
        load.start()
    first = counts_ref[own] - BAND
    leaf_count = faces_ref.shape[0]
    row = lax.broadcasted_iota(jnp.int32, (BAND, leaf_count), 0)
    col = lax.broadcasted_iota(jnp.int32, (BAND, leaf_count), 1)
    last_rows = jnp.where(col == row + first, 1.0, 0.0).astype(bf16)
    is_odd = jnp.bitwise_and(morton, 1) == 1
    loads[0].wait()
    fields = [vel_ref[comp] for comp in range(3)]
    fields += [dot(last_rows, vel_ref[comp]).astype(bf16) for comp in range(3)]
    fields = jnp.concatenate(fields, axis=0)
    loads[1].wait()
    stores = []
    for dim in range(3):
        picked = dot(fields, pick_ref[:, dim * LANES : (dim + 1) * LANES]).astype(bf16)
        for comp in range(3):
            lane = (dim * 3 + comp) * LANES
            faces_ref[:, lane : lane + LANES] = picked[comp * leaf_count : (comp + 1) * leaf_count]
            at = 3 * leaf_count + comp * BAND
            low = picked[comp * leaf_count : comp * leaf_count + BAND]
            high = picked[at : at + BAND]
            bands_ref[0, :, lane : lane + LANES] = jnp.where(is_odd, low, high)
            bands_ref[1, :, lane : lane + LANES] = jnp.where(is_odd, high, low)
        lanes = pl.ds(dim * FACES, FACES)
        stores.append(pltpu.make_async_copy(faces_ref.at[:, lanes], faces_hbm.at[:, lanes], sems.at[2 + dim]))
        stores[-1].start()
    stores.append(pltpu.make_async_copy(bands_ref.at[0], even_hbm, sems.at[5]))
    stores.append(pltpu.make_async_copy(bands_ref.at[1], odd_hbm, sems.at[6]))
    for store in stores[3:]:
        store.start()
    for store in stores:
        store.wait()


def pre_kernel(
    counts_ref, vel_ref, press_ref, visc_ref, levels_ref, keys_ref, nbrs_ref, dx_ref, dyz_ref, box_ref,
    shift_ref, powers_ref, part_ref, mass_ref, spots_ref, geom_ref, move_ref,
):
    sib_count = lax.axis_size("sib")
    morton_count = lax.axis_size("morton")
    morton = lax.axis_index("morton")
    own = morton * sib_count + lax.axis_index("sib")
    leaf_count = mass_ref.shape[0]
    live = lax.broadcasted_iota(jnp.int32, (leaf_count, NODES), 0) < counts_ref[own]
    node = lax.broadcasted_iota(jnp.int32, (1, NODES), 1)
    touching = jnp.zeros((1, NODES), f32)
    for shift in (6, 3, 0):
        idx = jnp.bitwise_and(jnp.right_shift(node, shift), 7)
        touching = touching + jnp.where((idx == 0) | (idx == 7), 1.0, 0.0)

    def rows(stack, at):
        return stack[at * leaf_count : (at + 1) * leaf_count]

    visc = visc_ref[...]
    fields = jnp.concatenate([vel_ref[0], vel_ref[1], vel_ref[2], press_ref[...]], axis=0)
    halves = [dot(fields[:, at : at + 256], dyz_ref[...]) for at in (0, 256)]
    grads = [
        dot(fields, dx_ref[...]),
        jnp.concatenate([half[:, :256] for half in halves], axis=1),
        jnp.concatenate([half[:, 256:] for half in halves], axis=1),
    ]
    mass = -(rows(grads[0], 0) + rows(grads[1], 1) + rows(grads[2], 2)) * mass_scale
    mass_ref[...] = jnp.where(live, mass, 0.0)
    stress = {}
    for first in range(3):
        for second in range(first, 3):
            value = (visc * (rows(grads[second], first) + rows(grads[first], second))).astype(bf16)
            stress[first, second] = stress[second, first] = value
    columns = [jnp.concatenate([stress[comp, dim] for comp in range(3)], axis=0) for dim in range(3)]
    rest = [
        dot(columns[1][:, at : at + 256], dyz_ref[:, :256]) + dot(columns[2][:, at : at + 256], dyz_ref[:, 256:])
        for at in (0, 256)
    ]
    div = dot(columns[0], dx_ref[...]) + jnp.concatenate(rest, axis=1)
    for comp in range(3):
        jump = touching * vel_ref[comp].astype(f32)
        part = (penalty * visc * jump - rows(div, comp) + rows(grads[comp], 3)) * out_scale
        part_ref[comp] = jnp.where(live, part, 0.0)

    nbrs = nbrs_ref[...]
    target = jnp.maximum(nbrs, 0)
    owner = target // leaf_count
    slot = target - owner * leaf_count
    owner_morton = owner // sib_count
    owner_sib = owner - owner_morton * sib_count
    apart = jnp.bitwise_xor(owner_sib, lax.axis_index("sib"))
    piece = jnp.zeros_like(apart)
    for at, other in enumerate(doubling(sib_count)):
        piece = jnp.where(apart == other, at, piece)
    step = owner_morton - morton
    below = jnp.maximum(morton - 1, 0) * sib_count
    band_start = jnp.zeros_like(slot)
    for sib in range(sib_count):
        band_start = jnp.where(owner_sib == sib, counts_ref[below + sib] - BAND, band_start)
    base = sib_count * leaf_count
    below_at = BAND * (1 - jnp.bitwise_and(morton, 1))
    spot = jnp.where(
        step == 0,
        piece * leaf_count + slot,
        base + piece * (2 * BAND) + jnp.where(step < 0, slot - band_start + below_at, slot + BAND - below_at),
    )
    spot = jnp.where(nbrs >= 0, spot, -1).astype(f32)
    padded = jnp.concatenate([spot, jnp.full((LANES - spot.shape[0], leaf_count), -1.0, f32)], axis=0)
    spots_ref[...] = padded.T

    box = box_ref[pl.ds(pl.multiple_of(morton * 8, 8), 8), :]
    shift_bits = 3 * (LMAX - levels_ref[...])
    anchor = jnp.left_shift(jnp.right_shift(keys_ref[...], shift_bits), shift_bits)
    span = jnp.left_shift(jnp.ones_like(shift_bits), LMAX - levels_ref[...]).astype(f32)
    finest = 1.0 / float(2**LMAX)
    places = []
    for dim, offset in enumerate((2, 1, 0)):
        cell = jnp.zeros_like(anchor)
        for bit in range(LMAX):
            picked = jnp.bitwise_and(jnp.right_shift(anchor, 3 * bit + offset), 1)
            cell = cell + jnp.left_shift(picked, bit)
        center = (cell.astype(f32) + 0.5 * span) * finest
        places.append((center - box[4 + dim : 5 + dim, :]) * box[7:8, :])
    places.append(0.5 * span * finest * box[7:8, :])
    places.append(jnp.zeros((4, leaf_count), f32))
    geom_ref[...] = jnp.concatenate(places, axis=0)
    move = shift_ref[...]
    powers = powers_ref[...]
    for dim in range(3):
        power = jnp.bitwise_and(jnp.right_shift(powers, 3 * dim), 7)
        along = box[dim : dim + 1, 3:4]
        factor = jnp.ones((1, 1), f32)
        for degree in range(1, DEG + 1):
            factor = factor * along
            move = move * jnp.where(power == degree, factor, 1.0)
    move_ref[...] = move


def shifted(tiles, geom):
    width = tiles[0].shape
    scale = jnp.broadcast_to(geom[3:4, :], width)
    level = lax.broadcasted_iota(jnp.int32, width, 0)
    depth = jnp.ones(width, f32)
    for power in range(1, DEG + 1):
        depth = depth * jnp.where(level >= power, scale, 1.0)
    scales = [depth]
    for _ in range(2 * DEG):
        scales.append(scales[-1] * scale)
    tiles = [tile * scales[at // 6 + at % 6] for at, tile in enumerate(tiles)]
    along = [jnp.broadcast_to(geom[dim : dim + 1, :], width) for dim in range(3)]
    for low in range(1, DEG + 1):
        for power in range(DEG, low - 1, -1):
            for other in range(6):
                at = power * 6 + other
                tiles[at] = tiles[at] + along[0] * tiles[at - 6]
            for other in range(6):
                at = other * 6 + power
                tiles[at] = tiles[at] + along[1] * tiles[at - 1]
    steps = [jnp.where(level >= low, along[2], 0.0) for low in range(1, DEG + 1)]
    for step in steps:
        tiles = [tile + step * pltpu.roll(tile, 1, 0) for tile in tiles]
    return tiles


def post_kernel(
    part_ref, visc_ref, spots_ref, geom_ref, box_ref, spread_ref, basis_ref, compact_ref, *refs
):
    window_refs, (force_hbm, sums_ref, force_ref, raw_ref, sems) = refs[:-5], refs[-5:]
    morton = lax.axis_index("morton")
    leaf_count = visc_ref.shape[0]
    spots = spots_ref[...].astype(jnp.int32)
    lane = lax.broadcasted_iota(jnp.int32, (leaf_count, FACES), 1)
    upper = jnp.bitwise_and(lane, 64) > 0
    window_rows = sum(window_ref.shape[0] for window_ref in window_refs)
    cols = lax.broadcasted_iota(jnp.int32, (leaf_count, window_rows), 1)
    chosen = []
    for dim in range(3):
        at = dim * FACES
        window = jnp.concatenate([ref[:, at : at + FACES] for ref in window_refs], axis=0)
        places = [jnp.broadcast_to(spots[:, face : face + 1], (leaf_count, 1)) for face in (2 * dim, 2 * dim + 1)]
        onehot = [jnp.where(cols == place, 1.0, 0.0).astype(bf16) for place in places]
        both = dot(jnp.concatenate(onehot, axis=0), window)
        chosen.append(jnp.where(upper, both[:leaf_count], both[leaf_count:]).astype(bf16))
    weight = visc_ref[...] * (penalty * out_scale)
    highs, lows, stores = [], [], []
    picked = [
        jnp.concatenate([block[:, comp * LANES : (comp + 1) * LANES] for block in chosen], axis=1) for comp in range(3)
    ]
    jumps = dot(jnp.concatenate(picked, axis=0), spread_ref[...])
    for comp in range(3):
        force = part_ref[comp] - weight * jumps[comp * leaf_count : (comp + 1) * leaf_count]
        force_ref[comp] = force
        stores.append(pltpu.make_async_copy(force_ref.at[comp], force_hbm.at[comp], sems.at[comp]))
        stores[-1].start()
        high = force.astype(bf16)
        highs.append(high)
        lows.append((force - high.astype(f32)).astype(bf16))
    high = jnp.concatenate(highs, axis=0)
    low = jnp.concatenate(lows, axis=0)
    raw = dot_nt(basis_ref[...], high)
    raw_ref[...] = raw[:ROWS] + raw[ROWS:] + dot_nt(basis_ref[:ROWS, :], low)
    geom = jnp.concatenate([geom_ref[...]] * 3, axis=1)
    tiles = shifted([raw_ref[8 * at : 8 * at + 8, :] for at in range(36)], geom)
    moved = jnp.concatenate(tiles, axis=0)
    group = lax.broadcasted_iota(jnp.int32, (3 * leaf_count, LANES), 0) // leaf_count
    column = lax.broadcasted_iota(jnp.int32, (3 * leaf_count, LANES), 1)
    gather = jnp.where((group == column) | (group + 3 == column), 1.0, 0.0)
    summed = jnp.dot(moved, gather, precision=highest, preferred_element_type=f32)
    box = box_ref[pl.ds(pl.multiple_of(morton * 8, 8), 8), :]
    both = shifted([summed[8 * at : 8 * at + 8, :] for at in range(36)], box)
    flat = jnp.concatenate(both, axis=0).T
    sums = jnp.dot(flat[:8], compact_ref[...], precision=highest, preferred_element_type=f32)
    sums_ref[...] = sums
    for store in stores:
        store.wait()


def share_kernel(own_ref, other_ref, sums_ref):
    sums = own_ref[...] + other_ref[...]
    blank = jnp.zeros((2, LANES), f32)
    to_box = jnp.concatenate([sums[:3, :LANES], sums[:3, LANES:], blank], axis=0)
    to_root = jnp.concatenate([sums[3:6, :LANES], sums[3:6, LANES:], blank], axis=0)
    morton = lax.axis_index("morton")
    in_box = lax.axis_size("sib") // 2
    for other in range(sums_ref.shape[0]):
        sums_ref[other] = jnp.where(morton == other // in_box, to_box, to_root)


def final_kernel(sums_ref, move_ref, box_ref, root_ref):
    in_box = lax.axis_size("sib") // 2
    morton = lax.axis_index("morton")
    box = jnp.zeros(sums_ref.shape[1:], f32)
    root = jnp.zeros(sums_ref.shape[1:], f32)
    for group in range(sums_ref.shape[0] // in_box):
        total = jnp.sum(sums_ref[group * in_box : (group + 1) * in_box], axis=0)
        box = box + jnp.where(morton == group, total, 0.0)
        root = root + jnp.where(morton == group, 0.0, total)
    box = jnp.concatenate([box[:3], box[3:6]], axis=1)
    root = jnp.concatenate([root[:3], root[3:6]], axis=1)
    box8 = jnp.concatenate([box, jnp.zeros((5, 2 * LANES), f32)], axis=0)
    root = root + jnp.dot(box8, move_ref[...], precision=highest, preferred_element_type=f32)[:3]
    for comp in range(3):
        box_ref[comp] = box[comp : comp + 1, :MOMENTS]
        root_ref[comp] = root[comp : comp + 1, :MOMENTS]


def call(kernel, shapes, flops, scalars, operands, scratch=(), place=pltpu.VMEM, outs=None, grant=32):
    specs = [pl.BlockSpec(memory_space=pltpu.SMEM)] * len(scalars)
    specs += [pl.BlockSpec(memory_space=place)] * len(operands)
    outs = outs or [pltpu.VMEM] * len(shapes)
    moved = sum(array.size * array.dtype.itemsize for array in operands)
    return pl.pallas_call(
        kernel,
        out_shape=[jax.ShapeDtypeStruct(shape, dtype) for shape, dtype in shapes],
        in_specs=specs,
        out_specs=[pl.BlockSpec(memory_space=out) for out in outs],
        scratch_shapes=list(scratch),
        compiler_params=pltpu.CompilerParams(vmem_limit_bytes=grant * 2**20),
        cost_estimate=pl.CostEstimate(flops=flops, bytes_accessed=moved, transcendentals=0),
    )(*scalars, *operands)


def on_device(velocity, pressure, viscosity, levels, morton_keys, counts, neighbors):
    leaf_count = velocity.shape[0]
    morton_count = lax.axis_size("morton")
    along_x, along_yz = operator_tables()
    dx_table = jnp.asarray(along_x.astype(np.float32)).astype(bf16)
    dyz_table = jnp.asarray(along_yz.astype(np.float32)).astype(bf16)
    pick = jnp.asarray(face_table().astype(np.float32)).astype(bf16)
    spread = jnp.asarray(spread_table().astype(np.float32)).astype(bf16)
    basis = jnp.asarray(np.concatenate(basis_tables(), axis=0))
    boxes = jnp.asarray(box_table(morton_count))
    vel = jnp.transpose(velocity, (1, 0, 2))
    nbrs = jnp.transpose(neighbors, (1, 0))

    width = 3 * FACES
    faces, even, odd = call(
        pack_kernel,
        [((leaf_count, width), bf16), ((BAND, width), bf16), ((BAND, width), bf16)],
        4 * 10**8,
        [counts],
        [vel, pick],
        [
            pltpu.VMEM(vel.shape, bf16),
            pltpu.VMEM(pick.shape, bf16),
            pltpu.VMEM((leaf_count, width), bf16),
            pltpu.VMEM((2, BAND, width), bf16),
            pltpu.SemaphoreType.DMA((7,)),
        ],
        place=pltpu.HBM,
        outs=[pltpu.HBM] * 3,
        grant=60,
    )
    sib_count = lax.axis_size("sib")
    shift, powers = move_tables(morton_count)
    part, continuity, spots, geom, move = call(
        pre_kernel,
        [
            ((3, leaf_count, NODES), f32),
            ((leaf_count, NODES), f32),
            ((leaf_count, LANES), f32),
            ((8, leaf_count), f32),
            ((256, 256), f32),
        ],
        2 * 10**9,
        [counts],
        [
            vel, pressure, viscosity, levels.reshape(1, -1), morton_keys.reshape(1, -1), nbrs,
            dx_table, dyz_table, boxes, jnp.asarray(shift), jnp.asarray(powers),
        ],
    )
    window = [faces]
    bands = [jnp.concatenate([pairs(even, 0), pairs(odd, 1)], axis=0)]
    for bit in reversed(range(sib_count.bit_length() - 1)):
        window += [swap(piece, "sib", 1 << bit) for piece in window]
        held = jnp.concatenate(bands, axis=0)
        if bit == 0:
            held, part = lax.optimization_barrier((held, part))
        bands = [held, swap(held, "sib", 1 << bit)]

    force, sums = call(
        post_kernel,
        [((3, leaf_count, NODES), f32), ((8, 2 * LANES), f32)],
        10**9,
        [],
        [
            part, viscosity, spots, geom, boxes, spread, basis,
            jnp.asarray(compact_table()), *window, *bands,
        ],
        [
            pltpu.VMEM((3, leaf_count, NODES), f32),
            pltpu.VMEM((ROWS, 3 * leaf_count), f32),
            pltpu.SemaphoreType.DMA((3,)),
        ],
        outs=[pltpu.HBM, pltpu.VMEM],
    )
    total = morton_count * sib_count
    (shared,) = call(
        share_kernel,
        [((total // 2, 8, LANES), f32)],
        10**5,
        [],
        [sums, swap(sums, "sib", 1)],
    )
    halves = [list(range(side, total, 2)) for side in range(2)]
    every = lax.all_to_all(shared, ("morton", "sib"), 0, 0, axis_index_groups=halves, tiled=True)
    box, root = call(
        final_kernel,
        [((3, 1, MOMENTS), f32), ((3, 1, MOMENTS), f32)],
        10**5,
        [],
        [every, move],
    )
    return (
        jnp.transpose(force, (1, 0, 2)),
        continuity,
        jnp.transpose(box, (1, 0, 2)),
        jnp.transpose(root, (1, 0, 2)),
    )


def solution(mesh):
    spread_all = ("morton", "sib")
    in_specs = (
        P(spread_all, None, None),
        P(spread_all, None),
        P(spread_all, None),
        P(spread_all),
        P(spread_all),
        P(),
        P(spread_all, None),
    )
    out_specs = (
        P(spread_all, None, None),
        P(spread_all, None),
        P("morton", None, None),
        P("morton", None, None),
    )
    return jax.shard_map(
        on_device, mesh=mesh, in_specs=in_specs, out_specs=out_specs, check_vma=False
    )
```

```python
import jax
import jax.numpy as jnp
import numpy as np
from jax import lax
from jax.experimental import pallas as pl
from jax.experimental.pallas import tpu as pltpu
from jax.sharding import PartitionSpec as P

DEG = 5
LMAX = 7
MOMENTS = 216
BAND = 32
NODES = 512
FACES = 384
ROWS = 288
LANES = 128

penalty = 256.0
out_scale = 1.0 / 1024.0
mass_scale = 1.0 / 32.0
highest = lax.Precision.HIGHEST
f32 = jnp.float32
bf16 = jnp.bfloat16


def cheb_matrix():
    points = -np.cos(np.pi * np.arange(8) / 7.0)
    weights = np.array([(-1.0) ** node for node in range(8)])
    weights[0] *= 0.5
    weights[7] *= 0.5
    derivative = np.zeros((8, 8))
    for row in range(8):
        for col in range(8):
            if row != col:
                derivative[row, col] = weights[col] / weights[row] / (points[row] - points[col])
        derivative[row, row] = -np.sum(derivative[row])
    return points, derivative


def operator_tables():
    _, derivative = cheb_matrix()
    along_x = np.kron(derivative, np.eye(64)).T
    along_y = np.kron(np.eye(4), np.kron(derivative, np.eye(8))).T
    along_z = np.kron(np.eye(32), derivative).T
    return along_x, np.concatenate([along_y, along_z], axis=1)


def face_table():
    pick = np.zeros((NODES, FACES))
    for face in range(6):
        for first in range(8):
            for second in range(8):
                coords = [first, second]
                coords.insert(face // 2, 7 * (face % 2))
                node = 64 * coords[0] + 8 * coords[1] + coords[2]
                pick[node, face * 64 + first * 8 + second] = 1.0
    return pick


def spread_table():
    pick = face_table()
    order = np.concatenate([np.arange(64) + 64 * (face ^ 1) for face in range(6)])
    return pick[:, order].T


def basis_tables():
    points, _ = cheb_matrix()
    powers = np.stack([points**power for power in range(DEG + 1)])
    basis = np.zeros((6, 6, 8, 8, 8, 8))
    basis[:, :, :6] = np.einsum("xa,yb,zc->xyzabc", powers, powers, powers)
    basis = basis.reshape(ROWS, NODES).astype(np.float32)
    top = np.asarray(basis.astype(jnp.bfloat16))
    rest = np.asarray((basis - top.astype(np.float32)).astype(jnp.bfloat16))
    return top, rest


def compact_table():
    table = np.zeros((ROWS, 256), np.float32)
    for group in range(36):
        for power in range(6):
            table[group * 8 + power, group * 6 + power] = 1.0 / 512.0
    return table


def box_table(morton_count):
    bits = morton_count.bit_length() - 1
    key_bits = 3 * LMAX - bits
    table = np.zeros((morton_count, 8, LANES), np.float32)
    for morton in range(morton_count):
        base = morton << key_bits
        lows, sides = [], []
        for offset in (2, 1, 0):
            free = max(0, min(LMAX, (key_bits - offset + 2) // 3))
            cell = sum(((base >> (3 * bit + offset)) & 1) << bit for bit in range(LMAX))
            sides.append(2.0**free / 2.0**LMAX)
            lows.append(cell / 2.0**LMAX)
        scale = 0.5 * max(sides)
        for dim in range(3):
            center = lows[dim] + 0.5 * sides[dim]
            table[morton, dim, 3:6] = (center - 0.5) / 0.5
            table[morton, 4 + dim] = center
        table[morton, 3] = 1.0
        table[morton, 3, 3:6] = scale / 0.5
        table[morton, 7] = 1.0 / scale
    return table.reshape(morton_count * 8, LANES)


def doubling(count):
    order = [0]
    for bit in reversed(range(count.bit_length() - 1)):
        order += [other ^ 1 << bit for other in order]
    return order


def swap(block, axis, apart):
    return lax.ppermute(block, axis, [(at, at ^ apart) for at in range(lax.axis_size(axis))])


def exchange(block, mask):
    total = lax.axis_size("morton") * lax.axis_size("sib")
    return lax.ppermute(block, ("morton", "sib"), [(at, at ^ mask) for at in range(total)])


def pairs(block, first):
    route = []
    for low in range(first, lax.axis_size("morton") - 1, 2):
        route += [(low, low + 1), (low + 1, low)]
    return lax.ppermute(block, "morton", route)


def dot(left, right):
    return jnp.dot(left, right, preferred_element_type=f32)


def dot_nt(left, right, precision=None):
    return lax.dot_general(
        left, right, (((1,), (1,)), ((), ())), preferred_element_type=f32, precision=precision
    )


def pack_kernel(counts_ref, vel_ref, pick_ref, faces_ref, even_ref, odd_ref):
    sib_count = lax.axis_size("sib")
    morton = lax.axis_index("morton")
    own = morton * sib_count + lax.axis_index("sib")
    leaf_count = faces_ref.shape[0]
    picked = dot(vel_ref[...].reshape(3 * leaf_count, NODES), pick_ref[...]).astype(bf16)
    for comp in range(3):
        for dim in range(3):
            lane = (dim * 3 + comp) * LANES
            rows = picked[comp * leaf_count : (comp + 1) * leaf_count]
            faces_ref[:, lane : lane + LANES] = rows[:, dim * LANES : (dim + 1) * LANES]
    first = counts_ref[own] - BAND
    row = lax.broadcasted_iota(jnp.int32, (BAND, leaf_count), 0)
    col = lax.broadcasted_iota(jnp.int32, (BAND, leaf_count), 1)
    last_rows = jnp.where(col == row + first, 1.0, 0.0).astype(bf16)
    high = dot(last_rows, faces_ref[...]).astype(bf16)
    low = faces_ref[:BAND, :]
    is_odd = jnp.bitwise_and(morton, 1) == 1
    even_ref[...] = jnp.where(is_odd, low, high)
    odd_ref[...] = jnp.where(is_odd, high, low)


def pre_kernel(
    counts_ref, vel_ref, press_ref, visc_ref, levels_ref, keys_ref, nbrs_ref, dx_ref, dyz_ref, box_ref,
    part_ref, mass_ref, spots_ref, geom_ref,
):
    sib_count = lax.axis_size("sib")
    morton_count = lax.axis_size("morton")
    morton = lax.axis_index("morton")
    own = morton * sib_count + lax.axis_index("sib")
    leaf_count = mass_ref.shape[0]
    live = lax.broadcasted_iota(jnp.int32, (leaf_count, NODES), 0) < counts_ref[own]
    node = lax.broadcasted_iota(jnp.int32, (1, NODES), 1)
    touching = jnp.zeros((1, NODES), f32)
    for shift in (6, 3, 0):
        idx = jnp.bitwise_and(jnp.right_shift(node, shift), 7)
        touching = touching + jnp.where((idx == 0) | (idx == 7), 1.0, 0.0)

    def rows(stack, at):
        return stack[at * leaf_count : (at + 1) * leaf_count]

    visc = visc_ref[...]
    fields = jnp.concatenate([vel_ref[0], vel_ref[1], vel_ref[2], press_ref[...]], axis=0)
    halves = [dot(fields[:, at : at + 256], dyz_ref[...]) for at in (0, 256)]
    grads = [
        dot(fields, dx_ref[...]),
        jnp.concatenate([half[:, :256] for half in halves], axis=1),
        jnp.concatenate([half[:, 256:] for half in halves], axis=1),
    ]
    mass = -(rows(grads[0], 0) + rows(grads[1], 1) + rows(grads[2], 2)) * mass_scale
    mass_ref[...] = jnp.where(live, mass, 0.0)
    stress = {}
    for first in range(3):
        for second in range(first, 3):
            value = (visc * (rows(grads[second], first) + rows(grads[first], second))).astype(bf16)
            stress[first, second] = stress[second, first] = value
    columns = [jnp.concatenate([stress[comp, dim] for comp in range(3)], axis=0) for dim in range(3)]
    rest = [
        dot(columns[1][:, at : at + 256], dyz_ref[:, :256]) + dot(columns[2][:, at : at + 256], dyz_ref[:, 256:])
        for at in (0, 256)
    ]
    div = dot(columns[0], dx_ref[...]) + jnp.concatenate(rest, axis=1)
    for comp in range(3):
        jump = touching * vel_ref[comp].astype(f32)
        part = (penalty * visc * jump - rows(div, comp) + rows(grads[comp], 3)) * out_scale
        part_ref[comp] = jnp.where(live, part, 0.0)

    nbrs = nbrs_ref[...]
    target = jnp.maximum(nbrs, 0)
    owner = target // leaf_count
    slot = target - owner * leaf_count
    owner_morton = owner // sib_count
    owner_sib = owner - owner_morton * sib_count
    apart = jnp.bitwise_xor(owner_sib, lax.axis_index("sib"))
    piece = jnp.zeros_like(apart)
    for at, other in enumerate(doubling(sib_count)):
        piece = jnp.where(apart == other, at, piece)
    step = owner_morton - morton
    below = jnp.maximum(morton - 1, 0) * sib_count
    band_start = jnp.zeros_like(slot)
    for sib in range(sib_count):
        band_start = jnp.where(owner_sib == sib, counts_ref[below + sib] - BAND, band_start)
    base = sib_count * leaf_count
    below_at = BAND * (1 - jnp.bitwise_and(morton, 1))
    spot = jnp.where(
        step == 0,
        piece * leaf_count + slot,
        base + piece * (2 * BAND) + jnp.where(step < 0, slot - band_start + below_at, slot + BAND - below_at),
    )
    spot = jnp.where(nbrs >= 0, spot, -1).astype(f32)
    padded = jnp.concatenate([spot, jnp.full((LANES - spot.shape[0], leaf_count), -1.0, f32)], axis=0)
    spots_ref[...] = padded.T

    box = box_ref[pl.ds(pl.multiple_of(morton * 8, 8), 8), :]
    shift_bits = 3 * (LMAX - levels_ref[...])
    anchor = jnp.left_shift(jnp.right_shift(keys_ref[...], shift_bits), shift_bits)
    span = jnp.left_shift(jnp.ones_like(shift_bits), LMAX - levels_ref[...]).astype(f32)
    finest = 1.0 / float(2**LMAX)
    places = []
    for dim, offset in enumerate((2, 1, 0)):
        cell = jnp.zeros_like(anchor)
        for bit in range(LMAX):
            picked = jnp.bitwise_and(jnp.right_shift(anchor, 3 * bit + offset), 1)
            cell = cell + jnp.left_shift(picked, bit)
        center = (cell.astype(f32) + 0.5 * span) * finest
        places.append((center - box[4 + dim : 5 + dim, :]) * box[7:8, :])
    places.append(0.5 * span * finest * box[7:8, :])
    places.append(jnp.zeros((4, leaf_count), f32))
    geom_ref[...] = jnp.concatenate(places, axis=0)


def shifted(tiles, geom):
    width = tiles[0].shape
    scale = jnp.broadcast_to(geom[3:4, :], width)
    level = lax.broadcasted_iota(jnp.int32, width, 0)
    depth = jnp.ones(width, f32)
    for power in range(1, DEG + 1):
        depth = depth * jnp.where(level >= power, scale, 1.0)
    scales = [depth]
    for _ in range(2 * DEG):
        scales.append(scales[-1] * scale)
    tiles = [tile * scales[at // 6 + at % 6] for at, tile in enumerate(tiles)]
    along = [jnp.broadcast_to(geom[dim : dim + 1, :], width) for dim in range(3)]
    for low in range(1, DEG + 1):
        for power in range(DEG, low - 1, -1):
            for other in range(6):
                at = power * 6 + other
                tiles[at] = tiles[at] + along[0] * tiles[at - 6]
            for other in range(6):
                at = other * 6 + power
                tiles[at] = tiles[at] + along[1] * tiles[at - 1]
    steps = [jnp.where(level >= low, along[2], 0.0) for low in range(1, DEG + 1)]
    for step in steps:
        tiles = [tile + step * pltpu.roll(tile, 1, 0) for tile in tiles]
    return tiles


def post_kernel(
    part_ref, visc_ref, spots_ref, geom_ref, box_ref, spread_ref, basis_ref, compact_ref, *refs
):
    window_refs, (force_hbm, sums_ref, force_ref, raw_ref, sems) = refs[:-5], refs[-5:]
    morton = lax.axis_index("morton")
    leaf_count = visc_ref.shape[0]
    spots = spots_ref[...].astype(jnp.int32)
    lane = lax.broadcasted_iota(jnp.int32, (leaf_count, FACES), 1)
    upper = jnp.bitwise_and(lane, 64) > 0
    window_rows = sum(window_ref.shape[0] for window_ref in window_refs)
    cols = lax.broadcasted_iota(jnp.int32, (leaf_count, window_rows), 1)
    chosen = []
    for dim in range(3):
        at = dim * FACES
        window = jnp.concatenate([ref[:, at : at + FACES] for ref in window_refs], axis=0)
        places = [jnp.broadcast_to(spots[:, face : face + 1], (leaf_count, 1)) for face in (2 * dim, 2 * dim + 1)]
        onehot = [jnp.where(cols == place, 1.0, 0.0).astype(bf16) for place in places]
        both = dot(jnp.concatenate(onehot, axis=0), window)
        chosen.append(jnp.where(upper, both[:leaf_count], both[leaf_count:]).astype(bf16))
    weight = visc_ref[...] * (penalty * out_scale)
    highs, lows, stores = [], [], []
    picked = [
        jnp.concatenate([block[:, comp * LANES : (comp + 1) * LANES] for block in chosen], axis=1) for comp in range(3)
    ]
    jumps = dot(jnp.concatenate(picked, axis=0), spread_ref[...])
    for comp in range(3):
        force = part_ref[comp] - weight * jumps[comp * leaf_count : (comp + 1) * leaf_count]
        force_ref[comp] = force
        stores.append(pltpu.make_async_copy(force_ref.at[comp], force_hbm.at[comp], sems.at[comp]))
        stores[-1].start()
        high = force.astype(bf16)
        highs.append(high)
        lows.append((force - high.astype(f32)).astype(bf16))
    high = jnp.concatenate(highs, axis=0)
    low = jnp.concatenate(lows, axis=0)
    raw = dot_nt(basis_ref[...], high)
    raw_ref[...] = raw[:ROWS] + raw[ROWS:] + dot_nt(basis_ref[:ROWS, :], low)
    geom = jnp.concatenate([geom_ref[...]] * 3, axis=1)
    tiles = shifted([raw_ref[8 * at : 8 * at + 8, :] for at in range(36)], geom)
    moved = jnp.concatenate(tiles, axis=0)
    group = lax.broadcasted_iota(jnp.int32, (3 * leaf_count, LANES), 0) // leaf_count
    column = lax.broadcasted_iota(jnp.int32, (3 * leaf_count, LANES), 1)
    gather = jnp.where((group == column) | (group + 3 == column), 1.0, 0.0)
    summed = jnp.dot(moved, gather, precision=highest, preferred_element_type=f32)
    box = box_ref[pl.ds(pl.multiple_of(morton * 8, 8), 8), :]
    both = shifted([summed[8 * at : 8 * at + 8, :] for at in range(36)], box)
    flat = jnp.concatenate(both, axis=0).T
    sums = jnp.dot(flat[:8], compact_ref[...], precision=highest, preferred_element_type=f32)
    sums_ref[...] = sums
    for store in stores:
        store.wait()


def final_kernel(sums_ref, *refs):
    others, (box_ref, root_ref) = refs[:-2], refs[-2:]
    root = sums_ref[3:6, :] + others[0][3:6, :]
    if len(others) > 1:
        root = root + (others[1][3:6, :] + others[2][3:6, :])
    for comp in range(3):
        box_ref[comp] = sums_ref[comp : comp + 1, :MOMENTS]
        root_ref[comp] = root[comp : comp + 1, :MOMENTS]


def call(kernel, shapes, flops, scalars, operands, scratch=(), place=pltpu.VMEM, outs=None, grant=32):
    specs = [pl.BlockSpec(memory_space=pltpu.SMEM)] * len(scalars)
    specs += [pl.BlockSpec(memory_space=place)] * len(operands)
    outs = outs or [pltpu.VMEM] * len(shapes)
    moved = sum(array.size * array.dtype.itemsize for array in operands)
    return pl.pallas_call(
        kernel,
        out_shape=[jax.ShapeDtypeStruct(shape, dtype) for shape, dtype in shapes],
        in_specs=specs,
        out_specs=[pl.BlockSpec(memory_space=out) for out in outs],
        scratch_shapes=list(scratch),
        compiler_params=pltpu.CompilerParams(vmem_limit_bytes=grant * 2**20),
        cost_estimate=pl.CostEstimate(flops=flops, bytes_accessed=moved, transcendentals=0),
    )(*scalars, *operands)


def on_device(velocity, pressure, viscosity, levels, morton_keys, counts, neighbors):
    leaf_count = velocity.shape[0]
    morton_count = lax.axis_size("morton")
    along_x, along_yz = operator_tables()
    dx_table = jnp.asarray(along_x.astype(np.float32)).astype(bf16)
    dyz_table = jnp.asarray(along_yz.astype(np.float32)).astype(bf16)
    pick = jnp.asarray(face_table().astype(np.float32)).astype(bf16)
    spread = jnp.asarray(spread_table().astype(np.float32)).astype(bf16)
    basis = jnp.asarray(np.concatenate(basis_tables(), axis=0))
    boxes = jnp.asarray(box_table(morton_count))
    vel = jnp.transpose(velocity, (1, 0, 2))
    nbrs = jnp.transpose(neighbors, (1, 0))

    width = 3 * FACES
    faces, even, odd = call(
        pack_kernel,
        [((leaf_count, width), bf16), ((BAND, width), bf16), ((BAND, width), bf16)],
        4 * 10**8,
        [counts],
        [vel, pick],
        grant=60,
    )
    sib_count = lax.axis_size("sib")
    part, continuity, spots, geom = call(
        pre_kernel,
        [
            ((3, leaf_count, NODES), f32),
            ((leaf_count, NODES), f32),
            ((leaf_count, LANES), f32),
            ((8, leaf_count), f32),
        ],
        2 * 10**9,
        [counts],
        [
            vel, pressure, viscosity, levels.reshape(1, -1), morton_keys.reshape(1, -1), nbrs,
            dx_table, dyz_table, boxes,
        ],
    )
    window = [faces]
    bands = [jnp.concatenate([pairs(even, 0), pairs(odd, 1)], axis=0)]
    for bit in reversed(range(sib_count.bit_length() - 1)):
        window += [swap(piece, "sib", 1 << bit) for piece in window]
        held = jnp.concatenate(bands, axis=0)
        if bit == 0:
            held, part = lax.optimization_barrier((held, part))
        bands = [held, swap(held, "sib", 1 << bit)]

    force, sums = call(
        post_kernel,
        [((3, leaf_count, NODES), f32), ((8, 2 * LANES), f32)],
        10**9,
        [],
        [
            part, viscosity, spots, geom, boxes, spread, basis,
            jnp.asarray(compact_table()), *window, *bands,
        ],
        [
            pltpu.VMEM((3, leaf_count, NODES), f32),
            pltpu.VMEM((ROWS, 3 * leaf_count), f32),
            pltpu.SemaphoreType.DMA((3,)),
        ],
        outs=[pltpu.HBM, pltpu.VMEM],
    )
    bits = (morton_count * sib_count).bit_length() - 1
    rounds = [[1]]
    for bit in range(1, bits, 2):
        rounds.append([part << bit for part in ((1, 2, 3) if bit + 1 < bits else (1,))])
    is_box = jnp.arange(8)[:, None] < 3
    for masks in rounds[:-1]:
        got = [exchange(sums, mask) for mask in masks]
        pair = sums + got[0]
        every = pair + (got[1] + got[2]) if len(got) > 1 else pair
        inside = [sums, pair, every][sum(mask < sib_count for mask in masks[:2])]
        sums = jnp.where(is_box, inside, every)
    box, root = call(
        final_kernel,
        [((3, 1, MOMENTS), f32), ((3, 1, MOMENTS), f32)],
        10**5,
        [],
        [sums] + [exchange(sums, mask) for mask in rounds[-1]],
    )
    return (
        jnp.transpose(force, (1, 0, 2)),
        continuity,
        jnp.transpose(box, (1, 0, 2)),
        jnp.transpose(root, (1, 0, 2)),
    )


def solution(mesh):
    spread_all = ("morton", "sib")
    in_specs = (
        P(spread_all, None, None),
        P(spread_all, None),
        P(spread_all, None),
        P(spread_all),
        P(spread_all),
        P(),
        P(spread_all, None),
    )
    out_specs = (
        P(spread_all, None, None),
        P(spread_all, None),
        P("morton", None, None),
        P("morton", None, None),
    )
    return jax.shard_map(
        on_device, mesh=mesh, in_specs=in_specs, out_specs=out_specs, check_vma=False
    )
```

```python
import math

import jax
import jax.numpy as jnp
import numpy as np
from jax import lax
from jax.experimental import pallas as pl
from jax.experimental.pallas import tpu as pltpu
from jax.sharding import PartitionSpec as P

DEG = 5
LMAX = 7
MOMENTS = 216
BAND = 32
NODES = 512
FACES = 384
ROWS = 288
LANES = 128

penalty = 256.0
out_scale = 1.0 / 1024.0
mass_scale = 1.0 / 32.0
highest = lax.Precision.HIGHEST
f32 = jnp.float32
bf16 = jnp.bfloat16


def cheb_matrix():
    points = -np.cos(np.pi * np.arange(8) / 7.0)
    weights = np.array([(-1.0) ** node for node in range(8)])
    weights[0] *= 0.5
    weights[7] *= 0.5
    derivative = np.zeros((8, 8))
    for row in range(8):
        for col in range(8):
            if row != col:
                derivative[row, col] = weights[col] / weights[row] / (points[row] - points[col])
        derivative[row, row] = -np.sum(derivative[row])
    return points, derivative


def operator_tables():
    _, derivative = cheb_matrix()
    along_x = np.kron(derivative, np.eye(64)).T
    along_y = np.kron(np.eye(4), np.kron(derivative, np.eye(8))).T
    along_z = np.kron(np.eye(32), derivative).T
    return along_x, np.concatenate([along_y, along_z], axis=1)


def face_table():
    pick = np.zeros((NODES, FACES))
    for face in range(6):
        for first in range(8):
            for second in range(8):
                coords = [first, second]
                coords.insert(face // 2, 7 * (face % 2))
                node = 64 * coords[0] + 8 * coords[1] + coords[2]
                pick[node, face * 64 + first * 8 + second] = 1.0
    return pick


def spread_table():
    pick = face_table()
    order = np.concatenate([np.arange(64) + 64 * (face ^ 1) for face in range(6)])
    return pick[:, order].T


def basis_tables():
    points, _ = cheb_matrix()
    powers = np.stack([points**power for power in range(DEG + 1)])
    basis = np.zeros((6, 6, 8, 8, 8, 8))
    basis[:, :, :6] = np.einsum("xa,yb,zc->xyzabc", powers, powers, powers)
    basis = basis.reshape(ROWS, NODES).astype(np.float32)
    top = np.asarray(basis.astype(jnp.bfloat16))
    rest = np.asarray((basis - top.astype(np.float32)).astype(jnp.bfloat16))
    return top, rest


def compact_table():
    table = np.zeros((ROWS, 256), np.float32)
    for group in range(36):
        for power in range(6):
            table[group * 8 + power, group * 6 + power] = 1.0 / 512.0
    return table


def box_table(morton_count):
    bits = morton_count.bit_length() - 1
    key_bits = 3 * LMAX - bits
    table = np.zeros((morton_count, 8, LANES), np.float32)
    for morton in range(morton_count):
        base = morton << key_bits
        lows, sides = [], []
        for offset in (2, 1, 0):
            free = max(0, min(LMAX, (key_bits - offset + 2) // 3))
            cell = sum(((base >> (3 * bit + offset)) & 1) << bit for bit in range(LMAX))
            sides.append(2.0**free / 2.0**LMAX)
            lows.append(cell / 2.0**LMAX)
        scale = 0.5 * max(sides)
        for dim in range(3):
            center = lows[dim] + 0.5 * sides[dim]
            table[morton, dim, 3:6] = (center - 0.5) / 0.5
            table[morton, 4 + dim] = center
        table[morton, 3] = 1.0
        table[morton, 3, 3:6] = scale / 0.5
        table[morton, 7] = 1.0 / scale
    return table.reshape(morton_count * 8, LANES)


def swap(block, axis, apart):
    return lax.ppermute(block, axis, [(at, at ^ apart) for at in range(lax.axis_size(axis))])


def move_tables(morton_count):
    bits = 3 * LMAX - (morton_count.bit_length() - 1)
    ratio = 2.0 ** max(max(0, min(LMAX, (bits - offset + 2) // 3)) for offset in range(3)) / 2.0**LMAX
    shift = np.zeros((256, 256), np.float32)
    powers = np.zeros((256, 256), np.int32)
    triples = list(np.ndindex(6, 6, 6))
    for row, beta in enumerate(triples):
        for col, alpha in enumerate(triples):
            if all(b <= a for a, b in zip(alpha, beta)):
                shift[row, col] = math.prod(math.comb(a, b) for a, b in zip(alpha, beta)) * ratio ** sum(beta)
                powers[row, col] = sum((a - b) << 3 * dim for dim, (a, b) in enumerate(zip(alpha, beta)))
    return shift, powers


def pairs(block, first):
    route = []
    for low in range(first, lax.axis_size("morton") - 1, 2):
        route += [(low, low + 1), (low + 1, low)]
    return lax.ppermute(block, "morton", route)


def dot(left, right):
    return jnp.dot(left, right, preferred_element_type=f32)


def dot_nt(left, right, precision=None):
    return lax.dot_general(
        left, right, (((1,), (1,)), ((), ())), preferred_element_type=f32, precision=precision
    )


def pack_kernel(counts_ref, vel_ref, nbrs_ref, pick_ref, faces_ref, even_ref, odd_ref, *spots_refs):
    sib_count = lax.axis_size("sib")
    morton = lax.axis_index("morton")
    sib = lax.axis_index("sib")
    own = morton * sib_count + sib
    leaf_count = faces_ref.shape[0]
    picked = dot(vel_ref[...].reshape(3 * leaf_count, NODES), pick_ref[...]).astype(bf16)
    for comp in range(3):
        for dim in range(3):
            lane = (dim * 3 + comp) * LANES
            rows = picked[comp * leaf_count : (comp + 1) * leaf_count]
            faces_ref[:, lane : lane + LANES] = rows[:, dim * LANES : (dim + 1) * LANES]
    first = counts_ref[own] - BAND
    row = lax.broadcasted_iota(jnp.int32, (BAND, leaf_count), 0)
    col = lax.broadcasted_iota(jnp.int32, (BAND, leaf_count), 1)
    last_rows = jnp.where(col == row + first, 1.0, 0.0).astype(bf16)
    high = dot(last_rows, faces_ref[...]).astype(bf16)
    low = faces_ref[:BAND, :]
    is_odd = jnp.bitwise_and(morton, 1) == 1
    even_ref[...] = jnp.where(is_odd, low, high)
    odd_ref[...] = jnp.where(is_odd, high, low)

    nbrs = nbrs_ref[...]
    target = jnp.maximum(nbrs, 0)
    owner = target // leaf_count
    slot = target - owner * leaf_count
    owner_morton = owner // sib_count
    owner_sib = owner - owner_morton * sib_count
    step = owner_morton - morton
    below = jnp.maximum(morton - 1, 0) * sib_count
    band_start = jnp.zeros_like(slot)
    for other in range(sib_count):
        band_start = jnp.where(owner_sib == other, counts_ref[below + other] - BAND, band_start)
    below_at = BAND * (1 - jnp.bitwise_and(morton, 1))
    in_band = jnp.where(step < 0, slot - band_start + below_at, slot + BAND - below_at)
    for side, spots_ref in enumerate(spots_refs):
        piece = jnp.bitwise_xor(owner_sib, jnp.bitwise_xor(sib, 2 * side))
        spot = jnp.where(step == 0, piece * leaf_count + slot, 2 * leaf_count + piece * (2 * BAND) + in_band)
        spot = jnp.where((nbrs >= 0) & (piece < 2), spot, -1).astype(f32)
        spots_ref[...] = jnp.concatenate([spot, jnp.full((2, leaf_count), -1.0, f32)], axis=0)


def gathered(spots, window_refs):
    leaf_count = spots.shape[1]
    rows = sum(ref.shape[0] for ref in window_refs)
    filled = jnp.concatenate([spots, jnp.full((LANES - spots.shape[0], leaf_count), -1.0, f32)], axis=0)
    places = filled.T.astype(jnp.int32)
    cols = lax.broadcasted_iota(jnp.int32, (leaf_count, rows), 1)
    upper = jnp.bitwise_and(lax.broadcasted_iota(jnp.int32, (leaf_count, FACES), 1), 64) > 0
    chosen = []
    for dim in range(3):
        at = dim * FACES
        window = jnp.concatenate([ref[:, at : at + FACES] for ref in window_refs], axis=0)
        faces = (2 * dim, 2 * dim + 1)
        onehot = [jnp.where(cols == places[:, face : face + 1], 1.0, 0.0).astype(bf16) for face in faces]
        both = dot(jnp.concatenate(onehot, axis=0), window)
        chosen.append(jnp.where(upper, both[:leaf_count], both[leaf_count:]).astype(bf16))
    return chosen


def spread_out(chosen, spread):
    comps = [
        jnp.concatenate([block[:, comp * LANES : (comp + 1) * LANES] for block in chosen], axis=1) for comp in range(3)
    ]
    return dot(jnp.concatenate(comps, axis=0), spread)


def serve_kernel(spots_ref, *refs):
    window_refs, out_ref = refs[:-1], refs[-1]
    for dim, block in enumerate(gathered(spots_ref[...], window_refs)):
        out_ref[:, dim * FACES : (dim + 1) * FACES] = block


def pre_kernel(
    counts_ref, vel_ref, press_ref, visc_ref, levels_ref, keys_ref, spots_ref, dx_ref, dyz_ref, box_ref,
    shift_ref, powers_ref, spread_ref, *refs,
):
    window_refs, (part_ref, mass_ref, geom_ref, move_ref) = refs[:-4], refs[-4:]
    sib_count = lax.axis_size("sib")
    morton_count = lax.axis_size("morton")
    morton = lax.axis_index("morton")
    own = morton * sib_count + lax.axis_index("sib")
    leaf_count = mass_ref.shape[0]
    live = lax.broadcasted_iota(jnp.int32, (leaf_count, NODES), 0) < counts_ref[own]
    node = lax.broadcasted_iota(jnp.int32, (1, NODES), 1)
    touching = jnp.zeros((1, NODES), f32)
    for shift in (6, 3, 0):
        idx = jnp.bitwise_and(jnp.right_shift(node, shift), 7)
        touching = touching + jnp.where((idx == 0) | (idx == 7), 1.0, 0.0)

    def rows(stack, at):
        return stack[at * leaf_count : (at + 1) * leaf_count]

    visc = visc_ref[...]
    fields = jnp.concatenate([vel_ref[0], vel_ref[1], vel_ref[2], press_ref[...]], axis=0)
    halves = [dot(fields[:, at : at + 256], dyz_ref[...]) for at in (0, 256)]
    grads = [
        dot(fields, dx_ref[...]),
        jnp.concatenate([half[:, :256] for half in halves], axis=1),
        jnp.concatenate([half[:, 256:] for half in halves], axis=1),
    ]
    mass = -(rows(grads[0], 0) + rows(grads[1], 1) + rows(grads[2], 2)) * mass_scale
    mass_ref[...] = jnp.where(live, mass, 0.0)
    stress = {}
    for first in range(3):
        for second in range(first, 3):
            value = (visc * (rows(grads[second], first) + rows(grads[first], second))).astype(bf16)
            stress[first, second] = stress[second, first] = value
    columns = [jnp.concatenate([stress[comp, dim] for comp in range(3)], axis=0) for dim in range(3)]
    rest = [
        dot(columns[1][:, at : at + 256], dyz_ref[:, :256]) + dot(columns[2][:, at : at + 256], dyz_ref[:, 256:])
        for at in (0, 256)
    ]
    div = dot(columns[0], dx_ref[...]) + jnp.concatenate(rest, axis=1)
    nearby = spread_out(gathered(spots_ref[...], window_refs), spread_ref[...])
    for comp in range(3):
        jump = touching * vel_ref[comp].astype(f32) - rows(nearby, comp)
        part = (penalty * visc * jump - rows(div, comp) + rows(grads[comp], 3)) * out_scale
        part_ref[comp] = jnp.where(live, part, 0.0)

    box = box_ref[pl.ds(pl.multiple_of(morton * 8, 8), 8), :]
    shift_bits = 3 * (LMAX - levels_ref[...])
    anchor = jnp.left_shift(jnp.right_shift(keys_ref[...], shift_bits), shift_bits)
    span = jnp.left_shift(jnp.ones_like(shift_bits), LMAX - levels_ref[...]).astype(f32)
    finest = 1.0 / float(2**LMAX)
    places = []
    for dim, offset in enumerate((2, 1, 0)):
        cell = jnp.zeros_like(anchor)
        for bit in range(LMAX):
            picked = jnp.bitwise_and(jnp.right_shift(anchor, 3 * bit + offset), 1)
            cell = cell + jnp.left_shift(picked, bit)
        center = (cell.astype(f32) + 0.5 * span) * finest
        places.append((center - box[4 + dim : 5 + dim, :]) * box[7:8, :])
    places.append(0.5 * span * finest * box[7:8, :])
    places.append(jnp.zeros((4, leaf_count), f32))
    geom_ref[...] = jnp.concatenate(places, axis=0)
    move = shift_ref[...]
    powers = powers_ref[...]
    for dim in range(3):
        power = jnp.bitwise_and(jnp.right_shift(powers, 3 * dim), 7)
        along = box[dim : dim + 1, 3:4]
        factor = jnp.ones((1, 1), f32)
        for degree in range(1, DEG + 1):
            factor = factor * along
            move = move * jnp.where(power == degree, factor, 1.0)
    move_ref[...] = move


def shifted(tiles, geom):
    width = tiles[0].shape
    scale = jnp.broadcast_to(geom[3:4, :], width)
    level = lax.broadcasted_iota(jnp.int32, width, 0)
    depth = jnp.ones(width, f32)
    for power in range(1, DEG + 1):
        depth = depth * jnp.where(level >= power, scale, 1.0)
    scales = [depth]
    for _ in range(2 * DEG):
        scales.append(scales[-1] * scale)
    tiles = [tile * scales[at // 6 + at % 6] for at, tile in enumerate(tiles)]
    along = [jnp.broadcast_to(geom[dim : dim + 1, :], width) for dim in range(3)]
    for low in range(1, DEG + 1):
        for power in range(DEG, low - 1, -1):
            for other in range(6):
                at = power * 6 + other
                tiles[at] = tiles[at] + along[0] * tiles[at - 6]
            for other in range(6):
                at = other * 6 + power
                tiles[at] = tiles[at] + along[1] * tiles[at - 1]
    steps = [jnp.where(level >= low, along[2], 0.0) for low in range(1, DEG + 1)]
    for step in steps:
        tiles = [tile + step * pltpu.roll(tile, 1, 0) for tile in tiles]
    return tiles


def post_kernel(
    part_ref, visc_ref, geom_ref, box_ref, spread_ref, basis_ref, compact_ref, *refs
):
    got_refs, (force_hbm, sums_ref, force_ref, raw_ref, sems) = refs[:-5], refs[-5:]
    morton = lax.axis_index("morton")
    leaf_count = visc_ref.shape[0]
    chosen = []
    for dim in range(3):
        lanes = slice(dim * FACES, (dim + 1) * FACES)
        chosen.append(got_refs[0][:, lanes])
        for got_ref in got_refs[1:]:
            chosen[dim] = chosen[dim] + got_ref[:, lanes]
    jumps = spread_out(chosen, spread_ref[...])
    weight = visc_ref[...] * (penalty * out_scale)
    highs, lows, stores = [], [], []
    for comp in range(3):
        force = part_ref[comp] - weight * jumps[comp * leaf_count : (comp + 1) * leaf_count]
        force_ref[comp] = force
        stores.append(pltpu.make_async_copy(force_ref.at[comp], force_hbm.at[comp], sems.at[comp]))
        stores[-1].start()
        high = force.astype(bf16)
        highs.append(high)
        lows.append((force - high.astype(f32)).astype(bf16))
    high = jnp.concatenate(highs, axis=0)
    low = jnp.concatenate(lows, axis=0)
    raw = dot_nt(basis_ref[...], high)
    raw_ref[...] = raw[:ROWS] + raw[ROWS:] + dot_nt(basis_ref[:ROWS, :], low)
    geom = jnp.concatenate([geom_ref[...]] * 3, axis=1)
    tiles = shifted([raw_ref[8 * at : 8 * at + 8, :] for at in range(36)], geom)
    moved = jnp.concatenate(tiles, axis=0)
    group = lax.broadcasted_iota(jnp.int32, (3 * leaf_count, LANES), 0) // leaf_count
    column = lax.broadcasted_iota(jnp.int32, (3 * leaf_count, LANES), 1)
    gather = jnp.where((group == column) | (group + 3 == column), 1.0, 0.0)
    summed = jnp.dot(moved, gather, precision=highest, preferred_element_type=f32)
    box = box_ref[pl.ds(pl.multiple_of(morton * 8, 8), 8), :]
    both = shifted([summed[8 * at : 8 * at + 8, :] for at in range(36)], box)
    flat = jnp.concatenate(both, axis=0).T
    sums = jnp.dot(flat[:8], compact_ref[...], precision=highest, preferred_element_type=f32)
    blank = jnp.zeros((2, LANES), f32)
    to_box = jnp.concatenate([sums[:3, :LANES], sums[:3, LANES:], blank], axis=0)
    to_root = jnp.concatenate([sums[3:6, :LANES], sums[3:6, LANES:], blank], axis=0)
    sib_count = lax.axis_size("sib")
    for other in range(sums_ref.shape[0]):
        sums_ref[other] = jnp.where(morton == other // sib_count, to_box, to_root)
    for store in stores:
        store.wait()


def final_kernel(sums_ref, move_ref, box_ref, root_ref):
    sib_count = lax.axis_size("sib")
    morton = lax.axis_index("morton")
    box = jnp.zeros(sums_ref.shape[1:], f32)
    root = jnp.zeros(sums_ref.shape[1:], f32)
    for group in range(sums_ref.shape[0] // sib_count):
        total = jnp.sum(sums_ref[group * sib_count : (group + 1) * sib_count], axis=0)
        box = box + jnp.where(morton == group, total, 0.0)
        root = root + jnp.where(morton == group, 0.0, total)
    box = jnp.concatenate([box[:3], box[3:6]], axis=1)
    root = jnp.concatenate([root[:3], root[3:6]], axis=1)
    box8 = jnp.concatenate([box, jnp.zeros((5, 2 * LANES), f32)], axis=0)
    root = root + jnp.dot(box8, move_ref[...], precision=highest, preferred_element_type=f32)[:3]
    for comp in range(3):
        box_ref[comp] = box[comp : comp + 1, :MOMENTS]
        root_ref[comp] = root[comp : comp + 1, :MOMENTS]


def call(kernel, shapes, flops, scalars, operands, scratch=(), place=pltpu.VMEM, outs=None, grant=32):
    specs = [pl.BlockSpec(memory_space=pltpu.SMEM)] * len(scalars)
    specs += [pl.BlockSpec(memory_space=place)] * len(operands)
    outs = outs or [pltpu.VMEM] * len(shapes)
    moved = sum(array.size * array.dtype.itemsize for array in operands)
    return pl.pallas_call(
        kernel,
        out_shape=[jax.ShapeDtypeStruct(shape, dtype) for shape, dtype in shapes],
        in_specs=specs,
        out_specs=[pl.BlockSpec(memory_space=out) for out in outs],
        scratch_shapes=list(scratch),
        compiler_params=pltpu.CompilerParams(vmem_limit_bytes=grant * 2**20),
        cost_estimate=pl.CostEstimate(flops=flops, bytes_accessed=moved, transcendentals=0),
    )(*scalars, *operands)


def on_device(velocity, pressure, viscosity, levels, morton_keys, counts, neighbors):
    leaf_count = velocity.shape[0]
    morton_count = lax.axis_size("morton")
    along_x, along_yz = operator_tables()
    dx_table = jnp.asarray(along_x.astype(np.float32)).astype(bf16)
    dyz_table = jnp.asarray(along_yz.astype(np.float32)).astype(bf16)
    pick = jnp.asarray(face_table().astype(np.float32)).astype(bf16)
    spread = jnp.asarray(spread_table().astype(np.float32)).astype(bf16)
    basis = jnp.asarray(np.concatenate(basis_tables(), axis=0))
    boxes = jnp.asarray(box_table(morton_count))
    vel = jnp.transpose(velocity, (1, 0, 2))
    nbrs = jnp.transpose(neighbors, (1, 0))

    width = 3 * FACES
    sib_count = lax.axis_size("sib")
    sides = sib_count // 2
    faces, even, odd, *spots = call(
        pack_kernel,
        [
            ((leaf_count, width), bf16),
            ((BAND, width), bf16),
            ((BAND, width), bf16),
        ]
        + [((8, leaf_count), f32)] * sides,
        4 * 10**8,
        [counts],
        [vel, nbrs, pick],
        grant=60,
    )
    asked = [swap(spots[side], "sib", 2 * side) for side in range(1, sides)]
    bands = jnp.concatenate([pairs(even, 0), pairs(odd, 1)], axis=0)
    bands, *asked = lax.optimization_barrier((bands, *asked))
    window = [faces, swap(faces, "sib", 1), bands, swap(bands, "sib", 1)]
    got = []
    for side in range(1, sides):
        (served,) = call(
            serve_kernel, [((leaf_count, width), bf16)], 4 * 10**8, [], [asked[side - 1], *window]
        )
        got.append(swap(served, "sib", 2 * side))

    shift, powers = move_tables(morton_count)
    part, continuity, geom, move = call(
        pre_kernel,
        [
            ((3, leaf_count, NODES), f32),
            ((leaf_count, NODES), f32),
            ((8, leaf_count), f32),
            ((256, 256), f32),
        ],
        2 * 10**9,
        [counts],
        [
            vel, pressure, viscosity, levels.reshape(1, -1), morton_keys.reshape(1, -1), spots[0],
            dx_table, dyz_table, boxes, jnp.asarray(shift), jnp.asarray(powers), spread, *window,
        ],
    )
    force, sums = call(
        post_kernel,
        [((3, leaf_count, NODES), f32), ((morton_count * sib_count, 8, LANES), f32)],
        10**9,
        [],
        [part, viscosity, geom, boxes, spread, basis, jnp.asarray(compact_table()), *got],
        [
            pltpu.VMEM((3, leaf_count, NODES), f32),
            pltpu.VMEM((ROWS, 3 * leaf_count), f32),
            pltpu.SemaphoreType.DMA((3,)),
        ],
        outs=[pltpu.HBM, pltpu.VMEM],
    )
    every = lax.all_to_all(sums, ("morton", "sib"), 0, 0, tiled=True)
    box, root = call(
        final_kernel,
        [((3, 1, MOMENTS), f32), ((3, 1, MOMENTS), f32)],
        10**5,
        [],
        [every, move],
    )
    return (
        jnp.transpose(force, (1, 0, 2)),
        continuity,
        jnp.transpose(box, (1, 0, 2)),
        jnp.transpose(root, (1, 0, 2)),
    )


def solution(mesh):
    spread_all = ("morton", "sib")
    in_specs = (
        P(spread_all, None, None),
        P(spread_all, None),
        P(spread_all, None),
        P(spread_all),
        P(spread_all),
        P(),
        P(spread_all, None),
    )
    out_specs = (
        P(spread_all, None, None),
        P(spread_all, None),
        P("morton", None, None),
        P("morton", None, None),
    )
    return jax.shard_map(
        on_device, mesh=mesh, in_specs=in_specs, out_specs=out_specs, check_vma=False
    )
```

```python
import math

import jax
import jax.numpy as jnp
import numpy as np
from jax import lax
from jax.experimental import pallas as pl
from jax.experimental.pallas import tpu as pltpu
from jax.sharding import PartitionSpec as P

DEG = 5
LMAX = 7
MOMENTS = 216
BAND = 32
NODES = 512
FACES = 384
ROWS = 288
LANES = 128

penalty = 256.0
out_scale = 1.0 / 1024.0
mass_scale = 1.0 / 32.0
highest = lax.Precision.HIGHEST
f32 = jnp.float32
bf16 = jnp.bfloat16


def cheb_matrix():
    points = -np.cos(np.pi * np.arange(8) / 7.0)
    weights = np.array([(-1.0) ** node for node in range(8)])
    weights[0] *= 0.5
    weights[7] *= 0.5
    derivative = np.zeros((8, 8))
    for row in range(8):
        for col in range(8):
            if row != col:
                derivative[row, col] = weights[col] / weights[row] / (points[row] - points[col])
        derivative[row, row] = -np.sum(derivative[row])
    return points, derivative


def operator_tables():
    _, derivative = cheb_matrix()
    along_x = np.kron(derivative, np.eye(64)).T
    along_y = np.kron(np.eye(4), np.kron(derivative, np.eye(8))).T
    along_z = np.kron(np.eye(32), derivative).T
    return along_x, np.concatenate([along_y, along_z], axis=1)


def face_table():
    pick = np.zeros((NODES, FACES))
    for face in range(6):
        for first in range(8):
            for second in range(8):
                coords = [first, second]
                coords.insert(face // 2, 7 * (face % 2))
                node = 64 * coords[0] + 8 * coords[1] + coords[2]
                pick[node, face * 64 + first * 8 + second] = 1.0
    return pick


def spread_table():
    pick = face_table()
    order = np.concatenate([np.arange(64) + 64 * (face ^ 1) for face in range(6)])
    return pick[:, order].T


def basis_tables():
    points, _ = cheb_matrix()
    powers = np.stack([points**power for power in range(DEG + 1)])
    basis = np.zeros((6, 6, 8, 8, 8, 8))
    basis[:, :, :6] = np.einsum("xa,yb,zc->xyzabc", powers, powers, powers)
    basis = basis.reshape(ROWS, NODES).astype(np.float32)
    top = np.asarray(basis.astype(jnp.bfloat16))
    rest = np.asarray((basis - top.astype(np.float32)).astype(jnp.bfloat16))
    return top, rest


def compact_table():
    table = np.zeros((ROWS, 256), np.float32)
    for group in range(36):
        for power in range(6):
            table[group * 8 + power, group * 6 + power] = 1.0 / 512.0
    return table


def box_table(morton_count):
    bits = morton_count.bit_length() - 1
    key_bits = 3 * LMAX - bits
    table = np.zeros((morton_count, 8, LANES), np.float32)
    for morton in range(morton_count):
        base = morton << key_bits
        lows, sides = [], []
        for offset in (2, 1, 0):
            free = max(0, min(LMAX, (key_bits - offset + 2) // 3))
            cell = sum(((base >> (3 * bit + offset)) & 1) << bit for bit in range(LMAX))
            sides.append(2.0**free / 2.0**LMAX)
            lows.append(cell / 2.0**LMAX)
        scale = 0.5 * max(sides)
        for dim in range(3):
            center = lows[dim] + 0.5 * sides[dim]
            table[morton, dim, 3:6] = (center - 0.5) / 0.5
            table[morton, 4 + dim] = center
        table[morton, 3] = 1.0
        table[morton, 3, 3:6] = scale / 0.5
        table[morton, 7] = 1.0 / scale
    return table.reshape(morton_count * 8, LANES)


def swap(block, axis, apart):
    return lax.ppermute(block, axis, [(at, at ^ apart) for at in range(lax.axis_size(axis))])


def move_tables(morton_count):
    bits = 3 * LMAX - (morton_count.bit_length() - 1)
    ratio = 2.0 ** max(max(0, min(LMAX, (bits - offset + 2) // 3)) for offset in range(3)) / 2.0**LMAX
    shift = np.zeros((256, 256), np.float32)
    powers = np.zeros((256, 256), np.int32)
    triples = list(np.ndindex(6, 6, 6))
    for row, beta in enumerate(triples):
        for col, alpha in enumerate(triples):
            if all(b <= a for a, b in zip(alpha, beta)):
                shift[row, col] = math.prod(math.comb(a, b) for a, b in zip(alpha, beta)) * ratio ** sum(beta)
                powers[row, col] = sum((a - b) << 3 * dim for dim, (a, b) in enumerate(zip(alpha, beta)))
    return shift, powers


def pairs(block, first):
    route = []
    for low in range(first, lax.axis_size("morton") - 1, 2):
        route += [(low, low + 1), (low + 1, low)]
    return lax.ppermute(block, "morton", route)


def dot(left, right):
    return jnp.dot(left, right, preferred_element_type=f32)


def dot_nt(left, right, precision=None):
    return lax.dot_general(
        left, right, (((1,), (1,)), ((), ())), preferred_element_type=f32, precision=precision
    )


def pack_kernel(
    counts_ref, vel_ref, nbrs_ref, levels_ref, keys_ref, box_ref, pick_ref, faces_ref, even_ref, odd_ref, *spots_refs
):
    sib_count = lax.axis_size("sib")
    morton = lax.axis_index("morton")
    sib = lax.axis_index("sib")
    own = morton * sib_count + sib
    leaf_count = faces_ref.shape[0]
    picked = dot(vel_ref[...].reshape(3 * leaf_count, NODES), pick_ref[...]).astype(bf16)
    for comp in range(3):
        for dim in range(3):
            lane = (dim * 3 + comp) * LANES
            rows = picked[comp * leaf_count : (comp + 1) * leaf_count]
            faces_ref[:, lane : lane + LANES] = rows[:, dim * LANES : (dim + 1) * LANES]
    first = counts_ref[own] - BAND
    row = lax.broadcasted_iota(jnp.int32, (BAND, leaf_count), 0)
    col = lax.broadcasted_iota(jnp.int32, (BAND, leaf_count), 1)
    last_rows = jnp.where(col == row + first, 1.0, 0.0).astype(bf16)
    high = dot(last_rows, faces_ref[...]).astype(bf16)
    low = faces_ref[:BAND, :]
    is_odd = jnp.bitwise_and(morton, 1) == 1
    even_ref[...] = jnp.where(is_odd, low, high)
    odd_ref[...] = jnp.where(is_odd, high, low)

    nbrs = nbrs_ref[...]
    target = jnp.maximum(nbrs, 0)
    owner = target // leaf_count
    slot = target - owner * leaf_count
    owner_morton = owner // sib_count
    owner_sib = owner - owner_morton * sib_count
    step = owner_morton - morton
    below = jnp.maximum(morton - 1, 0) * sib_count
    band_start = jnp.zeros_like(slot)
    for other in range(sib_count):
        band_start = jnp.where(owner_sib == other, counts_ref[below + other] - BAND, band_start)
    below_at = BAND * (1 - jnp.bitwise_and(morton, 1))
    in_band = jnp.where(step < 0, slot - band_start + below_at, slot + BAND - below_at)
    box = box_ref[pl.ds(pl.multiple_of(morton * 8, 8), 8), :]
    shift_bits = 3 * (LMAX - levels_ref[...])
    anchor = jnp.left_shift(jnp.right_shift(keys_ref[...], shift_bits), shift_bits)
    span = jnp.left_shift(jnp.ones_like(shift_bits), LMAX - levels_ref[...]).astype(f32)
    finest = 1.0 / float(2**LMAX)
    places = []
    for dim, offset in enumerate((2, 1, 0)):
        cell = jnp.zeros_like(anchor)
        for bit in range(LMAX):
            picked = jnp.bitwise_and(jnp.right_shift(anchor, 3 * bit + offset), 1)
            cell = cell + jnp.left_shift(picked, bit)
        center = (cell.astype(f32) + 0.5 * span) * finest
        places.append((center - box[4 + dim : 5 + dim, :]) * box[7:8, :])
    places.append(0.5 * span * finest * box[7:8, :])
    places.append(jnp.zeros((4, leaf_count), f32))
    geom = jnp.concatenate(places, axis=0)
    for side, spots_ref in enumerate(spots_refs):
        piece = jnp.bitwise_xor(owner_sib, jnp.bitwise_xor(sib, 2 * side))
        spot = jnp.where(step == 0, piece * leaf_count + slot, 2 * leaf_count + piece * (2 * BAND) + in_band)
        spot = jnp.where((nbrs >= 0) & (piece < 2), spot, -1).astype(f32)
        spots_ref[...] = jnp.concatenate([spot, jnp.full((2, leaf_count), -1.0, f32), geom], axis=0)


def gathered(asked, window_refs):
    leaf_count = asked[0].shape[1]
    rows = sum(ref.shape[0] for ref in window_refs)
    blank = jnp.full((LANES - 8 * len(asked), leaf_count), -1.0, f32)
    places = jnp.concatenate([spots[:8] for spots in asked] + [blank], axis=0).T.astype(jnp.int32)
    cols = lax.broadcasted_iota(jnp.int32, (leaf_count, rows), 1)
    upper = jnp.bitwise_and(lax.broadcasted_iota(jnp.int32, (leaf_count, FACES), 1), 64) > 0
    chosen = [[] for _ in asked]
    for dim in range(3):
        at = dim * FACES
        window = jnp.concatenate([ref[:, at : at + FACES] for ref in window_refs], axis=0)
        faces = [8 * who + face for who in range(len(asked)) for face in (2 * dim, 2 * dim + 1)]
        onehot = [jnp.where(cols == places[:, face : face + 1], 1.0, 0.0).astype(bf16) for face in faces]
        found = dot(jnp.concatenate(onehot, axis=0), window)
        for who in range(len(asked)):
            first, second = (found[(2 * who + side) * leaf_count : (2 * who + side + 1) * leaf_count] for side in (0, 1))
            chosen[who].append(jnp.where(upper, first, second).astype(bf16))
    return chosen


def by_comp(chosen):
    comps = [
        jnp.concatenate([block[:, comp * LANES : (comp + 1) * LANES] for block in chosen], axis=1) for comp in range(3)
    ]
    return jnp.concatenate(comps, axis=0)


def pre_kernel(
    counts_ref, vel_ref, press_ref, visc_ref, dx_ref, dyz_ref, box_ref, shift_ref, powers_ref,
    part_ref, mass_ref, move_ref,
):
    sib_count = lax.axis_size("sib")
    morton_count = lax.axis_size("morton")
    morton = lax.axis_index("morton")
    own = morton * sib_count + lax.axis_index("sib")
    leaf_count = mass_ref.shape[0]
    live = lax.broadcasted_iota(jnp.int32, (leaf_count, NODES), 0) < counts_ref[own]
    node = lax.broadcasted_iota(jnp.int32, (1, NODES), 1)
    touching = jnp.zeros((1, NODES), f32)
    for shift in (6, 3, 0):
        idx = jnp.bitwise_and(jnp.right_shift(node, shift), 7)
        touching = touching + jnp.where((idx == 0) | (idx == 7), 1.0, 0.0)

    def rows(stack, at):
        return stack[at * leaf_count : (at + 1) * leaf_count]

    visc = visc_ref[...]
    fields = jnp.concatenate([vel_ref[0], vel_ref[1], vel_ref[2], press_ref[...]], axis=0)
    halves = [dot(fields[:, at : at + 256], dyz_ref[...]) for at in (0, 256)]
    grads = [
        dot(fields, dx_ref[...]),
        jnp.concatenate([half[:, :256] for half in halves], axis=1),
        jnp.concatenate([half[:, 256:] for half in halves], axis=1),
    ]
    mass = -(rows(grads[0], 0) + rows(grads[1], 1) + rows(grads[2], 2)) * mass_scale
    mass_ref[...] = jnp.where(live, mass, 0.0)
    stress = {}
    for first in range(3):
        for second in range(first, 3):
            value = (visc * (rows(grads[second], first) + rows(grads[first], second))).astype(bf16)
            stress[first, second] = stress[second, first] = value
    columns = [jnp.concatenate([stress[comp, dim] for comp in range(3)], axis=0) for dim in range(3)]
    rest = [
        dot(columns[1][:, at : at + 256], dyz_ref[:, :256]) + dot(columns[2][:, at : at + 256], dyz_ref[:, 256:])
        for at in (0, 256)
    ]
    div = dot(columns[0], dx_ref[...]) + jnp.concatenate(rest, axis=1)
    for comp in range(3):
        jump = touching * vel_ref[comp].astype(f32)
        part = (penalty * visc * jump - rows(div, comp) + rows(grads[comp], 3)) * out_scale
        part_ref[comp] = jnp.where(live, part, 0.0)

    box = box_ref[pl.ds(pl.multiple_of(morton * 8, 8), 8), :]
    move = shift_ref[...]
    powers = powers_ref[...]
    for dim in range(3):
        power = jnp.bitwise_and(jnp.right_shift(powers, 3 * dim), 7)
        along = box[dim : dim + 1, 3:4]
        factor = jnp.ones((1, 1), f32)
        for degree in range(1, DEG + 1):
            factor = factor * along
            move = move * jnp.where(power == degree, factor, 1.0)
    move_ref[...] = move


def shifted(tiles, geom):
    width = tiles[0].shape
    scale = jnp.broadcast_to(geom[3:4, :], width)
    level = lax.broadcasted_iota(jnp.int32, width, 0)
    depth = jnp.ones(width, f32)
    for power in range(1, DEG + 1):
        depth = depth * jnp.where(level >= power, scale, 1.0)
    scales = [depth]
    for _ in range(2 * DEG):
        scales.append(scales[-1] * scale)
    tiles = [tile * scales[at // 6 + at % 6] for at, tile in enumerate(tiles)]
    along = [jnp.broadcast_to(geom[dim : dim + 1, :], width) for dim in range(3)]
    for low in range(1, DEG + 1):
        for power in range(DEG, low - 1, -1):
            for other in range(6):
                at = power * 6 + other
                tiles[at] = tiles[at] + along[0] * tiles[at - 6]
            for other in range(6):
                at = other * 6 + power
                tiles[at] = tiles[at] + along[1] * tiles[at - 1]
    steps = [jnp.where(level >= low, along[2], 0.0) for low in range(1, DEG + 1)]
    for step in steps:
        tiles = [tile + step * pltpu.roll(tile, 1, 0) for tile in tiles]
    return tiles


def moment_kernel(
    part_ref, visc_ref, box_ref, spread_ref, basis_ref, compact_ref, spots_ref, *refs
):
    sides = lax.axis_size("sib") // 2
    window_refs = refs[:4]
    asked_refs, their_visc_refs = refs[4 : 3 + sides], refs[3 + sides : 2 + 2 * sides]
    near_ref, served_refs, sums_ref, raw_ref = refs[2 + 2 * sides], refs[3 + 2 * sides : -2], refs[-2], refs[-1]
    morton = lax.axis_index("morton")
    leaf_count = visc_ref.shape[0]
    asked = [spots_ref[...]] + [ref[...] for ref in asked_refs]
    chosen = gathered(asked, window_refs)
    for blocks, out_ref in zip(chosen, (near_ref, *served_refs)):
        for dim, block in enumerate(blocks):
            out_ref[:, dim * FACES : (dim + 1) * FACES] = block
    jumps = dot(jnp.concatenate([by_comp(blocks) for blocks in chosen], axis=0), spread_ref[...])
    highs, lows = [], []
    for who, ref in enumerate((visc_ref, *their_visc_refs)):
        weight = ref[...] * (penalty * out_scale)
        for comp in range(3):
            at = (3 * who + comp) * leaf_count
            force = -weight * jumps[at : at + leaf_count]
            if who == 0:
                force = force + part_ref[comp]
            high = force.astype(bf16)
            highs.append(high)
            lows.append((force - high.astype(f32)).astype(bf16))
    high = jnp.concatenate(highs, axis=0)
    low = jnp.concatenate(lows, axis=0)
    raw = dot_nt(basis_ref[...], high)
    raw_ref[...] = raw[:ROWS] + raw[ROWS:] + dot_nt(basis_ref[:ROWS, :], low)
    geom = jnp.concatenate([spots[8:] for spots in asked for _ in range(3)], axis=1)
    tiles = shifted([raw_ref[8 * at : 8 * at + 8, :] for at in range(36)], geom)
    moved = jnp.concatenate(tiles, axis=0)
    group = lax.broadcasted_iota(jnp.int32, (raw_ref.shape[1], LANES), 0) // leaf_count % 3
    column = lax.broadcasted_iota(jnp.int32, (raw_ref.shape[1], LANES), 1)
    gather = jnp.where((group == column) | (group + 3 == column), 1.0, 0.0)
    summed = jnp.dot(moved, gather, precision=highest, preferred_element_type=f32)
    box = box_ref[pl.ds(pl.multiple_of(morton * 8, 8), 8), :]
    both = shifted([summed[8 * at : 8 * at + 8, :] for at in range(36)], box)
    flat = jnp.concatenate(both, axis=0).T
    sums = jnp.dot(flat[:8], compact_ref[...], precision=highest, preferred_element_type=f32)
    blank = jnp.zeros((2, LANES), f32)
    to_box = jnp.concatenate([sums[:3, :LANES], sums[:3, LANES:], blank], axis=0)
    to_root = jnp.concatenate([sums[3:6, :LANES], sums[3:6, LANES:], blank], axis=0)
    sib_count = lax.axis_size("sib")
    for other in range(sums_ref.shape[0]):
        sums_ref[other] = jnp.where(morton == other // sib_count, to_box, to_root)


def force_kernel(part_ref, visc_ref, spread_ref, near_ref, *refs):
    got_refs, (force_hbm, force_ref, sems) = refs[:-3], refs[-3:]
    faces = near_ref[...]
    for got_ref in got_refs:
        faces = faces + got_ref[...]
    weight = visc_ref[...] * (penalty * out_scale)
    stores = []
    for comp in range(3):
        lanes = [(dim * 3 + comp) * LANES for dim in range(3)]
        jump = dot(jnp.concatenate([faces[:, at : at + LANES] for at in lanes], axis=1), spread_ref[...])
        force_ref[comp] = part_ref[comp] - weight * jump
        stores.append(pltpu.make_async_copy(force_ref.at[comp], force_hbm.at[comp], sems.at[comp]))
        stores[-1].start()
    for store in stores:
        store.wait()


def final_kernel(sums_ref, move_ref, box_ref, root_ref):
    sib_count = lax.axis_size("sib")
    morton = lax.axis_index("morton")
    box = jnp.zeros(sums_ref.shape[1:], f32)
    root = jnp.zeros(sums_ref.shape[1:], f32)
    for group in range(sums_ref.shape[0] // sib_count):
        total = jnp.sum(sums_ref[group * sib_count : (group + 1) * sib_count], axis=0)
        box = box + jnp.where(morton == group, total, 0.0)
        root = root + jnp.where(morton == group, 0.0, total)
    box = jnp.concatenate([box[:3], box[3:6]], axis=1)
    root = jnp.concatenate([root[:3], root[3:6]], axis=1)
    box8 = jnp.concatenate([box, jnp.zeros((5, 2 * LANES), f32)], axis=0)
    root = root + jnp.dot(box8, move_ref[...], precision=highest, preferred_element_type=f32)[:3]
    for comp in range(3):
        box_ref[comp] = box[comp : comp + 1, :MOMENTS]
        root_ref[comp] = root[comp : comp + 1, :MOMENTS]


def call(kernel, shapes, flops, scalars, operands, scratch=(), place=pltpu.VMEM, outs=None, grant=32):
    specs = [pl.BlockSpec(memory_space=pltpu.SMEM)] * len(scalars)
    specs += [pl.BlockSpec(memory_space=place)] * len(operands)
    outs = outs or [pltpu.VMEM] * len(shapes)
    moved = sum(array.size * array.dtype.itemsize for array in operands)
    return pl.pallas_call(
        kernel,
        out_shape=[jax.ShapeDtypeStruct(shape, dtype) for shape, dtype in shapes],
        in_specs=specs,
        out_specs=[pl.BlockSpec(memory_space=out) for out in outs],
        scratch_shapes=list(scratch),
        compiler_params=pltpu.CompilerParams(vmem_limit_bytes=grant * 2**20),
        cost_estimate=pl.CostEstimate(flops=flops, bytes_accessed=moved, transcendentals=0),
    )(*scalars, *operands)


def on_device(velocity, pressure, viscosity, levels, morton_keys, counts, neighbors):
    leaf_count = velocity.shape[0]
    morton_count = lax.axis_size("morton")
    along_x, along_yz = operator_tables()
    dx_table = jnp.asarray(along_x.astype(np.float32)).astype(bf16)
    dyz_table = jnp.asarray(along_yz.astype(np.float32)).astype(bf16)
    pick = jnp.asarray(face_table().astype(np.float32)).astype(bf16)
    spread = jnp.asarray(spread_table().astype(np.float32)).astype(bf16)
    basis = jnp.asarray(np.concatenate(basis_tables(), axis=0))
    boxes = jnp.asarray(box_table(morton_count))
    vel = jnp.transpose(velocity, (1, 0, 2))
    nbrs = jnp.transpose(neighbors, (1, 0))

    width = 3 * FACES
    sib_count = lax.axis_size("sib")
    sides = sib_count // 2
    other_sides = [2 * side for side in range(1, sides)]
    their_visc = [swap(viscosity, "sib", apart) for apart in other_sides]
    faces, even, odd, *spots = call(
        pack_kernel,
        [
            ((leaf_count, width), bf16),
            ((BAND, width), bf16),
            ((BAND, width), bf16),
        ]
        + [((16, leaf_count), f32)] * sides,
        4 * 10**8,
        [counts],
        [vel, nbrs, levels.reshape(1, -1), morton_keys.reshape(1, -1), boxes, pick],
        grant=60,
    )
    asked = [swap(block, "sib", apart) for block, apart in zip(spots[1:], other_sides)]
    bands = jnp.concatenate([pairs(even, 0), pairs(odd, 1)], axis=0)
    window = [faces, swap(faces, "sib", 1), bands, swap(bands, "sib", 1)]
    shift, powers = move_tables(morton_count)
    part, continuity, move = call(
        pre_kernel,
        [
            ((3, leaf_count, NODES), f32),
            ((leaf_count, NODES), f32),
            ((256, 256), f32),
        ],
        2 * 10**9,
        [counts],
        [vel, pressure, viscosity, dx_table, dyz_table, boxes, jnp.asarray(shift), jnp.asarray(powers)],
    )
    near, *served, sums = call(
        moment_kernel,
        [((leaf_count, width), bf16)] * sides + [((morton_count * sib_count, 8, LANES), f32)],
        2 * 10**9,
        [],
        [
            part, viscosity, boxes, spread, basis, jnp.asarray(compact_table()), spots[0],
            *window, *asked, *their_visc,
        ],
        [pltpu.VMEM((ROWS, 3 * sides * leaf_count), f32)],
    )
    got = [swap(block, "sib", apart) for block, apart in zip(served, other_sides)]
    every = lax.all_to_all(sums, ("morton", "sib"), 0, 0, tiled=True)
    every, *got = lax.optimization_barrier((every, *got))
    (force,) = call(
        force_kernel,
        [((3, leaf_count, NODES), f32)],
        2 * 10**8,
        [],
        [part, viscosity, spread, near, *got],
        [pltpu.VMEM((3, leaf_count, NODES), f32), pltpu.SemaphoreType.DMA((3,))],
        outs=[pltpu.HBM],
    )
    box, root = call(
        final_kernel,
        [((3, 1, MOMENTS), f32), ((3, 1, MOMENTS), f32)],
        10**5,
        [],
        [every, move],
    )
    return (
        jnp.transpose(force, (1, 0, 2)),
        continuity,
        jnp.transpose(box, (1, 0, 2)),
        jnp.transpose(root, (1, 0, 2)),
    )


def solution(mesh):
    spread_all = ("morton", "sib")
    in_specs = (
        P(spread_all, None, None),
        P(spread_all, None),
        P(spread_all, None),
        P(spread_all),
        P(spread_all),
        P(),
        P(spread_all, None),
    )
    out_specs = (
        P(spread_all, None, None),
        P(spread_all, None),
        P("morton", None, None),
        P("morton", None, None),
    )
    return jax.shard_map(
        on_device, mesh=mesh, in_specs=in_specs, out_specs=out_specs, check_vma=False
    )
```

```python
import math

import jax
import jax.numpy as jnp
import numpy as np
from jax import lax
from jax.experimental import pallas as pl
from jax.experimental.pallas import tpu as pltpu
from jax.sharding import PartitionSpec as P

DEG = 5
LMAX = 7
MOMENTS = 216
BAND = 32
NODES = 512
FACES = 384
ROWS = 288
LANES = 128

penalty = 256.0
out_scale = 1.0 / 1024.0
mass_scale = 1.0 / 32.0
highest = lax.Precision.HIGHEST
f32 = jnp.float32
bf16 = jnp.bfloat16


def cheb_matrix():
    points = -np.cos(np.pi * np.arange(8) / 7.0)
    weights = np.array([(-1.0) ** node for node in range(8)])
    weights[0] *= 0.5
    weights[7] *= 0.5
    derivative = np.zeros((8, 8))
    for row in range(8):
        for col in range(8):
            if row != col:
                derivative[row, col] = weights[col] / weights[row] / (points[row] - points[col])
        derivative[row, row] = -np.sum(derivative[row])
    return points, derivative


def operator_tables():
    _, derivative = cheb_matrix()
    along_x = np.kron(derivative, np.eye(64)).T
    along_y = np.kron(np.eye(4), np.kron(derivative, np.eye(8))).T
    along_z = np.kron(np.eye(32), derivative).T
    return along_x, np.concatenate([along_y, along_z], axis=1)


def face_table():
    pick = np.zeros((NODES, FACES))
    for face in range(6):
        for first in range(8):
            for second in range(8):
                coords = [first, second]
                coords.insert(face // 2, 7 * (face % 2))
                node = 64 * coords[0] + 8 * coords[1] + coords[2]
                pick[node, face * 64 + first * 8 + second] = 1.0
    return pick


def spread_table():
    pick = face_table()
    order = np.concatenate([np.arange(64) + 64 * (face ^ 1) for face in range(6)])
    return pick[:, order].T


def basis_tables():
    points, _ = cheb_matrix()
    powers = np.stack([points**power for power in range(DEG + 1)])
    basis = np.zeros((6, 6, 8, 8, 8, 8))
    basis[:, :, :6] = np.einsum("xa,yb,zc->xyzabc", powers, powers, powers)
    basis = basis.reshape(ROWS, NODES).astype(np.float32)
    top = np.asarray(basis.astype(jnp.bfloat16))
    rest = np.asarray((basis - top.astype(np.float32)).astype(jnp.bfloat16))
    return np.concatenate([top, rest], axis=0)


def compact_table():
    table = np.zeros((ROWS, 256), np.float32)
    for group in range(36):
        for power in range(6):
            table[group * 8 + power, group * 6 + power] = 1.0 / 512.0
    return table


def box_table(morton_count):
    bits = morton_count.bit_length() - 1
    key_bits = 3 * LMAX - bits
    table = np.zeros((morton_count, 8, LANES), np.float32)
    for morton in range(morton_count):
        base = morton << key_bits
        lows, sides = [], []
        for offset in (2, 1, 0):
            free = max(0, min(LMAX, (key_bits - offset + 2) // 3))
            cell = sum(((base >> (3 * bit + offset)) & 1) << bit for bit in range(LMAX))
            sides.append(2.0**free / 2.0**LMAX)
            lows.append(cell / 2.0**LMAX)
        scale = 0.5 * max(sides)
        for dim in range(3):
            center = lows[dim] + 0.5 * sides[dim]
            table[morton, dim, 3:6] = (center - 0.5) / 0.5
            table[morton, 4 + dim] = center
        table[morton, 3] = 1.0
        table[morton, 3, 3:6] = scale / 0.5
        table[morton, 7] = 1.0 / scale
    return table.reshape(morton_count * 8, LANES)


def swap(block, axis, apart):
    return lax.ppermute(block, axis, [(at, at ^ apart) for at in range(lax.axis_size(axis))])


def move_table(morton_count):
    bits = 3 * LMAX - (morton_count.bit_length() - 1)
    ratio = 2.0 ** max(max(0, min(LMAX, (bits - offset + 2) // 3)) for offset in range(3)) / 2.0**LMAX
    table = np.zeros((256, 256), np.float32)
    triples = list(np.ndindex(6, 6, 6))
    for row, beta in enumerate(triples):
        for col, alpha in enumerate(triples):
            if all(b <= a for a, b in zip(alpha, beta)):
                table[row, col] = math.prod(math.comb(a, b) for a, b in zip(alpha, beta)) * ratio ** sum(beta)
    return table


def pairs(block, first):
    route = []
    for low in range(first, lax.axis_size("morton") - 1, 2):
        route += [(low, low + 1), (low + 1, low)]
    return lax.ppermute(block, "morton", route)


def dot(left, right):
    return jnp.dot(left, right, preferred_element_type=f32)


def dot_nt(left, right, precision=None):
    return lax.dot_general(
        left, right, (((1,), (1,)), ((), ())), preferred_element_type=f32, precision=precision
    )


def pack_kernel(
    counts_ref, vel_ref, visc_ref, nbrs_ref, levels_ref, keys_ref, box_ref, pick_ref,
    faces_ref, even_ref, odd_ref, weight_ref, *spots_refs,
):
    sib_count = lax.axis_size("sib")
    morton = lax.axis_index("morton")
    sib = lax.axis_index("sib")
    own = morton * sib_count + sib
    leaf_count = faces_ref.shape[0]
    fields = jnp.concatenate([vel_ref[0], vel_ref[1], vel_ref[2], visc_ref[...].astype(bf16)], axis=0)
    picked = dot(fields, pick_ref[...])
    for dim in range(3):
        block = picked[3 * leaf_count :, dim * LANES : (dim + 1) * LANES]
        weight_ref[:, dim * LANES : (dim + 1) * LANES] = pltpu.roll(block, LANES // 2, 1).astype(bf16)
    picked = picked[: 3 * leaf_count].astype(bf16)
    for comp in range(3):
        for dim in range(3):
            lane = (dim * 3 + comp) * LANES
            rows = picked[comp * leaf_count : (comp + 1) * leaf_count]
            faces_ref[:, lane : lane + LANES] = rows[:, dim * LANES : (dim + 1) * LANES]
    first = counts_ref[own] - BAND
    row = lax.broadcasted_iota(jnp.int32, (BAND, leaf_count), 0)
    col = lax.broadcasted_iota(jnp.int32, (BAND, leaf_count), 1)
    last_rows = jnp.where(col == row + first, 1.0, 0.0).astype(bf16)
    high = dot(last_rows, faces_ref[...]).astype(bf16)
    low = faces_ref[:BAND, :]
    is_odd = jnp.bitwise_and(morton, 1) == 1
    even_ref[...] = jnp.where(is_odd, low, high)
    odd_ref[...] = jnp.where(is_odd, high, low)

    nbrs = nbrs_ref[...]
    target = jnp.maximum(nbrs, 0)
    owner = target // leaf_count
    slot = target - owner * leaf_count
    owner_morton = owner // sib_count
    owner_sib = owner - owner_morton * sib_count
    step = owner_morton - morton
    below = jnp.maximum(morton - 1, 0) * sib_count
    band_start = jnp.zeros_like(slot)
    for other in range(sib_count):
        band_start = jnp.where(owner_sib == other, counts_ref[below + other] - BAND, band_start)
    below_at = BAND * (1 - jnp.bitwise_and(morton, 1))
    in_band = jnp.where(step < 0, slot - band_start + below_at, slot + BAND - below_at)
    box = box_ref[pl.ds(pl.multiple_of(morton * 8, 8), 8), :]
    shift_bits = 3 * (LMAX - levels_ref[...])
    anchor = jnp.left_shift(jnp.right_shift(keys_ref[...], shift_bits), shift_bits)
    span = jnp.left_shift(jnp.ones_like(shift_bits), LMAX - levels_ref[...]).astype(f32)
    finest = 1.0 / float(2**LMAX)
    places = []
    for dim, offset in enumerate((2, 1, 0)):
        cell = jnp.zeros_like(anchor)
        for bit in range(LMAX):
            picked = jnp.bitwise_and(jnp.right_shift(anchor, 3 * bit + offset), 1)
            cell = cell + jnp.left_shift(picked, bit)
        center = (cell.astype(f32) + 0.5 * span) * finest
        places.append((center - box[4 + dim : 5 + dim, :]) * box[7:8, :])
    places.append(0.5 * span * finest * box[7:8, :])
    places.append(jnp.zeros((4, leaf_count), f32))
    geom = jnp.concatenate(places, axis=0)
    for side, spots_ref in enumerate(spots_refs):
        piece = jnp.bitwise_xor(owner_sib, jnp.bitwise_xor(sib, 2 * side))
        spot = jnp.where(step == 0, piece * leaf_count + slot, 2 * leaf_count + piece * (2 * BAND) + in_band)
        spot = jnp.where((nbrs >= 0) & (piece < 2), spot, -1).astype(f32)
        spots_ref[...] = jnp.concatenate([spot, jnp.full((2, leaf_count), -1.0, f32), geom], axis=0)


def gathered(asked, window_refs):
    leaf_count = asked[0].shape[1]
    rows = sum(ref.shape[0] for ref in window_refs)
    blank = jnp.full((LANES - 8 * len(asked), leaf_count), -1.0, f32)
    places = jnp.concatenate([spots[:8] for spots in asked] + [blank], axis=0).T.astype(jnp.int32)
    cols = lax.broadcasted_iota(jnp.int32, (leaf_count, rows), 1)
    upper = jnp.bitwise_and(lax.broadcasted_iota(jnp.int32, (leaf_count, FACES), 1), 64) > 0
    chosen = [[] for _ in asked]
    for dim in range(3):
        at = dim * FACES
        window = jnp.concatenate([ref[:, at : at + FACES] for ref in window_refs], axis=0)
        faces = [8 * who + face for who in range(len(asked)) for face in (2 * dim, 2 * dim + 1)]
        onehot = [jnp.where(cols == places[:, face : face + 1], 1.0, 0.0).astype(bf16) for face in faces]
        found = dot(jnp.concatenate(onehot, axis=0), window)
        for who in range(len(asked)):
            first, second = (found[(2 * who + side) * leaf_count : (2 * who + side + 1) * leaf_count] for side in (0, 1))
            chosen[who].append(jnp.where(upper, first, second).astype(bf16))
    return chosen


def by_comp(chosen):
    comps = [
        jnp.concatenate([block[:, comp * LANES : (comp + 1) * LANES] for block in chosen], axis=1) for comp in range(3)
    ]
    return jnp.concatenate(comps, axis=0)


def pre_kernel(
    counts_ref, vel_ref, press_ref, visc_ref, dx_ref, dyz_ref, box_ref, binomial_ref,
    part_ref, mass_ref, move_ref,
):
    sib_count = lax.axis_size("sib")
    morton_count = lax.axis_size("morton")
    morton = lax.axis_index("morton")
    own = morton * sib_count + lax.axis_index("sib")
    leaf_count = mass_ref.shape[0]
    live = lax.broadcasted_iota(jnp.int32, (leaf_count, NODES), 0) < counts_ref[own]
    node = lax.broadcasted_iota(jnp.int32, (1, NODES), 1)
    touching = jnp.zeros((1, NODES), f32)
    for shift in (6, 3, 0):
        idx = jnp.bitwise_and(jnp.right_shift(node, shift), 7)
        touching = touching + jnp.where((idx == 0) | (idx == 7), 1.0, 0.0)

    def rows(stack, at):
        return stack[at * leaf_count : (at + 1) * leaf_count]

    visc = visc_ref[...]
    fields = jnp.concatenate([vel_ref[0], vel_ref[1], vel_ref[2], press_ref[...]], axis=0)
    halves = [dot(fields[:, at : at + 256], dyz_ref[...]) for at in (0, 256)]
    grads = [
        dot(fields, dx_ref[...]),
        jnp.concatenate([half[:, :256] for half in halves], axis=1),
        jnp.concatenate([half[:, 256:] for half in halves], axis=1),
    ]
    mass = -(rows(grads[0], 0) + rows(grads[1], 1) + rows(grads[2], 2)) * mass_scale
    mass_ref[...] = jnp.where(live, mass, 0.0)
    stress = {}
    for first in range(3):
        for second in range(first, 3):
            value = (visc * (rows(grads[second], first) + rows(grads[first], second))).astype(bf16)
            stress[first, second] = stress[second, first] = value
    columns = [jnp.concatenate([stress[comp, dim] for comp in range(3)], axis=0) for dim in range(3)]
    rest = [
        dot(columns[1][:, at : at + 256], dyz_ref[:, :256]) + dot(columns[2][:, at : at + 256], dyz_ref[:, 256:])
        for at in (0, 256)
    ]
    div = dot(columns[0], dx_ref[...]) + jnp.concatenate(rest, axis=1)
    for comp in range(3):
        jump = touching * vel_ref[comp].astype(f32)
        part = (penalty * visc * jump - rows(div, comp) + rows(grads[comp], 3)) * out_scale
        part_ref[comp] = jnp.where(live, part, 0.0)

    box = box_ref[pl.ds(pl.multiple_of(morton * 8, 8), 8), :]
    move = binomial_ref[...]
    for dim, stride in enumerate((36, 6, 1)):
        col = lax.broadcasted_iota(jnp.int32, (1, 256), 1) // stride % 6
        row = lax.broadcasted_iota(jnp.int32, (256, 1), 0) // stride % 6
        power = col - row
        along = box[dim : dim + 1, 3:4]
        factor = jnp.ones((1, 1), f32)
        raised = jnp.ones((256, 256), f32)
        for degree in range(1, DEG + 1):
            factor = factor * along
            raised = jnp.where(power == degree, factor, raised)
        move = move * raised
    move_ref[...] = move


def shifted(tiles, geom):
    width = tiles[0].shape
    scale = jnp.broadcast_to(geom[3:4, :], width)
    level = lax.broadcasted_iota(jnp.int32, width, 0)
    depth = jnp.ones(width, f32)
    for power in range(1, DEG + 1):
        depth = depth * jnp.where(level >= power, scale, 1.0)
    scales = [depth]
    for _ in range(2 * DEG):
        scales.append(scales[-1] * scale)
    tiles = [tile * scales[at // 6 + at % 6] for at, tile in enumerate(tiles)]
    along = [jnp.broadcast_to(geom[dim : dim + 1, :], width) for dim in range(3)]
    for low in range(1, DEG + 1):
        for power in range(DEG, low - 1, -1):
            for other in range(6):
                at = power * 6 + other
                tiles[at] = tiles[at] + along[0] * tiles[at - 6]
            for other in range(6):
                at = other * 6 + power
                tiles[at] = tiles[at] + along[1] * tiles[at - 1]
    steps = [jnp.where(level >= low, along[2], 0.0) for low in range(1, DEG + 1)]
    for step in steps:
        tiles = [tile + step * pltpu.roll(tile, 1, 0) for tile in tiles]
    return tiles


def split(values, parts):
    pieces = []
    for _ in range(parts):
        pieces.append(values.astype(bf16))
        values = values - pieces[-1].astype(f32)
    return pieces


def moment_kernel(
    part_ref, visc_ref, box_ref, spread_ref, basis_ref, face_basis_ref, compact_ref, spots_ref, *refs
):
    sides = lax.axis_size("sib") // 2
    window_refs = refs[:4]
    asked_refs, their_weight_refs = refs[4 : 3 + sides], refs[3 + sides : 2 + 2 * sides]
    near_ref, served_refs, sums_ref, raw_ref = refs[2 + 2 * sides], refs[3 + 2 * sides : -2], refs[-2], refs[-1]
    morton = lax.axis_index("morton")
    leaf_count = visc_ref.shape[0]
    asked = [spots_ref[...]] + [ref[...] for ref in asked_refs]
    chosen = gathered(asked, window_refs)
    for blocks, out_ref in zip(chosen, (near_ref, *served_refs)):
        for dim, block in enumerate(blocks):
            out_ref[:, dim * FACES : (dim + 1) * FACES] = block

    def add_moments(who, values, table_ref):
        high, low = split(values, 2)
        raw = dot_nt(table_ref[...], high)
        lanes = slice(3 * who * leaf_count, 3 * (who + 1) * leaf_count)
        raw_ref[:, lanes] = raw[:ROWS] + raw[ROWS:] + dot_nt(table_ref[:ROWS, :], low)

    for who, ref in enumerate(their_weight_refs, 1):
        weight = ref[...].astype(f32) * (-penalty * out_scale)
        weight = jnp.concatenate([weight] * 3, axis=0)
        add_moments(who, weight * by_comp(chosen[who]).astype(f32), face_basis_ref)
    jumps = dot(by_comp(chosen[0]), spread_ref[...])
    weight = visc_ref[...] * (penalty * out_scale)
    force = [
        part_ref[comp] - weight * jumps[comp * leaf_count : (comp + 1) * leaf_count] for comp in range(3)
    ]
    add_moments(0, jnp.concatenate(force, axis=0), basis_ref)
    geom = jnp.concatenate([spots[8:] for spots in asked for _ in range(3)], axis=1)
    tiles = shifted([raw_ref[8 * at : 8 * at + 8, :] for at in range(36)], geom)
    span = 3 * leaf_count
    tiles = [sum(tile[:, span * who : span * (who + 1)] for who in range(sides)) for tile in tiles]
    group = lax.broadcasted_iota(jnp.int32, (span, LANES), 0) // leaf_count
    column = lax.broadcasted_iota(jnp.int32, (span, LANES), 1)
    gather = jnp.where((group == column) | (group + 3 == column), 1.0, 0.0).astype(bf16)
    summed = sum(dot(piece, gather) for piece in split(jnp.concatenate(tiles, axis=0), 3))
    box = box_ref[pl.ds(pl.multiple_of(morton * 8, 8), 8), :]
    both = shifted([summed[8 * at : 8 * at + 8, :] for at in range(36)], box)
    flat = jnp.concatenate(both, axis=0).T
    sums = jnp.dot(flat[:8], compact_ref[...], precision=highest, preferred_element_type=f32)
    blank = jnp.zeros((2, LANES), f32)
    to_box = jnp.concatenate([sums[:3, :LANES], sums[:3, LANES:], blank], axis=0)
    to_root = jnp.concatenate([sums[3:6, :LANES], sums[3:6, LANES:], blank], axis=0)
    sib_count = lax.axis_size("sib")
    for other in range(sums_ref.shape[0]):
        sums_ref[other] = jnp.where(morton == other // sib_count, to_box, to_root)


def force_kernel(part_ref, visc_ref, spread_ref, near_ref, *refs):
    got_refs, (force_hbm, force_ref, sems) = refs[:-3], refs[-3:]
    faces = near_ref[...]
    for got_ref in got_refs:
        faces = faces + got_ref[...]
    weight = visc_ref[...] * (penalty * out_scale)
    stores = []
    for comp in range(3):
        lanes = [(dim * 3 + comp) * LANES for dim in range(3)]
        jump = dot(jnp.concatenate([faces[:, at : at + LANES] for at in lanes], axis=1), spread_ref[...])
        force_ref[comp] = part_ref[comp] - weight * jump
        stores.append(pltpu.make_async_copy(force_ref.at[comp], force_hbm.at[comp], sems.at[comp]))
        stores[-1].start()
    for store in stores:
        store.wait()


def final_kernel(sums_ref, move_ref, box_ref, root_ref):
    sib_count = lax.axis_size("sib")
    morton = lax.axis_index("morton")
    box = jnp.zeros(sums_ref.shape[1:], f32)
    root = jnp.zeros(sums_ref.shape[1:], f32)
    for group in range(sums_ref.shape[0] // sib_count):
        total = jnp.sum(sums_ref[group * sib_count : (group + 1) * sib_count], axis=0)
        box = box + jnp.where(morton == group, total, 0.0)
        root = root + jnp.where(morton == group, 0.0, total)
    box = jnp.concatenate([box[:3], box[3:6]], axis=1)
    root = jnp.concatenate([root[:3], root[3:6]], axis=1)
    box8 = jnp.concatenate([box, jnp.zeros((5, 2 * LANES), f32)], axis=0)
    root = root + jnp.dot(box8, move_ref[...], precision=highest, preferred_element_type=f32)[:3]
    for comp in range(3):
        box_ref[comp] = box[comp : comp + 1, :MOMENTS]
        root_ref[comp] = root[comp : comp + 1, :MOMENTS]


def call(kernel, shapes, flops, scalars, operands, scratch=(), place=pltpu.VMEM, outs=None, grant=32):
    specs = [pl.BlockSpec(memory_space=pltpu.SMEM)] * len(scalars)
    specs += [pl.BlockSpec(memory_space=place)] * len(operands)
    outs = outs or [pltpu.VMEM] * len(shapes)
    moved = sum(array.size * array.dtype.itemsize for array in operands)
    return pl.pallas_call(
        kernel,
        out_shape=[jax.ShapeDtypeStruct(shape, dtype) for shape, dtype in shapes],
        in_specs=specs,
        out_specs=[pl.BlockSpec(memory_space=out) for out in outs],
        scratch_shapes=list(scratch),
        compiler_params=pltpu.CompilerParams(vmem_limit_bytes=grant * 2**20),
        cost_estimate=pl.CostEstimate(flops=flops, bytes_accessed=moved, transcendentals=0),
    )(*scalars, *operands)


def on_device(velocity, pressure, viscosity, levels, morton_keys, counts, neighbors):
    leaf_count = velocity.shape[0]
    morton_count = lax.axis_size("morton")
    along_x, along_yz = operator_tables()
    dx_table = jnp.asarray(along_x.astype(np.float32)).astype(bf16)
    dyz_table = jnp.asarray(along_yz.astype(np.float32)).astype(bf16)
    pick = jnp.asarray(face_table().astype(np.float32)).astype(bf16)
    spread = jnp.asarray(spread_table().astype(np.float32)).astype(bf16)
    basis = basis_tables()
    face_basis = (basis.astype(np.float32) @ spread_table().T.astype(np.float32)).astype(jnp.bfloat16)
    basis, face_basis = jnp.asarray(basis), jnp.asarray(face_basis)
    boxes = jnp.asarray(box_table(morton_count))
    vel = jnp.transpose(velocity, (1, 0, 2))
    nbrs = jnp.transpose(neighbors, (1, 0))

    width = 3 * FACES
    sib_count = lax.axis_size("sib")
    sides = sib_count // 2
    other_sides = [2 * side for side in range(1, sides)]
    faces, even, odd, weights, *spots = call(
        pack_kernel,
        [
            ((leaf_count, width), bf16),
            ((BAND, width), bf16),
            ((BAND, width), bf16),
            ((leaf_count, FACES), bf16),
        ]
        + [((16, leaf_count), f32)] * sides,
        4 * 10**8,
        [counts],
        [vel, viscosity, nbrs, levels.reshape(1, -1), morton_keys.reshape(1, -1), boxes, pick],
        grant=60,
    )
    odd, even = pairs(odd, 1), pairs(even, 0)
    asked = [swap(block, "sib", apart) for block, apart in zip(spots[1:], other_sides)]
    their_weights = [swap(weights, "sib", apart) for apart in other_sides]
    bands = jnp.concatenate([even, odd], axis=0)
    part, continuity, move = call(
        pre_kernel,
        [
            ((3, leaf_count, NODES), f32),
            ((leaf_count, NODES), f32),
            ((256, 256), f32),
        ],
        2 * 10**9,
        [counts],
        [vel, pressure, viscosity, dx_table, dyz_table, boxes, jnp.asarray(move_table(morton_count))],
    )
    bands, part, asked, their_weights = lax.optimization_barrier((bands, part, asked, their_weights))
    window = [faces, swap(faces, "sib", 1), bands, swap(bands, "sib", 1)]
    near, *served, sums = call(
        moment_kernel,
        [((leaf_count, width), bf16)] * sides + [((morton_count * sib_count, 8, LANES), f32)],
        2 * 10**9,
        [],
        [
            part, viscosity, boxes, spread, basis, face_basis, jnp.asarray(compact_table()), spots[0],
            *window, *asked, *their_weights,
        ],
        [pltpu.VMEM((ROWS, 3 * sides * leaf_count), f32)],
    )
    got = [swap(block, "sib", apart) for block, apart in zip(served, other_sides)]
    every = lax.all_to_all(sums, ("morton", "sib"), 0, 0, tiled=True)
    every, *got = lax.optimization_barrier((every, *got))
    (force,) = call(
        force_kernel,
        [((3, leaf_count, NODES), f32)],
        2 * 10**8,
        [],
        [part, viscosity, spread, near, *got],
        [pltpu.VMEM((3, leaf_count, NODES), f32), pltpu.SemaphoreType.DMA((3,))],
        outs=[pltpu.HBM],
    )
    box, root = call(
        final_kernel,
        [((3, 1, MOMENTS), f32), ((3, 1, MOMENTS), f32)],
        10**5,
        [],
        [every, move],
    )
    return (
        jnp.transpose(force, (1, 0, 2)),
        continuity,
        jnp.transpose(box, (1, 0, 2)),
        jnp.transpose(root, (1, 0, 2)),
    )


def solution(mesh):
    spread_all = ("morton", "sib")
    in_specs = (
        P(spread_all, None, None),
        P(spread_all, None),
        P(spread_all, None),
        P(spread_all),
        P(spread_all),
        P(),
        P(spread_all, None),
    )
    out_specs = (
        P(spread_all, None, None),
        P(spread_all, None),
        P("morton", None, None),
        P("morton", None, None),
    )
    return jax.shard_map(
        on_device, mesh=mesh, in_specs=in_specs, out_specs=out_specs, check_vma=False
    )
```

```python
import math

import jax
import jax.numpy as jnp
import numpy as np
from jax import lax
from jax.experimental import pallas as pl
from jax.experimental.pallas import tpu as pltpu
from jax.sharding import PartitionSpec as P

DEG = 5
LMAX = 7
MOMENTS = 216
BAND = 32
NODES = 512
FACES = 384
ROWS = 288
LANES = 128

penalty = 256.0
out_scale = 1.0 / 1024.0
mass_scale = 1.0 / 32.0
highest = lax.Precision.HIGHEST
f32 = jnp.float32
bf16 = jnp.bfloat16


def cheb_matrix():
    points = -np.cos(np.pi * np.arange(8) / 7.0)
    weights = np.array([(-1.0) ** node for node in range(8)])
    weights[0] *= 0.5
    weights[7] *= 0.5
    derivative = np.zeros((8, 8))
    for row in range(8):
        for col in range(8):
            if row != col:
                derivative[row, col] = weights[col] / weights[row] / (points[row] - points[col])
        derivative[row, row] = -np.sum(derivative[row])
    return points, derivative


def operator_tables():
    _, derivative = cheb_matrix()
    along_x = np.kron(derivative, np.eye(64)).T
    along_y = np.kron(np.eye(4), np.kron(derivative, np.eye(8))).T
    along_z = np.kron(np.eye(32), derivative).T
    return np.concatenate([along_x, np.concatenate([along_y, along_z], axis=1)], axis=0)


def face_table():
    pick = np.zeros((NODES, FACES))
    for face in range(6):
        for first in range(8):
            for second in range(8):
                coords = [first, second]
                coords.insert(face // 2, 7 * (face % 2))
                node = 64 * coords[0] + 8 * coords[1] + coords[2]
                pick[node, face * 64 + first * 8 + second] = 1.0
    return pick


def spread_table():
    pick = face_table()
    order = np.concatenate([np.arange(64) + 64 * (face ^ 1) for face in range(6)])
    return pick[:, order].T


def basis_tables():
    points, _ = cheb_matrix()
    powers = np.stack([points**power for power in range(DEG + 1)])
    basis = np.zeros((6, 6, 8, 8, 8, 8))
    basis[:, :, :6] = np.einsum("xa,yb,zc->xyzabc", powers, powers, powers)
    basis = basis.reshape(ROWS, NODES).astype(np.float32)
    top = np.asarray(basis.astype(jnp.bfloat16))
    rest = np.asarray((basis - top.astype(np.float32)).astype(jnp.bfloat16))
    return np.concatenate([top, rest], axis=0)


def compact_table():
    table = np.zeros((ROWS, 256), np.float32)
    for group in range(36):
        for power in range(6):
            table[group * 8 + power, group * 6 + power] = 1.0 / 512.0
    return table


def box_table(morton_count):
    bits = morton_count.bit_length() - 1
    key_bits = 3 * LMAX - bits
    table = np.zeros((morton_count, 8, LANES), np.float32)
    for morton in range(morton_count):
        base = morton << key_bits
        lows, sides = [], []
        for offset in (2, 1, 0):
            free = max(0, min(LMAX, (key_bits - offset + 2) // 3))
            cell = sum(((base >> (3 * bit + offset)) & 1) << bit for bit in range(LMAX))
            sides.append(2.0**free / 2.0**LMAX)
            lows.append(cell / 2.0**LMAX)
        scale = 0.5 * max(sides)
        for dim in range(3):
            center = lows[dim] + 0.5 * sides[dim]
            table[morton, dim, 3:6] = (center - 0.5) / 0.5
            table[morton, 4 + dim] = center
        table[morton, 3] = 1.0
        table[morton, 3, 3:6] = scale / 0.5
        table[morton, 7] = 1.0 / scale
    return table.reshape(morton_count * 8, LANES)


def swap(block, axis, apart):
    return lax.ppermute(block, axis, [(at, at ^ apart) for at in range(lax.axis_size(axis))])


def pairs(block, first):
    route = []
    for low in range(first, lax.axis_size("morton") - 1, 2):
        route += [(low, low + 1), (low + 1, low)]
    return lax.ppermute(block, "morton", route)


def dot(left, right):
    return jnp.dot(left, right, preferred_element_type=f32)


def dot_nt(left, right, precision=None):
    return lax.dot_general(
        left, right, (((1,), (1,)), ((), ())), preferred_element_type=f32, precision=precision
    )


def pack_kernel(
    counts_ref, vel_ref, visc_ref, nbrs_ref, levels_ref, keys_ref, box_ref, pick_ref,
    faces_ref, even_ref, odd_ref, spots_ref, *request_refs,
):
    sib_count = lax.axis_size("sib")
    morton = lax.axis_index("morton")
    sib = lax.axis_index("sib")
    own = morton * sib_count + sib
    leaf_count = faces_ref.shape[0]
    fields = jnp.concatenate([vel_ref[0], vel_ref[1], vel_ref[2], visc_ref[...].astype(bf16)], axis=0)
    picked = dot(fields, pick_ref[...])
    for dim in range(3):
        block = picked[3 * leaf_count :, dim * LANES : (dim + 1) * LANES]
        block = pltpu.roll(block, LANES // 2, 1).astype(bf16)
        for request_ref in request_refs:
            request_ref[:leaf_count, dim * LANES : (dim + 1) * LANES] = block
    picked = picked[: 3 * leaf_count].astype(bf16)
    for comp in range(3):
        for dim in range(3):
            lane = (dim * 3 + comp) * LANES
            rows = picked[comp * leaf_count : (comp + 1) * leaf_count]
            faces_ref[:, lane : lane + LANES] = rows[:, dim * LANES : (dim + 1) * LANES]
    first = counts_ref[own] - BAND
    row = lax.broadcasted_iota(jnp.int32, (BAND, leaf_count), 0)
    col = lax.broadcasted_iota(jnp.int32, (BAND, leaf_count), 1)
    last_rows = jnp.where(col == row + first, 1.0, 0.0).astype(bf16)
    high = dot(last_rows, faces_ref[...]).astype(bf16)
    low = faces_ref[:BAND, :]
    is_odd = jnp.bitwise_and(morton, 1) == 1
    even_ref[...] = jnp.where(is_odd, low, high)
    odd_ref[...] = jnp.where(is_odd, high, low)

    nbrs = nbrs_ref[...]
    target = jnp.maximum(nbrs, 0)
    owner = target // leaf_count
    slot = target - owner * leaf_count
    owner_morton = owner // sib_count
    owner_sib = owner - owner_morton * sib_count
    step = owner_morton - morton
    below = jnp.maximum(morton - 1, 0) * sib_count
    band_start = jnp.zeros_like(slot)
    for other in range(sib_count):
        band_start = jnp.where(owner_sib == other, counts_ref[below + other] - BAND, band_start)
    below_at = BAND * (1 - jnp.bitwise_and(morton, 1))
    in_band = jnp.where(step < 0, slot - band_start + below_at, slot + BAND - below_at)
    box = box_ref[pl.ds(pl.multiple_of(morton * 8, 8), 8), :]
    shift_bits = 3 * (LMAX - levels_ref[...])
    anchor = jnp.left_shift(jnp.right_shift(keys_ref[...], shift_bits), shift_bits)
    span = jnp.left_shift(jnp.ones_like(shift_bits), LMAX - levels_ref[...]).astype(f32)
    finest = 1.0 / float(2**LMAX)
    places = []
    for dim, offset in enumerate((2, 1, 0)):
        cell = jnp.zeros_like(anchor)
        for bit in range(LMAX):
            picked = jnp.bitwise_and(jnp.right_shift(anchor, 3 * bit + offset), 1)
            cell = cell + jnp.left_shift(picked, bit)
        center = (cell.astype(f32) + 0.5 * span) * finest
        places.append((center - box[4 + dim : 5 + dim, :]) * box[7:8, :])
    places.append(0.5 * span * finest * box[7:8, :])
    places.append(jnp.zeros((4, leaf_count), f32))
    geom = jnp.concatenate(places, axis=0)
    for side in range(sib_count // 2):
        piece = jnp.bitwise_xor(owner_sib, jnp.bitwise_xor(sib, 2 * side))
        spot = jnp.where(step == 0, piece * leaf_count + slot, 2 * leaf_count + piece * (2 * BAND) + in_band)
        spot = jnp.where((nbrs >= 0) & (piece < 2), spot, -1)
        if side == 0:
            spots_ref[...] = jnp.concatenate([spot.astype(f32), jnp.zeros((2, leaf_count), f32), geom], axis=0)
            continue
        whole = jnp.right_shift(spot, 4)
        parts = [whole.astype(f32), (spot - 16 * whole).astype(f32), geom[:4]]
        request_ref = request_refs[side - 1]
        request_ref[leaf_count:, :LANES] = jnp.concatenate(parts, axis=0).astype(bf16)
        request_ref[leaf_count:, LANES:] = jnp.zeros((16, FACES - LANES), bf16)


def gathered(asked, window_refs):
    leaf_count = asked[0].shape[1]
    rows = sum(ref.shape[0] for ref in window_refs)
    blank = jnp.full((LANES - 8 * len(asked), leaf_count), -1.0, f32)
    places = jnp.concatenate([spots[:8] for spots in asked] + [blank], axis=0).T.astype(jnp.int32)
    cols = lax.broadcasted_iota(jnp.int32, (leaf_count, rows), 1)
    upper = jnp.bitwise_and(lax.broadcasted_iota(jnp.int32, (leaf_count, FACES), 1), 64) > 0
    chosen = [[] for _ in asked]
    for dim in range(3):
        at = dim * FACES
        window = jnp.concatenate([ref[:, at : at + FACES] for ref in window_refs], axis=0)
        faces = [8 * who + face for who in range(len(asked)) for face in (2 * dim, 2 * dim + 1)]
        onehot = [jnp.where(cols == places[:, face : face + 1], 1.0, 0.0).astype(bf16) for face in faces]
        found = dot(jnp.concatenate(onehot, axis=0), window)
        for who in range(len(asked)):
            first, second = (found[(2 * who + side) * leaf_count : (2 * who + side + 1) * leaf_count] for side in (0, 1))
            chosen[who].append(jnp.where(upper, first, second).astype(bf16))
    return chosen


def by_comp(chosen):
    comps = [
        jnp.concatenate([block[:, comp * LANES : (comp + 1) * LANES] for block in chosen], axis=1) for comp in range(3)
    ]
    return jnp.concatenate(comps, axis=0)


def pre_kernel(
    counts_ref, vel_ref, press_ref, visc_ref, table_ref, box_ref,
    part_ref, mass_ref, move_ref,
):
    sib_count = lax.axis_size("sib")
    morton_count = lax.axis_size("morton")
    morton = lax.axis_index("morton")
    own = morton * sib_count + lax.axis_index("sib")
    leaf_count = mass_ref.shape[0]
    live = lax.broadcasted_iota(jnp.int32, (leaf_count, NODES), 0) < counts_ref[own]
    node = lax.broadcasted_iota(jnp.int32, (1, NODES), 1)
    touching = jnp.zeros((1, NODES), f32)
    for shift in (6, 3, 0):
        idx = jnp.bitwise_and(jnp.right_shift(node, shift), 7)
        touching = touching + jnp.where((idx == 0) | (idx == 7), 1.0, 0.0)

    def rows(stack, at):
        return stack[at * leaf_count : (at + 1) * leaf_count]

    visc = visc_ref[...]
    fields = jnp.concatenate([vel_ref[0], vel_ref[1], vel_ref[2], press_ref[...]], axis=0)
    halves = [dot(fields[:, at : at + 256], table_ref[NODES:, :]) for at in (0, 256)]
    grads = [
        dot(fields, table_ref[:NODES, :]),
        jnp.concatenate([half[:, :256] for half in halves], axis=1),
        jnp.concatenate([half[:, 256:] for half in halves], axis=1),
    ]
    mass = -(rows(grads[0], 0) + rows(grads[1], 1) + rows(grads[2], 2)) * mass_scale
    mass_ref[...] = jnp.where(live, mass, 0.0)
    stress = {}
    for first in range(3):
        for second in range(first, 3):
            value = (visc * (rows(grads[second], first) + rows(grads[first], second))).astype(bf16)
            stress[first, second] = stress[second, first] = value
    columns = [jnp.concatenate([stress[comp, dim] for comp in range(3)], axis=0) for dim in range(3)]
    rest = [
        dot(columns[1][:, at : at + 256], table_ref[NODES:, :256]) + dot(columns[2][:, at : at + 256], table_ref[NODES:, 256:])
        for at in (0, 256)
    ]
    div = dot(columns[0], table_ref[:NODES, :]) + jnp.concatenate(rest, axis=1)
    for comp in range(3):
        jump = touching * vel_ref[comp].astype(f32)
        part = (penalty * visc * jump - rows(div, comp) + rows(grads[comp], 3)) * out_scale
        part_ref[comp] = jnp.where(live, part, 0.0)

    box = box_ref[pl.ds(pl.multiple_of(morton * 8, 8), 8), :]
    move = jnp.ones((256, 256), f32)
    for dim, stride in enumerate((36, 6, 1)):
        col = lax.broadcasted_iota(jnp.int32, (1, 256), 1) // stride % 6
        row = lax.broadcasted_iota(jnp.int32, (256, 1), 0) // stride % 6
        along, scale = box[dim : dim + 1, 3:4], box[3:4, 3:4]
        powers = [jnp.ones((1, 1), f32)]
        for _ in range(DEG):
            powers.append(powers[-1] * along)
        factor = jnp.zeros((256, 256), f32)
        below = jnp.ones((1, 1), f32)
        for low in range(DEG + 1):
            line = jnp.zeros((1, 256), f32)
            for high in range(low, DEG + 1):
                line = jnp.where(col == high, powers[high - low] * below * float(math.comb(high, low)), line)
            factor = jnp.where(row == low, line, factor)
            below = below * scale
        move = move * factor
    move_ref[...] = move


def shifted(tiles, geom):
    width = tiles[0].shape
    scale = jnp.broadcast_to(geom[3:4, :], width)
    level = lax.broadcasted_iota(jnp.int32, width, 0)
    depth = jnp.ones(width, f32)
    for power in range(1, DEG + 1):
        depth = depth * jnp.where(level >= power, scale, 1.0)
    scales = [depth]
    for _ in range(2 * DEG):
        scales.append(scales[-1] * scale)
    tiles = [tile * scales[at // 6 + at % 6] for at, tile in enumerate(tiles)]
    along = [jnp.broadcast_to(geom[dim : dim + 1, :], width) for dim in range(3)]
    for low in range(1, DEG + 1):
        for power in range(DEG, low - 1, -1):
            for other in range(6):
                at = power * 6 + other
                tiles[at] = tiles[at] + along[0] * tiles[at - 6]
            for other in range(6):
                at = other * 6 + power
                tiles[at] = tiles[at] + along[1] * tiles[at - 1]
    steps = [jnp.where(level >= low, along[2], 0.0) for low in range(1, DEG + 1)]
    for step in steps:
        tiles = [tile + step * pltpu.roll(tile, 1, 0) for tile in tiles]
    return tiles


def split(values, parts):
    pieces = []
    for _ in range(parts):
        pieces.append(values.astype(bf16))
        values = values - pieces[-1].astype(f32)
    return pieces


def moment_kernel(
    part_ref, visc_ref, box_ref, spread_ref, basis_ref, face_basis_ref, compact_ref, spots_ref, *refs
):
    sides = lax.axis_size("sib") // 2
    window_refs = refs[:4]
    request_refs = refs[4 : 3 + sides]
    near_ref, served_refs, sums_ref, raw_ref = refs[3 + sides], refs[4 + sides : -2], refs[-2], refs[-1]
    morton = lax.axis_index("morton")
    leaf_count = visc_ref.shape[0]
    asked = [spots_ref[...]]
    for ref in request_refs:
        parts = ref[leaf_count:, :LANES].astype(f32)
        blank = jnp.zeros((2, leaf_count), f32)
        asked.append(
            jnp.concatenate([parts[:6] * 16.0 + parts[6:12], blank, parts[12:], jnp.zeros((4, leaf_count), f32)], axis=0)
        )
    chosen = gathered(asked, window_refs)
    for blocks, out_ref in zip(chosen, (near_ref, *served_refs)):
        for dim, block in enumerate(blocks):
            out_ref[:, dim * FACES : (dim + 1) * FACES] = block

    def add_moments(who, values, table_ref):
        high, low = split(values, 2)
        raw = dot_nt(table_ref[...], high)
        lanes = slice(3 * who * leaf_count, 3 * (who + 1) * leaf_count)
        raw_ref[:, lanes] = raw[:ROWS] + raw[ROWS:] + dot_nt(table_ref[:ROWS, :], low)

    for who, ref in enumerate(request_refs, 1):
        weight = ref[:leaf_count].astype(f32) * (-penalty * out_scale)
        weight = jnp.concatenate([weight] * 3, axis=0)
        add_moments(who, weight * by_comp(chosen[who]).astype(f32), face_basis_ref)
    jumps = dot(by_comp(chosen[0]), spread_ref[...])
    weight = visc_ref[...] * (penalty * out_scale)
    force = [
        part_ref[comp] - weight * jumps[comp * leaf_count : (comp + 1) * leaf_count] for comp in range(3)
    ]
    add_moments(0, jnp.concatenate(force, axis=0), basis_ref)
    geom = jnp.concatenate([spots[8:] for spots in asked for _ in range(3)], axis=1)
    tiles = shifted([raw_ref[8 * at : 8 * at + 8, :] for at in range(36)], geom)
    span = 3 * leaf_count
    tiles = [sum(tile[:, span * who : span * (who + 1)] for who in range(sides)) for tile in tiles]
    group = lax.broadcasted_iota(jnp.int32, (span, LANES), 0) // leaf_count
    column = lax.broadcasted_iota(jnp.int32, (span, LANES), 1)
    gather = jnp.where((group == column) | (group + 3 == column), 1.0, 0.0).astype(bf16)
    summed = sum(dot(piece, gather) for piece in split(jnp.concatenate(tiles, axis=0), 3))
    box = box_ref[pl.ds(pl.multiple_of(morton * 8, 8), 8), :]
    both = shifted([summed[8 * at : 8 * at + 8, :] for at in range(36)], box)
    flat = jnp.concatenate(both, axis=0).T
    sums = jnp.dot(flat[:8], compact_ref[...], precision=highest, preferred_element_type=f32)
    blank = jnp.zeros((2, LANES), f32)
    to_box = jnp.concatenate([sums[:3, :LANES], sums[:3, LANES:], blank], axis=0)
    to_root = jnp.concatenate([sums[3:6, :LANES], sums[3:6, LANES:], blank], axis=0)
    sib_count = lax.axis_size("sib")
    for other in range(sums_ref.shape[0]):
        sums_ref[other] = jnp.where(morton == other // sib_count, to_box, to_root)


def last_kernel(part_ref, visc_ref, spread_ref, sums_ref, move_ref, near_ref, *refs):
    got_refs, (force_hbm, box_ref, root_ref, force_ref, sems) = refs[:-5], refs[-5:]
    faces = near_ref[...]
    for got_ref in got_refs:
        faces = faces + got_ref[...]
    weight = visc_ref[...] * (penalty * out_scale)
    stores = []
    for comp in range(3):
        lanes = [(dim * 3 + comp) * LANES for dim in range(3)]
        jump = dot(jnp.concatenate([faces[:, at : at + LANES] for at in lanes], axis=1), spread_ref[...])
        force_ref[comp] = part_ref[comp] - weight * jump
        stores.append(pltpu.make_async_copy(force_ref.at[comp], force_hbm.at[comp], sems.at[comp]))
        stores[-1].start()
    sib_count = lax.axis_size("sib")
    morton = lax.axis_index("morton")
    box = jnp.zeros(sums_ref.shape[1:], f32)
    root = jnp.zeros(sums_ref.shape[1:], f32)
    for group in range(sums_ref.shape[0] // sib_count):
        total = jnp.sum(sums_ref[group * sib_count : (group + 1) * sib_count], axis=0)
        box = box + jnp.where(morton == group, total, 0.0)
        root = root + jnp.where(morton == group, 0.0, total)
    box = jnp.concatenate([box[:3], box[3:6]], axis=1)
    root = jnp.concatenate([root[:3], root[3:6]], axis=1)
    box8 = jnp.concatenate([box, jnp.zeros((5, 2 * LANES), f32)], axis=0)
    root = root + jnp.dot(box8, move_ref[...], precision=highest, preferred_element_type=f32)[:3]
    for comp in range(3):
        box_ref[comp] = box[comp : comp + 1, :MOMENTS]
        root_ref[comp] = root[comp : comp + 1, :MOMENTS]
    for store in stores:
        store.wait()


def call(kernel, shapes, flops, scalars, operands, scratch=(), place=pltpu.VMEM, outs=None, grant=32):
    specs = [pl.BlockSpec(memory_space=pltpu.SMEM)] * len(scalars)
    specs += [pl.BlockSpec(memory_space=place)] * len(operands)
    outs = outs or [pltpu.VMEM] * len(shapes)
    moved = sum(array.size * array.dtype.itemsize for array in operands)
    return pl.pallas_call(
        kernel,
        out_shape=[jax.ShapeDtypeStruct(shape, dtype) for shape, dtype in shapes],
        in_specs=specs,
        out_specs=[pl.BlockSpec(memory_space=out) for out in outs],
        scratch_shapes=list(scratch),
        compiler_params=pltpu.CompilerParams(vmem_limit_bytes=grant * 2**20),
        cost_estimate=pl.CostEstimate(flops=flops, bytes_accessed=moved, transcendentals=0),
    )(*scalars, *operands)


def on_device(velocity, pressure, viscosity, levels, morton_keys, counts, neighbors):
    leaf_count = velocity.shape[0]
    morton_count = lax.axis_size("morton")
    tables = jnp.asarray(operator_tables().astype(np.float32)).astype(bf16)
    pick = jnp.asarray(face_table().astype(np.float32)).astype(bf16)
    spread = jnp.asarray(spread_table().astype(np.float32)).astype(bf16)
    basis = basis_tables()
    face_basis = (basis.astype(np.float32) @ spread_table().T.astype(np.float32)).astype(jnp.bfloat16)
    basis, face_basis = jnp.asarray(basis), jnp.asarray(face_basis)
    boxes = jnp.asarray(box_table(morton_count))
    vel = jnp.transpose(velocity, (1, 0, 2))
    nbrs = jnp.transpose(neighbors, (1, 0))

    width = 3 * FACES
    sib_count = lax.axis_size("sib")
    sides = sib_count // 2
    other_sides = [2 * side for side in range(1, sides)]
    faces, even, odd, spots, *requests = call(
        pack_kernel,
        [
            ((leaf_count, width), bf16),
            ((BAND, width), bf16),
            ((BAND, width), bf16),
            ((16, leaf_count), f32),
        ]
        + [((leaf_count + 16, FACES), bf16)] * (sides - 1),
        4 * 10**8,
        [counts],
        [vel, viscosity, nbrs, levels.reshape(1, -1), morton_keys.reshape(1, -1), boxes, pick],
        grant=60,
    )
    odd, even = pairs(odd, 1), pairs(even, 0)
    even, requests, pressure = lax.optimization_barrier((even, requests, pressure))
    requests = [swap(block, "sib", apart) for block, apart in zip(requests, other_sides)]
    bands = jnp.concatenate([even, odd], axis=0)
    part, continuity, move = call(
        pre_kernel,
        [
            ((3, leaf_count, NODES), f32),
            ((leaf_count, NODES), f32),
            ((256, 256), f32),
        ],
        2 * 10**9,
        [counts],
        [vel, pressure, viscosity, tables, boxes],
    )
    bands, part, requests = lax.optimization_barrier((bands, part, requests))
    window = [faces, swap(faces, "sib", 1), bands, swap(bands, "sib", 1)]
    near, *served, sums = call(
        moment_kernel,
        [((leaf_count, width), bf16)] * sides + [((morton_count * sib_count, 8, LANES), f32)],
        2 * 10**9,
        [],
        [
            part, viscosity, boxes, spread, basis, face_basis, jnp.asarray(compact_table()), spots,
            *window, *requests,
        ],
        [pltpu.VMEM((ROWS, 3 * sides * leaf_count), f32)],
    )
    got = [swap(block, "sib", apart) for block, apart in zip(served, other_sides)]
    every = lax.all_to_all(sums, ("morton", "sib"), 0, 0, tiled=True)
    every, *got = lax.optimization_barrier((every, *got))
    force, box, root = call(
        last_kernel,
        [((3, leaf_count, NODES), f32), ((3, 1, MOMENTS), f32), ((3, 1, MOMENTS), f32)],
        2 * 10**8,
        [],
        [part, viscosity, spread, every, move, near, *got],
        [pltpu.VMEM((3, leaf_count, NODES), f32), pltpu.SemaphoreType.DMA((3,))],
        outs=[pltpu.HBM, pltpu.VMEM, pltpu.VMEM],
    )
    return (
        jnp.transpose(force, (1, 0, 2)),
        continuity,
        jnp.transpose(box, (1, 0, 2)),
        jnp.transpose(root, (1, 0, 2)),
    )


def solution(mesh):
    spread_all = ("morton", "sib")
    in_specs = (
        P(spread_all, None, None),
        P(spread_all, None),
        P(spread_all, None),
        P(spread_all),
        P(spread_all),
        P(),
        P(spread_all, None),
    )
    out_specs = (
        P(spread_all, None, None),
        P(spread_all, None),
        P("morton", None, None),
        P("morton", None, None),
    )
    return jax.shard_map(
        on_device, mesh=mesh, in_specs=in_specs, out_specs=out_specs, check_vma=False
    )
```

```python
import math

import jax
import jax.numpy as jnp
import numpy as np
from jax import lax
from jax.experimental import pallas as pl
from jax.experimental.pallas import tpu as pltpu
from jax.sharding import PartitionSpec as P

DEG = 5
LMAX = 7
MOMENTS = 216
BAND = 32
NODES = 512
FACES = 384
ROWS = 288
LANES = 128

penalty = 256.0
out_scale = 1.0 / 1024.0
mass_scale = 1.0 / 32.0
highest = lax.Precision.HIGHEST
f32 = jnp.float32
bf16 = jnp.bfloat16


def cheb_matrix():
    points = -np.cos(np.pi * np.arange(8) / 7.0)
    weights = np.array([(-1.0) ** node for node in range(8)])
    weights[0] *= 0.5
    weights[7] *= 0.5
    derivative = np.zeros((8, 8))
    for row in range(8):
        for col in range(8):
            if row != col:
                derivative[row, col] = weights[col] / weights[row] / (points[row] - points[col])
        derivative[row, row] = -np.sum(derivative[row])
    return points, derivative


def operator_tables():
    _, derivative = cheb_matrix()
    along_x = np.kron(derivative, np.eye(64)).T
    along_y = np.kron(np.eye(4), np.kron(derivative, np.eye(8))).T
    along_z = np.kron(np.eye(32), derivative).T
    return np.concatenate([along_x, np.concatenate([along_y, along_z], axis=1)], axis=0)


def face_table():
    pick = np.zeros((NODES, FACES))
    for face in range(6):
        for first in range(8):
            for second in range(8):
                coords = [first, second]
                coords.insert(face // 2, 7 * (face % 2))
                node = 64 * coords[0] + 8 * coords[1] + coords[2]
                pick[node, face * 64 + first * 8 + second] = 1.0
    return pick


def spread_table():
    pick = face_table()
    order = np.concatenate([np.arange(64) + 64 * (face ^ 1) for face in range(6)])
    return pick[:, order].T


def basis_tables():
    points, _ = cheb_matrix()
    powers = np.stack([points**power for power in range(DEG + 1)])
    basis = np.zeros((6, 6, 8, 8, 8, 8))
    basis[:, :, :6] = np.einsum("xa,yb,zc->xyzabc", powers, powers, powers)
    basis = basis.reshape(ROWS, NODES).astype(np.float32)
    top = np.asarray(basis.astype(jnp.bfloat16))
    rest = np.asarray((basis - top.astype(np.float32)).astype(jnp.bfloat16))
    return np.concatenate([top, rest], axis=0)


def compact_table():
    table = np.zeros((ROWS, 256), np.float32)
    for group in range(36):
        for power in range(6):
            table[group * 8 + power, group * 6 + power] = 1.0 / 512.0
    return table


def box_table(morton_count):
    bits = morton_count.bit_length() - 1
    key_bits = 3 * LMAX - bits
    table = np.zeros((morton_count, 8, LANES), np.float32)
    for morton in range(morton_count):
        base = morton << key_bits
        lows, sides = [], []
        for offset in (2, 1, 0):
            free = max(0, min(LMAX, (key_bits - offset + 2) // 3))
            cell = sum(((base >> (3 * bit + offset)) & 1) << bit for bit in range(LMAX))
            sides.append(2.0**free / 2.0**LMAX)
            lows.append(cell / 2.0**LMAX)
        scale = 0.5 * max(sides)
        for dim in range(3):
            center = lows[dim] + 0.5 * sides[dim]
            table[morton, dim, 3:6] = (center - 0.5) / 0.5
            table[morton, 4 + dim] = center
        table[morton, 3] = 1.0
        table[morton, 3, 3:6] = scale / 0.5
        table[morton, 7] = 1.0 / scale
    return table.reshape(morton_count * 8, LANES)


def swap(block, axis, apart):
    return lax.ppermute(block, axis, [(at, at ^ apart) for at in range(lax.axis_size(axis))])


def pairs(block, first):
    route = []
    for low in range(first, lax.axis_size("morton") - 1, 2):
        route += [(low, low + 1), (low + 1, low)]
    return lax.ppermute(block, "morton", route)


def dot(left, right):
    return jnp.dot(left, right, preferred_element_type=f32)


def dot_nt(left, right, precision=None):
    return lax.dot_general(
        left, right, (((1,), (1,)), ((), ())), preferred_element_type=f32, precision=precision
    )


def pack_kernel(
    counts_ref, vel_ref, visc_ref, nbrs_ref, levels_ref, keys_ref, box_ref, pick_ref,
    faces_ref, even_ref, odd_ref, spots_ref, *request_refs,
):
    sib_count = lax.axis_size("sib")
    morton = lax.axis_index("morton")
    sib = lax.axis_index("sib")
    own = morton * sib_count + sib
    leaf_count = faces_ref.shape[0]
    fields = jnp.concatenate([vel_ref[0], vel_ref[1], vel_ref[2], visc_ref[...].astype(bf16)], axis=0)
    picked = dot(fields, pick_ref[...])
    for dim in range(3):
        block = picked[3 * leaf_count :, dim * LANES : (dim + 1) * LANES]
        block = pltpu.roll(block, LANES // 2, 1).astype(bf16)
        for request_ref in request_refs:
            request_ref[:leaf_count, dim * LANES : (dim + 1) * LANES] = block
    picked = picked[: 3 * leaf_count].astype(bf16)
    for comp in range(3):
        for dim in range(3):
            lane = (dim * 3 + comp) * LANES
            rows = picked[comp * leaf_count : (comp + 1) * leaf_count]
            faces_ref[:, lane : lane + LANES] = rows[:, dim * LANES : (dim + 1) * LANES]
    first = counts_ref[own] - BAND
    row = lax.broadcasted_iota(jnp.int32, (BAND, leaf_count), 0)
    col = lax.broadcasted_iota(jnp.int32, (BAND, leaf_count), 1)
    last_rows = jnp.where(col == row + first, 1.0, 0.0).astype(bf16)
    high = dot(last_rows, faces_ref[...]).astype(bf16)
    low = faces_ref[:BAND, :]
    is_odd = jnp.bitwise_and(morton, 1) == 1
    even_ref[...] = jnp.where(is_odd, low, high)
    odd_ref[...] = jnp.where(is_odd, high, low)

    nbrs = nbrs_ref[...]
    target = jnp.maximum(nbrs, 0)
    owner = target // leaf_count
    slot = target - owner * leaf_count
    owner_morton = owner // sib_count
    owner_sib = owner - owner_morton * sib_count
    step = owner_morton - morton
    below = jnp.maximum(morton - 1, 0) * sib_count
    band_start = jnp.zeros_like(slot)
    for other in range(sib_count):
        band_start = jnp.where(owner_sib == other, counts_ref[below + other] - BAND, band_start)
    below_at = BAND * jnp.bitwise_and(morton, 1)
    in_band = jnp.where(step < 0, slot - band_start + below_at, slot + BAND - below_at)
    box = box_ref[pl.ds(pl.multiple_of(morton * 8, 8), 8), :]
    shift_bits = 3 * (LMAX - levels_ref[...])
    anchor = jnp.left_shift(jnp.right_shift(keys_ref[...], shift_bits), shift_bits)
    span = jnp.left_shift(jnp.ones_like(shift_bits), LMAX - levels_ref[...]).astype(f32)
    finest = 1.0 / float(2**LMAX)
    places = []
    for dim, offset in enumerate((2, 1, 0)):
        cell = jnp.zeros_like(anchor)
        for bit in range(LMAX):
            picked = jnp.bitwise_and(jnp.right_shift(anchor, 3 * bit + offset), 1)
            cell = cell + jnp.left_shift(picked, bit)
        center = (cell.astype(f32) + 0.5 * span) * finest
        places.append((center - box[4 + dim : 5 + dim, :]) * box[7:8, :])
    places.append(0.5 * span * finest * box[7:8, :])
    places.append(jnp.zeros((4, leaf_count), f32))
    geom = jnp.concatenate(places, axis=0)
    for side in range(sib_count // 2):
        piece = jnp.bitwise_xor(owner_sib, jnp.bitwise_xor(sib, 2 * side))
        spot = jnp.where(step == 0, piece * leaf_count + slot, 2 * leaf_count + piece * (2 * BAND) + in_band)
        spot = jnp.where((nbrs >= 0) & (piece < 2), spot, -1)
        if side == 0:
            spots_ref[...] = jnp.concatenate([spot.astype(f32), jnp.zeros((2, leaf_count), f32), geom], axis=0)
            continue
        whole = jnp.right_shift(spot, 4)
        parts = [whole.astype(f32), (spot - 16 * whole).astype(f32), geom[:4]]
        request_ref = request_refs[side - 1]
        request_ref[leaf_count:, :LANES] = jnp.concatenate(parts, axis=0).astype(bf16)
        request_ref[leaf_count:, LANES:] = jnp.zeros((16, FACES - LANES), bf16)


def gathered(asked, window_refs):
    leaf_count = asked[0].shape[1]
    rows = sum(ref.shape[0] for ref in window_refs)
    blank = jnp.full((LANES - 8 * len(asked), leaf_count), -1.0, f32)
    places = jnp.concatenate([spots[:8] for spots in asked] + [blank], axis=0).T.astype(jnp.int32)
    cols = lax.broadcasted_iota(jnp.int32, (leaf_count, rows), 1)
    upper = jnp.bitwise_and(lax.broadcasted_iota(jnp.int32, (leaf_count, FACES), 1), 64) > 0
    chosen = [[] for _ in asked]
    for dim in range(3):
        at = dim * FACES
        window = jnp.concatenate([ref[:, at : at + FACES] for ref in window_refs], axis=0)
        faces = [8 * who + face for who in range(len(asked)) for face in (2 * dim, 2 * dim + 1)]
        onehot = [jnp.where(cols == places[:, face : face + 1], 1.0, 0.0).astype(bf16) for face in faces]
        found = dot(jnp.concatenate(onehot, axis=0), window)
        for who in range(len(asked)):
            first, second = (found[(2 * who + side) * leaf_count : (2 * who + side + 1) * leaf_count] for side in (0, 1))
            chosen[who].append(jnp.where(upper, first, second).astype(bf16))
    return chosen


def by_comp(chosen):
    comps = [
        jnp.concatenate([block[:, comp * LANES : (comp + 1) * LANES] for block in chosen], axis=1) for comp in range(3)
    ]
    return jnp.concatenate(comps, axis=0)


def pre_kernel(
    counts_ref, vel_ref, press_ref, visc_ref, table_ref, box_ref,
    part_ref, mass_ref, move_ref,
):
    sib_count = lax.axis_size("sib")
    morton_count = lax.axis_size("morton")
    morton = lax.axis_index("morton")
    own = morton * sib_count + lax.axis_index("sib")
    leaf_count = mass_ref.shape[0]
    live = lax.broadcasted_iota(jnp.int32, (leaf_count, NODES), 0) < counts_ref[own]
    node = lax.broadcasted_iota(jnp.int32, (1, NODES), 1)
    touching = jnp.zeros((1, NODES), f32)
    for shift in (6, 3, 0):
        idx = jnp.bitwise_and(jnp.right_shift(node, shift), 7)
        touching = touching + jnp.where((idx == 0) | (idx == 7), 1.0, 0.0)

    def rows(stack, at):
        return stack[at * leaf_count : (at + 1) * leaf_count]

    visc = visc_ref[...]
    fields = jnp.concatenate([vel_ref[0], vel_ref[1], vel_ref[2], press_ref[...]], axis=0)
    halves = [dot(fields[:, at : at + 256], table_ref[NODES:, :]) for at in (0, 256)]
    grads = [
        dot(fields, table_ref[:NODES, :]),
        jnp.concatenate([half[:, :256] for half in halves], axis=1),
        jnp.concatenate([half[:, 256:] for half in halves], axis=1),
    ]
    mass = -(rows(grads[0], 0) + rows(grads[1], 1) + rows(grads[2], 2)) * mass_scale
    mass_ref[...] = jnp.where(live, mass, 0.0)
    stress = {}
    for first in range(3):
        for second in range(first, 3):
            value = (visc * (rows(grads[second], first) + rows(grads[first], second))).astype(bf16)
            stress[first, second] = stress[second, first] = value
    columns = [jnp.concatenate([stress[comp, dim] for comp in range(3)], axis=0) for dim in range(3)]
    rest = [
        dot(columns[1][:, at : at + 256], table_ref[NODES:, :256]) + dot(columns[2][:, at : at + 256], table_ref[NODES:, 256:])
        for at in (0, 256)
    ]
    div = dot(columns[0], table_ref[:NODES, :]) + jnp.concatenate(rest, axis=1)
    for comp in range(3):
        jump = touching * vel_ref[comp].astype(f32)
        part = (penalty * visc * jump - rows(div, comp) + rows(grads[comp], 3)) * out_scale
        part_ref[comp] = jnp.where(live, part, 0.0)

    box = box_ref[pl.ds(pl.multiple_of(morton * 8, 8), 8), :]
    move = jnp.ones((256, 256), f32)
    for dim, stride in enumerate((36, 6, 1)):
        col = lax.broadcasted_iota(jnp.int32, (1, 256), 1) // stride % 6
        row = lax.broadcasted_iota(jnp.int32, (256, 1), 0) // stride % 6
        along, scale = box[dim : dim + 1, 3:4], box[3:4, 3:4]
        powers = [jnp.ones((1, 1), f32)]
        for _ in range(DEG):
            powers.append(powers[-1] * along)
        factor = jnp.zeros((256, 256), f32)
        below = jnp.ones((1, 1), f32)
        for low in range(DEG + 1):
            line = jnp.zeros((1, 256), f32)
            for high in range(low, DEG + 1):
                line = jnp.where(col == high, powers[high - low] * below * float(math.comb(high, low)), line)
            factor = jnp.where(row == low, line, factor)
            below = below * scale
        move = move * factor
    move_ref[...] = move


def shifted(tiles, geom):
    width = tiles[0].shape
    scale = jnp.broadcast_to(geom[3:4, :], width)
    level = lax.broadcasted_iota(jnp.int32, width, 0)
    depth = jnp.ones(width, f32)
    for power in range(1, DEG + 1):
        depth = depth * jnp.where(level >= power, scale, 1.0)
    scales = [depth]
    for _ in range(2 * DEG):
        scales.append(scales[-1] * scale)
    tiles = [tile * scales[at // 6 + at % 6] for at, tile in enumerate(tiles)]
    along = [jnp.broadcast_to(geom[dim : dim + 1, :], width) for dim in range(3)]
    for low in range(1, DEG + 1):
        for power in range(DEG, low - 1, -1):
            for other in range(6):
                at = power * 6 + other
                tiles[at] = tiles[at] + along[0] * tiles[at - 6]
            for other in range(6):
                at = other * 6 + power
                tiles[at] = tiles[at] + along[1] * tiles[at - 1]
    steps = [jnp.where(level >= low, along[2], 0.0) for low in range(1, DEG + 1)]
    for step in steps:
        tiles = [tile + step * pltpu.roll(tile, 1, 0) for tile in tiles]
    return tiles


def split(values, parts):
    pieces = []
    for _ in range(parts):
        pieces.append(values.astype(bf16))
        values = values - pieces[-1].astype(f32)
    return pieces


def moment_kernel(
    part_ref, visc_ref, box_ref, spread_ref, basis_ref, face_basis_ref, compact_ref, spots_ref, *refs
):
    sides = lax.axis_size("sib") // 2
    window_refs = refs[:4]
    request_refs = refs[4 : 3 + sides]
    near_ref, served_refs, sums_ref, raw_ref = refs[3 + sides], refs[4 + sides : -2], refs[-2], refs[-1]
    morton = lax.axis_index("morton")
    leaf_count = visc_ref.shape[0]
    asked = [spots_ref[...]]
    for ref in request_refs:
        parts = ref[leaf_count:, :LANES].astype(f32)
        blank = jnp.zeros((2, leaf_count), f32)
        asked.append(
            jnp.concatenate([parts[:6] * 16.0 + parts[6:12], blank, parts[12:], jnp.zeros((4, leaf_count), f32)], axis=0)
        )
    chosen = gathered(asked, window_refs)
    for blocks, out_ref in zip(chosen, (near_ref, *served_refs)):
        for dim, block in enumerate(blocks):
            out_ref[:, dim * FACES : (dim + 1) * FACES] = block

    def add_moments(who, values, table_ref):
        high, low = split(values, 2)
        raw = dot_nt(table_ref[...], high)
        lanes = slice(3 * who * leaf_count, 3 * (who + 1) * leaf_count)
        raw_ref[:, lanes] = raw[:ROWS] + raw[ROWS:] + dot_nt(table_ref[:ROWS, :], low)

    for who, ref in enumerate(request_refs, 1):
        weight = ref[:leaf_count].astype(f32) * (-penalty * out_scale)
        weight = jnp.concatenate([weight] * 3, axis=0)
        add_moments(who, weight * by_comp(chosen[who]).astype(f32), face_basis_ref)
    jumps = dot(by_comp(chosen[0]), spread_ref[...])
    weight = visc_ref[...] * (penalty * out_scale)
    force = [
        part_ref[comp] - weight * jumps[comp * leaf_count : (comp + 1) * leaf_count] for comp in range(3)
    ]
    add_moments(0, jnp.concatenate(force, axis=0), basis_ref)
    geom = jnp.concatenate([spots[8:] for spots in asked for _ in range(3)], axis=1)
    tiles = shifted([raw_ref[8 * at : 8 * at + 8, :] for at in range(36)], geom)
    span = 3 * leaf_count
    tiles = [sum(tile[:, span * who : span * (who + 1)] for who in range(sides)) for tile in tiles]
    group = lax.broadcasted_iota(jnp.int32, (span, LANES), 0) // leaf_count
    column = lax.broadcasted_iota(jnp.int32, (span, LANES), 1)
    gather = jnp.where((group == column) | (group + 3 == column), 1.0, 0.0).astype(bf16)
    summed = sum(dot(piece, gather) for piece in split(jnp.concatenate(tiles, axis=0), 3))
    box = box_ref[pl.ds(pl.multiple_of(morton * 8, 8), 8), :]
    both = shifted([summed[8 * at : 8 * at + 8, :] for at in range(36)], box)
    flat = jnp.concatenate(both, axis=0).T
    sums = jnp.dot(flat[:8], compact_ref[...], precision=highest, preferred_element_type=f32)
    blank = jnp.zeros((2, LANES), f32)
    to_box = jnp.concatenate([sums[:3, :LANES], sums[:3, LANES:], blank], axis=0)
    to_root = jnp.concatenate([sums[3:6, :LANES], sums[3:6, LANES:], blank], axis=0)
    sib_count = lax.axis_size("sib")
    for other in range(sums_ref.shape[0]):
        sums_ref[other] = jnp.where(morton == other // sib_count, to_box, to_root)


def last_kernel(part_ref, visc_ref, spread_ref, sums_ref, move_ref, near_ref, *refs):
    got_refs, (force_hbm, box_ref, root_ref, force_ref, sems) = refs[:-5], refs[-5:]
    faces = near_ref[...]
    for got_ref in got_refs:
        faces = faces + got_ref[...]
    weight = visc_ref[...] * (penalty * out_scale)
    stores = []
    for comp in range(3):
        lanes = [(dim * 3 + comp) * LANES for dim in range(3)]
        jump = dot(jnp.concatenate([faces[:, at : at + LANES] for at in lanes], axis=1), spread_ref[...])
        force_ref[comp] = part_ref[comp] - weight * jump
        stores.append(pltpu.make_async_copy(force_ref.at[comp], force_hbm.at[comp], sems.at[comp]))
        stores[-1].start()
    sib_count = lax.axis_size("sib")
    morton = lax.axis_index("morton")
    box = jnp.zeros(sums_ref.shape[1:], f32)
    root = jnp.zeros(sums_ref.shape[1:], f32)
    for group in range(sums_ref.shape[0] // sib_count):
        total = jnp.sum(sums_ref[group * sib_count : (group + 1) * sib_count], axis=0)
        box = box + jnp.where(morton == group, total, 0.0)
        root = root + jnp.where(morton == group, 0.0, total)
    box = jnp.concatenate([box[:3], box[3:6]], axis=1)
    root = jnp.concatenate([root[:3], root[3:6]], axis=1)
    box8 = jnp.concatenate([box, jnp.zeros((5, 2 * LANES), f32)], axis=0)
    root = root + jnp.dot(box8, move_ref[...], precision=highest, preferred_element_type=f32)[:3]
    for comp in range(3):
        box_ref[comp] = box[comp : comp + 1, :MOMENTS]
        root_ref[comp] = root[comp : comp + 1, :MOMENTS]
    for store in stores:
        store.wait()


def call(kernel, shapes, flops, scalars, operands, scratch=(), place=pltpu.VMEM, outs=None, grant=32):
    specs = [pl.BlockSpec(memory_space=pltpu.SMEM)] * len(scalars)
    specs += [pl.BlockSpec(memory_space=place)] * len(operands)
    outs = outs or [pltpu.VMEM] * len(shapes)
    moved = sum(array.size * array.dtype.itemsize for array in operands)
    return pl.pallas_call(
        kernel,
        out_shape=[jax.ShapeDtypeStruct(shape, dtype) for shape, dtype in shapes],
        in_specs=specs,
        out_specs=[pl.BlockSpec(memory_space=out) for out in outs],
        scratch_shapes=list(scratch),
        compiler_params=pltpu.CompilerParams(vmem_limit_bytes=grant * 2**20),
        cost_estimate=pl.CostEstimate(flops=flops, bytes_accessed=moved, transcendentals=0),
    )(*scalars, *operands)


def on_device(velocity, pressure, viscosity, levels, morton_keys, counts, neighbors):
    leaf_count = velocity.shape[0]
    morton_count = lax.axis_size("morton")
    tables = jnp.asarray(operator_tables().astype(np.float32)).astype(bf16)
    pick = jnp.asarray(face_table().astype(np.float32)).astype(bf16)
    spread = jnp.asarray(spread_table().astype(np.float32)).astype(bf16)
    basis = basis_tables()
    face_basis = (basis.astype(np.float32) @ spread_table().T.astype(np.float32)).astype(jnp.bfloat16)
    basis, face_basis = jnp.asarray(basis), jnp.asarray(face_basis)
    boxes = jnp.asarray(box_table(morton_count))
    vel = jnp.transpose(velocity, (1, 0, 2))
    nbrs = jnp.transpose(neighbors, (1, 0))

    width = 3 * FACES
    sib_count = lax.axis_size("sib")
    sides = sib_count // 2
    other_sides = [2 * side for side in range(1, sides)]
    faces, even, odd, spots, *requests = call(
        pack_kernel,
        [
            ((leaf_count, width), bf16),
            ((BAND, width), bf16),
            ((BAND, width), bf16),
            ((16, leaf_count), f32),
        ]
        + [((leaf_count + 16, FACES), bf16)] * (sides - 1),
        4 * 10**8,
        [counts],
        [vel, viscosity, nbrs, levels.reshape(1, -1), morton_keys.reshape(1, -1), boxes, pick],
        grant=60,
    )
    odd, even = pairs(odd, 1), pairs(even, 0)
    across = swap(faces, "sib", 1)
    across, requests, pressure = lax.optimization_barrier((across, requests, pressure))
    requests = [swap(block, "sib", apart) for block, apart in zip(requests, other_sides)]
    part, continuity, move = call(
        pre_kernel,
        [
            ((3, leaf_count, NODES), f32),
            ((leaf_count, NODES), f32),
            ((256, 256), f32),
        ],
        2 * 10**9,
        [counts],
        [vel, pressure, viscosity, tables, boxes],
    )
    odd, even, part, requests = lax.optimization_barrier((odd, even, part, requests))
    bands = jnp.concatenate([odd, even], axis=0)
    window = [faces, across, bands, swap(bands, "sib", 1)]
    near, *served, sums = call(
        moment_kernel,
        [((leaf_count, width), bf16)] * sides + [((morton_count * sib_count, 8, LANES), f32)],
        2 * 10**9,
        [],
        [
            part, viscosity, boxes, spread, basis, face_basis, jnp.asarray(compact_table()), spots,
            *window, *requests,
        ],
        [pltpu.VMEM((ROWS, 3 * sides * leaf_count), f32)],
    )
    got = [swap(block, "sib", apart) for block, apart in zip(served, other_sides)]
    every = lax.all_to_all(sums, ("morton", "sib"), 0, 0, tiled=True)
    every, *got = lax.optimization_barrier((every, *got))
    force, box, root = call(
        last_kernel,
        [((3, leaf_count, NODES), f32), ((3, 1, MOMENTS), f32), ((3, 1, MOMENTS), f32)],
        2 * 10**8,
        [],
        [part, viscosity, spread, every, move, near, *got],
        [pltpu.VMEM((3, leaf_count, NODES), f32), pltpu.SemaphoreType.DMA((3,))],
        outs=[pltpu.HBM, pltpu.VMEM, pltpu.VMEM],
    )
    return (
        jnp.transpose(force, (1, 0, 2)),
        continuity,
        jnp.transpose(box, (1, 0, 2)),
        jnp.transpose(root, (1, 0, 2)),
    )


def solution(mesh):
    spread_all = ("morton", "sib")
    in_specs = (
        P(spread_all, None, None),
        P(spread_all, None),
        P(spread_all, None),
        P(spread_all),
        P(spread_all),
        P(),
        P(spread_all, None),
    )
    out_specs = (
        P(spread_all, None, None),
        P(spread_all, None),
        P("morton", None, None),
        P("morton", None, None),
    )
    return jax.shard_map(
        on_device, mesh=mesh, in_specs=in_specs, out_specs=out_specs, check_vma=False
    )
```

```python
import math

import jax
import jax.numpy as jnp
import numpy as np
from jax import lax
from jax.experimental import pallas as pl
from jax.experimental.pallas import tpu as pltpu
from jax.sharding import PartitionSpec as P

DEG = 5
LMAX = 7
MOMENTS = 216
BAND = 32
NODES = 512
FACES = 384
ROWS = 288
LANES = 128

penalty = 256.0
out_scale = 1.0 / 1024.0
mass_scale = 1.0 / 32.0
highest = lax.Precision.HIGHEST
f32 = jnp.float32
bf16 = jnp.bfloat16


def cheb_matrix():
    points = -np.cos(np.pi * np.arange(8) / 7.0)
    weights = np.array([(-1.0) ** node for node in range(8)])
    weights[0] *= 0.5
    weights[7] *= 0.5
    derivative = np.zeros((8, 8))
    for row in range(8):
        for col in range(8):
            if row != col:
                derivative[row, col] = weights[col] / weights[row] / (points[row] - points[col])
        derivative[row, row] = -np.sum(derivative[row])
    return points, derivative


def derivative_rows():
    _, derivative = cheb_matrix()
    lane = np.arange(NODES)
    return np.concatenate([derivative[lane // 64 % 8].T, derivative[lane // 8 % 8].T, derivative[lane % 8].T], axis=0)


def face_table():
    pick = np.zeros((NODES, FACES))
    for face in range(6):
        for first in range(8):
            for second in range(8):
                coords = [first, second]
                coords.insert(face // 2, 7 * (face % 2))
                node = 64 * coords[0] + 8 * coords[1] + coords[2]
                pick[node, face * 64 + first * 8 + second] = 1.0
    return pick


def spread_table():
    pick = face_table()
    order = np.concatenate([np.arange(64) + 64 * (face ^ 1) for face in range(6)])
    return pick[:, order].T


def basis_tables():
    points, _ = cheb_matrix()
    powers = np.stack([points**power for power in range(DEG + 1)])
    basis = np.zeros((6, 6, 8, 8, 8, 8))
    basis[:, :, :6] = np.einsum("xa,yb,zc->xyzabc", powers, powers, powers)
    basis = basis.reshape(ROWS, NODES).astype(np.float32)
    top = np.asarray(basis.astype(jnp.bfloat16))
    rest = np.asarray((basis - top.astype(np.float32)).astype(jnp.bfloat16))
    return np.concatenate([top, rest], axis=0)


def compact_table():
    table = np.zeros((ROWS, 256), jnp.bfloat16)
    for group in range(36):
        for power in range(6):
            table[group * 8 + power, group * 6 + power] = 1.0 / 512.0
    return table


def box_table(morton_count):
    bits = morton_count.bit_length() - 1
    key_bits = 3 * LMAX - bits
    table = np.zeros((morton_count, 8, LANES), np.float32)
    for morton in range(morton_count):
        base = morton << key_bits
        lows, sides = [], []
        for offset in (2, 1, 0):
            free = max(0, min(LMAX, (key_bits - offset + 2) // 3))
            cell = sum(((base >> (3 * bit + offset)) & 1) << bit for bit in range(LMAX))
            sides.append(2.0**free / 2.0**LMAX)
            lows.append(cell / 2.0**LMAX)
        scale = 0.5 * max(sides)
        for dim in range(3):
            center = lows[dim] + 0.5 * sides[dim]
            table[morton, dim, 3:6] = (center - 0.5) / 0.5
            table[morton, 4 + dim] = center
        table[morton, 3] = 1.0
        table[morton, 3, 3:6] = scale / 0.5
        table[morton, 7] = 1.0 / scale
    return table.reshape(morton_count * 8, LANES)


def swap(block, axis, apart):
    return lax.ppermute(block, axis, [(at, at ^ apart) for at in range(lax.axis_size(axis))])


def pairs(block, first):
    route = []
    for low in range(first, lax.axis_size("morton") - 1, 2):
        route += [(low, low + 1), (low + 1, low)]
    return lax.ppermute(block, "morton", route)


def dot(left, right):
    return jnp.dot(left, right, preferred_element_type=f32)


def dot_nt(left, right, precision=None):
    return lax.dot_general(
        left, right, (((1,), (1,)), ((), ())), preferred_element_type=f32, precision=precision
    )


def pack_kernel(
    counts_ref, vel_ref, visc_ref, nbrs_ref, levels_ref, keys_ref, box_ref, pick_ref,
    faces_ref, even_ref, odd_ref, spots_ref, *request_refs,
):
    sib_count = lax.axis_size("sib")
    morton = lax.axis_index("morton")
    sib = lax.axis_index("sib")
    own = morton * sib_count + sib
    leaf_count = faces_ref.shape[0]
    fields = jnp.concatenate([vel_ref[0], vel_ref[1], vel_ref[2], visc_ref[...].astype(bf16)], axis=0)
    picked = dot(fields, pick_ref[...])
    for dim in range(3):
        block = picked[3 * leaf_count :, dim * LANES : (dim + 1) * LANES]
        block = pltpu.roll(block, LANES // 2, 1).astype(bf16)
        for request_ref in request_refs:
            request_ref[:leaf_count, dim * LANES : (dim + 1) * LANES] = block
    picked = picked[: 3 * leaf_count].astype(bf16)
    for comp in range(3):
        for dim in range(3):
            lane = (dim * 3 + comp) * LANES
            rows = picked[comp * leaf_count : (comp + 1) * leaf_count]
            faces_ref[:, lane : lane + LANES] = rows[:, dim * LANES : (dim + 1) * LANES]
    first = counts_ref[own] - BAND
    row = lax.broadcasted_iota(jnp.int32, (BAND, leaf_count), 0)
    col = lax.broadcasted_iota(jnp.int32, (BAND, leaf_count), 1)
    last_rows = jnp.where(col == row + first, 1.0, 0.0).astype(bf16)
    high = dot(last_rows, faces_ref[...]).astype(bf16)
    low = faces_ref[:BAND, :]
    is_odd = jnp.bitwise_and(morton, 1) == 1
    even_ref[...] = jnp.where(is_odd, low, high)
    odd_ref[...] = jnp.where(is_odd, high, low)

    nbrs = nbrs_ref[...]
    target = jnp.maximum(nbrs, 0)
    owner = target // leaf_count
    slot = target - owner * leaf_count
    owner_morton = owner // sib_count
    owner_sib = owner - owner_morton * sib_count
    step = owner_morton - morton
    below = jnp.maximum(morton - 1, 0) * sib_count
    band_start = jnp.zeros_like(slot)
    for other in range(sib_count):
        band_start = jnp.where(owner_sib == other, counts_ref[below + other] - BAND, band_start)
    below_at = BAND * jnp.bitwise_and(morton, 1)
    in_band = jnp.where(step < 0, slot - band_start + below_at, slot + BAND - below_at)
    box = box_ref[pl.ds(pl.multiple_of(morton * 8, 8), 8), :]
    shift_bits = 3 * (LMAX - levels_ref[...])
    anchor = jnp.left_shift(jnp.right_shift(keys_ref[...], shift_bits), shift_bits)
    span = jnp.left_shift(jnp.ones_like(shift_bits), LMAX - levels_ref[...]).astype(f32)
    finest = 1.0 / float(2**LMAX)
    places = []
    for dim, offset in enumerate((2, 1, 0)):
        cell = jnp.zeros_like(anchor)
        for bit in range(LMAX):
            picked = jnp.bitwise_and(jnp.right_shift(anchor, 3 * bit + offset), 1)
            cell = cell + jnp.left_shift(picked, bit)
        center = (cell.astype(f32) + 0.5 * span) * finest
        places.append((center - box[4 + dim : 5 + dim, :]) * box[7:8, :])
    places.append(0.5 * span * finest * box[7:8, :])
    places.append(jnp.zeros((4, leaf_count), f32))
    geom = jnp.concatenate(places, axis=0)
    for side in range(sib_count // 2):
        piece = jnp.bitwise_xor(owner_sib, jnp.bitwise_xor(sib, 2 * side))
        spot = jnp.where(step == 0, piece * leaf_count + slot, 2 * leaf_count + piece * (2 * BAND) + in_band)
        spot = jnp.where((nbrs >= 0) & (piece < 2), spot, -1)
        if side == 0:
            spots_ref[...] = jnp.concatenate([spot.astype(f32), jnp.zeros((2, leaf_count), f32), geom], axis=0)
            continue
        whole = jnp.right_shift(spot, 4)
        parts = [whole.astype(f32), (spot - 16 * whole).astype(f32), geom[:4]]
        request_ref = request_refs[side - 1]
        request_ref[leaf_count:, :LANES] = jnp.concatenate(parts, axis=0).astype(bf16)
        request_ref[leaf_count:, LANES:] = jnp.zeros((16, FACES - LANES), bf16)


def gathered(asked, window_refs):
    leaf_count = asked[0].shape[1]
    rows = sum(ref.shape[0] for ref in window_refs)
    blank = jnp.full((LANES - 8 * len(asked), leaf_count), -1.0, f32)
    places = jnp.concatenate([spots[:8] for spots in asked] + [blank], axis=0).T.astype(jnp.int32)
    cols = lax.broadcasted_iota(jnp.int32, (leaf_count, rows), 1)
    upper = jnp.bitwise_and(lax.broadcasted_iota(jnp.int32, (leaf_count, FACES), 1), 64) > 0
    chosen = [[] for _ in asked]
    for dim in range(3):
        at = dim * FACES
        window = jnp.concatenate([ref[:, at : at + FACES] for ref in window_refs], axis=0)
        faces = [8 * who + face for who in range(len(asked)) for face in (2 * dim, 2 * dim + 1)]
        onehot = [jnp.where(cols == places[:, face : face + 1], 1.0, 0.0).astype(bf16) for face in faces]
        found = dot(jnp.concatenate(onehot, axis=0), window)
        for who in range(len(asked)):
            first, second = (found[(2 * who + side) * leaf_count : (2 * who + side + 1) * leaf_count] for side in (0, 1))
            chosen[who].append(jnp.where(upper, first, second).astype(bf16))
    return chosen


def by_comp(chosen):
    comps = [
        jnp.concatenate([block[:, comp * LANES : (comp + 1) * LANES] for block in chosen], axis=1) for comp in range(3)
    ]
    return jnp.concatenate(comps, axis=0)


def fill_tables(rows_ref, dx_ref, dyz_ref):
    row = lax.broadcasted_iota(jnp.int32, (64, NODES), 0)
    col = lax.broadcasted_iota(jnp.int32, (64, NODES), 1)
    same = row == jnp.bitwise_and(col, 63)
    for at in range(8):
        dx_ref[64 * at : 64 * at + 64, :] = jnp.where(same, rows_ref[at : at + 1, :], 0.0).astype(bf16)
    row = lax.broadcasted_iota(jnp.int32, (8, 256), 0)
    col = lax.broadcasted_iota(jnp.int32, (8, 256), 1)
    same = row == jnp.bitwise_and(col, 7)
    group = jnp.right_shift(col, 3)
    for pair in range(16):
        blocks = []
        for at in (2 * pair, 2 * pair + 1):
            here = same & (jnp.right_shift(group, 3) == at // 8)
            along_y = jnp.where(here, rows_ref[8 + at % 8 : 9 + at % 8, :256], 0.0)
            along_z = jnp.where(group == at, rows_ref[16:24, :256], 0.0)
            blocks.append(jnp.concatenate([along_y, along_z], axis=1))
        dyz_ref[16 * pair : 16 * pair + 16, :] = jnp.concatenate(blocks, axis=0).astype(bf16)


def stress_kernel(
    counts_ref, vel_ref, press_ref, visc_ref, rows_ref,
    part_ref, mass_ref, stress_ref, dx_ref, dyz_ref,
):
    sib_count = lax.axis_size("sib")
    own = lax.axis_index("morton") * sib_count + lax.axis_index("sib")
    leaf_count = mass_ref.shape[0]
    live = lax.broadcasted_iota(jnp.int32, (leaf_count, NODES), 0) < counts_ref[own]
    node = lax.broadcasted_iota(jnp.int32, (1, NODES), 1)
    touching = jnp.zeros((1, NODES), f32)
    for shift in (6, 3, 0):
        idx = jnp.bitwise_and(jnp.right_shift(node, shift), 7)
        touching = touching + jnp.where((idx == 0) | (idx == 7), 1.0, 0.0)
    fill_tables(rows_ref, dx_ref, dyz_ref)

    def rows(stack, at):
        return stack[at * leaf_count : (at + 1) * leaf_count]

    visc = visc_ref[...]
    fields = jnp.concatenate([vel_ref[0], vel_ref[1], vel_ref[2], press_ref[...]], axis=0)
    halves = [dot(fields[:, at : at + 256], dyz_ref[...]) for at in (0, 256)]
    grads = [
        dot(fields, dx_ref[...]),
        jnp.concatenate([half[:, :256] for half in halves], axis=1),
        jnp.concatenate([half[:, 256:] for half in halves], axis=1),
    ]
    mass = -(rows(grads[0], 0) + rows(grads[1], 1) + rows(grads[2], 2)) * mass_scale
    mass_ref[...] = jnp.where(live, mass, 0.0)
    pairs_at = [(first, second) for first in range(3) for second in range(first, 3)]
    for at, (first, second) in enumerate(pairs_at):
        stress_ref[at] = (visc * (rows(grads[second], first) + rows(grads[first], second))).astype(bf16)
    for comp in range(3):
        jump = touching * vel_ref[comp].astype(f32)
        part_ref[comp] = (penalty * visc * jump + rows(grads[comp], 3)) * out_scale


def divergence_kernel(counts_ref, part_ref, stress_ref, dx_ref, dyz_ref, box_ref, full_ref, move_ref):
    sib_count = lax.axis_size("sib")
    morton = lax.axis_index("morton")
    leaf_count = part_ref.shape[1]
    live = lax.broadcasted_iota(jnp.int32, (leaf_count, NODES), 0) < counts_ref[morton * sib_count + lax.axis_index("sib")]
    at_pair = {(0, 0): 0, (0, 1): 1, (0, 2): 2, (1, 1): 3, (1, 2): 4, (2, 2): 5}
    columns = [
        jnp.concatenate([stress_ref[at_pair[min(comp, dim), max(comp, dim)]] for comp in range(3)], axis=0)
        for dim in range(3)
    ]
    rest = [
        dot(columns[1][:, at : at + 256], dyz_ref[:, :256]) + dot(columns[2][:, at : at + 256], dyz_ref[:, 256:])
        for at in (0, 256)
    ]
    div = dot(columns[0], dx_ref[...]) + jnp.concatenate(rest, axis=1)
    for comp in range(3):
        part = part_ref[comp] - div[comp * leaf_count : (comp + 1) * leaf_count] * out_scale
        full_ref[comp] = jnp.where(live, part, 0.0)
    box = box_ref[pl.ds(pl.multiple_of(morton * 8, 8), 8), :]
    move = jnp.ones((256, 256), f32)
    for dim, stride in enumerate((36, 6, 1)):
        col = lax.broadcasted_iota(jnp.int32, (1, 256), 1) // stride % 6
        row = lax.broadcasted_iota(jnp.int32, (256, 1), 0) // stride % 6
        along, scale = box[dim : dim + 1, 3:4], box[3:4, 3:4]
        powers = [jnp.ones((1, 1), f32)]
        for _ in range(DEG):
            powers.append(powers[-1] * along)
        factor = jnp.zeros((256, 256), f32)
        below = jnp.ones((1, 1), f32)
        for low in range(DEG + 1):
            line = jnp.zeros((1, 256), f32)
            for high in range(low, DEG + 1):
                line = jnp.where(col == high, powers[high - low] * below * float(math.comb(high, low)), line)
            factor = jnp.where(row == low, line, factor)
            below = below * scale
        move = move * factor
    move_ref[...] = move


def shifted(tiles, geom):
    width = tiles[0].shape
    scale = jnp.broadcast_to(geom[3:4, :], width)
    level = lax.broadcasted_iota(jnp.int32, width, 0)
    depth = jnp.ones(width, f32)
    for power in range(1, DEG + 1):
        depth = depth * jnp.where(level >= power, scale, 1.0)
    scales = [depth]
    for _ in range(2 * DEG):
        scales.append(scales[-1] * scale)
    tiles = [tile * scales[at // 6 + at % 6] for at, tile in enumerate(tiles)]
    along = [jnp.broadcast_to(geom[dim : dim + 1, :], width) for dim in range(3)]
    for low in range(1, DEG + 1):
        for power in range(DEG, low - 1, -1):
            for other in range(6):
                at = power * 6 + other
                tiles[at] = tiles[at] + along[0] * tiles[at - 6]
            for other in range(6):
                at = other * 6 + power
                tiles[at] = tiles[at] + along[1] * tiles[at - 1]
    steps = [jnp.where(level >= low, along[2], 0.0) for low in range(1, DEG + 1)]
    for step in steps:
        tiles = [tile + step * pltpu.roll(tile, 1, 0) for tile in tiles]
    return tiles


def split(values, parts):
    pieces = []
    for _ in range(parts):
        pieces.append(values.astype(bf16))
        values = values - pieces[-1].astype(f32)
    return pieces


def moment_kernel(
    part_ref, visc_ref, box_ref, spread_ref, basis_ref, face_basis_ref, compact_ref, spots_ref, *refs
):
    sides = lax.axis_size("sib") // 2
    window_refs = refs[:4]
    request_refs = refs[4 : 3 + sides]
    near_ref, served_refs, sums_ref, raw_ref = refs[3 + sides], refs[4 + sides : -2], refs[-2], refs[-1]
    morton = lax.axis_index("morton")
    leaf_count = visc_ref.shape[0]
    asked = [spots_ref[...]]
    for ref in request_refs:
        parts = ref[leaf_count:, :LANES].astype(f32)
        blank = jnp.zeros((2, leaf_count), f32)
        asked.append(
            jnp.concatenate([parts[:6] * 16.0 + parts[6:12], blank, parts[12:], jnp.zeros((4, leaf_count), f32)], axis=0)
        )
    chosen = gathered(asked, window_refs)
    for blocks, out_ref in zip(chosen, (near_ref, *served_refs)):
        for dim, block in enumerate(blocks):
            out_ref[:, dim * FACES : (dim + 1) * FACES] = block

    def add_moments(who, values, table_ref):
        high, low = split(values, 2)
        raw = dot_nt(table_ref[...], high)
        lanes = slice(3 * who * leaf_count, 3 * (who + 1) * leaf_count)
        raw_ref[:, lanes] = raw[:ROWS] + raw[ROWS:] + dot_nt(table_ref[:ROWS, :], low)

    for who, ref in enumerate(request_refs, 1):
        weight = ref[:leaf_count].astype(f32) * (-penalty * out_scale)
        weight = jnp.concatenate([weight] * 3, axis=0)
        add_moments(who, weight * by_comp(chosen[who]).astype(f32), face_basis_ref)
    jumps = dot(by_comp(chosen[0]), spread_ref[...])
    weight = visc_ref[...] * (penalty * out_scale)
    force = [
        part_ref[comp] - weight * jumps[comp * leaf_count : (comp + 1) * leaf_count] for comp in range(3)
    ]
    add_moments(0, jnp.concatenate(force, axis=0), basis_ref)
    geom = jnp.concatenate([spots[8:] for spots in asked for _ in range(3)], axis=1)
    tiles = shifted([raw_ref[8 * at : 8 * at + 8, :] for at in range(36)], geom)
    span = 3 * leaf_count
    tiles = [sum(tile[:, span * who : span * (who + 1)] for who in range(sides)) for tile in tiles]
    group = lax.broadcasted_iota(jnp.int32, (span, LANES), 0) // leaf_count
    column = lax.broadcasted_iota(jnp.int32, (span, LANES), 1)
    gather = jnp.where((group == column) | (group + 3 == column), 1.0, 0.0).astype(bf16)
    summed = sum(dot(piece, gather) for piece in split(jnp.concatenate(tiles, axis=0), 3))
    box = box_ref[pl.ds(pl.multiple_of(morton * 8, 8), 8), :]
    both = shifted([summed[8 * at : 8 * at + 8, :] for at in range(36)], box)
    flat = jnp.concatenate(both, axis=0).T
    sums = sum(dot(piece, compact_ref[...]) for piece in split(flat[:8], 3))
    blank = jnp.zeros((2, LANES), f32)
    to_box = jnp.concatenate([sums[:3, :LANES], sums[:3, LANES:], blank], axis=0)
    to_root = jnp.concatenate([sums[3:6, :LANES], sums[3:6, LANES:], blank], axis=0)
    sib_count = lax.axis_size("sib")
    for other in range(sums_ref.shape[0]):
        sums_ref[other] = jnp.where(morton == other // sib_count, to_box, to_root)


def last_kernel(part_ref, visc_ref, spread_ref, sums_ref, move_ref, near_ref, *refs):
    got_refs, (force_hbm, box_hbm, root_hbm, force_ref, box_ref, root_ref, sems) = refs[:-7], refs[-7:]
    sib_count = lax.axis_size("sib")
    morton = lax.axis_index("morton")
    box = jnp.zeros(sums_ref.shape[1:], f32)
    root = jnp.zeros(sums_ref.shape[1:], f32)
    for group in range(sums_ref.shape[0] // sib_count):
        total = jnp.sum(sums_ref[group * sib_count : (group + 1) * sib_count], axis=0)
        box = box + jnp.where(morton == group, total, 0.0)
        root = root + jnp.where(morton == group, 0.0, total)
    box = jnp.concatenate([box[:3], box[3:6]], axis=1)
    root = jnp.concatenate([root[:3], root[3:6]], axis=1)
    box8 = jnp.concatenate([box, jnp.zeros((5, 2 * LANES), f32)], axis=0)
    root = root + jnp.dot(box8, move_ref[...], precision=highest, preferred_element_type=f32)[:3]
    for comp in range(3):
        box_ref[comp] = box[comp : comp + 1, :MOMENTS]
        root_ref[comp] = root[comp : comp + 1, :MOMENTS]
    stores = [
        pltpu.make_async_copy(box_ref, box_hbm, sems.at[3]),
        pltpu.make_async_copy(root_ref, root_hbm, sems.at[4]),
    ]
    for store in stores:
        store.start()
    faces = near_ref[...]
    for got_ref in got_refs:
        faces = faces + got_ref[...]
    weight = visc_ref[...] * (penalty * out_scale)
    for comp in range(3):
        lanes = [(dim * 3 + comp) * LANES for dim in range(3)]
        jump = dot(jnp.concatenate([faces[:, at : at + LANES] for at in lanes], axis=1), spread_ref[...])
        force_ref[comp] = part_ref[comp] - weight * jump
        stores.append(pltpu.make_async_copy(force_ref.at[comp], force_hbm.at[comp], sems.at[comp]))
        stores[-1].start()
    for store in stores:
        store.wait()


def call(kernel, shapes, flops, scalars, operands, scratch=(), place=pltpu.VMEM, outs=None, grant=32):
    specs = [pl.BlockSpec(memory_space=pltpu.SMEM)] * len(scalars)
    specs += [pl.BlockSpec(memory_space=place)] * len(operands)
    outs = outs or [pltpu.VMEM] * len(shapes)
    moved = sum(array.size * array.dtype.itemsize for array in operands)
    return pl.pallas_call(
        kernel,
        out_shape=[jax.ShapeDtypeStruct(shape, dtype) for shape, dtype in shapes],
        in_specs=specs,
        out_specs=[pl.BlockSpec(memory_space=out) for out in outs],
        scratch_shapes=list(scratch),
        compiler_params=pltpu.CompilerParams(vmem_limit_bytes=grant * 2**20),
        cost_estimate=pl.CostEstimate(flops=flops, bytes_accessed=moved, transcendentals=0),
    )(*scalars, *operands)


def on_device(velocity, pressure, viscosity, levels, morton_keys, counts, neighbors):
    leaf_count = velocity.shape[0]
    morton_count = lax.axis_size("morton")
    rows = jnp.asarray(derivative_rows().astype(np.float32))
    pick = jnp.asarray(face_table().astype(np.float32)).astype(bf16)
    spread = jnp.asarray(spread_table().astype(np.float32)).astype(bf16)
    basis = basis_tables()
    face_basis = (basis.astype(np.float32) @ spread_table().T.astype(np.float32)).astype(jnp.bfloat16)
    basis, face_basis = jnp.asarray(basis), jnp.asarray(face_basis)
    boxes = jnp.asarray(box_table(morton_count))
    vel = jnp.transpose(velocity, (1, 0, 2))
    nbrs = jnp.transpose(neighbors, (1, 0))

    width = 3 * FACES
    sib_count = lax.axis_size("sib")
    sides = sib_count // 2
    other_sides = [2 * side for side in range(1, sides)]
    faces, even, odd, spots, *requests = call(
        pack_kernel,
        [
            ((leaf_count, width), bf16),
            ((BAND, width), bf16),
            ((BAND, width), bf16),
            ((16, leaf_count), f32),
        ]
        + [((leaf_count + 16, FACES), bf16)] * (sides - 1),
        4 * 10**8,
        [counts],
        [vel, viscosity, nbrs, levels.reshape(1, -1), morton_keys.reshape(1, -1), boxes, pick],
        grant=60,
    )
    odd, even = pairs(odd, 1), pairs(even, 0)
    across = swap(faces, "sib", 1)
    across, requests, pressure = lax.optimization_barrier((across, requests, pressure))
    requests = [swap(block, "sib", apart) for block, apart in zip(requests, other_sides)]
    part, continuity, stress, along_x, along_yz = call(
        stress_kernel,
        [
            ((3, leaf_count, NODES), f32),
            ((leaf_count, NODES), f32),
            ((6, leaf_count, NODES), bf16),
            ((NODES, NODES), bf16),
            ((256, NODES), bf16),
        ],
        2 * 10**9,
        [counts],
        [vel, pressure, viscosity, rows],
    )
    odd, even, part, requests = lax.optimization_barrier((odd, even, part, requests))
    bands = jnp.concatenate([odd, even], axis=0)
    window = [faces, across, bands, swap(bands, "sib", 1)]
    part, move = call(
        divergence_kernel,
        [((3, leaf_count, NODES), f32), ((256, 256), f32)],
        10**9,
        [counts],
        [part, stress, along_x, along_yz, boxes],
    )
    near, *served, sums = call(
        moment_kernel,
        [((leaf_count, width), bf16)] * sides + [((morton_count * sib_count, 8, LANES), f32)],
        2 * 10**9,
        [],
        [
            part, viscosity, boxes, spread, basis, face_basis, jnp.asarray(compact_table()), spots,
            *window, *requests,
        ],
        [pltpu.VMEM((ROWS, 3 * sides * leaf_count), f32)],
    )
    got = [swap(block, "sib", apart) for block, apart in zip(served, other_sides)]
    every = lax.all_to_all(sums, ("morton", "sib"), 0, 0, tiled=True)
    every, *got = lax.optimization_barrier((every, *got))
    force, box, root = call(
        last_kernel,
        [((3, leaf_count, NODES), f32), ((3, 1, MOMENTS), f32), ((3, 1, MOMENTS), f32)],
        2 * 10**8,
        [],
        [part, viscosity, spread, every, move, near, *got],
        [
            pltpu.VMEM((3, leaf_count, NODES), f32),
            pltpu.VMEM((3, 1, MOMENTS), f32),
            pltpu.VMEM((3, 1, MOMENTS), f32),
            pltpu.SemaphoreType.DMA((5,)),
        ],
        outs=[pltpu.HBM] * 3,
    )
    return (
        jnp.transpose(force, (1, 0, 2)),
        continuity,
        jnp.transpose(box, (1, 0, 2)),
        jnp.transpose(root, (1, 0, 2)),
    )


def solution(mesh):
    spread_all = ("morton", "sib")
    in_specs = (
        P(spread_all, None, None),
        P(spread_all, None),
        P(spread_all, None),
        P(spread_all),
        P(spread_all),
        P(),
        P(spread_all, None),
    )
    out_specs = (
        P(spread_all, None, None),
        P(spread_all, None),
        P("morton", None, None),
        P("morton", None, None),
    )
    return jax.shard_map(
        on_device, mesh=mesh, in_specs=in_specs, out_specs=out_specs, check_vma=False
    )
```

```python
import math

import jax
import jax.numpy as jnp
import numpy as np
from jax import lax
from jax.experimental import pallas as pl
from jax.experimental.pallas import tpu as pltpu
from jax.sharding import PartitionSpec as P

DEG = 5
LMAX = 7
MOMENTS = 216
BAND = 32
NODES = 512
FACES = 384
ROWS = 288
LANES = 128

penalty = 256.0
out_scale = 1.0 / 1024.0
mass_scale = 1.0 / 32.0
highest = lax.Precision.HIGHEST
f32 = jnp.float32
bf16 = jnp.bfloat16


def cheb_matrix():
    points = -np.cos(np.pi * np.arange(8) / 7.0)
    weights = np.array([(-1.0) ** node for node in range(8)])
    weights[0] *= 0.5
    weights[7] *= 0.5
    derivative = np.zeros((8, 8))
    for row in range(8):
        for col in range(8):
            if row != col:
                derivative[row, col] = weights[col] / weights[row] / (points[row] - points[col])
        derivative[row, row] = -np.sum(derivative[row])
    return points, derivative


def derivative_rows():
    _, derivative = cheb_matrix()
    lane = np.arange(NODES)
    return np.concatenate([derivative[lane // 64 % 8].T, derivative[lane // 8 % 8].T, derivative[lane % 8].T], axis=0)


def face_table():
    pick = np.zeros((NODES, FACES))
    for face in range(6):
        for first in range(8):
            for second in range(8):
                coords = [first, second]
                coords.insert(face // 2, 7 * (face % 2))
                node = 64 * coords[0] + 8 * coords[1] + coords[2]
                pick[node, face * 64 + first * 8 + second] = 1.0
    return pick


def spread_table():
    pick = face_table()
    order = np.concatenate([np.arange(64) + 64 * (face ^ 1) for face in range(6)])
    return pick[:, order].T


def basis_tables():
    points, _ = cheb_matrix()
    powers = np.stack([points**power for power in range(DEG + 1)])
    basis = np.zeros((6, 6, 8, 8, 8, 8))
    basis[:, :, :6] = np.einsum("xa,yb,zc->xyzabc", powers, powers, powers)
    basis = basis.reshape(ROWS, NODES).astype(np.float32)
    top = np.asarray(basis.astype(jnp.bfloat16))
    rest = np.asarray((basis - top.astype(np.float32)).astype(jnp.bfloat16))
    return np.concatenate([top, rest], axis=0)


def compact_table():
    table = np.zeros((ROWS, 256), jnp.bfloat16)
    for group in range(36):
        for power in range(6):
            table[group * 8 + power, group * 6 + power] = 1.0 / 512.0
    return table


def box_table(morton_count):
    bits = morton_count.bit_length() - 1
    key_bits = 3 * LMAX - bits
    table = np.zeros((morton_count, 8, LANES), np.float32)
    for morton in range(morton_count):
        base = morton << key_bits
        lows, sides = [], []
        for offset in (2, 1, 0):
            free = max(0, min(LMAX, (key_bits - offset + 2) // 3))
            cell = sum(((base >> (3 * bit + offset)) & 1) << bit for bit in range(LMAX))
            sides.append(2.0**free / 2.0**LMAX)
            lows.append(cell / 2.0**LMAX)
        scale = 0.5 * max(sides)
        for dim in range(3):
            center = lows[dim] + 0.5 * sides[dim]
            table[morton, dim, 3:6] = (center - 0.5) / 0.5
            table[morton, 4 + dim] = center
        table[morton, 3] = 1.0
        table[morton, 3, 3:6] = scale / 0.5
        table[morton, 7] = 1.0 / scale
    return table.reshape(morton_count * 8, LANES)


def swap(block, axis, apart):
    return lax.ppermute(block, axis, [(at, at ^ apart) for at in range(lax.axis_size(axis))])


def pairs(block, first):
    route = []
    for low in range(first, lax.axis_size("morton") - 1, 2):
        route += [(low, low + 1), (low + 1, low)]
    return lax.ppermute(block, "morton", route)


def dot(left, right):
    return jnp.dot(left, right, preferred_element_type=f32)


def dot_nt(left, right, precision=None):
    return lax.dot_general(
        left, right, (((1,), (1,)), ((), ())), preferred_element_type=f32, precision=precision
    )


def pack_kernel(
    counts_ref, vel_ref, visc_ref, nbrs_ref, levels_ref, keys_ref, box_ref, pick_ref,
    faces_ref, even_ref, odd_ref, spots_ref, *request_refs,
):
    sib_count = lax.axis_size("sib")
    morton = lax.axis_index("morton")
    sib = lax.axis_index("sib")
    own = morton * sib_count + sib
    leaf_count = faces_ref.shape[0]
    fields = jnp.concatenate([vel_ref[0], vel_ref[1], vel_ref[2], visc_ref[...].astype(bf16)], axis=0)
    picked = dot(fields, pick_ref[...])
    for dim in range(3):
        block = picked[3 * leaf_count :, dim * LANES : (dim + 1) * LANES]
        block = pltpu.roll(block, LANES // 2, 1).astype(bf16)
        for request_ref in request_refs:
            request_ref[:leaf_count, dim * LANES : (dim + 1) * LANES] = block
    picked = picked[: 3 * leaf_count].astype(bf16)
    for comp in range(3):
        for dim in range(3):
            lane = (dim * 3 + comp) * LANES
            rows = picked[comp * leaf_count : (comp + 1) * leaf_count]
            faces_ref[:, lane : lane + LANES] = rows[:, dim * LANES : (dim + 1) * LANES]
    first = counts_ref[own] - BAND
    row = lax.broadcasted_iota(jnp.int32, (BAND, leaf_count), 0)
    col = lax.broadcasted_iota(jnp.int32, (BAND, leaf_count), 1)
    last_rows = jnp.where(col == row + first, 1.0, 0.0).astype(bf16)
    high = dot(last_rows, faces_ref[...]).astype(bf16)
    low = faces_ref[:BAND, :]
    is_odd = jnp.bitwise_and(morton, 1) == 1
    even_ref[...] = jnp.where(is_odd, low, high)
    odd_ref[...] = jnp.where(is_odd, high, low)

    nbrs = nbrs_ref[...]
    target = jnp.maximum(nbrs, 0)
    owner = target // leaf_count
    slot = target - owner * leaf_count
    owner_morton = owner // sib_count
    owner_sib = owner - owner_morton * sib_count
    step = owner_morton - morton
    below = jnp.maximum(morton - 1, 0) * sib_count
    band_start = jnp.zeros_like(slot)
    for other in range(sib_count):
        band_start = jnp.where(owner_sib == other, counts_ref[below + other] - BAND, band_start)
    below_at = BAND * jnp.bitwise_and(morton, 1)
    in_band = jnp.where(step < 0, slot - band_start + below_at, slot + BAND - below_at)
    box = box_ref[pl.ds(pl.multiple_of(morton * 8, 8), 8), :]
    shift_bits = 3 * (LMAX - levels_ref[...])
    anchor = jnp.left_shift(jnp.right_shift(keys_ref[...], shift_bits), shift_bits)
    span = jnp.left_shift(jnp.ones_like(shift_bits), LMAX - levels_ref[...]).astype(f32)
    finest = 1.0 / float(2**LMAX)
    places = []
    for dim, offset in enumerate((2, 1, 0)):
        cell = jnp.zeros_like(anchor)
        for bit in range(LMAX):
            picked = jnp.bitwise_and(jnp.right_shift(anchor, 3 * bit + offset), 1)
            cell = cell + jnp.left_shift(picked, bit)
        center = (cell.astype(f32) + 0.5 * span) * finest
        places.append((center - box[4 + dim : 5 + dim, :]) * box[7:8, :])
    places.append(0.5 * span * finest * box[7:8, :])
    places.append(jnp.zeros((4, leaf_count), f32))
    geom = jnp.concatenate(places, axis=0)
    for side in range(sib_count // 2):
        piece = jnp.bitwise_xor(owner_sib, jnp.bitwise_xor(sib, 2 * side))
        spot = jnp.where(step == 0, piece * leaf_count + slot, 2 * leaf_count + piece * (2 * BAND) + in_band)
        spot = jnp.where((nbrs >= 0) & (piece < 2), spot, -1)
        if side == 0:
            spots_ref[...] = jnp.concatenate([spot.astype(f32), jnp.zeros((2, leaf_count), f32), geom], axis=0)
            continue
        whole = jnp.right_shift(spot, 4)
        parts = [whole.astype(f32), (spot - 16 * whole).astype(f32), geom[:4]]
        request_ref = request_refs[side - 1]
        request_ref[leaf_count:, :LANES] = jnp.concatenate(parts, axis=0).astype(bf16)
        request_ref[leaf_count:, LANES:] = jnp.zeros((16, FACES - LANES), bf16)


def gathered(asked, window_refs, start):
    leaf_count = asked[0].shape[1]
    rows = sum(ref.shape[0] for ref in window_refs)
    blank = jnp.full((LANES - 8 * len(asked), leaf_count), -1.0, f32)
    places = jnp.concatenate([spots[:8] for spots in asked] + [blank], axis=0).T.astype(jnp.int32)
    cols = lax.broadcasted_iota(jnp.int32, (leaf_count, rows), 1) + start
    upper = jnp.bitwise_and(lax.broadcasted_iota(jnp.int32, (leaf_count, FACES), 1), 64) > 0
    chosen = [[] for _ in asked]
    for dim in range(3):
        at = dim * FACES
        window = jnp.concatenate([ref[:, at : at + FACES] for ref in window_refs], axis=0)
        faces = [8 * who + face for who in range(len(asked)) for face in (2 * dim, 2 * dim + 1)]
        onehot = [jnp.where(cols == places[:, face : face + 1], 1.0, 0.0).astype(bf16) for face in faces]
        found = dot(jnp.concatenate(onehot, axis=0), window)
        for who in range(len(asked)):
            first, second = (found[(2 * who + side) * leaf_count : (2 * who + side + 1) * leaf_count] for side in (0, 1))
            chosen[who].append(jnp.where(upper, first, second).astype(bf16))
    return chosen


def requested(ref):
    leaf_count = ref.shape[0] - 16
    parts = ref[leaf_count:, :LANES].astype(f32)
    blank = jnp.zeros((2, leaf_count), f32)
    rows = [parts[:6] * 16.0 + parts[6:12], blank, parts[12:], jnp.zeros((4, leaf_count), f32)]
    return jnp.concatenate(rows, axis=0)


def by_comp(chosen):
    comps = [
        jnp.concatenate([block[:, comp * LANES : (comp + 1) * LANES] for block in chosen], axis=1) for comp in range(3)
    ]
    return jnp.concatenate(comps, axis=0)


def fill_tables(rows_ref, dx_ref, dyz_ref):
    row = lax.broadcasted_iota(jnp.int32, (64, NODES), 0)
    col = lax.broadcasted_iota(jnp.int32, (64, NODES), 1)
    same = row == jnp.bitwise_and(col, 63)
    for at in range(8):
        dx_ref[64 * at : 64 * at + 64, :] = jnp.where(same, rows_ref[at : at + 1, :], 0.0).astype(bf16)
    row = lax.broadcasted_iota(jnp.int32, (8, 256), 0)
    col = lax.broadcasted_iota(jnp.int32, (8, 256), 1)
    same = row == jnp.bitwise_and(col, 7)
    group = jnp.right_shift(col, 3)
    for pair in range(16):
        blocks = []
        for at in (2 * pair, 2 * pair + 1):
            here = same & (jnp.right_shift(group, 3) == at // 8)
            along_y = jnp.where(here, rows_ref[8 + at % 8 : 9 + at % 8, :256], 0.0)
            along_z = jnp.where(group == at, rows_ref[16:24, :256], 0.0)
            blocks.append(jnp.concatenate([along_y, along_z], axis=1))
        dyz_ref[16 * pair : 16 * pair + 16, :] = jnp.concatenate(blocks, axis=0).astype(bf16)


def operator_kernel(
    counts_ref, vel_ref, press_ref, visc_ref, rows_ref,
    part_ref, mass_ref, dx_ref, dyz_ref,
):
    sib_count = lax.axis_size("sib")
    own = lax.axis_index("morton") * sib_count + lax.axis_index("sib")
    leaf_count = mass_ref.shape[0]
    live = lax.broadcasted_iota(jnp.int32, (leaf_count, NODES), 0) < counts_ref[own]
    node = lax.broadcasted_iota(jnp.int32, (1, NODES), 1)
    touching = jnp.zeros((1, NODES), f32)
    for shift in (6, 3, 0):
        idx = jnp.bitwise_and(jnp.right_shift(node, shift), 7)
        touching = touching + jnp.where((idx == 0) | (idx == 7), 1.0, 0.0)
    fill_tables(rows_ref, dx_ref, dyz_ref)

    def rows(stack, at):
        return stack[at * leaf_count : (at + 1) * leaf_count]

    visc = visc_ref[...]
    fields = jnp.concatenate([vel_ref[0], vel_ref[1], vel_ref[2], press_ref[...]], axis=0)
    halves = [dot(fields[:, at : at + 256], dyz_ref[...]) for at in (0, 256)]
    grads = [
        dot(fields, dx_ref[...]),
        jnp.concatenate([half[:, :256] for half in halves], axis=1),
        jnp.concatenate([half[:, 256:] for half in halves], axis=1),
    ]
    mass = -(rows(grads[0], 0) + rows(grads[1], 1) + rows(grads[2], 2)) * mass_scale
    mass_ref[...] = jnp.where(live, mass, 0.0)
    stress = {}
    for first in range(3):
        for second in range(first, 3):
            value = (visc * (rows(grads[second], first) + rows(grads[first], second))).astype(bf16)
            stress[first, second] = stress[second, first] = value
    columns = [jnp.concatenate([stress[comp, dim] for comp in range(3)], axis=0) for dim in range(3)]
    rest = [
        dot(columns[1][:, at : at + 256], dyz_ref[:, :256]) + dot(columns[2][:, at : at + 256], dyz_ref[:, 256:])
        for at in (0, 256)
    ]
    div = dot(columns[0], dx_ref[...]) + jnp.concatenate(rest, axis=1)
    for comp in range(3):
        jump = touching * vel_ref[comp].astype(f32)
        part = (penalty * visc * jump - rows(div, comp) + rows(grads[comp], 3)) * out_scale
        part_ref[comp] = jnp.where(live, part, 0.0)


def group_kernel(box_ref, spots_ref, *refs):
    sides = lax.axis_size("sib") // 2
    request_refs, window_refs, move_ref, out_refs = refs[: sides - 1], refs[sides - 1 : sides + 1], refs[sides + 1], refs[sides + 2 :]
    chosen = gathered([spots_ref[...]] + [requested(ref) for ref in request_refs], window_refs, 0)
    for blocks, out_ref in zip(chosen, out_refs):
        for dim, block in enumerate(blocks):
            out_ref[:, dim * FACES : (dim + 1) * FACES] = block
    morton = lax.axis_index("morton")
    box = box_ref[pl.ds(pl.multiple_of(morton * 8, 8), 8), :]
    move = jnp.ones((256, 256), f32)
    for dim, stride in enumerate((36, 6, 1)):
        col = lax.broadcasted_iota(jnp.int32, (1, 256), 1) // stride % 6
        row = lax.broadcasted_iota(jnp.int32, (256, 1), 0) // stride % 6
        along, scale = box[dim : dim + 1, 3:4], box[3:4, 3:4]
        powers = [jnp.ones((1, 1), f32)]
        for _ in range(DEG):
            powers.append(powers[-1] * along)
        factor = jnp.zeros((256, 256), f32)
        below = jnp.ones((1, 1), f32)
        for low in range(DEG + 1):
            line = jnp.zeros((1, 256), f32)
            for high in range(low, DEG + 1):
                line = jnp.where(col == high, powers[high - low] * below * float(math.comb(high, low)), line)
            factor = jnp.where(row == low, line, factor)
            below = below * scale
        move = move * factor
    move_ref[...] = move


def shifted(tiles, geom):
    width = tiles[0].shape
    scale = jnp.broadcast_to(geom[3:4, :], width)
    level = lax.broadcasted_iota(jnp.int32, width, 0)
    depth = jnp.ones(width, f32)
    for power in range(1, DEG + 1):
        depth = depth * jnp.where(level >= power, scale, 1.0)
    scales = [depth]
    for _ in range(2 * DEG):
        scales.append(scales[-1] * scale)
    tiles = [tile * scales[at // 6 + at % 6] for at, tile in enumerate(tiles)]
    along = [jnp.broadcast_to(geom[dim : dim + 1, :], width) for dim in range(3)]
    for low in range(1, DEG + 1):
        for power in range(DEG, low - 1, -1):
            for other in range(6):
                at = power * 6 + other
                tiles[at] = tiles[at] + along[0] * tiles[at - 6]
            for other in range(6):
                at = other * 6 + power
                tiles[at] = tiles[at] + along[1] * tiles[at - 1]
    steps = [jnp.where(level >= low, along[2], 0.0) for low in range(1, DEG + 1)]
    for step in steps:
        tiles = [tile + step * pltpu.roll(tile, 1, 0) for tile in tiles]
    return tiles


def split(values, parts):
    pieces = []
    for _ in range(parts):
        pieces.append(values.astype(bf16))
        values = values - pieces[-1].astype(f32)
    return pieces


def moment_kernel(
    part_ref, visc_ref, box_ref, spread_ref, basis_ref, face_basis_ref, compact_ref, spots_ref, *refs
):
    sides = lax.axis_size("sib") // 2
    window_refs, request_refs, group_refs = refs[:2], refs[2 : 1 + sides], refs[1 + sides : 1 + 2 * sides]
    near_ref, served_refs, sums_ref, raw_ref = refs[1 + 2 * sides], refs[2 + 2 * sides : -2], refs[-2], refs[-1]
    morton = lax.axis_index("morton")
    leaf_count = visc_ref.shape[0]
    asked = [spots_ref[...]] + [requested(ref) for ref in request_refs]
    chosen = gathered(asked, window_refs, 2 * leaf_count)
    for blocks, group_ref, out_ref in zip(chosen, group_refs, (near_ref, *served_refs)):
        for dim in range(3):
            lanes = slice(dim * FACES, (dim + 1) * FACES)
            blocks[dim] = blocks[dim] + group_ref[:, lanes]
            out_ref[:, lanes] = blocks[dim]

    def add_moments(who, values, table_ref):
        high, low = split(values, 2)
        raw = dot_nt(table_ref[...], high)
        lanes = slice(3 * who * leaf_count, 3 * (who + 1) * leaf_count)
        raw_ref[:, lanes] = raw[:ROWS] + raw[ROWS:] + dot_nt(table_ref[:ROWS, :], low)

    for who, ref in enumerate(request_refs, 1):
        weight = ref[:leaf_count].astype(f32) * (-penalty * out_scale)
        weight = jnp.concatenate([weight] * 3, axis=0)
        add_moments(who, weight * by_comp(chosen[who]).astype(f32), face_basis_ref)
    jumps = dot(by_comp(chosen[0]), spread_ref[...])
    weight = visc_ref[...] * (penalty * out_scale)
    force = [
        part_ref[comp] - weight * jumps[comp * leaf_count : (comp + 1) * leaf_count] for comp in range(3)
    ]
    add_moments(0, jnp.concatenate(force, axis=0), basis_ref)
    geom = jnp.concatenate([spots[8:] for spots in asked for _ in range(3)], axis=1)
    tiles = shifted([raw_ref[8 * at : 8 * at + 8, :] for at in range(36)], geom)
    span = 3 * leaf_count
    tiles = [sum(tile[:, span * who : span * (who + 1)] for who in range(sides)) for tile in tiles]
    group = lax.broadcasted_iota(jnp.int32, (span, LANES), 0) // leaf_count
    column = lax.broadcasted_iota(jnp.int32, (span, LANES), 1)
    gather = jnp.where((group == column) | (group + 3 == column), 1.0, 0.0).astype(bf16)
    summed = sum(dot(piece, gather) for piece in split(jnp.concatenate(tiles, axis=0), 3))
    box = box_ref[pl.ds(pl.multiple_of(morton * 8, 8), 8), :]
    both = shifted([summed[8 * at : 8 * at + 8, :] for at in range(36)], box)
    flat = jnp.concatenate(both, axis=0).T
    sums = sum(dot(piece, compact_ref[...]) for piece in split(flat[:8], 3))
    blank = jnp.zeros((2, LANES), f32)
    to_box = jnp.concatenate([sums[:3, :LANES], sums[:3, LANES:], blank], axis=0)
    to_root = jnp.concatenate([sums[3:6, :LANES], sums[3:6, LANES:], blank], axis=0)
    sib_count = lax.axis_size("sib")
    for other in range(sums_ref.shape[0]):
        sums_ref[other] = jnp.where(morton == other // sib_count, to_box, to_root)


def last_kernel(part_ref, visc_ref, spread_ref, sums_ref, move_ref, near_ref, *refs):
    got_refs, (force_hbm, box_hbm, root_hbm, force_ref, box_ref, root_ref, sems) = refs[:-7], refs[-7:]
    sib_count = lax.axis_size("sib")
    morton = lax.axis_index("morton")
    box = jnp.zeros(sums_ref.shape[1:], f32)
    root = jnp.zeros(sums_ref.shape[1:], f32)
    for group in range(sums_ref.shape[0] // sib_count):
        total = jnp.sum(sums_ref[group * sib_count : (group + 1) * sib_count], axis=0)
        box = box + jnp.where(morton == group, total, 0.0)
        root = root + jnp.where(morton == group, 0.0, total)
    box = jnp.concatenate([box[:3], box[3:6]], axis=1)
    root = jnp.concatenate([root[:3], root[3:6]], axis=1)
    box8 = jnp.concatenate([box, jnp.zeros((5, 2 * LANES), f32)], axis=0)
    root = root + jnp.dot(box8, move_ref[...], precision=highest, preferred_element_type=f32)[:3]
    for comp in range(3):
        box_ref[comp] = box[comp : comp + 1, :MOMENTS]
        root_ref[comp] = root[comp : comp + 1, :MOMENTS]
    stores = [
        pltpu.make_async_copy(box_ref, box_hbm, sems.at[3]),
        pltpu.make_async_copy(root_ref, root_hbm, sems.at[4]),
    ]
    for store in stores:
        store.start()
    faces = near_ref[...]
    for got_ref in got_refs:
        faces = faces + got_ref[...]
    weight = visc_ref[...] * (penalty * out_scale)
    for comp in range(3):
        lanes = [(dim * 3 + comp) * LANES for dim in range(3)]
        jump = dot(jnp.concatenate([faces[:, at : at + LANES] for at in lanes], axis=1), spread_ref[...])
        force_ref[comp] = part_ref[comp] - weight * jump
        stores.append(pltpu.make_async_copy(force_ref.at[comp], force_hbm.at[comp], sems.at[comp]))
        stores[-1].start()
    for store in stores:
        store.wait()


def call(kernel, shapes, flops, scalars, operands, scratch=(), place=pltpu.VMEM, outs=None, grant=32):
    specs = [pl.BlockSpec(memory_space=pltpu.SMEM)] * len(scalars)
    specs += [pl.BlockSpec(memory_space=place)] * len(operands)
    outs = outs or [pltpu.VMEM] * len(shapes)
    moved = sum(array.size * array.dtype.itemsize for array in operands)
    return pl.pallas_call(
        kernel,
        out_shape=[jax.ShapeDtypeStruct(shape, dtype) for shape, dtype in shapes],
        in_specs=specs,
        out_specs=[pl.BlockSpec(memory_space=out) for out in outs],
        scratch_shapes=list(scratch),
        compiler_params=pltpu.CompilerParams(vmem_limit_bytes=grant * 2**20),
        cost_estimate=pl.CostEstimate(flops=flops, bytes_accessed=moved, transcendentals=0),
    )(*scalars, *operands)


def on_device(velocity, pressure, viscosity, levels, morton_keys, counts, neighbors):
    leaf_count = velocity.shape[0]
    morton_count = lax.axis_size("morton")
    rows = jnp.asarray(derivative_rows().astype(np.float32))
    pick = jnp.asarray(face_table().astype(np.float32)).astype(bf16)
    spread = jnp.asarray(spread_table().astype(np.float32)).astype(bf16)
    basis = basis_tables()
    face_basis = (basis.astype(np.float32) @ spread_table().T.astype(np.float32)).astype(jnp.bfloat16)
    basis, face_basis = jnp.asarray(basis), jnp.asarray(face_basis)
    boxes = jnp.asarray(box_table(morton_count))
    vel = jnp.transpose(velocity, (1, 0, 2))
    nbrs = jnp.transpose(neighbors, (1, 0))

    width = 3 * FACES
    sib_count = lax.axis_size("sib")
    sides = sib_count // 2
    other_sides = [2 * side for side in range(1, sides)]
    faces, even, odd, spots, *requests = call(
        pack_kernel,
        [
            ((leaf_count, width), bf16),
            ((BAND, width), bf16),
            ((BAND, width), bf16),
            ((16, leaf_count), f32),
        ]
        + [((leaf_count + 16, FACES), bf16)] * (sides - 1),
        4 * 10**8,
        [counts],
        [vel, viscosity, nbrs, levels.reshape(1, -1), morton_keys.reshape(1, -1), boxes, pick],
        grant=60,
    )
    odd = pairs(odd, 1)
    across = swap(faces, "sib", 1)
    across, requests, even, pressure = lax.optimization_barrier((across, requests, even, pressure))
    requests = [swap(block, "sib", apart) for block, apart in zip(requests, other_sides)]
    even = pairs(even, 0)
    part, continuity = call(
        operator_kernel,
        [((3, leaf_count, NODES), f32), ((leaf_count, NODES), f32)],
        2 * 10**9,
        [counts],
        [vel, pressure, viscosity, rows],
        [pltpu.VMEM((NODES, NODES), bf16), pltpu.VMEM((256, NODES), bf16)],
    )
    odd, even, part, requests = lax.optimization_barrier((odd, even, part, requests))
    bands = jnp.concatenate([odd, even], axis=0)
    move, *group = call(
        group_kernel,
        [((256, 256), f32)] + [((leaf_count, width), bf16)] * sides,
        10**9,
        [],
        [boxes, spots, *requests, faces, across],
    )
    near, *served, sums = call(
        moment_kernel,
        [((leaf_count, width), bf16)] * sides + [((morton_count * sib_count, 8, LANES), f32)],
        2 * 10**9,
        [],
        [
            part, viscosity, boxes, spread, basis, face_basis, jnp.asarray(compact_table()), spots,
            bands, swap(bands, "sib", 1), *requests, *group,
        ],
        [pltpu.VMEM((ROWS, 3 * sides * leaf_count), f32)],
    )
    got = [swap(block, "sib", apart) for block, apart in zip(served, other_sides)]
    every = lax.all_to_all(sums, ("morton", "sib"), 0, 0, tiled=True)
    every, *got = lax.optimization_barrier((every, *got))
    force, box, root = call(
        last_kernel,
        [((3, leaf_count, NODES), f32), ((3, 1, MOMENTS), f32), ((3, 1, MOMENTS), f32)],
        2 * 10**8,
        [],
        [part, viscosity, spread, every, move, near, *got],
        [
            pltpu.VMEM((3, leaf_count, NODES), f32),
            pltpu.VMEM((3, 1, MOMENTS), f32),
            pltpu.VMEM((3, 1, MOMENTS), f32),
            pltpu.SemaphoreType.DMA((5,)),
        ],
        outs=[pltpu.HBM] * 3,
    )
    return (
        jnp.transpose(force, (1, 0, 2)),
        continuity,
        jnp.transpose(box, (1, 0, 2)),
        jnp.transpose(root, (1, 0, 2)),
    )


def solution(mesh):
    spread_all = ("morton", "sib")
    in_specs = (
        P(spread_all, None, None),
        P(spread_all, None),
        P(spread_all, None),
        P(spread_all),
        P(spread_all),
        P(),
        P(spread_all, None),
    )
    out_specs = (
        P(spread_all, None, None),
        P(spread_all, None),
        P("morton", None, None),
        P("morton", None, None),
    )
    return jax.shard_map(
        on_device, mesh=mesh, in_specs=in_specs, out_specs=out_specs, check_vma=False
    )
```

```python
import math

import jax
import jax.numpy as jnp
import numpy as np
from jax import lax
from jax.experimental import pallas as pl
from jax.experimental.pallas import tpu as pltpu
from jax.sharding import PartitionSpec as P

DEG = 5
LMAX = 7
MOMENTS = 216
BAND = 32
NODES = 512
FACES = 384
ROWS = 224
LANES = 128

penalty = 256.0
out_scale = 1.0 / 1024.0
mass_scale = 1.0 / 32.0
highest = lax.Precision.HIGHEST
f32 = jnp.float32
bf16 = jnp.bfloat16


def cheb_matrix():
    points = -np.cos(np.pi * np.arange(8) / 7.0)
    weights = np.array([(-1.0) ** node for node in range(8)])
    weights[0] *= 0.5
    weights[7] *= 0.5
    derivative = np.zeros((8, 8))
    for row in range(8):
        for col in range(8):
            if row != col:
                derivative[row, col] = weights[col] / weights[row] / (points[row] - points[col])
        derivative[row, row] = -np.sum(derivative[row])
    return points, derivative


def derivative_rows():
    _, derivative = cheb_matrix()
    lane = np.arange(NODES)
    return np.concatenate([derivative[lane // 64 % 8].T, derivative[lane // 8 % 8].T, derivative[lane % 8].T], axis=0)


def face_table():
    pick = np.zeros((NODES, FACES))
    for face in range(6):
        for first in range(8):
            for second in range(8):
                coords = [first, second]
                coords.insert(face // 2, 7 * (face % 2))
                node = 64 * coords[0] + 8 * coords[1] + coords[2]
                pick[node, face * 64 + first * 8 + second] = 1.0
    return pick


def spread_table():
    pick = face_table()
    order = np.concatenate([np.arange(64) + 64 * (face ^ 1) for face in range(6)])
    return pick[:, order].T


def basis_tables():
    points, _ = cheb_matrix()
    powers = np.stack([points**power for power in range(DEG + 1)])
    basis = np.zeros((ROWS, NODES), np.float32)
    basis[:MOMENTS] = np.einsum("xa,yb,zc->xyzabc", powers, powers, powers).reshape(MOMENTS, NODES)
    top = np.asarray(basis.astype(jnp.bfloat16))
    rest = np.asarray((basis - top.astype(np.float32)).astype(jnp.bfloat16))
    return np.concatenate([top, rest], axis=0)


def box_table(morton_count):
    bits = morton_count.bit_length() - 1
    key_bits = 3 * LMAX - bits
    table = np.zeros((morton_count, 8, LANES), np.float32)
    for morton in range(morton_count):
        base = morton << key_bits
        lows, sides = [], []
        for offset in (2, 1, 0):
            free = max(0, min(LMAX, (key_bits - offset + 2) // 3))
            cell = sum(((base >> (3 * bit + offset)) & 1) << bit for bit in range(LMAX))
            sides.append(2.0**free / 2.0**LMAX)
            lows.append(cell / 2.0**LMAX)
        scale = 0.5 * max(sides)
        for dim in range(3):
            center = lows[dim] + 0.5 * sides[dim]
            table[morton, dim, 3:6] = (center - 0.5) / 0.5
            table[morton, 4 + dim] = center
        table[morton, 3] = 1.0
        table[morton, 3, 3:6] = scale / 0.5
        table[morton, 7] = 1.0 / scale
    return table.reshape(morton_count * 8, LANES)


def swap(block, axis, apart):
    return lax.ppermute(block, axis, [(at, at ^ apart) for at in range(lax.axis_size(axis))])


def pairs(block, first):
    route = []
    for low in range(first, lax.axis_size("morton") - 1, 2):
        route += [(low, low + 1), (low + 1, low)]
    return lax.ppermute(block, "morton", route)


def dot(left, right):
    return jnp.dot(left, right, preferred_element_type=f32)


def dot_nt(left, right, precision=None):
    return lax.dot_general(
        left, right, (((1,), (1,)), ((), ())), preferred_element_type=f32, precision=precision
    )


def pack_kernel(
    counts_ref, vel_ref, visc_ref, nbrs_ref, levels_ref, keys_ref, box_ref, pick_ref,
    faces_ref, even_ref, odd_ref, spots_ref, *request_refs,
):
    sib_count = lax.axis_size("sib")
    morton = lax.axis_index("morton")
    sib = lax.axis_index("sib")
    own = morton * sib_count + sib
    leaf_count = faces_ref.shape[0]
    fields = jnp.concatenate([vel_ref[0], vel_ref[1], vel_ref[2], visc_ref[...].astype(bf16)], axis=0)
    picked = dot(fields, pick_ref[...])
    for dim in range(3):
        block = picked[3 * leaf_count :, dim * LANES : (dim + 1) * LANES]
        block = pltpu.roll(block, LANES // 2, 1).astype(bf16)
        for request_ref in request_refs:
            request_ref[:leaf_count, dim * LANES : (dim + 1) * LANES] = block
    picked = picked[: 3 * leaf_count].astype(bf16)
    for comp in range(3):
        for dim in range(3):
            lane = (dim * 3 + comp) * LANES
            rows = picked[comp * leaf_count : (comp + 1) * leaf_count]
            faces_ref[:, lane : lane + LANES] = rows[:, dim * LANES : (dim + 1) * LANES]
    first = counts_ref[own] - BAND
    row = lax.broadcasted_iota(jnp.int32, (BAND, leaf_count), 0)
    col = lax.broadcasted_iota(jnp.int32, (BAND, leaf_count), 1)
    last_rows = jnp.where(col == row + first, 1.0, 0.0).astype(bf16)
    high = dot(last_rows, faces_ref[...]).astype(bf16)
    low = faces_ref[:BAND, :]
    is_odd = jnp.bitwise_and(morton, 1) == 1
    even_ref[...] = jnp.where(is_odd, low, high)
    odd_ref[...] = jnp.where(is_odd, high, low)

    nbrs = nbrs_ref[...]
    target = jnp.maximum(nbrs, 0)
    owner = target // leaf_count
    slot = target - owner * leaf_count
    owner_morton = owner // sib_count
    owner_sib = owner - owner_morton * sib_count
    step = owner_morton - morton
    below = jnp.maximum(morton - 1, 0) * sib_count
    band_start = jnp.zeros_like(slot)
    for other in range(sib_count):
        band_start = jnp.where(owner_sib == other, counts_ref[below + other] - BAND, band_start)
    below_at = BAND * jnp.bitwise_and(morton, 1)
    in_band = jnp.where(step < 0, slot - band_start + below_at, slot + BAND - below_at)
    box = box_ref[pl.ds(pl.multiple_of(morton * 8, 8), 8), :]
    shift_bits = 3 * (LMAX - levels_ref[...])
    anchor = jnp.left_shift(jnp.right_shift(keys_ref[...], shift_bits), shift_bits)
    span = jnp.left_shift(jnp.ones_like(shift_bits), LMAX - levels_ref[...]).astype(f32)
    finest = 1.0 / float(2**LMAX)
    places = []
    for dim, offset in enumerate((2, 1, 0)):
        cell = jnp.zeros_like(anchor)
        for bit in range(LMAX):
            picked = jnp.bitwise_and(jnp.right_shift(anchor, 3 * bit + offset), 1)
            cell = cell + jnp.left_shift(picked, bit)
        center = (cell.astype(f32) + 0.5 * span) * finest
        places.append((center - box[4 + dim : 5 + dim, :]) * box[7:8, :])
    places.append(0.5 * span * finest * box[7:8, :])
    places.append(jnp.zeros((4, leaf_count), f32))
    geom = jnp.concatenate(places, axis=0)
    for side in range(sib_count // 2):
        piece = jnp.bitwise_xor(owner_sib, jnp.bitwise_xor(sib, 2 * side))
        spot = jnp.where(step == 0, piece * leaf_count + slot, 2 * leaf_count + piece * (2 * BAND) + in_band)
        spot = jnp.where((nbrs >= 0) & (piece < 2), spot, -1)
        if side == 0:
            spots_ref[...] = jnp.concatenate([spot.astype(f32), jnp.zeros((2, leaf_count), f32), geom], axis=0)
            continue
        whole = jnp.right_shift(spot, 4)
        parts = [whole.astype(f32), (spot - 16 * whole).astype(f32), geom[:4]]
        request_ref = request_refs[side - 1]
        request_ref[leaf_count:, :LANES] = jnp.concatenate(parts, axis=0).astype(bf16)
        request_ref[leaf_count:, LANES:] = jnp.zeros((16, FACES - LANES), bf16)


def gathered(asked, window_refs, start):
    leaf_count = asked[0].shape[1]
    rows = sum(ref.shape[0] for ref in window_refs)
    blank = jnp.full((LANES - 8 * len(asked), leaf_count), -1.0, f32)
    places = jnp.concatenate([spots[:8] for spots in asked] + [blank], axis=0).T.astype(jnp.int32)
    cols = lax.broadcasted_iota(jnp.int32, (leaf_count, rows), 1) + start
    upper = jnp.bitwise_and(lax.broadcasted_iota(jnp.int32, (leaf_count, FACES), 1), 64) > 0
    chosen = [[] for _ in asked]
    for dim in range(3):
        at = dim * FACES
        window = jnp.concatenate([ref[:, at : at + FACES] for ref in window_refs], axis=0)
        faces = [8 * who + face for who in range(len(asked)) for face in (2 * dim, 2 * dim + 1)]
        onehot = [jnp.where(cols == places[:, face : face + 1], 1.0, 0.0).astype(bf16) for face in faces]
        found = dot(jnp.concatenate(onehot, axis=0), window)
        for who in range(len(asked)):
            first, second = (found[(2 * who + side) * leaf_count : (2 * who + side + 1) * leaf_count] for side in (0, 1))
            chosen[who].append(jnp.where(upper, first, second).astype(bf16))
    return chosen


def requested(ref):
    leaf_count = ref.shape[0] - 16
    parts = ref[leaf_count:, :LANES].astype(f32)
    blank = jnp.zeros((2, leaf_count), f32)
    rows = [parts[:6] * 16.0 + parts[6:12], blank, parts[12:], jnp.zeros((4, leaf_count), f32)]
    return jnp.concatenate(rows, axis=0)


def by_comp(chosen):
    comps = [
        jnp.concatenate([block[:, comp * LANES : (comp + 1) * LANES] for block in chosen], axis=1) for comp in range(3)
    ]
    return jnp.concatenate(comps, axis=0)


def fill_tables(rows_ref, dx_ref, dyz_ref):
    row = lax.broadcasted_iota(jnp.int32, (64, NODES), 0)
    col = lax.broadcasted_iota(jnp.int32, (64, NODES), 1)
    same = row == jnp.bitwise_and(col, 63)
    for at in range(8):
        dx_ref[64 * at : 64 * at + 64, :] = jnp.where(same, rows_ref[at : at + 1, :], 0.0).astype(bf16)
    row = lax.broadcasted_iota(jnp.int32, (8, 256), 0)
    col = lax.broadcasted_iota(jnp.int32, (8, 256), 1)
    same = row == jnp.bitwise_and(col, 7)
    group = jnp.right_shift(col, 3)
    for pair in range(16):
        blocks = []
        for at in (2 * pair, 2 * pair + 1):
            here = same & (jnp.right_shift(group, 3) == at // 8)
            along_y = jnp.where(here, rows_ref[8 + at % 8 : 9 + at % 8, :256], 0.0)
            along_z = jnp.where(group == at, rows_ref[16:24, :256], 0.0)
            blocks.append(jnp.concatenate([along_y, along_z], axis=1))
        dyz_ref[16 * pair : 16 * pair + 16, :] = jnp.concatenate(blocks, axis=0).astype(bf16)


def operator_kernel(
    counts_ref, vel_ref, press_ref, visc_ref, rows_ref,
    part_ref, mass_ref, dx_ref, dyz_ref,
):
    sib_count = lax.axis_size("sib")
    own = lax.axis_index("morton") * sib_count + lax.axis_index("sib")
    leaf_count = mass_ref.shape[0]
    live = lax.broadcasted_iota(jnp.int32, (leaf_count, NODES), 0) < counts_ref[own]
    node = lax.broadcasted_iota(jnp.int32, (1, NODES), 1)
    touching = jnp.zeros((1, NODES), f32)
    for shift in (6, 3, 0):
        idx = jnp.bitwise_and(jnp.right_shift(node, shift), 7)
        touching = touching + jnp.where((idx == 0) | (idx == 7), 1.0, 0.0)
    fill_tables(rows_ref, dx_ref, dyz_ref)

    def rows(stack, at):
        return stack[at * leaf_count : (at + 1) * leaf_count]

    visc = visc_ref[...]
    fields = jnp.concatenate([vel_ref[0], vel_ref[1], vel_ref[2], press_ref[...]], axis=0)
    halves = [dot(fields[:, at : at + 256], dyz_ref[...]) for at in (0, 256)]
    grads = [
        dot(fields, dx_ref[...]),
        jnp.concatenate([half[:, :256] for half in halves], axis=1),
        jnp.concatenate([half[:, 256:] for half in halves], axis=1),
    ]
    mass = -(rows(grads[0], 0) + rows(grads[1], 1) + rows(grads[2], 2)) * mass_scale
    mass_ref[...] = jnp.where(live, mass, 0.0)
    stress = {}
    for first in range(3):
        for second in range(first, 3):
            value = (visc * (rows(grads[second], first) + rows(grads[first], second))).astype(bf16)
            stress[first, second] = stress[second, first] = value
    columns = [jnp.concatenate([stress[comp, dim] for comp in range(3)], axis=0) for dim in range(3)]
    rest = [
        dot(columns[1][:, at : at + 256], dyz_ref[:, :256]) + dot(columns[2][:, at : at + 256], dyz_ref[:, 256:])
        for at in (0, 256)
    ]
    div = dot(columns[0], dx_ref[...]) + jnp.concatenate(rest, axis=1)
    for comp in range(3):
        jump = touching * vel_ref[comp].astype(f32)
        part = (penalty * visc * jump - rows(div, comp) + rows(grads[comp], 3)) * out_scale
        part_ref[comp] = jnp.where(live, part, 0.0)


def group_kernel(box_ref, spots_ref, *refs):
    sides = lax.axis_size("sib") // 2
    request_refs, window_refs, move_ref, out_refs = refs[: sides - 1], refs[sides - 1 : sides + 1], refs[sides + 1], refs[sides + 2 :]
    chosen = gathered([spots_ref[...]] + [requested(ref) for ref in request_refs], window_refs, 0)
    for blocks, out_ref in zip(chosen, out_refs):
        for dim, block in enumerate(blocks):
            out_ref[:, dim * FACES : (dim + 1) * FACES] = block
    morton = lax.axis_index("morton")
    box = box_ref[pl.ds(pl.multiple_of(morton * 8, 8), 8), :]
    move = jnp.ones((256, 256), f32)
    for dim, stride in enumerate((36, 6, 1)):
        col = lax.broadcasted_iota(jnp.int32, (1, 256), 1) // stride % 6
        row = lax.broadcasted_iota(jnp.int32, (256, 1), 0) // stride % 6
        along, scale = box[dim : dim + 1, 3:4], box[3:4, 3:4]
        powers = [jnp.ones((1, 1), f32)]
        for _ in range(DEG):
            powers.append(powers[-1] * along)
        factor = jnp.zeros((256, 256), f32)
        below = jnp.ones((1, 1), f32)
        for low in range(DEG + 1):
            line = jnp.zeros((1, 256), f32)
            for high in range(low, DEG + 1):
                line = jnp.where(col == high, powers[high - low] * below * float(math.comb(high, low)), line)
            factor = jnp.where(row == low, line, factor)
            below = below * scale
        move = move * factor
    move_ref[...] = move


def shifted(load, geom, width):
    def rows(at):
        return jnp.concatenate([leaf[at : at + 1, :] for leaf in geom for _ in range(3)], axis=0)

    scales = [None, rows(3)]
    for _ in range(2, 3 * DEG + 1):
        scales.append(scales[-1] * scales[1])
    tiles = {}
    for ax in range(width):
        for ay in range(width):
            for az in range(width):
                tile = load((ax * width + ay) * width + az)
                degree = ax + ay + az
                tiles[ax, ay, az] = tile * scales[degree] if degree else tile
    for dim in (2, 1, 0):
        along = rows(dim)
        for first in range(width):
            for second in range(width):
                places = [tuple(np.insert([first, second], dim, power)) for power in range(width)]
                for low in range(1, width):
                    for power in range(width - 1, low - 1, -1):
                        tiles[places[power]] = tiles[places[power]] + along * tiles[places[power - 1]]
    return [tiles[place] for place in np.ndindex(width, width, width)]


def split(values, parts):
    pieces = []
    for _ in range(parts):
        pieces.append(values.astype(bf16))
        values = values - pieces[-1].astype(f32)
    return pieces


def moment_kernel(
    part_ref, visc_ref, spread_ref, basis_ref, face_basis_ref, move_ref, spots_ref, *refs
):
    sides = lax.axis_size("sib") // 2
    window_refs, request_refs, group_refs = refs[:2], refs[2 : 1 + sides], refs[1 + sides : 1 + 2 * sides]
    near_ref, served_refs, (sums_ref, raw_ref, moved_ref) = refs[1 + 2 * sides], refs[2 + 2 * sides : -3], refs[-3:]
    morton = lax.axis_index("morton")
    leaf_count = visc_ref.shape[0]
    asked = [spots_ref[...]] + [requested(ref) for ref in request_refs]
    chosen = gathered(asked, window_refs, 2 * leaf_count)
    for blocks, group_ref, out_ref in zip(chosen, group_refs, (near_ref, *served_refs)):
        for dim in range(3):
            lanes = slice(dim * FACES, (dim + 1) * FACES)
            blocks[dim] = blocks[dim] + group_ref[:, lanes]
            out_ref[:, lanes] = blocks[dim]

    def add_moments(who, values, table_ref):
        high, low = split(values, 2)
        raw = dot_nt(table_ref[...], high)
        raw = raw[:ROWS] + raw[ROWS:] + dot_nt(table_ref[:ROWS, :], low)
        for comp in range(3):
            at = (3 * who + comp) * ROWS
            raw_ref[at : at + ROWS, :] = raw[:, comp * leaf_count : (comp + 1) * leaf_count]

    for who, ref in enumerate(request_refs, 1):
        weight = ref[:leaf_count].astype(f32) * (-penalty * out_scale)
        weight = jnp.concatenate([weight] * 3, axis=0)
        add_moments(who, weight * by_comp(chosen[who]).astype(f32), face_basis_ref)
    jumps = dot(by_comp(chosen[0]), spread_ref[...])
    weight = visc_ref[...] * (penalty * out_scale)
    force = [
        part_ref[comp] - weight * jumps[comp * leaf_count : (comp + 1) * leaf_count] for comp in range(3)
    ]
    add_moments(0, jnp.concatenate(force, axis=0), basis_ref)
    tiles = shifted(
        lambda at: raw_ref[pl.ds(at, 3 * sides, stride=ROWS), :], [spots[8:12] for spots in asked], DEG + 1
    )
    for at, tile in enumerate(tiles):
        moved_ref[8 * at : 8 * at + 3 * sides, :] = tile
    row = lax.broadcasted_iota(jnp.int32, (8, leaf_count), 0)
    box = jnp.zeros((8, MOMENTS), f32)
    for comp in range(3):
        leaves = sum(moved_ref[pl.ds(3 * who + comp, MOMENTS, stride=8), :] for who in range(sides))
        ones = jnp.where(row == comp, 1.0, 0.0).astype(bf16)
        box = box + sum(dot_nt(ones, piece) for piece in split(leaves, 3))
    box = jnp.concatenate([box * (1.0 / 512.0), jnp.zeros((8, 256 - MOMENTS), f32)], axis=1)
    root = jnp.dot(box, move_ref[...], precision=highest, preferred_element_type=f32)
    blank = jnp.zeros((2, LANES), f32)
    to_box = jnp.concatenate([box[:3, :LANES], box[:3, LANES:], blank], axis=0)
    to_root = jnp.concatenate([root[:3, :LANES], root[:3, LANES:], blank], axis=0)
    sib_count = lax.axis_size("sib")
    for other in range(sums_ref.shape[0]):
        sums_ref[other] = jnp.where(morton == other // sib_count, to_box, to_root)


def last_kernel(part_ref, visc_ref, spread_ref, sums_ref, move_ref, near_ref, *refs):
    got_refs, (force_hbm, box_hbm, root_hbm, force_ref, box_ref, root_ref, sems) = refs[:-7], refs[-7:]
    sib_count = lax.axis_size("sib")
    morton = lax.axis_index("morton")
    box = jnp.zeros(sums_ref.shape[1:], f32)
    root = jnp.zeros(sums_ref.shape[1:], f32)
    for group in range(sums_ref.shape[0] // sib_count):
        total = jnp.sum(sums_ref[group * sib_count : (group + 1) * sib_count], axis=0)
        box = box + jnp.where(morton == group, total, 0.0)
        root = root + jnp.where(morton == group, 0.0, total)
    box = jnp.concatenate([box[:3], box[3:6]], axis=1)
    root = jnp.concatenate([root[:3], root[3:6]], axis=1)
    box8 = jnp.concatenate([box, jnp.zeros((5, 2 * LANES), f32)], axis=0)
    root = root + jnp.dot(box8, move_ref[...], precision=highest, preferred_element_type=f32)[:3]
    for comp in range(3):
        box_ref[comp] = box[comp : comp + 1, :MOMENTS]
        root_ref[comp] = root[comp : comp + 1, :MOMENTS]
    stores = [
        pltpu.make_async_copy(box_ref, box_hbm, sems.at[3]),
        pltpu.make_async_copy(root_ref, root_hbm, sems.at[4]),
    ]
    for store in stores:
        store.start()
    faces = near_ref[...]
    for got_ref in got_refs:
        faces = faces + got_ref[...]
    weight = visc_ref[...] * (penalty * out_scale)
    for comp in range(3):
        lanes = [(dim * 3 + comp) * LANES for dim in range(3)]
        jump = dot(jnp.concatenate([faces[:, at : at + LANES] for at in lanes], axis=1), spread_ref[...])
        force_ref[comp] = part_ref[comp] - weight * jump
        stores.append(pltpu.make_async_copy(force_ref.at[comp], force_hbm.at[comp], sems.at[comp]))
        stores[-1].start()
    for store in stores:
        store.wait()


def call(kernel, shapes, flops, scalars, operands, scratch=(), place=pltpu.VMEM, outs=None, grant=32):
    specs = [pl.BlockSpec(memory_space=pltpu.SMEM)] * len(scalars)
    specs += [pl.BlockSpec(memory_space=place)] * len(operands)
    outs = outs or [pltpu.VMEM] * len(shapes)
    moved = sum(array.size * array.dtype.itemsize for array in operands)
    return pl.pallas_call(
        kernel,
        out_shape=[jax.ShapeDtypeStruct(shape, dtype) for shape, dtype in shapes],
        in_specs=specs,
        out_specs=[pl.BlockSpec(memory_space=out) for out in outs],
        scratch_shapes=list(scratch),
        compiler_params=pltpu.CompilerParams(vmem_limit_bytes=grant * 2**20),
        cost_estimate=pl.CostEstimate(flops=flops, bytes_accessed=moved, transcendentals=0),
    )(*scalars, *operands)


def on_device(velocity, pressure, viscosity, levels, morton_keys, counts, neighbors):
    leaf_count = velocity.shape[0]
    morton_count = lax.axis_size("morton")
    rows = jnp.asarray(derivative_rows().astype(np.float32))
    pick = jnp.asarray(face_table().astype(np.float32)).astype(bf16)
    spread = jnp.asarray(spread_table().astype(np.float32)).astype(bf16)
    basis = basis_tables()
    face_basis = (basis.astype(np.float32) @ spread_table().T.astype(np.float32)).astype(jnp.bfloat16)
    basis, face_basis = jnp.asarray(basis), jnp.asarray(face_basis)
    boxes = jnp.asarray(box_table(morton_count))
    vel = jnp.transpose(velocity, (1, 0, 2))
    nbrs = jnp.transpose(neighbors, (1, 0))

    width = 3 * FACES
    sib_count = lax.axis_size("sib")
    sides = sib_count // 2
    other_sides = [2 * side for side in range(1, sides)]
    faces, even, odd, spots, *requests = call(
        pack_kernel,
        [
            ((leaf_count, width), bf16),
            ((BAND, width), bf16),
            ((BAND, width), bf16),
            ((16, leaf_count), f32),
        ]
        + [((leaf_count + 16, FACES), bf16)] * (sides - 1),
        4 * 10**8,
        [counts],
        [vel, viscosity, nbrs, levels.reshape(1, -1), morton_keys.reshape(1, -1), boxes, pick],
        grant=60,
    )
    odd = pairs(odd, 1)
    across = swap(faces, "sib", 1)
    across, requests, even, pressure = lax.optimization_barrier((across, requests, even, pressure))
    requests = [swap(block, "sib", apart) for block, apart in zip(requests, other_sides)]
    even = pairs(even, 0)
    part, continuity = call(
        operator_kernel,
        [((3, leaf_count, NODES), f32), ((leaf_count, NODES), f32)],
        2 * 10**9,
        [counts],
        [vel, pressure, viscosity, rows],
        [pltpu.VMEM((NODES, NODES), bf16), pltpu.VMEM((256, NODES), bf16)],
    )
    odd, even, part, requests = lax.optimization_barrier((odd, even, part, requests))
    bands = jnp.concatenate([odd, even], axis=0)
    move, *group = call(
        group_kernel,
        [((256, 256), f32)] + [((leaf_count, width), bf16)] * sides,
        10**9,
        [],
        [boxes, spots, *requests, faces, across],
    )
    near, *served, sums = call(
        moment_kernel,
        [((leaf_count, width), bf16)] * sides + [((morton_count * sib_count, 8, LANES), f32)],
        2 * 10**9,
        [],
        [
            part, viscosity, spread, basis, face_basis, move, spots,
            bands, swap(bands, "sib", 1), *requests, *group,
        ],
        [pltpu.VMEM((3 * sides * ROWS, leaf_count), f32), pltpu.VMEM((8 * MOMENTS, leaf_count), f32)],
    )
    got = [swap(block, "sib", apart) for block, apart in zip(served, other_sides)]
    every = lax.all_to_all(sums, ("morton", "sib"), 0, 0, tiled=True)
    every, *got = lax.optimization_barrier((every, *got))
    force, box, root = call(
        last_kernel,
        [((3, leaf_count, NODES), f32), ((3, 1, MOMENTS), f32), ((3, 1, MOMENTS), f32)],
        2 * 10**8,
        [],
        [part, viscosity, spread, every, move, near, *got],
        [
            pltpu.VMEM((3, leaf_count, NODES), f32),
            pltpu.VMEM((3, 1, MOMENTS), f32),
            pltpu.VMEM((3, 1, MOMENTS), f32),
            pltpu.SemaphoreType.DMA((5,)),
        ],
        outs=[pltpu.HBM] * 3,
    )
    return (
        jnp.transpose(force, (1, 0, 2)),
        continuity,
        jnp.transpose(box, (1, 0, 2)),
        jnp.transpose(root, (1, 0, 2)),
    )


def solution(mesh):
    spread_all = ("morton", "sib")
    in_specs = (
        P(spread_all, None, None),
        P(spread_all, None),
        P(spread_all, None),
        P(spread_all),
        P(spread_all),
        P(),
        P(spread_all, None),
    )
    out_specs = (
        P(spread_all, None, None),
        P(spread_all, None),
        P("morton", None, None),
        P("morton", None, None),
    )
    return jax.shard_map(
        on_device, mesh=mesh, in_specs=in_specs, out_specs=out_specs, check_vma=False
    )
```

```python
import math

import jax
import jax.numpy as jnp
import numpy as np
from jax import lax
from jax.experimental import pallas as pl
from jax.experimental.pallas import tpu as pltpu
from jax.sharding import PartitionSpec as P

DEG = 5
LMAX = 7
MOMENTS = 216
BAND = 32
NODES = 512
FACES = 384
ROWS = 288
LANES = 128

penalty = 256.0
out_scale = 1.0 / 1024.0
mass_scale = 1.0 / 32.0
highest = lax.Precision.HIGHEST
f32 = jnp.float32
bf16 = jnp.bfloat16


def cheb_matrix():
    points = -np.cos(np.pi * np.arange(8) / 7.0)
    weights = np.array([(-1.0) ** node for node in range(8)])
    weights[0] *= 0.5
    weights[7] *= 0.5
    derivative = np.zeros((8, 8))
    for row in range(8):
        for col in range(8):
            if row != col:
                derivative[row, col] = weights[col] / weights[row] / (points[row] - points[col])
        derivative[row, row] = -np.sum(derivative[row])
    return points, derivative


def derivative_rows():
    _, derivative = cheb_matrix()
    lane = np.arange(NODES)
    return np.concatenate([derivative[lane // 64 % 8].T, derivative[lane // 8 % 8].T, derivative[lane % 8].T], axis=0)


def face_table():
    pick = np.zeros((NODES, FACES))
    for face in range(6):
        for first in range(8):
            for second in range(8):
                coords = [first, second]
                coords.insert(face // 2, 7 * (face % 2))
                node = 64 * coords[0] + 8 * coords[1] + coords[2]
                pick[node, face * 64 + first * 8 + second] = 1.0
    return pick


def spread_table():
    pick = face_table()
    order = np.concatenate([np.arange(64) + 64 * (face ^ 1) for face in range(6)])
    return pick[:, order].T


def basis_tables():
    points, _ = cheb_matrix()
    powers = np.stack([points**power for power in range(DEG + 1)])
    basis = np.zeros((6, 6, 8, 8, 8, 8))
    basis[:, :, :6] = np.einsum("xa,yb,zc->xyzabc", powers, powers, powers)
    basis = basis.reshape(ROWS, NODES).astype(np.float32)
    top = np.asarray(basis.astype(jnp.bfloat16))
    rest = np.asarray((basis - top.astype(np.float32)).astype(jnp.bfloat16))
    return np.concatenate([top, rest], axis=0)


def compact_table():
    table = np.zeros((ROWS, 256), jnp.bfloat16)
    for group in range(36):
        for power in range(6):
            table[group * 8 + power, group * 6 + power] = 1.0 / 512.0
    return table


def box_table(morton_count):
    bits = morton_count.bit_length() - 1
    key_bits = 3 * LMAX - bits
    table = np.zeros((morton_count, 8, LANES), np.float32)
    for morton in range(morton_count):
        base = morton << key_bits
        lows, sides = [], []
        for offset in (2, 1, 0):
            free = max(0, min(LMAX, (key_bits - offset + 2) // 3))
            cell = sum(((base >> (3 * bit + offset)) & 1) << bit for bit in range(LMAX))
            sides.append(2.0**free / 2.0**LMAX)
            lows.append(cell / 2.0**LMAX)
        scale = 0.5 * max(sides)
        for dim in range(3):
            center = lows[dim] + 0.5 * sides[dim]
            table[morton, dim, 3:6] = (center - 0.5) / 0.5
            table[morton, 4 + dim] = center
        table[morton, 3] = 1.0
        table[morton, 3, 3:6] = scale / 0.5
        table[morton, 7] = 1.0 / scale
    return table.reshape(morton_count * 8, LANES)


def swap(block, axis, apart):
    return lax.ppermute(block, axis, [(at, at ^ apart) for at in range(lax.axis_size(axis))])


def pairs(block, first):
    route = []
    for low in range(first, lax.axis_size("morton") - 1, 2):
        route += [(low, low + 1), (low + 1, low)]
    return lax.ppermute(block, "morton", route)


def dot(left, right):
    return jnp.dot(left, right, preferred_element_type=f32)


def dot_nt(left, right, precision=None):
    return lax.dot_general(
        left, right, (((1,), (1,)), ((), ())), preferred_element_type=f32, precision=precision
    )


def pack_kernel(
    counts_ref, vel_ref, visc_ref, nbrs_ref, levels_ref, keys_ref, box_ref, pick_ref,
    faces_ref, even_ref, odd_ref, spots_ref, *request_refs,
):
    sib_count = lax.axis_size("sib")
    morton = lax.axis_index("morton")
    sib = lax.axis_index("sib")
    own = morton * sib_count + sib
    leaf_count = faces_ref.shape[0]
    fields = jnp.concatenate([vel_ref[0], vel_ref[1], vel_ref[2], visc_ref[...].astype(bf16)], axis=0)
    picked = dot(fields, pick_ref[...])
    for dim in range(3):
        block = picked[3 * leaf_count :, dim * LANES : (dim + 1) * LANES]
        block = pltpu.roll(block, LANES // 2, 1).astype(bf16)
        for request_ref in request_refs:
            request_ref[:leaf_count, dim * LANES : (dim + 1) * LANES] = block
    picked = picked[: 3 * leaf_count].astype(bf16)
    for comp in range(3):
        for dim in range(3):
            lane = (dim * 3 + comp) * LANES
            rows = picked[comp * leaf_count : (comp + 1) * leaf_count]
            faces_ref[:, lane : lane + LANES] = rows[:, dim * LANES : (dim + 1) * LANES]
    first = counts_ref[own] - BAND
    row = lax.broadcasted_iota(jnp.int32, (BAND, leaf_count), 0)
    col = lax.broadcasted_iota(jnp.int32, (BAND, leaf_count), 1)
    last_rows = jnp.where(col == row + first, 1.0, 0.0).astype(bf16)
    high = dot(last_rows, faces_ref[...]).astype(bf16)
    low = faces_ref[:BAND, :]
    is_odd = jnp.bitwise_and(morton, 1) == 1
    even_ref[...] = jnp.where(is_odd, low, high)
    odd_ref[...] = jnp.where(is_odd, high, low)

    nbrs = nbrs_ref[...]
    target = jnp.maximum(nbrs, 0)
    owner = target // leaf_count
    slot = target - owner * leaf_count
    owner_morton = owner // sib_count
    owner_sib = owner - owner_morton * sib_count
    step = owner_morton - morton
    below = jnp.maximum(morton - 1, 0) * sib_count
    band_start = jnp.zeros_like(slot)
    for other in range(sib_count):
        band_start = jnp.where(owner_sib == other, counts_ref[below + other] - BAND, band_start)
    below_at = BAND * jnp.bitwise_and(morton, 1)
    in_band = jnp.where(step < 0, slot - band_start + below_at, slot + BAND - below_at)
    box = box_ref[pl.ds(pl.multiple_of(morton * 8, 8), 8), :]
    shift_bits = 3 * (LMAX - levels_ref[...])
    anchor = jnp.left_shift(jnp.right_shift(keys_ref[...], shift_bits), shift_bits)
    span = jnp.left_shift(jnp.ones_like(shift_bits), LMAX - levels_ref[...]).astype(f32)
    finest = 1.0 / float(2**LMAX)
    places = []
    for dim, offset in enumerate((2, 1, 0)):
        cell = jnp.zeros_like(anchor)
        for bit in range(LMAX):
            picked = jnp.bitwise_and(jnp.right_shift(anchor, 3 * bit + offset), 1)
            cell = cell + jnp.left_shift(picked, bit)
        center = (cell.astype(f32) + 0.5 * span) * finest
        places.append((center - box[4 + dim : 5 + dim, :]) * box[7:8, :])
    places.append(0.5 * span * finest * box[7:8, :])
    places.append(jnp.zeros((4, leaf_count), f32))
    geom = jnp.concatenate(places, axis=0)
    for side in range(sib_count // 2):
        piece = jnp.bitwise_xor(owner_sib, jnp.bitwise_xor(sib, 2 * side))
        spot = jnp.where(step == 0, piece * leaf_count + slot, 2 * leaf_count + piece * (2 * BAND) + in_band)
        spot = jnp.where((nbrs >= 0) & (piece < 2), spot, -1)
        if side == 0:
            spots_ref[...] = jnp.concatenate([spot.astype(f32), jnp.zeros((2, leaf_count), f32), geom], axis=0)
            continue
        whole = jnp.right_shift(spot, 4)
        parts = [whole.astype(f32), (spot - 16 * whole).astype(f32), geom[:4]]
        request_ref = request_refs[side - 1]
        request_ref[leaf_count:, :LANES] = jnp.concatenate(parts, axis=0).astype(bf16)
        request_ref[leaf_count:, LANES:] = jnp.zeros((16, FACES - LANES), bf16)


def gathered(asked, window_refs, start):
    leaf_count = asked[0].shape[1]
    rows = sum(ref.shape[0] for ref in window_refs)
    blank = jnp.full((LANES - 8 * len(asked), leaf_count), -1.0, f32)
    places = jnp.concatenate([spots[:8] for spots in asked] + [blank], axis=0).T.astype(jnp.int32)
    cols = lax.broadcasted_iota(jnp.int32, (leaf_count, rows), 1) + start
    upper = jnp.bitwise_and(lax.broadcasted_iota(jnp.int32, (leaf_count, FACES), 1), 64) > 0
    chosen = [[] for _ in asked]
    for dim in range(3):
        at = dim * FACES
        window = jnp.concatenate([ref[:, at : at + FACES] for ref in window_refs], axis=0)
        faces = [8 * who + face for who in range(len(asked)) for face in (2 * dim, 2 * dim + 1)]
        onehot = [jnp.where(cols == places[:, face : face + 1], 1.0, 0.0).astype(bf16) for face in faces]
        found = dot(jnp.concatenate(onehot, axis=0), window)
        for who in range(len(asked)):
            first, second = (found[(2 * who + side) * leaf_count : (2 * who + side + 1) * leaf_count] for side in (0, 1))
            chosen[who].append(jnp.where(upper, first, second).astype(bf16))
    return chosen


def requested(ref):
    leaf_count = ref.shape[0] - 16
    parts = ref[leaf_count:, :LANES].astype(f32)
    blank = jnp.zeros((2, leaf_count), f32)
    rows = [parts[:6] * 16.0 + parts[6:12], blank, parts[12:], jnp.zeros((4, leaf_count), f32)]
    return jnp.concatenate(rows, axis=0)


def by_comp(chosen):
    comps = [
        jnp.concatenate([block[:, comp * LANES : (comp + 1) * LANES] for block in chosen], axis=1) for comp in range(3)
    ]
    return jnp.concatenate(comps, axis=0)


def fill_tables(rows_ref, dx_ref, dyz_ref):
    row = lax.broadcasted_iota(jnp.int32, (64, NODES), 0)
    col = lax.broadcasted_iota(jnp.int32, (64, NODES), 1)
    same = row == jnp.bitwise_and(col, 63)
    for at in range(8):
        dx_ref[64 * at : 64 * at + 64, :] = jnp.where(same, rows_ref[at : at + 1, :], 0.0).astype(bf16)
    row = lax.broadcasted_iota(jnp.int32, (8, 256), 0)
    col = lax.broadcasted_iota(jnp.int32, (8, 256), 1)
    same = row == jnp.bitwise_and(col, 7)
    group = jnp.right_shift(col, 3)
    for pair in range(16):
        blocks = []
        for at in (2 * pair, 2 * pair + 1):
            here = same & (jnp.right_shift(group, 3) == at // 8)
            along_y = jnp.where(here, rows_ref[8 + at % 8 : 9 + at % 8, :256], 0.0)
            along_z = jnp.where(group == at, rows_ref[16:24, :256], 0.0)
            blocks.append(jnp.concatenate([along_y, along_z], axis=1))
        dyz_ref[16 * pair : 16 * pair + 16, :] = jnp.concatenate(blocks, axis=0).astype(bf16)


def operator_kernel(
    counts_ref, vel_ref, press_ref, visc_ref, rows_ref,
    part_ref, mass_ref, dx_ref, dyz_ref,
):
    sib_count = lax.axis_size("sib")
    own = lax.axis_index("morton") * sib_count + lax.axis_index("sib")
    leaf_count = mass_ref.shape[0]
    live = lax.broadcasted_iota(jnp.int32, (leaf_count, NODES), 0) < counts_ref[own]
    node = lax.broadcasted_iota(jnp.int32, (1, NODES), 1)
    touching = jnp.zeros((1, NODES), f32)
    for shift in (6, 3, 0):
        idx = jnp.bitwise_and(jnp.right_shift(node, shift), 7)
        touching = touching + jnp.where((idx == 0) | (idx == 7), 1.0, 0.0)
    fill_tables(rows_ref, dx_ref, dyz_ref)

    def rows(stack, at):
        return stack[at * leaf_count : (at + 1) * leaf_count]

    visc = visc_ref[...]
    fields = jnp.concatenate([vel_ref[0], vel_ref[1], vel_ref[2], press_ref[...]], axis=0)
    halves = [dot(fields[:, at : at + 256], dyz_ref[...]) for at in (0, 256)]
    grads = [
        dot(fields, dx_ref[...]),
        jnp.concatenate([half[:, :256] for half in halves], axis=1),
        jnp.concatenate([half[:, 256:] for half in halves], axis=1),
    ]
    mass = -(rows(grads[0], 0) + rows(grads[1], 1) + rows(grads[2], 2)) * mass_scale
    mass_ref[...] = jnp.where(live, mass, 0.0)
    stress = {}
    for first in range(3):
        for second in range(first, 3):
            value = (visc * (rows(grads[second], first) + rows(grads[first], second))).astype(bf16)
            stress[first, second] = stress[second, first] = value
    columns = [jnp.concatenate([stress[comp, dim] for comp in range(3)], axis=0) for dim in range(3)]
    rest = [
        dot(columns[1][:, at : at + 256], dyz_ref[:, :256]) + dot(columns[2][:, at : at + 256], dyz_ref[:, 256:])
        for at in (0, 256)
    ]
    div = dot(columns[0], dx_ref[...]) + jnp.concatenate(rest, axis=1)
    for comp in range(3):
        jump = touching * vel_ref[comp].astype(f32)
        part = (penalty * visc * jump - rows(div, comp) + rows(grads[comp], 3)) * out_scale
        part_ref[comp] = jnp.where(live, part, 0.0)


def group_kernel(box_ref, spots_ref, *refs):
    sides = lax.axis_size("sib") // 2
    request_refs, window_refs, move_ref, out_refs = refs[: sides - 1], refs[sides - 1 : sides + 1], refs[sides + 1], refs[sides + 2 :]
    chosen = gathered([spots_ref[...]] + [requested(ref) for ref in request_refs], window_refs, 0)
    for blocks, out_ref in zip(chosen, out_refs):
        for dim, block in enumerate(blocks):
            out_ref[:, dim * FACES : (dim + 1) * FACES] = block
    morton = lax.axis_index("morton")
    box = box_ref[pl.ds(pl.multiple_of(morton * 8, 8), 8), :]
    move = jnp.ones((256, 256), f32)
    for dim, stride in enumerate((36, 6, 1)):
        col = lax.broadcasted_iota(jnp.int32, (1, 256), 1) // stride % 6
        row = lax.broadcasted_iota(jnp.int32, (256, 1), 0) // stride % 6
        along, scale = box[dim : dim + 1, 3:4], box[3:4, 3:4]
        powers = [jnp.ones((1, 1), f32)]
        for _ in range(DEG):
            powers.append(powers[-1] * along)
        factor = jnp.zeros((256, 256), f32)
        below = jnp.ones((1, 1), f32)
        for low in range(DEG + 1):
            line = jnp.zeros((1, 256), f32)
            for high in range(low, DEG + 1):
                line = jnp.where(col == high, powers[high - low] * below * float(math.comb(high, low)), line)
            factor = jnp.where(row == low, line, factor)
            below = below * scale
        move = move * factor
    move_ref[...] = move


def shifted(tiles, geom):
    width = tiles[0].shape
    scale = jnp.broadcast_to(geom[3:4, :], width)
    level = lax.broadcasted_iota(jnp.int32, width, 0)
    depth = jnp.ones(width, f32)
    for power in range(1, DEG + 1):
        depth = depth * jnp.where(level >= power, scale, 1.0)
    scales = [depth]
    for _ in range(2 * DEG):
        scales.append(scales[-1] * scale)
    tiles = [tile * scales[at // 6 + at % 6] for at, tile in enumerate(tiles)]
    along = [jnp.broadcast_to(geom[dim : dim + 1, :], width) for dim in range(3)]
    for low in range(1, DEG + 1):
        for power in range(DEG, low - 1, -1):
            for other in range(6):
                at = power * 6 + other
                tiles[at] = tiles[at] + along[0] * tiles[at - 6]
            for other in range(6):
                at = other * 6 + power
                tiles[at] = tiles[at] + along[1] * tiles[at - 1]
    steps = [jnp.where(level >= low, along[2], 0.0) for low in range(1, DEG + 1)]
    for step in steps:
        tiles = [tile + step * pltpu.roll(tile, 1, 0) for tile in tiles]
    return tiles


def split(values, parts):
    pieces = []
    for _ in range(parts):
        pieces.append(values.astype(bf16))
        values = values - pieces[-1].astype(f32)
    return pieces


def lane_sums(raw_ref, geoms):
    leaf_count = geoms[0].shape[1]
    geom = jnp.concatenate([leaf for leaf in geoms for _ in range(3)], axis=1)
    tiles = shifted([raw_ref[8 * at : 8 * at + 8, :] for at in range(36)], geom)
    span = 3 * leaf_count
    tiles = [sum(tile[:, span * who : span * (who + 1)] for who in range(len(geoms))) for tile in tiles]
    group = lax.broadcasted_iota(jnp.int32, (span, LANES), 0) // leaf_count
    column = lax.broadcasted_iota(jnp.int32, (span, LANES), 1)
    gather = jnp.where((group == column) | (group + 3 == column), 1.0, 0.0).astype(bf16)
    return sum(dot(piece, gather) for piece in split(jnp.concatenate(tiles, axis=0), 3))


def own_kernel(part_ref, basis_ref, spots_ref, summed_ref, raw_ref):
    leaf_count = part_ref.shape[1]
    high, low = split(part_ref[...].reshape(3 * leaf_count, NODES), 2)
    raw = dot_nt(basis_ref[...], high)
    raw_ref[...] = raw[:ROWS] + raw[ROWS:] + dot_nt(basis_ref[:ROWS, :], low)
    summed_ref[...] = lane_sums(raw_ref, [spots_ref[8:, :]])


def moment_kernel(
    summed_ref, box_ref, face_basis_ref, compact_ref, spots_ref, weights_ref, *refs
):
    sides = lax.axis_size("sib") // 2
    window_refs, request_refs, group_refs = refs[:2], refs[2 : 1 + sides], refs[1 + sides : 1 + 2 * sides]
    near_ref, served_refs, sums_ref, raw_ref = refs[1 + 2 * sides], refs[2 + 2 * sides : -2], refs[-2], refs[-1]
    morton = lax.axis_index("morton")
    leaf_count = spots_ref.shape[1]
    asked = [spots_ref[...]] + [requested(ref) for ref in request_refs]
    chosen = gathered(asked, window_refs, 2 * leaf_count)
    values = []
    for blocks, group_ref, out_ref, ref in zip(
        chosen, group_refs, (near_ref, *served_refs), (weights_ref, *request_refs)
    ):
        for dim in range(3):
            lanes = slice(dim * FACES, (dim + 1) * FACES)
            blocks[dim] = blocks[dim] + group_ref[:, lanes]
            out_ref[:, lanes] = blocks[dim]
        weight = ref[:leaf_count].astype(f32) * (-penalty * out_scale)
        values.append(jnp.concatenate([weight] * 3, axis=0) * by_comp(blocks).astype(f32))
    raw_ref[...] = dot_nt(face_basis_ref[...], jnp.concatenate(values, axis=0).astype(bf16))
    summed = summed_ref[...] + lane_sums(raw_ref, [spots[8:] for spots in asked])
    box = box_ref[pl.ds(pl.multiple_of(morton * 8, 8), 8), :]
    both = shifted([summed[8 * at : 8 * at + 8, :] for at in range(36)], box)
    flat = jnp.concatenate(both, axis=0).T
    sums = sum(dot(piece, compact_ref[...]) for piece in split(flat[:8], 3))
    blank = jnp.zeros((2, LANES), f32)
    to_box = jnp.concatenate([sums[:3, :LANES], sums[:3, LANES:], blank], axis=0)
    to_root = jnp.concatenate([sums[3:6, :LANES], sums[3:6, LANES:], blank], axis=0)
    sib_count = lax.axis_size("sib")
    for other in range(sums_ref.shape[0]):
        sums_ref[other] = jnp.where(morton == other // sib_count, to_box, to_root)


def last_kernel(part_ref, visc_ref, spread_ref, sums_ref, move_ref, near_ref, *refs):
    got_refs, (force_hbm, box_hbm, root_hbm, force_ref, box_ref, root_ref, sems) = refs[:-7], refs[-7:]
    sib_count = lax.axis_size("sib")
    morton = lax.axis_index("morton")
    box = jnp.zeros(sums_ref.shape[1:], f32)
    root = jnp.zeros(sums_ref.shape[1:], f32)
    for group in range(sums_ref.shape[0] // sib_count):
        total = jnp.sum(sums_ref[group * sib_count : (group + 1) * sib_count], axis=0)
        box = box + jnp.where(morton == group, total, 0.0)
        root = root + jnp.where(morton == group, 0.0, total)
    box = jnp.concatenate([box[:3], box[3:6]], axis=1)
    root = jnp.concatenate([root[:3], root[3:6]], axis=1)
    box8 = jnp.concatenate([box, jnp.zeros((5, 2 * LANES), f32)], axis=0)
    root = root + jnp.dot(box8, move_ref[...], precision=highest, preferred_element_type=f32)[:3]
    for comp in range(3):
        box_ref[comp] = box[comp : comp + 1, :MOMENTS]
        root_ref[comp] = root[comp : comp + 1, :MOMENTS]
    stores = [
        pltpu.make_async_copy(box_ref, box_hbm, sems.at[3]),
        pltpu.make_async_copy(root_ref, root_hbm, sems.at[4]),
    ]
    for store in stores:
        store.start()
    faces = near_ref[...]
    for got_ref in got_refs:
        faces = faces + got_ref[...]
    weight = visc_ref[...] * (penalty * out_scale)
    for comp in range(3):
        lanes = [(dim * 3 + comp) * LANES for dim in range(3)]
        jump = dot(jnp.concatenate([faces[:, at : at + LANES] for at in lanes], axis=1), spread_ref[...])
        force_ref[comp] = part_ref[comp] - weight * jump
        stores.append(pltpu.make_async_copy(force_ref.at[comp], force_hbm.at[comp], sems.at[comp]))
        stores[-1].start()
    for store in stores:
        store.wait()


def call(kernel, shapes, flops, scalars, operands, scratch=(), place=pltpu.VMEM, outs=None, grant=32):
    specs = [pl.BlockSpec(memory_space=pltpu.SMEM)] * len(scalars)
    specs += [pl.BlockSpec(memory_space=place)] * len(operands)
    outs = outs or [pltpu.VMEM] * len(shapes)
    moved = sum(array.size * array.dtype.itemsize for array in operands)
    return pl.pallas_call(
        kernel,
        out_shape=[jax.ShapeDtypeStruct(shape, dtype) for shape, dtype in shapes],
        in_specs=specs,
        out_specs=[pl.BlockSpec(memory_space=out) for out in outs],
        scratch_shapes=list(scratch),
        compiler_params=pltpu.CompilerParams(vmem_limit_bytes=grant * 2**20),
        cost_estimate=pl.CostEstimate(flops=flops, bytes_accessed=moved, transcendentals=0),
    )(*scalars, *operands)


def on_device(velocity, pressure, viscosity, levels, morton_keys, counts, neighbors):
    leaf_count = velocity.shape[0]
    morton_count = lax.axis_size("morton")
    rows = jnp.asarray(derivative_rows().astype(np.float32))
    pick = jnp.asarray(face_table().astype(np.float32)).astype(bf16)
    spread = jnp.asarray(spread_table().astype(np.float32)).astype(bf16)
    basis = basis_tables()
    face_basis = (basis.astype(np.float32) @ spread_table().T.astype(np.float32)).astype(jnp.bfloat16)
    basis, face_basis = jnp.asarray(basis), jnp.asarray(face_basis[:ROWS])
    boxes = jnp.asarray(box_table(morton_count))
    vel = jnp.transpose(velocity, (1, 0, 2))
    nbrs = jnp.transpose(neighbors, (1, 0))

    width = 3 * FACES
    sib_count = lax.axis_size("sib")
    sides = sib_count // 2
    other_sides = [2 * side for side in range(1, sides)]
    faces, even, odd, spots, *requests = call(
        pack_kernel,
        [
            ((leaf_count, width), bf16),
            ((BAND, width), bf16),
            ((BAND, width), bf16),
            ((16, leaf_count), f32),
        ]
        + [((leaf_count + 16, FACES), bf16)] * (sides - 1),
        4 * 10**8,
        [counts],
        [vel, viscosity, nbrs, levels.reshape(1, -1), morton_keys.reshape(1, -1), boxes, pick],
        grant=60,
    )
    weights = requests[0]
    odd = pairs(odd, 1)
    across = swap(faces, "sib", 1)
    across, requests, even, pressure = lax.optimization_barrier((across, requests, even, pressure))
    requests = [swap(block, "sib", apart) for block, apart in zip(requests, other_sides)]
    even = pairs(even, 0)
    part, continuity = call(
        operator_kernel,
        [((3, leaf_count, NODES), f32), ((leaf_count, NODES), f32)],
        2 * 10**9,
        [counts],
        [vel, pressure, viscosity, rows],
        [pltpu.VMEM((NODES, NODES), bf16), pltpu.VMEM((256, NODES), bf16)],
    )
    (summed,) = call(
        own_kernel,
        [((ROWS, LANES), f32)],
        10**9,
        [],
        [part, basis, spots],
        [pltpu.VMEM((ROWS, 3 * leaf_count), f32)],
    )
    odd, even, summed, requests = lax.optimization_barrier((odd, even, summed, requests))
    bands = jnp.concatenate([odd, even], axis=0)
    move, *group = call(
        group_kernel,
        [((256, 256), f32)] + [((leaf_count, width), bf16)] * sides,
        10**9,
        [],
        [boxes, spots, *requests, faces, across],
    )
    near, *served, sums = call(
        moment_kernel,
        [((leaf_count, width), bf16)] * sides + [((morton_count * sib_count, 8, LANES), f32)],
        2 * 10**9,
        [],
        [
            summed, boxes, face_basis, jnp.asarray(compact_table()), spots, weights,
            bands, swap(bands, "sib", 1), *requests, *group,
        ],
        [pltpu.VMEM((ROWS, 3 * sides * leaf_count), f32)],
    )
    got = [swap(block, "sib", apart) for block, apart in zip(served, other_sides)]
    every = lax.all_to_all(sums, ("morton", "sib"), 0, 0, tiled=True)
    every, *got = lax.optimization_barrier((every, *got))
    force, box, root = call(
        last_kernel,
        [((3, leaf_count, NODES), f32), ((3, 1, MOMENTS), f32), ((3, 1, MOMENTS), f32)],
        2 * 10**8,
        [],
        [part, viscosity, spread, every, move, near, *got],
        [
            pltpu.VMEM((3, leaf_count, NODES), f32),
            pltpu.VMEM((3, 1, MOMENTS), f32),
            pltpu.VMEM((3, 1, MOMENTS), f32),
            pltpu.SemaphoreType.DMA((5,)),
        ],
        outs=[pltpu.HBM] * 3,
    )
    return (
        jnp.transpose(force, (1, 0, 2)),
        continuity,
        jnp.transpose(box, (1, 0, 2)),
        jnp.transpose(root, (1, 0, 2)),
    )


def solution(mesh):
    spread_all = ("morton", "sib")
    in_specs = (
        P(spread_all, None, None),
        P(spread_all, None),
        P(spread_all, None),
        P(spread_all),
        P(spread_all),
        P(),
        P(spread_all, None),
    )
    out_specs = (
        P(spread_all, None, None),
        P(spread_all, None),
        P("morton", None, None),
        P("morton", None, None),
    )
    return jax.shard_map(
        on_device, mesh=mesh, in_specs=in_specs, out_specs=out_specs, check_vma=False
    )
```

```python
import math

import jax
import jax.numpy as jnp
import numpy as np
from jax import lax
from jax.experimental import pallas as pl
from jax.experimental.pallas import tpu as pltpu
from jax.sharding import PartitionSpec as P

DEG = 5
LMAX = 7
MOMENTS = 216
BAND = 32
NODES = 512
FACES = 384
ROWS = 288
LANES = 128

penalty = 256.0
out_scale = 1.0 / 1024.0
mass_scale = 1.0 / 32.0
highest = lax.Precision.HIGHEST
f32 = jnp.float32
bf16 = jnp.bfloat16


def cheb_matrix():
    points = -np.cos(np.pi * np.arange(8) / 7.0)
    weights = np.array([(-1.0) ** node for node in range(8)])
    weights[0] *= 0.5
    weights[7] *= 0.5
    derivative = np.zeros((8, 8))
    for row in range(8):
        for col in range(8):
            if row != col:
                derivative[row, col] = weights[col] / weights[row] / (points[row] - points[col])
        derivative[row, row] = -np.sum(derivative[row])
    return points, derivative


def derivative_rows():
    _, derivative = cheb_matrix()
    lane = np.arange(NODES)
    return np.concatenate([derivative[lane // 64 % 8].T, derivative[lane // 8 % 8].T, derivative[lane % 8].T], axis=0)


def face_table():
    pick = np.zeros((NODES, FACES))
    for face in range(6):
        for first in range(8):
            for second in range(8):
                coords = [first, second]
                coords.insert(face // 2, 7 * (face % 2))
                node = 64 * coords[0] + 8 * coords[1] + coords[2]
                pick[node, face * 64 + first * 8 + second] = 1.0
    return pick


def spread_table():
    pick = face_table()
    order = np.concatenate([np.arange(64) + 64 * (face ^ 1) for face in range(6)])
    return pick[:, order].T


def basis_tables():
    points, _ = cheb_matrix()
    powers = np.stack([points**power for power in range(DEG + 1)])
    basis = np.zeros((6, 6, 8, 8, 8, 8))
    basis[:, :, :6] = np.einsum("xa,yb,zc->xyzabc", powers, powers, powers)
    basis = basis.reshape(ROWS, NODES).astype(np.float32)
    top = np.asarray(basis.astype(jnp.bfloat16))
    rest = np.asarray((basis - top.astype(np.float32)).astype(jnp.bfloat16))
    return np.concatenate([top, rest], axis=0)


def compact_table():
    table = np.zeros((ROWS, 256), jnp.bfloat16)
    for group in range(36):
        for power in range(6):
            table[group * 8 + power, group * 6 + power] = 1.0 / 512.0
    return table


def box_table(morton_count):
    bits = morton_count.bit_length() - 1
    key_bits = 3 * LMAX - bits
    table = np.zeros((morton_count, 8, LANES), np.float32)
    for morton in range(morton_count):
        base = morton << key_bits
        lows, sides = [], []
        for offset in (2, 1, 0):
            free = max(0, min(LMAX, (key_bits - offset + 2) // 3))
            cell = sum(((base >> (3 * bit + offset)) & 1) << bit for bit in range(LMAX))
            sides.append(2.0**free / 2.0**LMAX)
            lows.append(cell / 2.0**LMAX)
        scale = 0.5 * max(sides)
        for dim in range(3):
            center = lows[dim] + 0.5 * sides[dim]
            table[morton, dim, 3:6] = (center - 0.5) / 0.5
            table[morton, 4 + dim] = center
        table[morton, 3] = 1.0
        table[morton, 3, 3:6] = scale / 0.5
        table[morton, 7] = 1.0 / scale
    return table.reshape(morton_count * 8, LANES)


def swap(block, axis, apart):
    return lax.ppermute(block, axis, [(at, at ^ apart) for at in range(lax.axis_size(axis))])


def pairs(block, first):
    route = []
    for low in range(first, lax.axis_size("morton") - 1, 2):
        route += [(low, low + 1), (low + 1, low)]
    return lax.ppermute(block, "morton", route)


def dot(left, right):
    return jnp.dot(left, right, preferred_element_type=f32)


def dot_nt(left, right, precision=None):
    return lax.dot_general(
        left, right, (((1,), (1,)), ((), ())), preferred_element_type=f32, precision=precision
    )


def pack_kernel(
    counts_ref, vel_ref, visc_ref, nbrs_ref, levels_ref, keys_ref, box_ref, pick_ref,
    faces_ref, even_ref, odd_ref, spots_ref, *request_refs,
):
    sib_count = lax.axis_size("sib")
    morton = lax.axis_index("morton")
    sib = lax.axis_index("sib")
    own = morton * sib_count + sib
    leaf_count = faces_ref.shape[0]
    fields = jnp.concatenate([vel_ref[0], vel_ref[1], vel_ref[2], visc_ref[...].astype(bf16)], axis=0)
    picked = dot(fields, pick_ref[...])
    for dim in range(3):
        block = picked[3 * leaf_count :, dim * LANES : (dim + 1) * LANES]
        block = pltpu.roll(block, LANES // 2, 1).astype(bf16)
        for request_ref in request_refs:
            request_ref[:leaf_count, dim * LANES : (dim + 1) * LANES] = block
    picked = picked[: 3 * leaf_count].astype(bf16)
    for comp in range(3):
        for dim in range(3):
            lane = (dim * 3 + comp) * LANES
            rows = picked[comp * leaf_count : (comp + 1) * leaf_count]
            faces_ref[:, lane : lane + LANES] = rows[:, dim * LANES : (dim + 1) * LANES]
    first = counts_ref[own] - BAND
    row = lax.broadcasted_iota(jnp.int32, (BAND, leaf_count), 0)
    col = lax.broadcasted_iota(jnp.int32, (BAND, leaf_count), 1)
    last_rows = jnp.where(col == row + first, 1.0, 0.0).astype(bf16)
    high = dot(last_rows, faces_ref[...]).astype(bf16)
    low = faces_ref[:BAND, :]
    is_odd = jnp.bitwise_and(morton, 1) == 1
    even_ref[...] = jnp.where(is_odd, low, high)
    odd_ref[...] = jnp.where(is_odd, high, low)

    nbrs = nbrs_ref[...]
    target = jnp.maximum(nbrs, 0)
    owner = target // leaf_count
    slot = target - owner * leaf_count
    owner_morton = owner // sib_count
    owner_sib = owner - owner_morton * sib_count
    step = owner_morton - morton
    below = jnp.maximum(morton - 1, 0) * sib_count
    band_start = jnp.zeros_like(slot)
    for other in range(sib_count):
        band_start = jnp.where(owner_sib == other, counts_ref[below + other] - BAND, band_start)
    below_at = BAND * jnp.bitwise_and(morton, 1)
    in_band = jnp.where(step < 0, slot - band_start + below_at, slot + BAND - below_at)
    box = box_ref[pl.ds(pl.multiple_of(morton * 8, 8), 8), :]
    shift_bits = 3 * (LMAX - levels_ref[...])
    anchor = jnp.left_shift(jnp.right_shift(keys_ref[...], shift_bits), shift_bits)
    span = jnp.left_shift(jnp.ones_like(shift_bits), LMAX - levels_ref[...]).astype(f32)
    finest = 1.0 / float(2**LMAX)
    places = []
    for dim, offset in enumerate((2, 1, 0)):
        cell = jnp.zeros_like(anchor)
        for bit in range(LMAX):
            picked = jnp.bitwise_and(jnp.right_shift(anchor, 3 * bit + offset), 1)
            cell = cell + jnp.left_shift(picked, bit)
        center = (cell.astype(f32) + 0.5 * span) * finest
        places.append((center - box[4 + dim : 5 + dim, :]) * box[7:8, :])
    places.append(0.5 * span * finest * box[7:8, :])
    places.append(jnp.zeros((4, leaf_count), f32))
    geom = jnp.concatenate(places, axis=0)
    for side in range(sib_count // 2):
        piece = jnp.bitwise_xor(owner_sib, jnp.bitwise_xor(sib, 2 * side))
        spot = jnp.where(step == 0, piece * leaf_count + slot, 2 * leaf_count + piece * (2 * BAND) + in_band)
        spot = jnp.where((nbrs >= 0) & (piece < 2), spot, -1)
        if side == 0:
            spots_ref[...] = jnp.concatenate([spot.astype(f32), jnp.zeros((2, leaf_count), f32), geom[:4], box[:4]], axis=0)
            continue
        whole = jnp.right_shift(spot, 4)
        parts = [whole.astype(f32), (spot - 16 * whole).astype(f32), geom[:4]]
        request_ref = request_refs[side - 1]
        request_ref[leaf_count:, :LANES] = jnp.concatenate(parts, axis=0).astype(bf16)
        request_ref[leaf_count:, LANES:] = jnp.zeros((16, FACES - LANES), bf16)


def gathered(asked, window_refs, start):
    leaf_count = asked[0].shape[1]
    rows = sum(ref.shape[0] for ref in window_refs)
    blank = jnp.full((LANES - 8 * len(asked), leaf_count), -1.0, f32)
    places = jnp.concatenate([spots[:8] for spots in asked] + [blank], axis=0).T.astype(jnp.int32)
    cols = lax.broadcasted_iota(jnp.int32, (leaf_count, rows), 1) + start
    upper = jnp.bitwise_and(lax.broadcasted_iota(jnp.int32, (leaf_count, FACES), 1), 64) > 0
    chosen = [[] for _ in asked]
    for dim in range(3):
        at = dim * FACES
        window = jnp.concatenate([ref[:, at : at + FACES] for ref in window_refs], axis=0)
        faces = [8 * who + face for who in range(len(asked)) for face in (2 * dim, 2 * dim + 1)]
        onehot = [jnp.where(cols == places[:, face : face + 1], 1.0, 0.0).astype(bf16) for face in faces]
        found = dot(jnp.concatenate(onehot, axis=0), window)
        for who in range(len(asked)):
            first, second = (found[(2 * who + side) * leaf_count : (2 * who + side + 1) * leaf_count] for side in (0, 1))
            chosen[who].append(jnp.where(upper, first, second).astype(bf16))
    return chosen


def requested(ref):
    leaf_count = ref.shape[0] - 16
    parts = ref[leaf_count:, :LANES].astype(f32)
    blank = jnp.zeros((2, leaf_count), f32)
    rows = [parts[:6] * 16.0 + parts[6:12], blank, parts[12:], jnp.zeros((4, leaf_count), f32)]
    return jnp.concatenate(rows, axis=0)


def by_comp(chosen):
    comps = [
        jnp.concatenate([block[:, comp * LANES : (comp + 1) * LANES] for block in chosen], axis=1) for comp in range(3)
    ]
    return jnp.concatenate(comps, axis=0)


def fill_tables(rows_ref, dx_ref, dyz_ref):
    row = lax.broadcasted_iota(jnp.int32, (64, NODES), 0)
    col = lax.broadcasted_iota(jnp.int32, (64, NODES), 1)
    same = row == jnp.bitwise_and(col, 63)
    for at in range(8):
        dx_ref[64 * at : 64 * at + 64, :] = jnp.where(same, rows_ref[at : at + 1, :], 0.0).astype(bf16)
    row = lax.broadcasted_iota(jnp.int32, (8, 256), 0)
    col = lax.broadcasted_iota(jnp.int32, (8, 256), 1)
    same = row == jnp.bitwise_and(col, 7)
    group = jnp.right_shift(col, 3)
    for pair in range(16):
        blocks = []
        for at in (2 * pair, 2 * pair + 1):
            here = same & (jnp.right_shift(group, 3) == at // 8)
            along_y = jnp.where(here, rows_ref[8 + at % 8 : 9 + at % 8, :256], 0.0)
            along_z = jnp.where(group == at, rows_ref[16:24, :256], 0.0)
            blocks.append(jnp.concatenate([along_y, along_z], axis=1))
        dyz_ref[16 * pair : 16 * pair + 16, :] = jnp.concatenate(blocks, axis=0).astype(bf16)


def operator_kernel(
    counts_ref, vel_ref, press_ref, visc_ref, rows_ref,
    part_ref, mass_ref, dx_ref, dyz_ref,
):
    sib_count = lax.axis_size("sib")
    own = lax.axis_index("morton") * sib_count + lax.axis_index("sib")
    leaf_count = mass_ref.shape[0]
    live = lax.broadcasted_iota(jnp.int32, (leaf_count, NODES), 0) < counts_ref[own]
    node = lax.broadcasted_iota(jnp.int32, (1, NODES), 1)
    touching = jnp.zeros((1, NODES), f32)
    for shift in (6, 3, 0):
        idx = jnp.bitwise_and(jnp.right_shift(node, shift), 7)
        touching = touching + jnp.where((idx == 0) | (idx == 7), 1.0, 0.0)
    fill_tables(rows_ref, dx_ref, dyz_ref)

    def rows(stack, at):
        return stack[at * leaf_count : (at + 1) * leaf_count]

    visc = visc_ref[...]
    fields = jnp.concatenate([vel_ref[0], vel_ref[1], vel_ref[2], press_ref[...]], axis=0)
    halves = [dot(fields[:, at : at + 256], dyz_ref[...]) for at in (0, 256)]
    grads = [
        dot(fields, dx_ref[...]),
        jnp.concatenate([half[:, :256] for half in halves], axis=1),
        jnp.concatenate([half[:, 256:] for half in halves], axis=1),
    ]
    mass = -(rows(grads[0], 0) + rows(grads[1], 1) + rows(grads[2], 2)) * mass_scale
    mass_ref[...] = jnp.where(live, mass, 0.0)
    stress = {}
    for first in range(3):
        for second in range(first, 3):
            value = (visc * (rows(grads[second], first) + rows(grads[first], second))).astype(bf16)
            stress[first, second] = stress[second, first] = value
    columns = [jnp.concatenate([stress[comp, dim] for comp in range(3)], axis=0) for dim in range(3)]
    rest = [
        dot(columns[1][:, at : at + 256], dyz_ref[:, :256]) + dot(columns[2][:, at : at + 256], dyz_ref[:, 256:])
        for at in (0, 256)
    ]
    div = dot(columns[0], dx_ref[...]) + jnp.concatenate(rest, axis=1)
    for comp in range(3):
        jump = touching * vel_ref[comp].astype(f32)
        part = (penalty * visc * jump - rows(div, comp) + rows(grads[comp], 3)) * out_scale
        part_ref[comp] = jnp.where(live, part, 0.0)


def group_kernel(spots_ref, *refs):
    sides = lax.axis_size("sib") // 2
    request_refs, window_refs, move_ref, out_refs = refs[: sides - 1], refs[sides - 1 : sides + 1], refs[sides + 1], refs[sides + 2 :]
    chosen = gathered([spots_ref[...]] + [requested(ref) for ref in request_refs], window_refs, 0)
    for blocks, out_ref in zip(chosen, out_refs):
        for dim, block in enumerate(blocks):
            out_ref[:, dim * FACES : (dim + 1) * FACES] = block
    box = spots_ref[12:, :]
    move = jnp.ones((256, 256), f32)
    for dim, stride in enumerate((36, 6, 1)):
        col = lax.broadcasted_iota(jnp.int32, (1, 256), 1) // stride % 6
        row = lax.broadcasted_iota(jnp.int32, (256, 1), 0) // stride % 6
        along, scale = box[dim : dim + 1, 3:4], box[3:4, 3:4]
        powers = [jnp.ones((1, 1), f32)]
        for _ in range(DEG):
            powers.append(powers[-1] * along)
        factor = jnp.zeros((256, 256), f32)
        below = jnp.ones((1, 1), f32)
        for low in range(DEG + 1):
            line = jnp.zeros((1, 256), f32)
            for high in range(low, DEG + 1):
                line = jnp.where(col == high, powers[high - low] * below * float(math.comb(high, low)), line)
            factor = jnp.where(row == low, line, factor)
            below = below * scale
        move = move * factor
    move_ref[...] = move


def shifted(tiles, geom):
    width = tiles[0].shape
    scale = jnp.broadcast_to(geom[3:4, :], width)
    level = lax.broadcasted_iota(jnp.int32, width, 0)
    depth = jnp.ones(width, f32)
    for power in range(1, DEG + 1):
        depth = depth * jnp.where(level >= power, scale, 1.0)
    scales = [depth]
    for _ in range(2 * DEG):
        scales.append(scales[-1] * scale)
    tiles = [tile * scales[at // 6 + at % 6] for at, tile in enumerate(tiles)]
    along = [jnp.broadcast_to(geom[dim : dim + 1, :], width) for dim in range(3)]
    for low in range(1, DEG + 1):
        for power in range(DEG, low - 1, -1):
            for other in range(6):
                at = power * 6 + other
                tiles[at] = tiles[at] + along[0] * tiles[at - 6]
            for other in range(6):
                at = other * 6 + power
                tiles[at] = tiles[at] + along[1] * tiles[at - 1]
    steps = [jnp.where(level >= low, along[2], 0.0) for low in range(1, DEG + 1)]
    for step in steps:
        tiles = [tile + step * pltpu.roll(tile, 1, 0) for tile in tiles]
    return tiles


def split(values, parts):
    pieces = []
    for _ in range(parts):
        pieces.append(values.astype(bf16))
        values = values - pieces[-1].astype(f32)
    return pieces


def lane_sums(raw_ref, geoms):
    leaf_count = geoms[0].shape[1]
    geom = jnp.concatenate([leaf for leaf in geoms for _ in range(3)], axis=1)
    tiles = shifted([raw_ref[8 * at : 8 * at + 8, :] for at in range(36)], geom)
    span = 3 * leaf_count
    tiles = [sum(tile[:, span * who : span * (who + 1)] for who in range(len(geoms))) for tile in tiles]
    group = lax.broadcasted_iota(jnp.int32, (span, LANES), 0) // leaf_count
    column = lax.broadcasted_iota(jnp.int32, (span, LANES), 1)
    gather = jnp.where((group == column) | (group + 3 == column), 1.0, 0.0).astype(bf16)
    return sum(dot(piece, gather) for piece in split(jnp.concatenate(tiles, axis=0), 3))


def own_kernel(part_ref, basis_ref, spots_ref, summed_ref, raw_ref):
    leaf_count = part_ref.shape[1]
    high, low = split(part_ref[...].reshape(3 * leaf_count, NODES), 2)
    raw = dot_nt(basis_ref[...], high)
    raw_ref[...] = raw[:ROWS] + raw[ROWS:] + dot_nt(basis_ref[:ROWS, :], low)
    summed_ref[...] = lane_sums(raw_ref, [spots_ref[8:, :]])


def moment_kernel(
    summed_ref, face_basis_ref, compact_ref, spots_ref, weights_ref, *refs
):
    sides = lax.axis_size("sib") // 2
    window_refs, request_refs, group_refs = refs[:2], refs[2 : 1 + sides], refs[1 + sides : 1 + 2 * sides]
    near_ref, served_refs, sums_ref, raw_ref = refs[1 + 2 * sides], refs[2 + 2 * sides : -2], refs[-2], refs[-1]
    morton = lax.axis_index("morton")
    leaf_count = spots_ref.shape[1]
    asked = [spots_ref[...]] + [requested(ref) for ref in request_refs]
    chosen = gathered(asked, window_refs, 2 * leaf_count)
    values = []
    for blocks, group_ref, out_ref, ref in zip(
        chosen, group_refs, (near_ref, *served_refs), (weights_ref, *request_refs)
    ):
        for dim in range(3):
            lanes = slice(dim * FACES, (dim + 1) * FACES)
            blocks[dim] = blocks[dim] + group_ref[:, lanes]
            out_ref[:, lanes] = blocks[dim]
        weight = ref[:leaf_count].astype(f32) * (-penalty * out_scale)
        values.append(jnp.concatenate([weight] * 3, axis=0) * by_comp(blocks).astype(f32))
    raw_ref[...] = dot_nt(face_basis_ref[...], jnp.concatenate(values, axis=0).astype(bf16))
    summed = summed_ref[...] + lane_sums(raw_ref, [spots[8:] for spots in asked])
    box = spots_ref[12:, :]
    both = shifted([summed[8 * at : 8 * at + 8, :] for at in range(36)], box)
    flat = jnp.concatenate(both, axis=0).T
    sums = sum(dot(piece, compact_ref[...]) for piece in split(flat[:8], 3))
    blank = jnp.zeros((2, LANES), f32)
    to_box = jnp.concatenate([sums[:3, :LANES], sums[:3, LANES:], blank], axis=0)
    to_root = jnp.concatenate([sums[3:6, :LANES], sums[3:6, LANES:], blank], axis=0)
    sib_count = lax.axis_size("sib")
    for other in range(sums_ref.shape[0]):
        sums_ref[other] = jnp.where(morton == other // sib_count, to_box, to_root)


def last_kernel(part_ref, visc_ref, spread_ref, sums_ref, move_ref, near_ref, *refs):
    got_refs, (force_hbm, box_hbm, root_hbm, force_ref, box_ref, root_ref, sems) = refs[:-7], refs[-7:]
    faces = near_ref[...]
    for got_ref in got_refs:
        faces = faces + got_ref[...]
    weight = visc_ref[...] * (penalty * out_scale)
    stores = []
    for comp in range(3):
        lanes = [(dim * 3 + comp) * LANES for dim in range(3)]
        jump = dot(jnp.concatenate([faces[:, at : at + LANES] for at in lanes], axis=1), spread_ref[...])
        force_ref[comp] = part_ref[comp] - weight * jump
        stores.append(pltpu.make_async_copy(force_ref.at[comp], force_hbm.at[comp], sems.at[comp]))
        stores[-1].start()
    sib_count = lax.axis_size("sib")
    morton = lax.axis_index("morton")
    box = jnp.zeros(sums_ref.shape[1:], f32)
    root = jnp.zeros(sums_ref.shape[1:], f32)
    for group in range(sums_ref.shape[0] // sib_count):
        total = jnp.sum(sums_ref[group * sib_count : (group + 1) * sib_count], axis=0)
        box = box + jnp.where(morton == group, total, 0.0)
        root = root + jnp.where(morton == group, 0.0, total)
    box = jnp.concatenate([box[:3], box[3:6]], axis=1)
    root = jnp.concatenate([root[:3], root[3:6]], axis=1)
    box_rows = jnp.concatenate([box, jnp.zeros((5, 2 * LANES), f32)], axis=0)
    pieces = jnp.concatenate([piece.astype(f32) for piece in split(box_rows, 3)], axis=0).astype(bf16)
    moved = sum(dot(pieces, table) for table in split(move_ref[...], 2))
    root = root + (moved[:3] + moved[8:11] + moved[16:19])
    for comp in range(3):
        box_ref[comp] = box[comp : comp + 1, :MOMENTS]
        root_ref[comp] = root[comp : comp + 1, :MOMENTS]
    stores.append(pltpu.make_async_copy(box_ref, box_hbm, sems.at[3]))
    stores.append(pltpu.make_async_copy(root_ref, root_hbm, sems.at[4]))
    for store in stores[3:]:
        store.start()
    for store in stores:
        store.wait()


def call(kernel, shapes, flops, scalars, operands, scratch=(), place=pltpu.VMEM, outs=None, grant=32):
    specs = [pl.BlockSpec(memory_space=pltpu.SMEM)] * len(scalars)
    specs += [pl.BlockSpec(memory_space=place)] * len(operands)
    outs = outs or [pltpu.VMEM] * len(shapes)
    moved = sum(array.size * array.dtype.itemsize for array in operands)
    return pl.pallas_call(
        kernel,
        out_shape=[jax.ShapeDtypeStruct(shape, dtype) for shape, dtype in shapes],
        in_specs=specs,
        out_specs=[pl.BlockSpec(memory_space=out) for out in outs],
        scratch_shapes=list(scratch),
        compiler_params=pltpu.CompilerParams(vmem_limit_bytes=grant * 2**20),
        cost_estimate=pl.CostEstimate(flops=flops, bytes_accessed=moved, transcendentals=0),
    )(*scalars, *operands)


def on_device(velocity, pressure, viscosity, levels, morton_keys, counts, neighbors):
    leaf_count = velocity.shape[0]
    morton_count = lax.axis_size("morton")
    rows = jnp.asarray(derivative_rows().astype(np.float32))
    pick = jnp.asarray(face_table().astype(np.float32)).astype(bf16)
    spread = jnp.asarray(spread_table().astype(np.float32)).astype(bf16)
    basis = basis_tables()
    face_basis = (basis.astype(np.float32) @ spread_table().T.astype(np.float32)).astype(jnp.bfloat16)
    basis, face_basis = jnp.asarray(basis), jnp.asarray(face_basis[:ROWS])
    boxes = jnp.asarray(box_table(morton_count))
    vel = jnp.transpose(velocity, (1, 0, 2))
    nbrs = jnp.transpose(neighbors, (1, 0))

    width = 3 * FACES
    sib_count = lax.axis_size("sib")
    sides = sib_count // 2
    other_sides = [2 * side for side in range(1, sides)]
    faces, even, odd, spots, *requests = call(
        pack_kernel,
        [
            ((leaf_count, width), bf16),
            ((BAND, width), bf16),
            ((BAND, width), bf16),
            ((16, leaf_count), f32),
        ]
        + [((leaf_count + 16, FACES), bf16)] * (sides - 1),
        4 * 10**8,
        [counts],
        [vel, viscosity, nbrs, levels.reshape(1, -1), morton_keys.reshape(1, -1), boxes, pick],
        grant=60,
    )
    weights = requests[0]
    even, odd = pairs(even, 0), pairs(odd, 1)
    across = swap(faces, "sib", 1)
    across, requests, pressure = lax.optimization_barrier((across, requests, pressure))
    requests = [swap(block, "sib", apart) for block, apart in zip(requests, other_sides)]
    part, continuity = call(
        operator_kernel,
        [((3, leaf_count, NODES), f32), ((leaf_count, NODES), f32)],
        2 * 10**9,
        [counts],
        [vel, pressure, viscosity, rows],
        [pltpu.VMEM((NODES, NODES), bf16), pltpu.VMEM((256, NODES), bf16)],
    )
    (summed,) = call(
        own_kernel,
        [((ROWS, LANES), f32)],
        10**9,
        [],
        [part, basis, spots],
        [pltpu.VMEM((ROWS, 3 * leaf_count), f32)],
    )
    even, odd, summed, requests = lax.optimization_barrier((even, odd, summed, requests))
    bands = jnp.concatenate([odd, even], axis=0)
    move, *group = call(
        group_kernel,
        [((256, 256), f32)] + [((leaf_count, width), bf16)] * sides,
        10**9,
        [],
        [spots, *requests, faces, across],
    )
    near, *served, sums = call(
        moment_kernel,
        [((leaf_count, width), bf16)] * sides + [((morton_count * sib_count, 8, LANES), f32)],
        2 * 10**9,
        [],
        [
            summed, face_basis, jnp.asarray(compact_table()), spots, weights,
            bands, swap(bands, "sib", 1), *requests, *group,
        ],
        [pltpu.VMEM((ROWS, 3 * sides * leaf_count), f32)],
    )
    got = [swap(block, "sib", apart) for block, apart in zip(served, other_sides)]
    every = lax.all_to_all(sums, ("morton", "sib"), 0, 0, tiled=True)
    every, *got = lax.optimization_barrier((every, *got))
    force, box, root = call(
        last_kernel,
        [((3, leaf_count, NODES), f32), ((3, 1, MOMENTS), f32), ((3, 1, MOMENTS), f32)],
        2 * 10**8,
        [],
        [part, viscosity, spread, every, move, near, *got],
        [
            pltpu.VMEM((3, leaf_count, NODES), f32),
            pltpu.VMEM((3, 1, MOMENTS), f32),
            pltpu.VMEM((3, 1, MOMENTS), f32),
            pltpu.SemaphoreType.DMA((5,)),
        ],
        outs=[pltpu.HBM] * 3,
    )
    return (
        jnp.transpose(force, (1, 0, 2)),
        continuity,
        jnp.transpose(box, (1, 0, 2)),
        jnp.transpose(root, (1, 0, 2)),
    )


def solution(mesh):
    spread_all = ("morton", "sib")
    in_specs = (
        P(spread_all, None, None),
        P(spread_all, None),
        P(spread_all, None),
        P(spread_all),
        P(spread_all),
        P(),
        P(spread_all, None),
    )
    out_specs = (
        P(spread_all, None, None),
        P(spread_all, None),
        P("morton", None, None),
        P("morton", None, None),
    )
    return jax.shard_map(
        on_device, mesh=mesh, in_specs=in_specs, out_specs=out_specs, check_vma=False
    )
```

```python
import math

import jax
import jax.numpy as jnp
import numpy as np
from jax import lax
from jax.experimental import pallas as pl
from jax.experimental.pallas import tpu as pltpu
from jax.sharding import PartitionSpec as P

DEG = 5
LMAX = 7
MOMENTS = 216
BAND = 32
NODES = 512
FACES = 384
ROWS = 288
LANES = 128

penalty = 256.0
out_scale = 1.0 / 1024.0
mass_scale = 1.0 / 32.0
highest = lax.Precision.HIGHEST
f32 = jnp.float32
bf16 = jnp.bfloat16


def cheb_matrix():
    points = -np.cos(np.pi * np.arange(8) / 7.0)
    weights = np.array([(-1.0) ** node for node in range(8)])
    weights[0] *= 0.5
    weights[7] *= 0.5
    derivative = np.zeros((8, 8))
    for row in range(8):
        for col in range(8):
            if row != col:
                derivative[row, col] = weights[col] / weights[row] / (points[row] - points[col])
        derivative[row, row] = -np.sum(derivative[row])
    return points, derivative


def derivative_rows():
    _, derivative = cheb_matrix()
    lane = np.arange(NODES)
    return np.concatenate([derivative[lane // 64 % 8].T, derivative[lane // 8 % 8].T, derivative[lane % 8].T], axis=0)


def face_table():
    pick = np.zeros((NODES, FACES))
    for face in range(6):
        for first in range(8):
            for second in range(8):
                coords = [first, second]
                coords.insert(face // 2, 7 * (face % 2))
                node = 64 * coords[0] + 8 * coords[1] + coords[2]
                pick[node, face * 64 + first * 8 + second] = 1.0
    return pick


def spread_table():
    pick = face_table()
    order = np.concatenate([np.arange(64) + 64 * (face ^ 1) for face in range(6)])
    return pick[:, order].T


def basis_tables():
    points, _ = cheb_matrix()
    powers = np.stack([points**power for power in range(DEG + 1)])
    basis = np.zeros((6, 6, 8, 8, 8, 8))
    basis[:, :, :6] = np.einsum("xa,yb,zc->xyzabc", powers, powers, powers)
    basis = basis.reshape(ROWS, NODES).astype(np.float32)
    top = np.asarray(basis.astype(jnp.bfloat16))
    rest = np.asarray((basis - top.astype(np.float32)).astype(jnp.bfloat16))
    return np.concatenate([top, rest], axis=0)


def compact_table():
    table = np.zeros((ROWS, 256), jnp.bfloat16)
    for group in range(36):
        for power in range(6):
            table[group * 8 + power, group * 6 + power] = 1.0 / 512.0
    return table


def box_table(morton_count):
    bits = morton_count.bit_length() - 1
    key_bits = 3 * LMAX - bits
    table = np.zeros((morton_count, 8, LANES), np.float32)
    for morton in range(morton_count):
        base = morton << key_bits
        lows, sides = [], []
        for offset in (2, 1, 0):
            free = max(0, min(LMAX, (key_bits - offset + 2) // 3))
            cell = sum(((base >> (3 * bit + offset)) & 1) << bit for bit in range(LMAX))
            sides.append(2.0**free / 2.0**LMAX)
            lows.append(cell / 2.0**LMAX)
        scale = 0.5 * max(sides)
        for dim in range(3):
            center = lows[dim] + 0.5 * sides[dim]
            table[morton, dim, 3:6] = (center - 0.5) / 0.5
            table[morton, 4 + dim] = center
        table[morton, 3] = 1.0
        table[morton, 3, 3:6] = scale / 0.5
        table[morton, 7] = 1.0 / scale
    return table.reshape(morton_count * 8, LANES)


def swap(block, axis, apart):
    return lax.ppermute(block, axis, [(at, at ^ apart) for at in range(lax.axis_size(axis))])


def pairs(block, first):
    route = []
    for low in range(first, lax.axis_size("morton") - 1, 2):
        route += [(low, low + 1), (low + 1, low)]
    return lax.ppermute(block, "morton", route)


def dot(left, right):
    return jnp.dot(left, right, preferred_element_type=f32)


def dot_nt(left, right, precision=None):
    return lax.dot_general(
        left, right, (((1,), (1,)), ((), ())), preferred_element_type=f32, precision=precision
    )


def pack_kernel(
    counts_ref, vel_ref, visc_ref, nbrs_ref, levels_ref, keys_ref, box_ref, pick_ref,
    faces_ref, even_ref, odd_ref, spots_ref, *request_refs,
):
    sib_count = lax.axis_size("sib")
    morton = lax.axis_index("morton")
    sib = lax.axis_index("sib")
    own = morton * sib_count + sib
    leaf_count = faces_ref.shape[0]
    fields = jnp.concatenate([vel_ref[0], vel_ref[1], vel_ref[2], visc_ref[...].astype(bf16)], axis=0)
    picked = dot(fields, pick_ref[...])
    for dim in range(3):
        block = picked[3 * leaf_count :, dim * LANES : (dim + 1) * LANES]
        block = pltpu.roll(block, LANES // 2, 1).astype(bf16)
        for request_ref in request_refs:
            request_ref[:leaf_count, dim * LANES : (dim + 1) * LANES] = block
    picked = picked[: 3 * leaf_count].astype(bf16)
    for comp in range(3):
        for dim in range(3):
            lane = (dim * 3 + comp) * LANES
            rows = picked[comp * leaf_count : (comp + 1) * leaf_count]
            faces_ref[:, lane : lane + LANES] = rows[:, dim * LANES : (dim + 1) * LANES]
    first = counts_ref[own] - BAND
    row = lax.broadcasted_iota(jnp.int32, (BAND, leaf_count), 0)
    col = lax.broadcasted_iota(jnp.int32, (BAND, leaf_count), 1)
    last_rows = jnp.where(col == row + first, 1.0, 0.0).astype(bf16)
    high = dot(last_rows, faces_ref[...]).astype(bf16)
    low = faces_ref[:BAND, :]
    is_odd = jnp.bitwise_and(morton, 1) == 1
    even_ref[...] = jnp.where(is_odd, low, high)
    odd_ref[...] = jnp.where(is_odd, high, low)

    nbrs = nbrs_ref[...]
    target = jnp.maximum(nbrs, 0)
    owner = target // leaf_count
    slot = target - owner * leaf_count
    owner_morton = owner // sib_count
    owner_sib = owner - owner_morton * sib_count
    step = owner_morton - morton
    below = jnp.maximum(morton - 1, 0) * sib_count
    band_start = jnp.zeros_like(slot)
    for other in range(sib_count):
        band_start = jnp.where(owner_sib == other, counts_ref[below + other] - BAND, band_start)
    below_at = BAND * jnp.bitwise_and(morton, 1)
    in_band = jnp.where(step < 0, slot - band_start + below_at, slot + BAND - below_at)
    box = box_ref[pl.ds(pl.multiple_of(morton * 8, 8), 8), :]
    shift_bits = 3 * (LMAX - levels_ref[...])
    anchor = jnp.left_shift(jnp.right_shift(keys_ref[...], shift_bits), shift_bits)
    span = jnp.left_shift(jnp.ones_like(shift_bits), LMAX - levels_ref[...]).astype(f32)
    finest = 1.0 / float(2**LMAX)
    places = []
    for dim, offset in enumerate((2, 1, 0)):
        cell = jnp.zeros_like(anchor)
        for bit in range(LMAX):
            picked = jnp.bitwise_and(jnp.right_shift(anchor, 3 * bit + offset), 1)
            cell = cell + jnp.left_shift(picked, bit)
        center = (cell.astype(f32) + 0.5 * span) * finest
        places.append((center - box[4 + dim : 5 + dim, :]) * box[7:8, :])
    places.append(0.5 * span * finest * box[7:8, :])
    places.append(jnp.zeros((4, leaf_count), f32))
    geom = jnp.concatenate(places, axis=0)
    for side in range(sib_count // 2):
        piece = jnp.bitwise_xor(owner_sib, jnp.bitwise_xor(sib, 2 * side))
        spot = jnp.where(step == 0, piece * leaf_count + slot, 2 * leaf_count + piece * (2 * BAND) + in_band)
        spot = jnp.where((nbrs >= 0) & (piece < 2), spot, -1)
        if side == 0:
            spots_ref[...] = jnp.concatenate([spot.astype(f32), jnp.zeros((2, leaf_count), f32), geom[:4], box[:4]], axis=0)
            continue
        whole = jnp.right_shift(spot, 4)
        parts = [whole.astype(f32), (spot - 16 * whole).astype(f32), geom[:4]]
        request_ref = request_refs[side - 1]
        request_ref[leaf_count:, :LANES] = jnp.concatenate(parts, axis=0).astype(bf16)
        request_ref[leaf_count:, LANES:] = jnp.zeros((16, FACES - LANES), bf16)


def gathered(asked, window_refs, start):
    leaf_count = asked[0].shape[1]
    rows = sum(ref.shape[0] for ref in window_refs)
    blank = jnp.full((LANES - 8 * len(asked), leaf_count), -1.0, f32)
    places = jnp.concatenate([spots[:8] for spots in asked] + [blank], axis=0).T.astype(jnp.int32)
    cols = lax.broadcasted_iota(jnp.int32, (leaf_count, rows), 1) + start
    upper = jnp.bitwise_and(lax.broadcasted_iota(jnp.int32, (leaf_count, FACES), 1), 64) > 0
    chosen = [[] for _ in asked]
    for dim in range(3):
        at = dim * FACES
        window = jnp.concatenate([ref[:, at : at + FACES] for ref in window_refs], axis=0)
        faces = [8 * who + face for who in range(len(asked)) for face in (2 * dim, 2 * dim + 1)]
        onehot = [jnp.where(cols == places[:, face : face + 1], 1.0, 0.0).astype(bf16) for face in faces]
        found = dot(jnp.concatenate(onehot, axis=0), window)
        for who in range(len(asked)):
            first, second = (found[(2 * who + side) * leaf_count : (2 * who + side + 1) * leaf_count] for side in (0, 1))
            chosen[who].append(jnp.where(upper, first, second).astype(bf16))
    return chosen


def requested(ref):
    leaf_count = ref.shape[0] - 16
    parts = ref[leaf_count:, :LANES].astype(f32)
    blank = jnp.zeros((2, leaf_count), f32)
    rows = [parts[:6] * 16.0 + parts[6:12], blank, parts[12:], jnp.zeros((4, leaf_count), f32)]
    return jnp.concatenate(rows, axis=0)


def by_comp(chosen):
    comps = [
        jnp.concatenate([block[:, comp * LANES : (comp + 1) * LANES] for block in chosen], axis=1) for comp in range(3)
    ]
    return jnp.concatenate(comps, axis=0)


def fill_tables(rows_ref, dx_ref, dyz_ref):
    row = lax.broadcasted_iota(jnp.int32, (64, NODES), 0)
    col = lax.broadcasted_iota(jnp.int32, (64, NODES), 1)
    same = row == jnp.bitwise_and(col, 63)
    for at in range(8):
        dx_ref[64 * at : 64 * at + 64, :] = jnp.where(same, rows_ref[at : at + 1, :], 0.0).astype(bf16)
    row = lax.broadcasted_iota(jnp.int32, (8, 256), 0)
    col = lax.broadcasted_iota(jnp.int32, (8, 256), 1)
    same = row == jnp.bitwise_and(col, 7)
    group = jnp.right_shift(col, 3)
    for pair in range(16):
        blocks = []
        for at in (2 * pair, 2 * pair + 1):
            here = same & (jnp.right_shift(group, 3) == at // 8)
            along_y = jnp.where(here, rows_ref[8 + at % 8 : 9 + at % 8, :256], 0.0)
            along_z = jnp.where(group == at, rows_ref[16:24, :256], 0.0)
            blocks.append(jnp.concatenate([along_y, along_z], axis=1))
        dyz_ref[16 * pair : 16 * pair + 16, :] = jnp.concatenate(blocks, axis=0).astype(bf16)


def operator_kernel(
    counts_ref, vel_ref, press_ref, visc_ref, rows_ref,
    part_ref, mass_ref, dx_ref, dyz_ref,
):
    sib_count = lax.axis_size("sib")
    own = lax.axis_index("morton") * sib_count + lax.axis_index("sib")
    leaf_count = mass_ref.shape[0]
    live = lax.broadcasted_iota(jnp.int32, (leaf_count, NODES), 0) < counts_ref[own]
    node = lax.broadcasted_iota(jnp.int32, (1, NODES), 1)
    touching = jnp.zeros((1, NODES), f32)
    for shift in (6, 3, 0):
        idx = jnp.bitwise_and(jnp.right_shift(node, shift), 7)
        touching = touching + jnp.where((idx == 0) | (idx == 7), 1.0, 0.0)
    fill_tables(rows_ref, dx_ref, dyz_ref)

    def rows(stack, at):
        return stack[at * leaf_count : (at + 1) * leaf_count]

    visc = visc_ref[...]
    fields = jnp.concatenate([vel_ref[0], vel_ref[1], vel_ref[2], press_ref[...]], axis=0)
    halves = [dot(fields[:, at : at + 256], dyz_ref[...]) for at in (0, 256)]
    grads = [
        dot(fields, dx_ref[...]),
        jnp.concatenate([half[:, :256] for half in halves], axis=1),
        jnp.concatenate([half[:, 256:] for half in halves], axis=1),
    ]
    mass = -(rows(grads[0], 0) + rows(grads[1], 1) + rows(grads[2], 2)) * mass_scale
    mass_ref[...] = jnp.where(live, mass, 0.0)
    stress = {}
    for first in range(3):
        for second in range(first, 3):
            value = (visc * (rows(grads[second], first) + rows(grads[first], second))).astype(bf16)
            stress[first, second] = stress[second, first] = value
    columns = [jnp.concatenate([stress[comp, dim] for comp in range(3)], axis=0) for dim in range(3)]
    rest = [
        dot(columns[1][:, at : at + 256], dyz_ref[:, :256]) + dot(columns[2][:, at : at + 256], dyz_ref[:, 256:])
        for at in (0, 256)
    ]
    div = dot(columns[0], dx_ref[...]) + jnp.concatenate(rest, axis=1)
    for comp in range(3):
        jump = touching * vel_ref[comp].astype(f32)
        part = (penalty * visc * jump - rows(div, comp) + rows(grads[comp], 3)) * out_scale
        part_ref[comp] = jnp.where(live, part, 0.0)


def group_kernel(spots_ref, *refs):
    sides = lax.axis_size("sib") // 2
    request_refs, window_refs, move_ref, out_refs = refs[: sides - 1], refs[sides - 1 : sides + 1], refs[sides + 1], refs[sides + 2 :]
    chosen = gathered([spots_ref[...]] + [requested(ref) for ref in request_refs], window_refs, 0)
    for blocks, out_ref in zip(chosen, out_refs):
        for dim, block in enumerate(blocks):
            out_ref[:, dim * FACES : (dim + 1) * FACES] = block
    box = spots_ref[12:, :]
    move = jnp.ones((256, 256), f32)
    for dim, stride in enumerate((36, 6, 1)):
        col = lax.broadcasted_iota(jnp.int32, (1, 256), 1) // stride % 6
        row = lax.broadcasted_iota(jnp.int32, (256, 1), 0) // stride % 6
        along, scale = box[dim : dim + 1, 3:4], box[3:4, 3:4]
        powers = [jnp.ones((1, 1), f32)]
        for _ in range(DEG):
            powers.append(powers[-1] * along)
        factor = jnp.zeros((256, 256), f32)
        below = jnp.ones((1, 1), f32)
        for low in range(DEG + 1):
            line = jnp.zeros((1, 256), f32)
            for high in range(low, DEG + 1):
                line = jnp.where(col == high, powers[high - low] * below * float(math.comb(high, low)), line)
            factor = jnp.where(row == low, line, factor)
            below = below * scale
        move = move * factor
    move_ref[...] = move


def shifted(tiles, geom):
    width = tiles[0].shape
    scale = jnp.broadcast_to(geom[3:4, :], width)
    level = lax.broadcasted_iota(jnp.int32, width, 0)
    depth = jnp.ones(width, f32)
    for power in range(1, DEG + 1):
        depth = depth * jnp.where(level >= power, scale, 1.0)
    scales = [depth]
    for _ in range(2 * DEG):
        scales.append(scales[-1] * scale)
    tiles = [tile * scales[at // 6 + at % 6] for at, tile in enumerate(tiles)]
    along = [jnp.broadcast_to(geom[dim : dim + 1, :], width) for dim in range(3)]
    for low in range(1, DEG + 1):
        for power in range(DEG, low - 1, -1):
            for other in range(6):
                at = power * 6 + other
                tiles[at] = tiles[at] + along[0] * tiles[at - 6]
            for other in range(6):
                at = other * 6 + power
                tiles[at] = tiles[at] + along[1] * tiles[at - 1]
    steps = [jnp.where(level >= low, along[2], 0.0) for low in range(1, DEG + 1)]
    for step in steps:
        tiles = [tile + step * pltpu.roll(tile, 1, 0) for tile in tiles]
    return tiles


def split(values, parts):
    pieces = []
    for _ in range(parts):
        pieces.append(values.astype(bf16))
        values = values - pieces[-1].astype(f32)
    return pieces


def lane_sums(raw_ref, geoms):
    leaf_count = geoms[0].shape[1]
    geom = jnp.concatenate([leaf for leaf in geoms for _ in range(3)], axis=1)
    tiles = shifted([raw_ref[8 * at : 8 * at + 8, :] for at in range(36)], geom)
    span = 3 * leaf_count
    tiles = [sum(tile[:, span * who : span * (who + 1)] for who in range(len(geoms))) for tile in tiles]
    group = lax.broadcasted_iota(jnp.int32, (span, LANES), 0) // leaf_count
    column = lax.broadcasted_iota(jnp.int32, (span, LANES), 1)
    gather = jnp.where((group == column) | (group + 3 == column), 1.0, 0.0).astype(bf16)
    return sum(dot(piece, gather) for piece in split(jnp.concatenate(tiles, axis=0), 3))


def own_kernel(part_ref, basis_ref, faces_ref, raw_ref):
    leaf_count = part_ref.shape[1]
    high, low = split(part_ref[...].reshape(3 * leaf_count, NODES), 2)
    raw = dot_nt(basis_ref[...], high)
    raw_ref[...] = raw[:ROWS] + raw[ROWS:] + dot_nt(basis_ref[:ROWS, :], low)


def moment_kernel(
    own_ref, face_basis_ref, compact_ref, spots_ref, weights_ref, *refs
):
    sides = lax.axis_size("sib") // 2
    window_refs, request_refs, group_refs = refs[:2], refs[2 : 1 + sides], refs[1 + sides : 1 + 2 * sides]
    near_ref, served_refs, sums_ref, raw_ref = refs[1 + 2 * sides], refs[2 + 2 * sides : -2], refs[-2], refs[-1]
    morton = lax.axis_index("morton")
    leaf_count = spots_ref.shape[1]
    asked = [spots_ref[...]] + [requested(ref) for ref in request_refs]
    chosen = gathered(asked, window_refs, 2 * leaf_count)
    values = []
    for blocks, group_ref, out_ref, ref in zip(
        chosen, group_refs, (near_ref, *served_refs), (weights_ref, *request_refs)
    ):
        for dim in range(3):
            lanes = slice(dim * FACES, (dim + 1) * FACES)
            blocks[dim] = blocks[dim] + group_ref[:, lanes]
            out_ref[:, lanes] = blocks[dim]
        weight = ref[:leaf_count].astype(f32) * (-penalty * out_scale)
        values.append(jnp.concatenate([weight] * 3, axis=0) * by_comp(blocks).astype(f32))
    raw = dot_nt(face_basis_ref[...], jnp.concatenate(values, axis=0).astype(bf16))
    span = 3 * leaf_count
    raw_ref[:, :span] = raw[:, :span] + own_ref[...]
    raw_ref[:, span:] = raw[:, span:]
    summed = lane_sums(raw_ref, [spots[8:] for spots in asked])
    box = spots_ref[12:, :]
    both = shifted([summed[8 * at : 8 * at + 8, :] for at in range(36)], box)
    flat = jnp.concatenate(both, axis=0).T
    sums = sum(dot(piece, compact_ref[...]) for piece in split(flat[:8], 3))
    blank = jnp.zeros((2, LANES), f32)
    to_box = jnp.concatenate([sums[:3, :LANES], sums[:3, LANES:], blank], axis=0)
    to_root = jnp.concatenate([sums[3:6, :LANES], sums[3:6, LANES:], blank], axis=0)
    sib_count = lax.axis_size("sib")
    for other in range(sums_ref.shape[0]):
        sums_ref[other] = jnp.where(morton == other // sib_count, to_box, to_root)


def last_kernel(part_ref, visc_ref, spread_ref, sums_ref, move_ref, near_ref, *refs):
    got_refs, (force_hbm, box_hbm, root_hbm, force_ref, box_ref, root_ref, sems) = refs[:-7], refs[-7:]
    faces = near_ref[...]
    for got_ref in got_refs:
        faces = faces + got_ref[...]
    weight = visc_ref[...] * (penalty * out_scale)
    stores = []
    for comp in range(3):
        lanes = [(dim * 3 + comp) * LANES for dim in range(3)]
        jump = dot(jnp.concatenate([faces[:, at : at + LANES] for at in lanes], axis=1), spread_ref[...])
        force_ref[comp] = part_ref[comp] - weight * jump
        stores.append(pltpu.make_async_copy(force_ref.at[comp], force_hbm.at[comp], sems.at[comp]))
        stores[-1].start()
    sib_count = lax.axis_size("sib")
    morton = lax.axis_index("morton")
    box = jnp.zeros(sums_ref.shape[1:], f32)
    root = jnp.zeros(sums_ref.shape[1:], f32)
    for group in range(sums_ref.shape[0] // sib_count):
        total = jnp.sum(sums_ref[group * sib_count : (group + 1) * sib_count], axis=0)
        box = box + jnp.where(morton == group, total, 0.0)
        root = root + jnp.where(morton == group, 0.0, total)
    box = jnp.concatenate([box[:3], box[3:6]], axis=1)
    root = jnp.concatenate([root[:3], root[3:6]], axis=1)
    box_rows = jnp.concatenate([box, jnp.zeros((5, 2 * LANES), f32)], axis=0)
    pieces = jnp.concatenate([piece.astype(f32) for piece in split(box_rows, 3)], axis=0).astype(bf16)
    moved = sum(dot(pieces, table) for table in split(move_ref[...], 2))
    root = root + (moved[:3] + moved[8:11] + moved[16:19])
    for comp in range(3):
        box_ref[comp] = box[comp : comp + 1, :MOMENTS]
        root_ref[comp] = root[comp : comp + 1, :MOMENTS]
    stores.append(pltpu.make_async_copy(box_ref, box_hbm, sems.at[3]))
    stores.append(pltpu.make_async_copy(root_ref, root_hbm, sems.at[4]))
    for store in stores[3:]:
        store.start()
    for store in stores:
        store.wait()


def call(kernel, shapes, flops, scalars, operands, scratch=(), place=pltpu.VMEM, outs=None, grant=32):
    specs = [pl.BlockSpec(memory_space=pltpu.SMEM)] * len(scalars)
    specs += [pl.BlockSpec(memory_space=place)] * len(operands)
    outs = outs or [pltpu.VMEM] * len(shapes)
    moved = sum(array.size * array.dtype.itemsize for array in operands)
    return pl.pallas_call(
        kernel,
        out_shape=[jax.ShapeDtypeStruct(shape, dtype) for shape, dtype in shapes],
        in_specs=specs,
        out_specs=[pl.BlockSpec(memory_space=out) for out in outs],
        scratch_shapes=list(scratch),
        compiler_params=pltpu.CompilerParams(vmem_limit_bytes=grant * 2**20),
        cost_estimate=pl.CostEstimate(flops=flops, bytes_accessed=moved, transcendentals=0),
    )(*scalars, *operands)


def on_device(velocity, pressure, viscosity, levels, morton_keys, counts, neighbors):
    leaf_count = velocity.shape[0]
    morton_count = lax.axis_size("morton")
    rows = jnp.asarray(derivative_rows().astype(np.float32))
    pick = jnp.asarray(face_table().astype(np.float32)).astype(bf16)
    spread = jnp.asarray(spread_table().astype(np.float32)).astype(bf16)
    basis = basis_tables()
    face_basis = (basis.astype(np.float32) @ spread_table().T.astype(np.float32)).astype(jnp.bfloat16)
    basis, face_basis = jnp.asarray(basis), jnp.asarray(face_basis[:ROWS])
    boxes = jnp.asarray(box_table(morton_count))
    vel = jnp.transpose(velocity, (1, 0, 2))
    nbrs = jnp.transpose(neighbors, (1, 0))

    width = 3 * FACES
    sib_count = lax.axis_size("sib")
    sides = sib_count // 2
    other_sides = [2 * side for side in range(1, sides)]
    faces, even, odd, spots, *requests = call(
        pack_kernel,
        [
            ((leaf_count, width), bf16),
            ((BAND, width), bf16),
            ((BAND, width), bf16),
            ((16, leaf_count), f32),
        ]
        + [((leaf_count + 16, FACES), bf16)] * (sides - 1),
        4 * 10**8,
        [counts],
        [vel, viscosity, nbrs, levels.reshape(1, -1), morton_keys.reshape(1, -1), boxes, pick],
        grant=60,
    )
    weights = requests[0]
    even, odd = pairs(even, 0), pairs(odd, 1)
    across = swap(faces, "sib", 1)
    across, requests, pressure = lax.optimization_barrier((across, requests, pressure))
    requests = [swap(block, "sib", apart) for block, apart in zip(requests, other_sides)]
    part, continuity = call(
        operator_kernel,
        [((3, leaf_count, NODES), f32), ((leaf_count, NODES), f32)],
        2 * 10**9,
        [counts],
        [vel, pressure, viscosity, rows],
        [pltpu.VMEM((NODES, NODES), bf16), pltpu.VMEM((256, NODES), bf16)],
    )
    (own_raw,) = call(
        own_kernel,
        [((ROWS, 3 * leaf_count), f32)],
        10**9,
        [],
        [part, basis, faces],
    )
    even, odd, own_raw, requests = lax.optimization_barrier((even, odd, own_raw, requests))
    bands = jnp.concatenate([odd, even], axis=0)
    move, *group = call(
        group_kernel,
        [((256, 256), f32)] + [((leaf_count, width), bf16)] * sides,
        10**9,
        [],
        [spots, *requests, faces, across],
    )
    near, *served, sums = call(
        moment_kernel,
        [((leaf_count, width), bf16)] * sides + [((morton_count * sib_count, 8, LANES), f32)],
        2 * 10**9,
        [],
        [
            own_raw, face_basis, jnp.asarray(compact_table()), spots, weights,
            bands, swap(bands, "sib", 1), *requests, *group,
        ],
        [pltpu.VMEM((ROWS, 3 * sides * leaf_count), f32)],
    )
    got = [swap(block, "sib", apart) for block, apart in zip(served, other_sides)]
    every = lax.all_to_all(sums, ("morton", "sib"), 0, 0, tiled=True)
    every, *got = lax.optimization_barrier((every, *got))
    force, box, root = call(
        last_kernel,
        [((3, leaf_count, NODES), f32), ((3, 1, MOMENTS), f32), ((3, 1, MOMENTS), f32)],
        2 * 10**8,
        [],
        [part, viscosity, spread, every, move, near, *got],
        [
            pltpu.VMEM((3, leaf_count, NODES), f32),
            pltpu.VMEM((3, 1, MOMENTS), f32),
            pltpu.VMEM((3, 1, MOMENTS), f32),
            pltpu.SemaphoreType.DMA((5,)),
        ],
        outs=[pltpu.HBM] * 3,
    )
    return (
        jnp.transpose(force, (1, 0, 2)),
        continuity,
        jnp.transpose(box, (1, 0, 2)),
        jnp.transpose(root, (1, 0, 2)),
    )


def solution(mesh):
    spread_all = ("morton", "sib")
    in_specs = (
        P(spread_all, None, None),
        P(spread_all, None),
        P(spread_all, None),
        P(spread_all),
        P(spread_all),
        P(),
        P(spread_all, None),
    )
    out_specs = (
        P(spread_all, None, None),
        P(spread_all, None),
        P("morton", None, None),
        P("morton", None, None),
    )
    return jax.shard_map(
        on_device, mesh=mesh, in_specs=in_specs, out_specs=out_specs, check_vma=False
    )
```

```python
import math

import jax
import jax.numpy as jnp
import numpy as np
from jax import lax
from jax.experimental import pallas as pl
from jax.experimental.pallas import tpu as pltpu
from jax.sharding import PartitionSpec as P

DEG = 5
LMAX = 7
MOMENTS = 216
BAND = 32
NODES = 512
FACES = 384
ROWS = 288
LANES = 128

penalty = 256.0
out_scale = 1.0 / 1024.0
mass_scale = 1.0 / 32.0
highest = lax.Precision.HIGHEST
f32 = jnp.float32
bf16 = jnp.bfloat16


def cheb_matrix():
    points = -np.cos(np.pi * np.arange(8) / 7.0)
    weights = np.array([(-1.0) ** node for node in range(8)])
    weights[0] *= 0.5
    weights[7] *= 0.5
    derivative = np.zeros((8, 8))
    for row in range(8):
        for col in range(8):
            if row != col:
                derivative[row, col] = weights[col] / weights[row] / (points[row] - points[col])
        derivative[row, row] = -np.sum(derivative[row])
    return points, derivative


def derivative_rows():
    _, derivative = cheb_matrix()
    lane = np.arange(NODES)
    return np.concatenate([derivative[lane // 64 % 8].T, derivative[lane // 8 % 8].T, derivative[lane % 8].T], axis=0)


def face_table():
    pick = np.zeros((NODES, FACES))
    for face in range(6):
        for first in range(8):
            for second in range(8):
                coords = [first, second]
                coords.insert(face // 2, 7 * (face % 2))
                node = 64 * coords[0] + 8 * coords[1] + coords[2]
                pick[node, face * 64 + first * 8 + second] = 1.0
    return pick


def spread_table():
    pick = face_table()
    order = np.concatenate([np.arange(64) + 64 * (face ^ 1) for face in range(6)])
    return pick[:, order].T


def basis_tables():
    points, _ = cheb_matrix()
    powers = np.stack([points**power for power in range(DEG + 1)])
    basis = np.zeros((6, 6, 8, 8, 8, 8))
    basis[:, :, :6] = np.einsum("xa,yb,zc->xyzabc", powers, powers, powers)
    basis = basis.reshape(ROWS, NODES).astype(np.float32)
    top = np.asarray(basis.astype(jnp.bfloat16))
    rest = np.asarray((basis - top.astype(np.float32)).astype(jnp.bfloat16))
    return np.concatenate([top, rest], axis=0)


def compact_table():
    table = np.zeros((ROWS, 256), jnp.bfloat16)
    for group in range(36):
        for power in range(6):
            table[group * 8 + power, group * 6 + power] = 1.0 / 512.0
    return table


def box_table(morton_count):
    bits = morton_count.bit_length() - 1
    key_bits = 3 * LMAX - bits
    table = np.zeros((morton_count, 8, LANES), np.float32)
    for morton in range(morton_count):
        base = morton << key_bits
        lows, sides = [], []
        for offset in (2, 1, 0):
            free = max(0, min(LMAX, (key_bits - offset + 2) // 3))
            cell = sum(((base >> (3 * bit + offset)) & 1) << bit for bit in range(LMAX))
            sides.append(2.0**free / 2.0**LMAX)
            lows.append(cell / 2.0**LMAX)
        scale = 0.5 * max(sides)
        for dim in range(3):
            center = lows[dim] + 0.5 * sides[dim]
            table[morton, dim, 3:6] = (center - 0.5) / 0.5
            table[morton, 4 + dim] = center
        table[morton, 3] = 1.0
        table[morton, 3, 3:6] = scale / 0.5
        table[morton, 7] = 1.0 / scale
    return table.reshape(morton_count * 8, LANES)


def swap(block, axis, apart):
    return lax.ppermute(block, axis, [(at, at ^ apart) for at in range(lax.axis_size(axis))])


def pairs(block, first):
    route = []
    for low in range(first, lax.axis_size("morton") - 1, 2):
        route += [(low, low + 1), (low + 1, low)]
    return lax.ppermute(block, "morton", route)


def dot(left, right):
    return jnp.dot(left, right, preferred_element_type=f32)


def dot_nt(left, right, precision=None):
    return lax.dot_general(
        left, right, (((1,), (1,)), ((), ())), preferred_element_type=f32, precision=precision
    )


def pack_kernel(
    counts_ref, vel_ref, visc_ref, nbrs_ref, levels_ref, keys_ref, box_ref, pick_ref,
    faces_ref, even_ref, odd_ref, spots_ref, *request_refs,
):
    sib_count = lax.axis_size("sib")
    morton = lax.axis_index("morton")
    sib = lax.axis_index("sib")
    own = morton * sib_count + sib
    leaf_count = faces_ref.shape[0]
    fields = jnp.concatenate([vel_ref[0], vel_ref[1], vel_ref[2], visc_ref[...].astype(bf16)], axis=0)
    picked = dot(fields, pick_ref[...])
    for dim in range(3):
        block = picked[3 * leaf_count :, dim * LANES : (dim + 1) * LANES]
        block = pltpu.roll(block, LANES // 2, 1).astype(bf16)
        for request_ref in request_refs:
            request_ref[:leaf_count, dim * LANES : (dim + 1) * LANES] = block
    picked = picked[: 3 * leaf_count].astype(bf16)
    for comp in range(3):
        for dim in range(3):
            lane = (dim * 3 + comp) * LANES
            rows = picked[comp * leaf_count : (comp + 1) * leaf_count]
            faces_ref[:, lane : lane + LANES] = rows[:, dim * LANES : (dim + 1) * LANES]
    first = counts_ref[own] - BAND
    row = lax.broadcasted_iota(jnp.int32, (BAND, leaf_count), 0)
    col = lax.broadcasted_iota(jnp.int32, (BAND, leaf_count), 1)
    last_rows = jnp.where(col == row + first, 1.0, 0.0).astype(bf16)
    high = dot(last_rows, faces_ref[...]).astype(bf16)
    low = faces_ref[:BAND, :]
    is_odd = jnp.bitwise_and(morton, 1) == 1
    even_ref[...] = jnp.where(is_odd, low, high)
    odd_ref[...] = jnp.where(is_odd, high, low)

    nbrs = nbrs_ref[...]
    target = jnp.maximum(nbrs, 0)
    owner = target // leaf_count
    slot = target - owner * leaf_count
    owner_morton = owner // sib_count
    owner_sib = owner - owner_morton * sib_count
    step = owner_morton - morton
    below = jnp.maximum(morton - 1, 0) * sib_count
    band_start = jnp.zeros_like(slot)
    for other in range(sib_count):
        band_start = jnp.where(owner_sib == other, counts_ref[below + other] - BAND, band_start)
    below_at = BAND * jnp.bitwise_and(morton, 1)
    in_band = jnp.where(step < 0, slot - band_start + below_at, slot + BAND - below_at)
    box = box_ref[pl.ds(pl.multiple_of(morton * 8, 8), 8), :]
    shift_bits = 3 * (LMAX - levels_ref[...])
    anchor = jnp.left_shift(jnp.right_shift(keys_ref[...], shift_bits), shift_bits)
    span = jnp.left_shift(jnp.ones_like(shift_bits), LMAX - levels_ref[...]).astype(f32)
    finest = 1.0 / float(2**LMAX)
    places = []
    for dim, offset in enumerate((2, 1, 0)):
        cell = jnp.zeros_like(anchor)
        for bit in range(LMAX):
            picked = jnp.bitwise_and(jnp.right_shift(anchor, 3 * bit + offset), 1)
            cell = cell + jnp.left_shift(picked, bit)
        center = (cell.astype(f32) + 0.5 * span) * finest
        places.append((center - box[4 + dim : 5 + dim, :]) * box[7:8, :])
    places.append(0.5 * span * finest * box[7:8, :])
    places.append(jnp.zeros((4, leaf_count), f32))
    geom = jnp.concatenate(places, axis=0)
    for side in range(sib_count // 2):
        piece = jnp.bitwise_xor(owner_sib, jnp.bitwise_xor(sib, 2 * side))
        spot = jnp.where(step == 0, piece * leaf_count + slot, 2 * leaf_count + piece * (2 * BAND) + in_band)
        spot = jnp.where((nbrs >= 0) & (piece < 2), spot, -1)
        if side == 0:
            spots_ref[...] = jnp.concatenate([spot.astype(f32), jnp.zeros((2, leaf_count), f32), geom[:4], box[:4]], axis=0)
            continue
        whole = jnp.right_shift(spot, 4)
        parts = [whole.astype(f32), (spot - 16 * whole).astype(f32), geom[:4]]
        request_ref = request_refs[side - 1]
        request_ref[leaf_count:, :LANES] = jnp.concatenate(parts, axis=0).astype(bf16)
        request_ref[leaf_count:, LANES:] = jnp.zeros((16, FACES - LANES), bf16)


def gathered(asked, window_refs, start):
    leaf_count = asked[0].shape[1]
    rows = sum(ref.shape[0] for ref in window_refs)
    blank = jnp.full((LANES - 8 * len(asked), leaf_count), -1.0, f32)
    places = jnp.concatenate([spots[:8] for spots in asked] + [blank], axis=0).T.astype(jnp.int32)
    cols = lax.broadcasted_iota(jnp.int32, (leaf_count, rows), 1) + start
    upper = jnp.bitwise_and(lax.broadcasted_iota(jnp.int32, (leaf_count, FACES), 1), 64) > 0
    chosen = [[] for _ in asked]
    for dim in range(3):
        at = dim * FACES
        window = jnp.concatenate([ref[:, at : at + FACES] for ref in window_refs], axis=0)
        faces = [8 * who + face for who in range(len(asked)) for face in (2 * dim, 2 * dim + 1)]
        onehot = [jnp.where(cols == places[:, face : face + 1], 1.0, 0.0).astype(bf16) for face in faces]
        found = dot(jnp.concatenate(onehot, axis=0), window)
        for who in range(len(asked)):
            first, second = (found[(2 * who + side) * leaf_count : (2 * who + side + 1) * leaf_count] for side in (0, 1))
            chosen[who].append(jnp.where(upper, first, second).astype(bf16))
    return chosen


def requested(ref):
    leaf_count = ref.shape[0] - 16
    parts = ref[leaf_count:, :LANES].astype(f32)
    blank = jnp.zeros((2, leaf_count), f32)
    rows = [parts[:6] * 16.0 + parts[6:12], blank, parts[12:], jnp.zeros((4, leaf_count), f32)]
    return jnp.concatenate(rows, axis=0)


def by_comp(chosen):
    comps = [
        jnp.concatenate([block[:, comp * LANES : (comp + 1) * LANES] for block in chosen], axis=1) for comp in range(3)
    ]
    return jnp.concatenate(comps, axis=0)


def fill_tables(rows_ref, dx_ref, dyz_ref):
    row = lax.broadcasted_iota(jnp.int32, (64, NODES), 0)
    col = lax.broadcasted_iota(jnp.int32, (64, NODES), 1)
    same = row == jnp.bitwise_and(col, 63)
    for at in range(8):
        dx_ref[64 * at : 64 * at + 64, :] = jnp.where(same, rows_ref[at : at + 1, :], 0.0).astype(bf16)
    row = lax.broadcasted_iota(jnp.int32, (8, 256), 0)
    col = lax.broadcasted_iota(jnp.int32, (8, 256), 1)
    same = row == jnp.bitwise_and(col, 7)
    group = jnp.right_shift(col, 3)
    for pair in range(16):
        blocks = []
        for at in (2 * pair, 2 * pair + 1):
            here = same & (jnp.right_shift(group, 3) == at // 8)
            along_y = jnp.where(here, rows_ref[8 + at % 8 : 9 + at % 8, :256], 0.0)
            along_z = jnp.where(group == at, rows_ref[16:24, :256], 0.0)
            blocks.append(jnp.concatenate([along_y, along_z], axis=1))
        dyz_ref[16 * pair : 16 * pair + 16, :] = jnp.concatenate(blocks, axis=0).astype(bf16)


def operator_kernel(
    counts_ref, vel_ref, press_ref, visc_ref, rows_ref,
    part_ref, mass_ref, dx_ref, dyz_ref,
):
    sib_count = lax.axis_size("sib")
    own = lax.axis_index("morton") * sib_count + lax.axis_index("sib")
    leaf_count = mass_ref.shape[0]
    live = lax.broadcasted_iota(jnp.int32, (leaf_count, NODES), 0) < counts_ref[own]
    node = lax.broadcasted_iota(jnp.int32, (1, NODES), 1)
    touching = jnp.zeros((1, NODES), f32)
    for shift in (6, 3, 0):
        idx = jnp.bitwise_and(jnp.right_shift(node, shift), 7)
        touching = touching + jnp.where((idx == 0) | (idx == 7), 1.0, 0.0)
    fill_tables(rows_ref, dx_ref, dyz_ref)

    def rows(stack, at):
        return stack[at * leaf_count : (at + 1) * leaf_count]

    visc = visc_ref[...]
    fields = jnp.concatenate([vel_ref[0], vel_ref[1], vel_ref[2], press_ref[...]], axis=0)
    halves = [dot(fields[:, at : at + 256], dyz_ref[...]) for at in (0, 256)]
    grads = [
        dot(fields, dx_ref[...]),
        jnp.concatenate([half[:, :256] for half in halves], axis=1),
        jnp.concatenate([half[:, 256:] for half in halves], axis=1),
    ]
    mass = -(rows(grads[0], 0) + rows(grads[1], 1) + rows(grads[2], 2)) * mass_scale
    mass_ref[...] = jnp.where(live, mass, 0.0)
    stress = {}
    for first in range(3):
        for second in range(first, 3):
            value = (visc * (rows(grads[second], first) + rows(grads[first], second))).astype(bf16)
            stress[first, second] = stress[second, first] = value
    columns = [jnp.concatenate([stress[comp, dim] for comp in range(3)], axis=0) for dim in range(3)]
    rest = [
        dot(columns[1][:, at : at + 256], dyz_ref[:, :256]) + dot(columns[2][:, at : at + 256], dyz_ref[:, 256:])
        for at in (0, 256)
    ]
    div = dot(columns[0], dx_ref[...]) + jnp.concatenate(rest, axis=1)
    for comp in range(3):
        jump = touching * vel_ref[comp].astype(f32)
        part = (penalty * visc * jump - rows(div, comp) + rows(grads[comp], 3)) * out_scale
        part_ref[comp] = jnp.where(live, part, 0.0)


def group_kernel(spots_ref, *refs):
    sides = lax.axis_size("sib") // 2
    request_refs, window_refs, move_ref, out_refs = refs[: sides - 1], refs[sides - 1 : sides + 1], refs[sides + 1], refs[sides + 2 :]
    chosen = gathered([spots_ref[...]] + [requested(ref) for ref in request_refs], window_refs, 0)
    for blocks, out_ref in zip(chosen, out_refs):
        for dim, block in enumerate(blocks):
            out_ref[:, dim * FACES : (dim + 1) * FACES] = block
    box = spots_ref[12:, :]
    move = jnp.ones((256, 256), f32)
    for dim, stride in enumerate((36, 6, 1)):
        col = lax.broadcasted_iota(jnp.int32, (1, 256), 1) // stride % 6
        row = lax.broadcasted_iota(jnp.int32, (256, 1), 0) // stride % 6
        along, scale = box[dim : dim + 1, 3:4], box[3:4, 3:4]
        powers = [jnp.ones((1, 1), f32)]
        for _ in range(DEG):
            powers.append(powers[-1] * along)
        factor = jnp.zeros((256, 256), f32)
        below = jnp.ones((1, 1), f32)
        for low in range(DEG + 1):
            line = jnp.zeros((1, 256), f32)
            for high in range(low, DEG + 1):
                line = jnp.where(col == high, powers[high - low] * below * float(math.comb(high, low)), line)
            factor = jnp.where(row == low, line, factor)
            below = below * scale
        move = move * factor
    move_ref[...] = move


def shifted(tiles, geom):
    width = tiles[0].shape
    scale = jnp.broadcast_to(geom[3:4, :], width)
    level = lax.broadcasted_iota(jnp.int32, width, 0)
    depth = jnp.ones(width, f32)
    for power in range(1, DEG + 1):
        depth = depth * jnp.where(level >= power, scale, 1.0)
    scales = [depth]
    for _ in range(2 * DEG):
        scales.append(scales[-1] * scale)
    tiles = [tile * scales[at // 6 + at % 6] for at, tile in enumerate(tiles)]
    along = [jnp.broadcast_to(geom[dim : dim + 1, :], width) for dim in range(3)]
    for low in range(1, DEG + 1):
        for power in range(DEG, low - 1, -1):
            for other in range(6):
                at = power * 6 + other
                tiles[at] = tiles[at] + along[0] * tiles[at - 6]
            for other in range(6):
                at = other * 6 + power
                tiles[at] = tiles[at] + along[1] * tiles[at - 1]
    steps = [jnp.where(level >= low, along[2], 0.0) for low in range(1, DEG + 1)]
    for step in steps:
        tiles = [tile + step * pltpu.roll(tile, 1, 0) for tile in tiles]
    return tiles


def split(values, parts):
    pieces = []
    for _ in range(parts):
        pieces.append(values.astype(bf16))
        values = values - pieces[-1].astype(f32)
    return pieces


def lane_sums(raw_ref, geoms):
    leaf_count = geoms[0].shape[1]
    geom = jnp.concatenate([leaf for leaf in geoms for _ in range(3)], axis=1)
    tiles = shifted([raw_ref[8 * at : 8 * at + 8, :] for at in range(36)], geom)
    span = 3 * leaf_count
    tiles = [sum(tile[:, span * who : span * (who + 1)] for who in range(len(geoms))) for tile in tiles]
    group = lax.broadcasted_iota(jnp.int32, (span, LANES), 0) // leaf_count
    column = lax.broadcasted_iota(jnp.int32, (span, LANES), 1)
    gather = jnp.where((group == column) | (group + 3 == column), 1.0, 0.0).astype(bf16)
    return sum(dot(piece, gather) for piece in split(jnp.concatenate(tiles, axis=0), 3))


def own_kernel(part_ref, basis_ref, faces_ref, spots_ref, raw_ref):
    leaf_count = part_ref.shape[1]
    high, low = split(part_ref[...].reshape(3 * leaf_count, NODES), 2)
    raw = dot_nt(basis_ref[...], high)
    raw_ref[...] = raw[:ROWS] + raw[ROWS:] + dot_nt(basis_ref[:ROWS, :], low)


def moment_kernel(
    own_ref, face_basis_ref, compact_ref, spots_ref, weights_ref, *refs
):
    sides = lax.axis_size("sib") // 2
    window_refs, request_refs, group_refs = refs[:2], refs[2 : 1 + sides], refs[1 + sides : 1 + 2 * sides]
    near_ref, served_refs, sums_ref, raw_ref = refs[1 + 2 * sides], refs[2 + 2 * sides : -2], refs[-2], refs[-1]
    morton = lax.axis_index("morton")
    leaf_count = spots_ref.shape[1]
    asked = [spots_ref[...]] + [requested(ref) for ref in request_refs]
    chosen = gathered(asked, window_refs, 2 * leaf_count)
    values = []
    for blocks, group_ref, out_ref, ref in zip(
        chosen, group_refs, (near_ref, *served_refs), (weights_ref, *request_refs)
    ):
        for dim in range(3):
            lanes = slice(dim * FACES, (dim + 1) * FACES)
            blocks[dim] = blocks[dim] + group_ref[:, lanes]
            out_ref[:, lanes] = blocks[dim]
        weight = ref[:leaf_count].astype(f32) * (-penalty * out_scale)
        values.append(jnp.concatenate([weight] * 3, axis=0) * by_comp(blocks).astype(f32))
    raw = dot_nt(face_basis_ref[...], jnp.concatenate(values, axis=0).astype(bf16))
    span = 3 * leaf_count
    raw_ref[:, :span] = raw[:, :span] + own_ref[...]
    raw_ref[:, span:] = raw[:, span:]
    summed = lane_sums(raw_ref, [spots[8:] for spots in asked])
    box = spots_ref[12:, :]
    both = shifted([summed[8 * at : 8 * at + 8, :] for at in range(36)], box)
    flat = jnp.concatenate(both, axis=0).T
    sums = sum(dot(piece, compact_ref[...]) for piece in split(flat[:8], 3))
    blank = jnp.zeros((2, LANES), f32)
    to_box = jnp.concatenate([sums[:3, :LANES], sums[:3, LANES:], blank], axis=0)
    to_root = jnp.concatenate([sums[3:6, :LANES], sums[3:6, LANES:], blank], axis=0)
    sib_count = lax.axis_size("sib")
    for other in range(sums_ref.shape[0]):
        sums_ref[other] = jnp.where(morton == other // sib_count, to_box, to_root)


def last_kernel(part_ref, visc_ref, spread_ref, sums_ref, move_ref, near_ref, *refs):
    got_refs, (force_hbm, box_hbm, root_hbm, force_ref, box_ref, root_ref, sems) = refs[:-7], refs[-7:]
    faces = near_ref[...]
    for got_ref in got_refs:
        faces = faces + got_ref[...]
    weight = visc_ref[...] * (penalty * out_scale)
    stores = []
    for comp in range(3):
        lanes = [(dim * 3 + comp) * LANES for dim in range(3)]
        jump = dot(jnp.concatenate([faces[:, at : at + LANES] for at in lanes], axis=1), spread_ref[...])
        force_ref[comp] = part_ref[comp] - weight * jump
        stores.append(pltpu.make_async_copy(force_ref.at[comp], force_hbm.at[comp], sems.at[comp]))
        stores[-1].start()
    sib_count = lax.axis_size("sib")
    morton = lax.axis_index("morton")
    box = jnp.zeros(sums_ref.shape[1:], f32)
    root = jnp.zeros(sums_ref.shape[1:], f32)
    for group in range(sums_ref.shape[0] // sib_count):
        total = jnp.sum(sums_ref[group * sib_count : (group + 1) * sib_count], axis=0)
        box = box + jnp.where(morton == group, total, 0.0)
        root = root + jnp.where(morton == group, 0.0, total)
    box = jnp.concatenate([box[:3], box[3:6]], axis=1)
    root = jnp.concatenate([root[:3], root[3:6]], axis=1)
    box_rows = jnp.concatenate([box, jnp.zeros((5, 2 * LANES), f32)], axis=0)
    pieces = jnp.concatenate([piece.astype(f32) for piece in split(box_rows, 3)], axis=0).astype(bf16)
    moved = sum(dot(pieces, table) for table in split(move_ref[...], 2))
    root = root + (moved[:3] + moved[8:11] + moved[16:19])
    for comp in range(3):
        box_ref[comp] = box[comp : comp + 1, :MOMENTS]
        root_ref[comp] = root[comp : comp + 1, :MOMENTS]
    stores.append(pltpu.make_async_copy(box_ref, box_hbm, sems.at[3]))
    stores.append(pltpu.make_async_copy(root_ref, root_hbm, sems.at[4]))
    for store in stores[3:]:
        store.start()
    for store in stores:
        store.wait()


def call(kernel, shapes, flops, scalars, operands, scratch=(), place=pltpu.VMEM, outs=None, grant=32):
    specs = [pl.BlockSpec(memory_space=pltpu.SMEM)] * len(scalars)
    specs += [pl.BlockSpec(memory_space=place)] * len(operands)
    outs = outs or [pltpu.VMEM] * len(shapes)
    moved = sum(array.size * array.dtype.itemsize for array in operands)
    return pl.pallas_call(
        kernel,
        out_shape=[jax.ShapeDtypeStruct(shape, dtype) for shape, dtype in shapes],
        in_specs=specs,
        out_specs=[pl.BlockSpec(memory_space=out) for out in outs],
        scratch_shapes=list(scratch),
        compiler_params=pltpu.CompilerParams(vmem_limit_bytes=grant * 2**20),
        cost_estimate=pl.CostEstimate(flops=flops, bytes_accessed=moved, transcendentals=0),
    )(*scalars, *operands)


def on_device(velocity, pressure, viscosity, levels, morton_keys, counts, neighbors):
    leaf_count = velocity.shape[0]
    morton_count = lax.axis_size("morton")
    rows = jnp.asarray(derivative_rows().astype(np.float32))
    pick = jnp.asarray(face_table().astype(np.float32)).astype(bf16)
    spread = jnp.asarray(spread_table().astype(np.float32)).astype(bf16)
    basis = basis_tables()
    face_basis = (basis.astype(np.float32) @ spread_table().T.astype(np.float32)).astype(jnp.bfloat16)
    basis, face_basis = jnp.asarray(basis), jnp.asarray(face_basis[:ROWS])
    boxes = jnp.asarray(box_table(morton_count))
    vel = jnp.transpose(velocity, (1, 0, 2))
    nbrs = jnp.transpose(neighbors, (1, 0))

    width = 3 * FACES
    sib_count = lax.axis_size("sib")
    sides = sib_count // 2
    other_sides = [2 * side for side in range(1, sides)]
    faces, even, odd, spots, *requests = call(
        pack_kernel,
        [
            ((leaf_count, width), bf16),
            ((BAND, width), bf16),
            ((BAND, width), bf16),
            ((16, leaf_count), f32),
        ]
        + [((leaf_count + 16, FACES), bf16)] * (sides - 1),
        4 * 10**8,
        [counts],
        [vel, viscosity, nbrs, levels.reshape(1, -1), morton_keys.reshape(1, -1), boxes, pick],
        grant=60,
    )
    weights = requests[0]
    odd = pairs(odd, 1)
    across = swap(faces, "sib", 1)
    across, requests, even, pressure = lax.optimization_barrier((across, requests, even, pressure))
    requests = [swap(block, "sib", apart) for block, apart in zip(requests, other_sides)]
    even = pairs(even, 0)
    part, continuity = call(
        operator_kernel,
        [((3, leaf_count, NODES), f32), ((leaf_count, NODES), f32)],
        2 * 10**9,
        [counts],
        [vel, pressure, viscosity, rows],
        [pltpu.VMEM((NODES, NODES), bf16), pltpu.VMEM((256, NODES), bf16)],
    )
    (own_raw,) = call(
        own_kernel,
        [((ROWS, 3 * leaf_count), f32)],
        10**9,
        [],
        [part, basis, faces, spots],
    )
    odd, even, own_raw, requests = lax.optimization_barrier((odd, even, own_raw, requests))
    bands = jnp.concatenate([odd, even], axis=0)
    move, *group = call(
        group_kernel,
        [((256, 256), f32)] + [((leaf_count, width), bf16)] * sides,
        10**9,
        [],
        [spots, *requests, faces, across],
    )
    near, *served, sums = call(
        moment_kernel,
        [((leaf_count, width), bf16)] * sides + [((morton_count * sib_count, 8, LANES), f32)],
        2 * 10**9,
        [],
        [
            own_raw, face_basis, jnp.asarray(compact_table()), spots, weights,
            bands, swap(bands, "sib", 1), *requests, *group,
        ],
        [pltpu.VMEM((ROWS, 3 * sides * leaf_count), f32)],
    )
    got = [swap(block, "sib", apart) for block, apart in zip(served, other_sides)]
    every = lax.all_to_all(sums, ("morton", "sib"), 0, 0, tiled=True)
    every, *got = lax.optimization_barrier((every, *got))
    force, box, root = call(
        last_kernel,
        [((3, leaf_count, NODES), f32), ((3, 1, MOMENTS), f32), ((3, 1, MOMENTS), f32)],
        2 * 10**8,
        [],
        [part, viscosity, spread, every, move, near, *got],
        [
            pltpu.VMEM((3, leaf_count, NODES), f32),
            pltpu.VMEM((3, 1, MOMENTS), f32),
            pltpu.VMEM((3, 1, MOMENTS), f32),
            pltpu.SemaphoreType.DMA((5,)),
        ],
        outs=[pltpu.HBM] * 3,
    )
    return (
        jnp.transpose(force, (1, 0, 2)),
        continuity,
        jnp.transpose(box, (1, 0, 2)),
        jnp.transpose(root, (1, 0, 2)),
    )


def solution(mesh):
    spread_all = ("morton", "sib")
    in_specs = (
        P(spread_all, None, None),
        P(spread_all, None),
        P(spread_all, None),
        P(spread_all),
        P(spread_all),
        P(),
        P(spread_all, None),
    )
    out_specs = (
        P(spread_all, None, None),
        P(spread_all, None),
        P("morton", None, None),
        P("morton", None, None),
    )
    return jax.shard_map(
        on_device, mesh=mesh, in_specs=in_specs, out_specs=out_specs, check_vma=False
    )
```

```python
import math

import jax
import jax.numpy as jnp
import numpy as np
from jax import lax
from jax.experimental import pallas as pl
from jax.experimental.pallas import tpu as pltpu
from jax.sharding import PartitionSpec as P

DEG = 5
LMAX = 7
MOMENTS = 216
BAND = 32
NODES = 512
FACES = 384
ROWS = 288
LANES = 128

penalty = 256.0
out_scale = 1.0 / 1024.0
mass_scale = 1.0 / 32.0
highest = lax.Precision.HIGHEST
f32 = jnp.float32
bf16 = jnp.bfloat16


def cheb_matrix():
    points = -np.cos(np.pi * np.arange(8) / 7.0)
    weights = np.array([(-1.0) ** node for node in range(8)])
    weights[0] *= 0.5
    weights[7] *= 0.5
    derivative = np.zeros((8, 8))
    for row in range(8):
        for col in range(8):
            if row != col:
                derivative[row, col] = weights[col] / weights[row] / (points[row] - points[col])
        derivative[row, row] = -np.sum(derivative[row])
    return points, derivative


def derivative_rows():
    _, derivative = cheb_matrix()
    lane = np.arange(NODES)
    return np.concatenate([derivative[lane // 64 % 8].T, derivative[lane // 8 % 8].T, derivative[lane % 8].T], axis=0)


def face_table():
    pick = np.zeros((NODES, FACES))
    for face in range(6):
        for first in range(8):
            for second in range(8):
                coords = [first, second]
                coords.insert(face // 2, 7 * (face % 2))
                node = 64 * coords[0] + 8 * coords[1] + coords[2]
                pick[node, face * 64 + first * 8 + second] = 1.0
    return pick


def spread_table():
    pick = face_table()
    order = np.concatenate([np.arange(64) + 64 * (face ^ 1) for face in range(6)])
    return pick[:, order].T


def basis_tables():
    points, _ = cheb_matrix()
    powers = np.stack([points**power for power in range(DEG + 1)])
    basis = np.zeros((6, 6, 8, 8, 8, 8))
    basis[:, :, :6] = np.einsum("xa,yb,zc->xyzabc", powers, powers, powers)
    basis = basis.reshape(ROWS, NODES).astype(np.float32)
    top = np.asarray(basis.astype(jnp.bfloat16))
    rest = np.asarray((basis - top.astype(np.float32)).astype(jnp.bfloat16))
    return np.concatenate([top, rest], axis=0)


def compact_table():
    table = np.zeros((ROWS, 256), jnp.bfloat16)
    for group in range(36):
        for power in range(6):
            table[group * 8 + power, group * 6 + power] = 1.0 / 512.0
    return table


def box_table(morton_count):
    bits = morton_count.bit_length() - 1
    key_bits = 3 * LMAX - bits
    table = np.zeros((morton_count, 8, LANES), np.float32)
    for morton in range(morton_count):
        base = morton << key_bits
        lows, sides = [], []
        for offset in (2, 1, 0):
            free = max(0, min(LMAX, (key_bits - offset + 2) // 3))
            cell = sum(((base >> (3 * bit + offset)) & 1) << bit for bit in range(LMAX))
            sides.append(2.0**free / 2.0**LMAX)
            lows.append(cell / 2.0**LMAX)
        scale = 0.5 * max(sides)
        for dim in range(3):
            center = lows[dim] + 0.5 * sides[dim]
            table[morton, dim, 3:6] = (center - 0.5) / 0.5
            table[morton, 4 + dim] = center
        table[morton, 3] = 1.0
        table[morton, 3, 3:6] = scale / 0.5
        table[morton, 7] = 1.0 / scale
    return table.reshape(morton_count * 8, LANES)


def swap(block, axis, apart):
    return lax.ppermute(block, axis, [(at, at ^ apart) for at in range(lax.axis_size(axis))])


def pairs(block, first):
    route = []
    for low in range(first, lax.axis_size("morton") - 1, 2):
        route += [(low, low + 1), (low + 1, low)]
    return lax.ppermute(block, "morton", route)


def dot(left, right):
    return jnp.dot(left, right, preferred_element_type=f32)


def dot_nt(left, right, precision=None):
    return lax.dot_general(
        left, right, (((1,), (1,)), ((), ())), preferred_element_type=f32, precision=precision
    )


def pack_kernel(
    counts_ref, vel_hbm, visc_hbm, nbrs_hbm, levels_hbm, keys_hbm, box_hbm, pick_hbm, *refs
):
    sides = lax.axis_size("sib") // 2
    out_hbms, refs = refs[: 3 + sides], refs[3 + sides :]
    faces_ref, even_ref, odd_ref, spots_ref, *request_refs = refs[: 3 + sides]
    vel_ref, visc_ref, nbrs_ref, levels_ref, keys_ref, box_ref, pick_ref, in_sems, out_sems = refs[3 + sides :]
    sib_count = lax.axis_size("sib")
    morton = lax.axis_index("morton")
    sib = lax.axis_index("sib")
    own = morton * sib_count + sib
    leaf_count = faces_ref.shape[0]
    box_rows = box_hbm.at[pl.ds(pl.multiple_of(morton * 8, 8), 8), :]
    loads = [
        pltpu.make_async_copy(source, target, in_sems.at[at])
        for at, (source, target) in enumerate(
            [
                (vel_hbm, vel_ref), (pick_hbm, pick_ref), (visc_hbm, visc_ref), (nbrs_hbm, nbrs_ref),
                (levels_hbm, levels_ref), (keys_hbm, keys_ref), (box_rows, box_ref),
            ]
        )
    ]
    stores = [
        pltpu.make_async_copy(source, target, out_sems.at[at])
        for at, (source, target) in enumerate(zip((faces_ref, even_ref, odd_ref, spots_ref, *request_refs), out_hbms))
    ]
    for load in loads:
        load.start()
    for load in loads[3:]:
        load.wait()

    nbrs = nbrs_ref[...]
    target = jnp.maximum(nbrs, 0)
    owner = target // leaf_count
    slot = target - owner * leaf_count
    owner_morton = owner // sib_count
    owner_sib = owner - owner_morton * sib_count
    step = owner_morton - morton
    below = jnp.maximum(morton - 1, 0) * sib_count
    band_start = jnp.zeros_like(slot)
    for other in range(sib_count):
        band_start = jnp.where(owner_sib == other, counts_ref[below + other] - BAND, band_start)
    below_at = BAND * jnp.bitwise_and(morton, 1)
    in_band = jnp.where(step < 0, slot - band_start + below_at, slot + BAND - below_at)
    box = box_ref[...]
    shift_bits = 3 * (LMAX - levels_ref[...])
    anchor = jnp.left_shift(jnp.right_shift(keys_ref[...], shift_bits), shift_bits)
    span = jnp.left_shift(jnp.ones_like(shift_bits), LMAX - levels_ref[...]).astype(f32)
    finest = 1.0 / float(2**LMAX)
    places = []
    for dim, offset in enumerate((2, 1, 0)):
        cell = jnp.zeros_like(anchor)
        for bit in range(LMAX):
            picked = jnp.bitwise_and(jnp.right_shift(anchor, 3 * bit + offset), 1)
            cell = cell + jnp.left_shift(picked, bit)
        center = (cell.astype(f32) + 0.5 * span) * finest
        places.append((center - box[4 + dim : 5 + dim, :]) * box[7:8, :])
    places.append(0.5 * span * finest * box[7:8, :])
    places.append(jnp.zeros((4, leaf_count), f32))
    geom = jnp.concatenate(places, axis=0)
    for side in range(sib_count // 2):
        piece = jnp.bitwise_xor(owner_sib, jnp.bitwise_xor(sib, 2 * side))
        spot = jnp.where(step == 0, piece * leaf_count + slot, 2 * leaf_count + piece * (2 * BAND) + in_band)
        spot = jnp.where((nbrs >= 0) & (piece < 2), spot, -1)
        if side == 0:
            spots_ref[...] = jnp.concatenate([spot.astype(f32), jnp.zeros((2, leaf_count), f32), geom[:4], box[:4]], axis=0)
            continue
        whole = jnp.right_shift(spot, 4)
        parts = [whole.astype(f32), (spot - 16 * whole).astype(f32), geom[:4]]
        request_ref = request_refs[side - 1]
        request_ref[leaf_count:, :LANES] = jnp.concatenate(parts, axis=0).astype(bf16)
        request_ref[leaf_count:, LANES:] = jnp.zeros((16, FACES - LANES), bf16)
    stores[3].start()

    for load in loads[:3]:
        load.wait()
    fields = jnp.concatenate([vel_ref[0], vel_ref[1], vel_ref[2], visc_ref[...].astype(bf16)], axis=0)
    picked = dot(fields, pick_ref[...])
    for comp in range(3):
        rows = picked[comp * leaf_count : (comp + 1) * leaf_count].astype(bf16)
        for dim in range(3):
            lane = (dim * 3 + comp) * LANES
            faces_ref[:, lane : lane + LANES] = rows[:, dim * LANES : (dim + 1) * LANES]
    stores[0].start()
    first = counts_ref[own] - BAND
    row = lax.broadcasted_iota(jnp.int32, (BAND, leaf_count), 0)
    col = lax.broadcasted_iota(jnp.int32, (BAND, leaf_count), 1)
    last_rows = jnp.where(col == row + first, 1.0, 0.0).astype(bf16)
    high = dot(last_rows, faces_ref[...]).astype(bf16)
    low = faces_ref[:BAND, :]
    is_odd = jnp.bitwise_and(morton, 1) == 1
    even_ref[...] = jnp.where(is_odd, low, high)
    odd_ref[...] = jnp.where(is_odd, high, low)
    for store in stores[1:3]:
        store.start()
    for dim in range(3):
        block = picked[3 * leaf_count :, dim * LANES : (dim + 1) * LANES]
        block = pltpu.roll(block, LANES // 2, 1).astype(bf16)
        for request_ref in request_refs:
            request_ref[:leaf_count, dim * LANES : (dim + 1) * LANES] = block
    for store in stores[4:]:
        store.start()
    for store in stores:
        store.wait()


def gathered(asked, window_refs, start):
    leaf_count = asked[0].shape[1]
    rows = sum(ref.shape[0] for ref in window_refs)
    blank = jnp.full((LANES - 8 * len(asked), leaf_count), -1.0, f32)
    places = jnp.concatenate([spots[:8] for spots in asked] + [blank], axis=0).T.astype(jnp.int32)
    cols = lax.broadcasted_iota(jnp.int32, (leaf_count, rows), 1) + start
    upper = jnp.bitwise_and(lax.broadcasted_iota(jnp.int32, (leaf_count, FACES), 1), 64) > 0
    chosen = [[] for _ in asked]
    for dim in range(3):
        at = dim * FACES
        window = jnp.concatenate([ref[:, at : at + FACES] for ref in window_refs], axis=0)
        faces = [8 * who + face for who in range(len(asked)) for face in (2 * dim, 2 * dim + 1)]
        onehot = [jnp.where(cols == places[:, face : face + 1], 1.0, 0.0).astype(bf16) for face in faces]
        found = dot(jnp.concatenate(onehot, axis=0), window)
        for who in range(len(asked)):
            first, second = (found[(2 * who + side) * leaf_count : (2 * who + side + 1) * leaf_count] for side in (0, 1))
            chosen[who].append(jnp.where(upper, first, second).astype(bf16))
    return chosen


def requested(ref):
    leaf_count = ref.shape[0] - 16
    parts = ref[leaf_count:, :LANES].astype(f32)
    blank = jnp.zeros((2, leaf_count), f32)
    rows = [parts[:6] * 16.0 + parts[6:12], blank, parts[12:], jnp.zeros((4, leaf_count), f32)]
    return jnp.concatenate(rows, axis=0)


def by_comp(chosen):
    comps = [
        jnp.concatenate([block[:, comp * LANES : (comp + 1) * LANES] for block in chosen], axis=1) for comp in range(3)
    ]
    return jnp.concatenate(comps, axis=0)


def fill_tables(rows_ref, dx_ref, dyz_ref):
    row = lax.broadcasted_iota(jnp.int32, (64, NODES), 0)
    col = lax.broadcasted_iota(jnp.int32, (64, NODES), 1)
    same = row == jnp.bitwise_and(col, 63)
    for at in range(8):
        dx_ref[64 * at : 64 * at + 64, :] = jnp.where(same, rows_ref[at : at + 1, :], 0.0).astype(bf16)
    row = lax.broadcasted_iota(jnp.int32, (8, 256), 0)
    col = lax.broadcasted_iota(jnp.int32, (8, 256), 1)
    same = row == jnp.bitwise_and(col, 7)
    group = jnp.right_shift(col, 3)
    for pair in range(16):
        blocks = []
        for at in (2 * pair, 2 * pair + 1):
            here = same & (jnp.right_shift(group, 3) == at // 8)
            along_y = jnp.where(here, rows_ref[8 + at % 8 : 9 + at % 8, :256], 0.0)
            along_z = jnp.where(group == at, rows_ref[16:24, :256], 0.0)
            blocks.append(jnp.concatenate([along_y, along_z], axis=1))
        dyz_ref[16 * pair : 16 * pair + 16, :] = jnp.concatenate(blocks, axis=0).astype(bf16)


def operator_kernel(
    counts_ref, vel_ref, press_ref, visc_ref, rows_ref,
    part_ref, mass_ref, dx_ref, dyz_ref,
):
    sib_count = lax.axis_size("sib")
    own = lax.axis_index("morton") * sib_count + lax.axis_index("sib")
    leaf_count = mass_ref.shape[0]
    live = lax.broadcasted_iota(jnp.int32, (leaf_count, NODES), 0) < counts_ref[own]
    node = lax.broadcasted_iota(jnp.int32, (1, NODES), 1)
    touching = jnp.zeros((1, NODES), f32)
    for shift in (6, 3, 0):
        idx = jnp.bitwise_and(jnp.right_shift(node, shift), 7)
        touching = touching + jnp.where((idx == 0) | (idx == 7), 1.0, 0.0)
    fill_tables(rows_ref, dx_ref, dyz_ref)

    def rows(stack, at):
        return stack[at * leaf_count : (at + 1) * leaf_count]

    visc = visc_ref[...]
    fields = jnp.concatenate([vel_ref[0], vel_ref[1], vel_ref[2], press_ref[...]], axis=0)
    halves = [dot(fields[:, at : at + 256], dyz_ref[...]) for at in (0, 256)]
    grads = [
        dot(fields, dx_ref[...]),
        jnp.concatenate([half[:, :256] for half in halves], axis=1),
        jnp.concatenate([half[:, 256:] for half in halves], axis=1),
    ]
    mass = -(rows(grads[0], 0) + rows(grads[1], 1) + rows(grads[2], 2)) * mass_scale
    mass_ref[...] = jnp.where(live, mass, 0.0)
    stress = {}
    for first in range(3):
        for second in range(first, 3):
            value = (visc * (rows(grads[second], first) + rows(grads[first], second))).astype(bf16)
            stress[first, second] = stress[second, first] = value
    columns = [jnp.concatenate([stress[comp, dim] for comp in range(3)], axis=0) for dim in range(3)]
    rest = [
        dot(columns[1][:, at : at + 256], dyz_ref[:, :256]) + dot(columns[2][:, at : at + 256], dyz_ref[:, 256:])
        for at in (0, 256)
    ]
    div = dot(columns[0], dx_ref[...]) + jnp.concatenate(rest, axis=1)
    for comp in range(3):
        jump = touching * vel_ref[comp].astype(f32)
        part = (penalty * visc * jump - rows(div, comp) + rows(grads[comp], 3)) * out_scale
        part_ref[comp] = jnp.where(live, part, 0.0)


def group_kernel(spots_ref, *refs):
    sides = lax.axis_size("sib") // 2
    request_refs, window_refs, move_ref, out_refs = refs[: sides - 1], refs[sides - 1 : sides + 1], refs[sides + 1], refs[sides + 2 :]
    chosen = gathered([spots_ref[...]] + [requested(ref) for ref in request_refs], window_refs, 0)
    for blocks, out_ref in zip(chosen, out_refs):
        for dim, block in enumerate(blocks):
            out_ref[:, dim * FACES : (dim + 1) * FACES] = block
    box = spots_ref[12:, :]
    move = jnp.ones((256, 256), f32)
    for dim, stride in enumerate((36, 6, 1)):
        col = lax.broadcasted_iota(jnp.int32, (1, 256), 1) // stride % 6
        row = lax.broadcasted_iota(jnp.int32, (256, 1), 0) // stride % 6
        along, scale = box[dim : dim + 1, 3:4], box[3:4, 3:4]
        powers = [jnp.ones((1, 1), f32)]
        for _ in range(DEG):
            powers.append(powers[-1] * along)
        factor = jnp.zeros((256, 256), f32)
        below = jnp.ones((1, 1), f32)
        for low in range(DEG + 1):
            line = jnp.zeros((1, 256), f32)
            for high in range(low, DEG + 1):
                line = jnp.where(col == high, powers[high - low] * below * float(math.comb(high, low)), line)
            factor = jnp.where(row == low, line, factor)
            below = below * scale
        move = move * factor
    move_ref[...] = move


def shifted(tiles, geom):
    width = tiles[0].shape
    scale = jnp.broadcast_to(geom[3:4, :], width)
    level = lax.broadcasted_iota(jnp.int32, width, 0)
    depth = jnp.ones(width, f32)
    for power in range(1, DEG + 1):
        depth = depth * jnp.where(level >= power, scale, 1.0)
    scales = [depth]
    for _ in range(2 * DEG):
        scales.append(scales[-1] * scale)
    tiles = [tile * scales[at // 6 + at % 6] for at, tile in enumerate(tiles)]
    along = [jnp.broadcast_to(geom[dim : dim + 1, :], width) for dim in range(3)]
    for low in range(1, DEG + 1):
        for power in range(DEG, low - 1, -1):
            for other in range(6):
                at = power * 6 + other
                tiles[at] = tiles[at] + along[0] * tiles[at - 6]
            for other in range(6):
                at = other * 6 + power
                tiles[at] = tiles[at] + along[1] * tiles[at - 1]
    steps = [jnp.where(level >= low, along[2], 0.0) for low in range(1, DEG + 1)]
    for step in steps:
        tiles = [tile + step * pltpu.roll(tile, 1, 0) for tile in tiles]
    return tiles


def split(values, parts):
    pieces = []
    for _ in range(parts):
        pieces.append(values.astype(bf16))
        values = values - pieces[-1].astype(f32)
    return pieces


def lane_sums(raw_ref, geoms):
    leaf_count = geoms[0].shape[1]
    geom = jnp.concatenate([leaf for leaf in geoms for _ in range(3)], axis=1)
    tiles = shifted([raw_ref[8 * at : 8 * at + 8, :] for at in range(36)], geom)
    span = 3 * leaf_count
    tiles = [sum(tile[:, span * who : span * (who + 1)] for who in range(len(geoms))) for tile in tiles]
    group = lax.broadcasted_iota(jnp.int32, (span, LANES), 0) // leaf_count
    column = lax.broadcasted_iota(jnp.int32, (span, LANES), 1)
    gather = jnp.where((group == column) | (group + 3 == column), 1.0, 0.0).astype(bf16)
    return sum(dot(piece, gather) for piece in split(jnp.concatenate(tiles, axis=0), 3))


def own_kernel(part_ref, basis_ref, faces_ref, spots_ref, raw_ref):
    leaf_count = part_ref.shape[1]
    high, low = split(part_ref[...].reshape(3 * leaf_count, NODES), 2)
    raw = dot_nt(basis_ref[...], high)
    raw_ref[...] = raw[:ROWS] + raw[ROWS:] + dot_nt(basis_ref[:ROWS, :], low)


def moment_kernel(
    own_ref, face_basis_ref, compact_ref, spots_ref, weights_ref, *refs
):
    sides = lax.axis_size("sib") // 2
    window_refs, request_refs, group_refs = refs[:2], refs[2 : 1 + sides], refs[1 + sides : 1 + 2 * sides]
    near_ref, served_refs, sums_ref, raw_ref = refs[1 + 2 * sides], refs[2 + 2 * sides : -2], refs[-2], refs[-1]
    morton = lax.axis_index("morton")
    leaf_count = spots_ref.shape[1]
    asked = [spots_ref[...]] + [requested(ref) for ref in request_refs]
    chosen = gathered(asked, window_refs, 2 * leaf_count)
    values = []
    for blocks, group_ref, out_ref, ref in zip(
        chosen, group_refs, (near_ref, *served_refs), (weights_ref, *request_refs)
    ):
        for dim in range(3):
            lanes = slice(dim * FACES, (dim + 1) * FACES)
            blocks[dim] = blocks[dim] + group_ref[:, lanes]
            out_ref[:, lanes] = blocks[dim]
        weight = ref[:leaf_count].astype(f32) * (-penalty * out_scale)
        values.append(jnp.concatenate([weight] * 3, axis=0) * by_comp(blocks).astype(f32))
    raw = dot_nt(face_basis_ref[...], jnp.concatenate(values, axis=0).astype(bf16))
    span = 3 * leaf_count
    raw_ref[:, :span] = raw[:, :span] + own_ref[...]
    raw_ref[:, span:] = raw[:, span:]
    summed = lane_sums(raw_ref, [spots[8:] for spots in asked])
    box = spots_ref[12:, :]
    both = shifted([summed[8 * at : 8 * at + 8, :] for at in range(36)], box)
    flat = jnp.concatenate(both, axis=0).T
    sums = sum(dot(piece, compact_ref[...]) for piece in split(flat[:8], 3))
    blank = jnp.zeros((2, LANES), f32)
    to_box = jnp.concatenate([sums[:3, :LANES], sums[:3, LANES:], blank], axis=0)
    to_root = jnp.concatenate([sums[3:6, :LANES], sums[3:6, LANES:], blank], axis=0)
    sib_count = lax.axis_size("sib")
    for other in range(sums_ref.shape[0]):
        sums_ref[other] = jnp.where(morton == other // sib_count, to_box, to_root)


def last_kernel(part_ref, visc_ref, spread_ref, sums_ref, move_ref, near_ref, *refs):
    got_refs, (force_hbm, box_hbm, root_hbm, force_ref, box_ref, root_ref, sems) = refs[:-7], refs[-7:]
    faces = near_ref[...]
    for got_ref in got_refs:
        faces = faces + got_ref[...]
    weight = visc_ref[...] * (penalty * out_scale)
    stores = []
    for comp in range(3):
        lanes = [(dim * 3 + comp) * LANES for dim in range(3)]
        jump = dot(jnp.concatenate([faces[:, at : at + LANES] for at in lanes], axis=1), spread_ref[...])
        force_ref[comp] = part_ref[comp] - weight * jump
        stores.append(pltpu.make_async_copy(force_ref.at[comp], force_hbm.at[comp], sems.at[comp]))
        stores[-1].start()
    sib_count = lax.axis_size("sib")
    morton = lax.axis_index("morton")
    box = jnp.zeros(sums_ref.shape[1:], f32)
    root = jnp.zeros(sums_ref.shape[1:], f32)
    for group in range(sums_ref.shape[0] // sib_count):
        total = jnp.sum(sums_ref[group * sib_count : (group + 1) * sib_count], axis=0)
        box = box + jnp.where(morton == group, total, 0.0)
        root = root + jnp.where(morton == group, 0.0, total)
    box = jnp.concatenate([box[:3], box[3:6]], axis=1)
    root = jnp.concatenate([root[:3], root[3:6]], axis=1)
    box_rows = jnp.concatenate([box, jnp.zeros((5, 2 * LANES), f32)], axis=0)
    pieces = jnp.concatenate([piece.astype(f32) for piece in split(box_rows, 3)], axis=0).astype(bf16)
    moved = sum(dot(pieces, table) for table in split(move_ref[...], 2))
    root = root + (moved[:3] + moved[8:11] + moved[16:19])
    for comp in range(3):
        box_ref[comp] = box[comp : comp + 1, :MOMENTS]
        root_ref[comp] = root[comp : comp + 1, :MOMENTS]
    stores.append(pltpu.make_async_copy(box_ref, box_hbm, sems.at[3]))
    stores.append(pltpu.make_async_copy(root_ref, root_hbm, sems.at[4]))
    for store in stores[3:]:
        store.start()
    for store in stores:
        store.wait()


def call(kernel, shapes, flops, scalars, operands, scratch=(), place=pltpu.VMEM, outs=None, grant=32):
    specs = [pl.BlockSpec(memory_space=pltpu.SMEM)] * len(scalars)
    specs += [pl.BlockSpec(memory_space=place)] * len(operands)
    outs = outs or [pltpu.VMEM] * len(shapes)
    moved = sum(array.size * array.dtype.itemsize for array in operands)
    return pl.pallas_call(
        kernel,
        out_shape=[jax.ShapeDtypeStruct(shape, dtype) for shape, dtype in shapes],
        in_specs=specs,
        out_specs=[pl.BlockSpec(memory_space=out) for out in outs],
        scratch_shapes=list(scratch),
        compiler_params=pltpu.CompilerParams(vmem_limit_bytes=grant * 2**20),
        cost_estimate=pl.CostEstimate(flops=flops, bytes_accessed=moved, transcendentals=0),
    )(*scalars, *operands)


def on_device(velocity, pressure, viscosity, levels, morton_keys, counts, neighbors):
    leaf_count = velocity.shape[0]
    morton_count = lax.axis_size("morton")
    rows = jnp.asarray(derivative_rows().astype(np.float32))
    pick = jnp.asarray(face_table().astype(np.float32)).astype(bf16)
    spread = jnp.asarray(spread_table().astype(np.float32)).astype(bf16)
    basis = basis_tables()
    face_basis = (basis.astype(np.float32) @ spread_table().T.astype(np.float32)).astype(jnp.bfloat16)
    basis, face_basis = jnp.asarray(basis), jnp.asarray(face_basis[:ROWS])
    boxes = jnp.asarray(box_table(morton_count))
    vel = jnp.transpose(velocity, (1, 0, 2))
    nbrs = jnp.transpose(neighbors, (1, 0))

    width = 3 * FACES
    sib_count = lax.axis_size("sib")
    sides = sib_count // 2
    other_sides = [2 * side for side in range(1, sides)]
    faces, even, odd, spots, *requests = call(
        pack_kernel,
        [
            ((leaf_count, width), bf16),
            ((BAND, width), bf16),
            ((BAND, width), bf16),
            ((16, leaf_count), f32),
        ]
        + [((leaf_count + 16, FACES), bf16)] * (sides - 1),
        4 * 10**8,
        [counts],
        [vel, viscosity, nbrs, levels.reshape(1, -1), morton_keys.reshape(1, -1), boxes, pick],
        [
            pltpu.VMEM((leaf_count, width), bf16),
            pltpu.VMEM((BAND, width), bf16),
            pltpu.VMEM((BAND, width), bf16),
            pltpu.VMEM((16, leaf_count), f32),
        ]
        + [pltpu.VMEM((leaf_count + 16, FACES), bf16)] * (sides - 1)
        + [
            pltpu.VMEM(vel.shape, bf16),
            pltpu.VMEM(viscosity.shape, f32),
            pltpu.VMEM(nbrs.shape, jnp.int32),
            pltpu.VMEM((1, leaf_count), jnp.int32),
            pltpu.VMEM((1, leaf_count), jnp.int32),
            pltpu.VMEM((8, LANES), f32),
            pltpu.VMEM(pick.shape, bf16),
            pltpu.SemaphoreType.DMA((7,)),
            pltpu.SemaphoreType.DMA((3 + sides,)),
        ],
        place=pltpu.HBM,
        outs=[pltpu.HBM] * (3 + sides),
        grant=60,
    )
    weights = requests[0]
    odd = pairs(odd, 1)
    across = swap(faces, "sib", 1)
    across, requests, even, pressure = lax.optimization_barrier((across, requests, even, pressure))
    requests = [swap(block, "sib", apart) for block, apart in zip(requests, other_sides)]
    even = pairs(even, 0)
    part, continuity = call(
        operator_kernel,
        [((3, leaf_count, NODES), f32), ((leaf_count, NODES), f32)],
        2 * 10**9,
        [counts],
        [vel, pressure, viscosity, rows],
        [pltpu.VMEM((NODES, NODES), bf16), pltpu.VMEM((256, NODES), bf16)],
    )
    (own_raw,) = call(
        own_kernel,
        [((ROWS, 3 * leaf_count), f32)],
        10**9,
        [],
        [part, basis, faces, spots],
    )
    odd, even, own_raw, requests = lax.optimization_barrier((odd, even, own_raw, requests))
    bands = jnp.concatenate([odd, even], axis=0)
    move, *group = call(
        group_kernel,
        [((256, 256), f32)] + [((leaf_count, width), bf16)] * sides,
        10**9,
        [],
        [spots, *requests, faces, across],
    )
    near, *served, sums = call(
        moment_kernel,
        [((leaf_count, width), bf16)] * sides + [((morton_count * sib_count, 8, LANES), f32)],
        2 * 10**9,
        [],
        [
            own_raw, face_basis, jnp.asarray(compact_table()), spots, weights,
            bands, swap(bands, "sib", 1), *requests, *group,
        ],
        [pltpu.VMEM((ROWS, 3 * sides * leaf_count), f32)],
    )
    got = [swap(block, "sib", apart) for block, apart in zip(served, other_sides)]
    every = lax.all_to_all(sums, ("morton", "sib"), 0, 0, tiled=True)
    every, *got = lax.optimization_barrier((every, *got))
    force, box, root = call(
        last_kernel,
        [((3, leaf_count, NODES), f32), ((3, 1, MOMENTS), f32), ((3, 1, MOMENTS), f32)],
        2 * 10**8,
        [],
        [part, viscosity, spread, every, move, near, *got],
        [
            pltpu.VMEM((3, leaf_count, NODES), f32),
            pltpu.VMEM((3, 1, MOMENTS), f32),
            pltpu.VMEM((3, 1, MOMENTS), f32),
            pltpu.SemaphoreType.DMA((5,)),
        ],
        outs=[pltpu.HBM] * 3,
    )
    return (
        jnp.transpose(force, (1, 0, 2)),
        continuity,
        jnp.transpose(box, (1, 0, 2)),
        jnp.transpose(root, (1, 0, 2)),
    )


def solution(mesh):
    spread_all = ("morton", "sib")
    in_specs = (
        P(spread_all, None, None),
        P(spread_all, None),
        P(spread_all, None),
        P(spread_all),
        P(spread_all),
        P(),
        P(spread_all, None),
    )
    out_specs = (
        P(spread_all, None, None),
        P(spread_all, None),
        P("morton", None, None),
        P("morton", None, None),
    )
    return jax.shard_map(
        on_device, mesh=mesh, in_specs=in_specs, out_specs=out_specs, check_vma=False
    )
```

```python
import math

import jax
import jax.numpy as jnp
import numpy as np
from jax import lax
from jax.experimental import pallas as pl
from jax.experimental.pallas import tpu as pltpu
from jax.sharding import PartitionSpec as P

DEG = 5
LMAX = 7
MOMENTS = 216
BAND = 32
NODES = 512
FACES = 384
ROWS = 288
LANES = 128

penalty = 256.0
out_scale = 1.0 / 1024.0
mass_scale = 1.0 / 32.0
highest = lax.Precision.HIGHEST
f32 = jnp.float32
bf16 = jnp.bfloat16


def cheb_matrix():
    points = -np.cos(np.pi * np.arange(8) / 7.0)
    weights = np.array([(-1.0) ** node for node in range(8)])
    weights[0] *= 0.5
    weights[7] *= 0.5
    derivative = np.zeros((8, 8))
    for row in range(8):
        for col in range(8):
            if row != col:
                derivative[row, col] = weights[col] / weights[row] / (points[row] - points[col])
        derivative[row, row] = -np.sum(derivative[row])
    return points, derivative


def derivative_rows():
    _, derivative = cheb_matrix()
    lane = np.arange(NODES)
    return np.concatenate([derivative[lane // 64 % 8].T, derivative[lane // 8 % 8].T, derivative[lane % 8].T], axis=0)


def face_table():
    pick = np.zeros((NODES, FACES))
    for face in range(6):
        for first in range(8):
            for second in range(8):
                coords = [first, second]
                coords.insert(face // 2, 7 * (face % 2))
                node = 64 * coords[0] + 8 * coords[1] + coords[2]
                pick[node, face * 64 + first * 8 + second] = 1.0
    return pick


def spread_table():
    pick = face_table()
    order = np.concatenate([np.arange(64) + 64 * (face ^ 1) for face in range(6)])
    return pick[:, order].T


def basis_tables():
    points, _ = cheb_matrix()
    powers = np.stack([points**power for power in range(DEG + 1)])
    basis = np.zeros((6, 6, 8, 8, 8, 8))
    basis[:, :, :6] = np.einsum("xa,yb,zc->xyzabc", powers, powers, powers)
    basis = basis.reshape(ROWS, NODES).astype(np.float32)
    top = np.asarray(basis.astype(jnp.bfloat16))
    rest = np.asarray((basis - top.astype(np.float32)).astype(jnp.bfloat16))
    return np.concatenate([top, rest], axis=0)


def compact_table():
    table = np.zeros((ROWS, 256), jnp.bfloat16)
    for group in range(36):
        for power in range(6):
            table[group * 8 + power, group * 6 + power] = 1.0 / 512.0
    return table


def box_rows():
    morton = lax.axis_index("morton")
    key_bits = 3 * LMAX - (lax.axis_size("morton").bit_length() - 1)
    base = jnp.full((1, LANES), morton, jnp.int32) << key_bits
    lane = lax.broadcasted_iota(jnp.int32, (1, LANES), 1)
    to_root = (lane >= 3) & (lane < 6)
    sides = [2.0 ** max(0, min(LMAX, (key_bits - offset + 2) // 3)) / 2.0**LMAX for offset in (2, 1, 0)]
    scale = 0.5 * max(sides)
    centers = []
    for side, offset in zip(sides, (2, 1, 0)):
        cell = jnp.zeros_like(base)
        for bit in range(LMAX):
            cell = cell + jnp.left_shift(jnp.bitwise_and(jnp.right_shift(base, 3 * bit + offset), 1), bit)
        centers.append(cell.astype(f32) * (1.0 / 2.0**LMAX) + 0.5 * side)
    shifts = [jnp.where(to_root, (center - 0.5) * 2.0, 0.0) for center in centers]
    ratio = jnp.where(to_root, scale * 2.0, 1.0)
    return jnp.concatenate(shifts + [ratio] + centers + [jnp.full((1, LANES), 1.0 / scale, f32)], axis=0)


def swap(block, axis, apart):
    return lax.ppermute(block, axis, [(at, at ^ apart) for at in range(lax.axis_size(axis))])


def pairs(block, first):
    route = []
    for low in range(first, lax.axis_size("morton") - 1, 2):
        route += [(low, low + 1), (low + 1, low)]
    return lax.ppermute(block, "morton", route)


def dot(left, right):
    return jnp.dot(left, right, preferred_element_type=f32)


def dot_nt(left, right, precision=None):
    return lax.dot_general(
        left, right, (((1,), (1,)), ((), ())), preferred_element_type=f32, precision=precision
    )


def pack_kernel(
    counts_ref, vel_ref, visc_ref, nbrs_ref, levels_ref, keys_ref,
    faces_ref, even_ref, odd_ref, spots_ref, *request_refs,
):
    sib_count = lax.axis_size("sib")
    morton = lax.axis_index("morton")
    sib = lax.axis_index("sib")
    own = morton * sib_count + sib
    leaf_count = faces_ref.shape[0]
    fields = jnp.concatenate([vel_ref[0], vel_ref[1], vel_ref[2], visc_ref[...].astype(bf16)], axis=0)
    lane = lax.broadcasted_iota(jnp.int32, (1, FACES), 1)
    first_at, second_at = jnp.bitwise_and(jnp.right_shift(lane, 3), 7), jnp.bitwise_and(lane, 7)
    end_at = 7 * jnp.bitwise_and(jnp.right_shift(lane, 6), 1)
    taken = jnp.where(
        lane < LANES,
        64 * end_at + 8 * first_at + second_at,
        jnp.where(
            lane < 2 * LANES, 64 * first_at + 8 * end_at + second_at, 64 * first_at + 8 * second_at + end_at
        ),
    )
    node = lax.broadcasted_iota(jnp.int32, (NODES, FACES), 0)
    picked = dot(fields, jnp.where(node == taken, 1.0, 0.0).astype(bf16))
    for dim in range(3):
        block = picked[3 * leaf_count :, dim * LANES : (dim + 1) * LANES]
        block = pltpu.roll(block, LANES // 2, 1).astype(bf16)
        for request_ref in request_refs:
            request_ref[:leaf_count, dim * LANES : (dim + 1) * LANES] = block
    picked = picked[: 3 * leaf_count].astype(bf16)
    for comp in range(3):
        for dim in range(3):
            lane = (dim * 3 + comp) * LANES
            rows = picked[comp * leaf_count : (comp + 1) * leaf_count]
            faces_ref[:, lane : lane + LANES] = rows[:, dim * LANES : (dim + 1) * LANES]
    first = counts_ref[own] - BAND
    row = lax.broadcasted_iota(jnp.int32, (BAND, leaf_count), 0)
    col = lax.broadcasted_iota(jnp.int32, (BAND, leaf_count), 1)
    last_rows = jnp.where(col == row + first, 1.0, 0.0).astype(bf16)
    high = dot(last_rows, faces_ref[...]).astype(bf16)
    low = faces_ref[:BAND, :]
    is_odd = jnp.bitwise_and(morton, 1) == 1
    even_ref[...] = jnp.where(is_odd, low, high)
    odd_ref[...] = jnp.where(is_odd, high, low)

    nbrs = nbrs_ref[...]
    target = jnp.maximum(nbrs, 0)
    owner = target // leaf_count
    slot = target - owner * leaf_count
    owner_morton = owner // sib_count
    owner_sib = owner - owner_morton * sib_count
    step = owner_morton - morton
    below = jnp.maximum(morton - 1, 0) * sib_count
    band_start = jnp.zeros_like(slot)
    for other in range(sib_count):
        band_start = jnp.where(owner_sib == other, counts_ref[below + other] - BAND, band_start)
    below_at = BAND * jnp.bitwise_and(morton, 1)
    in_band = jnp.where(step < 0, slot - band_start + below_at, slot + BAND - below_at)
    box = box_rows()
    shift_bits = 3 * (LMAX - levels_ref[...])
    anchor = jnp.left_shift(jnp.right_shift(keys_ref[...], shift_bits), shift_bits)
    span = jnp.left_shift(jnp.ones_like(shift_bits), LMAX - levels_ref[...]).astype(f32)
    finest = 1.0 / float(2**LMAX)
    places = []
    for dim, offset in enumerate((2, 1, 0)):
        cell = jnp.zeros_like(anchor)
        for bit in range(LMAX):
            picked = jnp.bitwise_and(jnp.right_shift(anchor, 3 * bit + offset), 1)
            cell = cell + jnp.left_shift(picked, bit)
        center = (cell.astype(f32) + 0.5 * span) * finest
        places.append((center - box[4 + dim : 5 + dim, :]) * box[7:8, :])
    places.append(0.5 * span * finest * box[7:8, :])
    places.append(jnp.zeros((4, leaf_count), f32))
    geom = jnp.concatenate(places, axis=0)
    for side in range(sib_count // 2):
        piece = jnp.bitwise_xor(owner_sib, jnp.bitwise_xor(sib, 2 * side))
        spot = jnp.where(step == 0, piece * leaf_count + slot, 2 * leaf_count + piece * (2 * BAND) + in_band)
        spot = jnp.where((nbrs >= 0) & (piece < 2), spot, -1)
        if side == 0:
            spots_ref[...] = jnp.concatenate([spot.astype(f32), jnp.zeros((2, leaf_count), f32), geom[:4], box[:4]], axis=0)
            continue
        whole = jnp.right_shift(spot, 4)
        parts = [whole.astype(f32), (spot - 16 * whole).astype(f32), geom[:4]]
        request_ref = request_refs[side - 1]
        request_ref[leaf_count:, :LANES] = jnp.concatenate(parts, axis=0).astype(bf16)
        request_ref[leaf_count:, LANES:] = jnp.zeros((16, FACES - LANES), bf16)


def gathered(asked, window_refs, start):
    leaf_count = asked[0].shape[1]
    rows = sum(ref.shape[0] for ref in window_refs)
    blank = jnp.full((LANES - 8 * len(asked), leaf_count), -1.0, f32)
    places = jnp.concatenate([spots[:8] for spots in asked] + [blank], axis=0).T.astype(jnp.int32)
    cols = lax.broadcasted_iota(jnp.int32, (leaf_count, rows), 1) + start
    upper = jnp.bitwise_and(lax.broadcasted_iota(jnp.int32, (leaf_count, FACES), 1), 64) > 0
    chosen = [[] for _ in asked]
    for dim in range(3):
        at = dim * FACES
        window = jnp.concatenate([ref[:, at : at + FACES] for ref in window_refs], axis=0)
        faces = [8 * who + face for who in range(len(asked)) for face in (2 * dim, 2 * dim + 1)]
        onehot = [jnp.where(cols == places[:, face : face + 1], 1.0, 0.0).astype(bf16) for face in faces]
        found = dot(jnp.concatenate(onehot, axis=0), window)
        for who in range(len(asked)):
            first, second = (found[(2 * who + side) * leaf_count : (2 * who + side + 1) * leaf_count] for side in (0, 1))
            chosen[who].append(jnp.where(upper, first, second).astype(bf16))
    return chosen


def requested(ref):
    leaf_count = ref.shape[0] - 16
    parts = ref[leaf_count:, :LANES].astype(f32)
    blank = jnp.zeros((2, leaf_count), f32)
    rows = [parts[:6] * 16.0 + parts[6:12], blank, parts[12:], jnp.zeros((4, leaf_count), f32)]
    return jnp.concatenate(rows, axis=0)


def by_comp(chosen):
    comps = [
        jnp.concatenate([block[:, comp * LANES : (comp + 1) * LANES] for block in chosen], axis=1) for comp in range(3)
    ]
    return jnp.concatenate(comps, axis=0)


def fill_tables(rows_ref, dx_ref, dyz_ref):
    row = lax.broadcasted_iota(jnp.int32, (64, NODES), 0)
    col = lax.broadcasted_iota(jnp.int32, (64, NODES), 1)
    same = row == jnp.bitwise_and(col, 63)
    for at in range(8):
        dx_ref[64 * at : 64 * at + 64, :] = jnp.where(same, rows_ref[at : at + 1, :], 0.0).astype(bf16)
    row = lax.broadcasted_iota(jnp.int32, (8, 256), 0)
    col = lax.broadcasted_iota(jnp.int32, (8, 256), 1)
    same = row == jnp.bitwise_and(col, 7)
    group = jnp.right_shift(col, 3)
    for pair in range(16):
        blocks = []
        for at in (2 * pair, 2 * pair + 1):
            here = same & (jnp.right_shift(group, 3) == at // 8)
            along_y = jnp.where(here, rows_ref[8 + at % 8 : 9 + at % 8, :256], 0.0)
            along_z = jnp.where(group == at, rows_ref[16:24, :256], 0.0)
            blocks.append(jnp.concatenate([along_y, along_z], axis=1))
        dyz_ref[16 * pair : 16 * pair + 16, :] = jnp.concatenate(blocks, axis=0).astype(bf16)


def operator_kernel(
    counts_ref, vel_ref, press_ref, visc_ref, rows_ref,
    part_ref, mass_ref, dx_ref, dyz_ref,
):
    sib_count = lax.axis_size("sib")
    own = lax.axis_index("morton") * sib_count + lax.axis_index("sib")
    leaf_count = mass_ref.shape[0]
    live = lax.broadcasted_iota(jnp.int32, (leaf_count, NODES), 0) < counts_ref[own]
    node = lax.broadcasted_iota(jnp.int32, (1, NODES), 1)
    touching = jnp.zeros((1, NODES), f32)
    for shift in (6, 3, 0):
        idx = jnp.bitwise_and(jnp.right_shift(node, shift), 7)
        touching = touching + jnp.where((idx == 0) | (idx == 7), 1.0, 0.0)
    fill_tables(rows_ref, dx_ref, dyz_ref)

    def rows(stack, at):
        return stack[at * leaf_count : (at + 1) * leaf_count]

    visc = visc_ref[...]
    fields = jnp.concatenate([vel_ref[0], vel_ref[1], vel_ref[2], press_ref[...]], axis=0)
    halves = [dot(fields[:, at : at + 256], dyz_ref[...]) for at in (0, 256)]
    grads = [
        dot(fields, dx_ref[...]),
        jnp.concatenate([half[:, :256] for half in halves], axis=1),
        jnp.concatenate([half[:, 256:] for half in halves], axis=1),
    ]
    mass = -(rows(grads[0], 0) + rows(grads[1], 1) + rows(grads[2], 2)) * mass_scale
    mass_ref[...] = jnp.where(live, mass, 0.0)
    stress = {}
    for first in range(3):
        for second in range(first, 3):
            value = (visc * (rows(grads[second], first) + rows(grads[first], second))).astype(bf16)
            stress[first, second] = stress[second, first] = value
    columns = [jnp.concatenate([stress[comp, dim] for comp in range(3)], axis=0) for dim in range(3)]
    rest = [
        dot(columns[1][:, at : at + 256], dyz_ref[:, :256]) + dot(columns[2][:, at : at + 256], dyz_ref[:, 256:])
        for at in (0, 256)
    ]
    div = dot(columns[0], dx_ref[...]) + jnp.concatenate(rest, axis=1)
    for comp in range(3):
        jump = touching * vel_ref[comp].astype(f32)
        part = (penalty * visc * jump - rows(div, comp) + rows(grads[comp], 3)) * out_scale
        part_ref[comp] = jnp.where(live, part, 0.0)


def group_kernel(spots_ref, *refs):
    sides = lax.axis_size("sib") // 2
    request_refs, window_refs, move_ref, out_refs = refs[: sides - 1], refs[sides - 1 : sides + 1], refs[sides + 1], refs[sides + 2 :]
    chosen = gathered([spots_ref[...]] + [requested(ref) for ref in request_refs], window_refs, 0)
    for blocks, out_ref in zip(chosen, out_refs):
        for dim, block in enumerate(blocks):
            out_ref[:, dim * FACES : (dim + 1) * FACES] = block
    box = spots_ref[12:, :]
    move = jnp.ones((256, 256), f32)
    for dim, stride in enumerate((36, 6, 1)):
        col = lax.broadcasted_iota(jnp.int32, (1, 256), 1) // stride % 6
        row = lax.broadcasted_iota(jnp.int32, (256, 1), 0) // stride % 6
        along, scale = box[dim : dim + 1, 3:4], box[3:4, 3:4]
        powers = [jnp.ones((1, 1), f32)]
        for _ in range(DEG):
            powers.append(powers[-1] * along)
        factor = jnp.zeros((256, 256), f32)
        below = jnp.ones((1, 1), f32)
        for low in range(DEG + 1):
            line = jnp.zeros((1, 256), f32)
            for high in range(low, DEG + 1):
                line = jnp.where(col == high, powers[high - low] * below * float(math.comb(high, low)), line)
            factor = jnp.where(row == low, line, factor)
            below = below * scale
        move = move * factor
    move_ref[...] = move


def shifted(tiles, geom):
    width = tiles[0].shape
    scale = jnp.broadcast_to(geom[3:4, :], width)
    level = lax.broadcasted_iota(jnp.int32, width, 0)
    depth = jnp.ones(width, f32)
    for power in range(1, DEG + 1):
        depth = depth * jnp.where(level >= power, scale, 1.0)
    scales = [depth]
    for _ in range(2 * DEG):
        scales.append(scales[-1] * scale)
    tiles = [tile * scales[at // 6 + at % 6] for at, tile in enumerate(tiles)]
    along = [jnp.broadcast_to(geom[dim : dim + 1, :], width) for dim in range(3)]
    for low in range(1, DEG + 1):
        for power in range(DEG, low - 1, -1):
            for other in range(6):
                at = power * 6 + other
                tiles[at] = tiles[at] + along[0] * tiles[at - 6]
            for other in range(6):
                at = other * 6 + power
                tiles[at] = tiles[at] + along[1] * tiles[at - 1]
    steps = [jnp.where(level >= low, along[2], 0.0) for low in range(1, DEG + 1)]
    for step in steps:
        tiles = [tile + step * pltpu.roll(tile, 1, 0) for tile in tiles]
    return tiles


def split(values, parts):
    pieces = []
    for _ in range(parts):
        pieces.append(values.astype(bf16))
        values = values - pieces[-1].astype(f32)
    return pieces


def lane_sums(raw_ref, geoms):
    leaf_count = geoms[0].shape[1]
    geom = jnp.concatenate([leaf for leaf in geoms for _ in range(3)], axis=1)
    tiles = shifted([raw_ref[8 * at : 8 * at + 8, :] for at in range(36)], geom)
    span = 3 * leaf_count
    tiles = [sum(tile[:, span * who : span * (who + 1)] for who in range(len(geoms))) for tile in tiles]
    group = lax.broadcasted_iota(jnp.int32, (span, LANES), 0) // leaf_count
    column = lax.broadcasted_iota(jnp.int32, (span, LANES), 1)
    gather = jnp.where((group == column) | (group + 3 == column), 1.0, 0.0).astype(bf16)
    return sum(dot(piece, gather) for piece in split(jnp.concatenate(tiles, axis=0), 3))


def own_kernel(part_ref, basis_ref, faces_ref, spots_ref, raw_ref):
    leaf_count = part_ref.shape[1]
    high, low = split(part_ref[...].reshape(3 * leaf_count, NODES), 2)
    raw = dot_nt(basis_ref[...], high)
    raw_ref[...] = raw[:ROWS] + raw[ROWS:] + dot_nt(basis_ref[:ROWS, :], low)


def moment_kernel(
    own_ref, face_basis_ref, compact_ref, spots_ref, weights_ref, *refs
):
    sides = lax.axis_size("sib") // 2
    window_refs, request_refs, group_refs = refs[:2], refs[2 : 1 + sides], refs[1 + sides : 1 + 2 * sides]
    near_ref, served_refs, sums_ref, raw_ref = refs[1 + 2 * sides], refs[2 + 2 * sides : -2], refs[-2], refs[-1]
    morton = lax.axis_index("morton")
    leaf_count = spots_ref.shape[1]
    asked = [spots_ref[...]] + [requested(ref) for ref in request_refs]
    chosen = gathered(asked, window_refs, 2 * leaf_count)
    values = []
    for blocks, group_ref, out_ref, ref in zip(
        chosen, group_refs, (near_ref, *served_refs), (weights_ref, *request_refs)
    ):
        for dim in range(3):
            lanes = slice(dim * FACES, (dim + 1) * FACES)
            blocks[dim] = blocks[dim] + group_ref[:, lanes]
            out_ref[:, lanes] = blocks[dim]
        weight = ref[:leaf_count].astype(f32) * (-penalty * out_scale)
        values.append(jnp.concatenate([weight] * 3, axis=0) * by_comp(blocks).astype(f32))
    raw = dot_nt(face_basis_ref[...], jnp.concatenate(values, axis=0).astype(bf16))
    span = 3 * leaf_count
    raw_ref[:, :span] = raw[:, :span] + own_ref[...]
    raw_ref[:, span:] = raw[:, span:]
    summed = lane_sums(raw_ref, [spots[8:] for spots in asked])
    box = spots_ref[12:, :]
    both = shifted([summed[8 * at : 8 * at + 8, :] for at in range(36)], box)
    flat = jnp.concatenate(both, axis=0).T
    sums = sum(dot(piece, compact_ref[...]) for piece in split(flat[:8], 3))
    blank = jnp.zeros((2, LANES), f32)
    to_box = jnp.concatenate([sums[:3, :LANES], sums[:3, LANES:], blank], axis=0)
    to_root = jnp.concatenate([sums[3:6, :LANES], sums[3:6, LANES:], blank], axis=0)
    sib_count = lax.axis_size("sib")
    for other in range(sums_ref.shape[0]):
        sums_ref[other] = jnp.where(morton == other // sib_count, to_box, to_root)


def last_kernel(part_ref, visc_ref, spread_ref, sums_ref, move_ref, near_ref, *refs):
    got_refs, (force_hbm, box_hbm, root_hbm, force_ref, box_ref, root_ref, sems) = refs[:-7], refs[-7:]
    faces = near_ref[...]
    for got_ref in got_refs:
        faces = faces + got_ref[...]
    weight = visc_ref[...] * (penalty * out_scale)
    stores = []
    for comp in range(3):
        lanes = [(dim * 3 + comp) * LANES for dim in range(3)]
        jump = dot(jnp.concatenate([faces[:, at : at + LANES] for at in lanes], axis=1), spread_ref[...])
        force_ref[comp] = part_ref[comp] - weight * jump
        stores.append(pltpu.make_async_copy(force_ref.at[comp], force_hbm.at[comp], sems.at[comp]))
        stores[-1].start()
    sib_count = lax.axis_size("sib")
    morton = lax.axis_index("morton")
    box = jnp.zeros(sums_ref.shape[1:], f32)
    root = jnp.zeros(sums_ref.shape[1:], f32)
    for group in range(sums_ref.shape[0] // sib_count):
        total = jnp.sum(sums_ref[group * sib_count : (group + 1) * sib_count], axis=0)
        box = box + jnp.where(morton == group, total, 0.0)
        root = root + jnp.where(morton == group, 0.0, total)
    box = jnp.concatenate([box[:3], box[3:6]], axis=1)
    root = jnp.concatenate([root[:3], root[3:6]], axis=1)
    box_rows = jnp.concatenate([box, jnp.zeros((5, 2 * LANES), f32)], axis=0)
    pieces = jnp.concatenate([piece.astype(f32) for piece in split(box_rows, 3)], axis=0).astype(bf16)
    moved = sum(dot(pieces, table) for table in split(move_ref[...], 2))
    root = root + (moved[:3] + moved[8:11] + moved[16:19])
    for comp in range(3):
        box_ref[comp] = box[comp : comp + 1, :MOMENTS]
        root_ref[comp] = root[comp : comp + 1, :MOMENTS]
    stores.append(pltpu.make_async_copy(box_ref, box_hbm, sems.at[3]))
    stores.append(pltpu.make_async_copy(root_ref, root_hbm, sems.at[4]))
    for store in stores[3:]:
        store.start()
    for store in stores:
        store.wait()


def call(kernel, shapes, flops, scalars, operands, scratch=(), place=pltpu.VMEM, outs=None, grant=32):
    specs = [pl.BlockSpec(memory_space=pltpu.SMEM)] * len(scalars)
    specs += [pl.BlockSpec(memory_space=place)] * len(operands)
    outs = outs or [pltpu.VMEM] * len(shapes)
    moved = sum(array.size * array.dtype.itemsize for array in operands)
    return pl.pallas_call(
        kernel,
        out_shape=[jax.ShapeDtypeStruct(shape, dtype) for shape, dtype in shapes],
        in_specs=specs,
        out_specs=[pl.BlockSpec(memory_space=out) for out in outs],
        scratch_shapes=list(scratch),
        compiler_params=pltpu.CompilerParams(vmem_limit_bytes=grant * 2**20),
        cost_estimate=pl.CostEstimate(flops=flops, bytes_accessed=moved, transcendentals=0),
    )(*scalars, *operands)


def on_device(velocity, pressure, viscosity, levels, morton_keys, counts, neighbors):
    leaf_count = velocity.shape[0]
    morton_count = lax.axis_size("morton")
    rows = jnp.asarray(derivative_rows().astype(np.float32))
    spread = jnp.asarray(spread_table().astype(np.float32)).astype(bf16)
    basis = basis_tables()
    face_basis = (basis.astype(np.float32) @ spread_table().T.astype(np.float32)).astype(jnp.bfloat16)
    basis, face_basis = jnp.asarray(basis), jnp.asarray(face_basis[:ROWS])
    vel = jnp.transpose(velocity, (1, 0, 2))
    nbrs = jnp.transpose(neighbors, (1, 0))

    width = 3 * FACES
    sib_count = lax.axis_size("sib")
    sides = sib_count // 2
    other_sides = [2 * side for side in range(1, sides)]
    faces, even, odd, spots, *requests = call(
        pack_kernel,
        [
            ((leaf_count, width), bf16),
            ((BAND, width), bf16),
            ((BAND, width), bf16),
            ((16, leaf_count), f32),
        ]
        + [((leaf_count + 16, FACES), bf16)] * (sides - 1),
        4 * 10**8,
        [counts],
        [vel, viscosity, nbrs, levels.reshape(1, -1), morton_keys.reshape(1, -1)],
        grant=60,
    )
    weights = requests[0]
    odd = pairs(odd, 1)
    across = swap(faces, "sib", 1)
    across, requests, even, pressure = lax.optimization_barrier((across, requests, even, pressure))
    requests = [swap(block, "sib", apart) for block, apart in zip(requests, other_sides)]
    even = pairs(even, 0)
    part, continuity = call(
        operator_kernel,
        [((3, leaf_count, NODES), f32), ((leaf_count, NODES), f32)],
        2 * 10**9,
        [counts],
        [vel, pressure, viscosity, rows],
        [pltpu.VMEM((NODES, NODES), bf16), pltpu.VMEM((256, NODES), bf16)],
    )
    (own_raw,) = call(
        own_kernel,
        [((ROWS, 3 * leaf_count), f32)],
        10**9,
        [],
        [part, basis, faces, spots],
    )
    odd, even, own_raw, requests = lax.optimization_barrier((odd, even, own_raw, requests))
    bands = jnp.concatenate([odd, even], axis=0)
    move, *group = call(
        group_kernel,
        [((256, 256), f32)] + [((leaf_count, width), bf16)] * sides,
        10**9,
        [],
        [spots, *requests, faces, across],
    )
    near, *served, sums = call(
        moment_kernel,
        [((leaf_count, width), bf16)] * sides + [((morton_count * sib_count, 8, LANES), f32)],
        2 * 10**9,
        [],
        [
            own_raw, face_basis, jnp.asarray(compact_table()), spots, weights,
            bands, swap(bands, "sib", 1), *requests, *group,
        ],
        [pltpu.VMEM((ROWS, 3 * sides * leaf_count), f32)],
    )
    got = [swap(block, "sib", apart) for block, apart in zip(served, other_sides)]
    every = lax.all_to_all(sums, ("morton", "sib"), 0, 0, tiled=True)
    every, *got = lax.optimization_barrier((every, *got))
    force, box, root = call(
        last_kernel,
        [((3, leaf_count, NODES), f32), ((3, 1, MOMENTS), f32), ((3, 1, MOMENTS), f32)],
        2 * 10**8,
        [],
        [part, viscosity, spread, every, move, near, *got],
        [
            pltpu.VMEM((3, leaf_count, NODES), f32),
            pltpu.VMEM((3, 1, MOMENTS), f32),
            pltpu.VMEM((3, 1, MOMENTS), f32),
            pltpu.SemaphoreType.DMA((5,)),
        ],
        outs=[pltpu.HBM] * 3,
    )
    return (
        jnp.transpose(force, (1, 0, 2)),
        continuity,
        jnp.transpose(box, (1, 0, 2)),
        jnp.transpose(root, (1, 0, 2)),
    )


def solution(mesh):
    spread_all = ("morton", "sib")
    in_specs = (
        P(spread_all, None, None),
        P(spread_all, None),
        P(spread_all, None),
        P(spread_all),
        P(spread_all),
        P(),
        P(spread_all, None),
    )
    out_specs = (
        P(spread_all, None, None),
        P(spread_all, None),
        P("morton", None, None),
        P("morton", None, None),
    )
    return jax.shard_map(
        on_device, mesh=mesh, in_specs=in_specs, out_specs=out_specs, check_vma=False
    )
```

```python
import math

import jax
import jax.numpy as jnp
import numpy as np
from jax import lax
from jax.experimental import pallas as pl
from jax.experimental.pallas import tpu as pltpu
from jax.sharding import PartitionSpec as P

DEG = 5
LMAX = 7
MOMENTS = 216
BAND = 32
NODES = 512
FACES = 384
ROWS = 288
LANES = 128

penalty = 256.0
out_scale = 1.0 / 1024.0
mass_scale = 1.0 / 32.0
highest = lax.Precision.HIGHEST
f32 = jnp.float32
bf16 = jnp.bfloat16


def cheb_matrix():
    points = -np.cos(np.pi * np.arange(8) / 7.0)
    weights = np.array([(-1.0) ** node for node in range(8)])
    weights[0] *= 0.5
    weights[7] *= 0.5
    derivative = np.zeros((8, 8))
    for row in range(8):
        for col in range(8):
            if row != col:
                derivative[row, col] = weights[col] / weights[row] / (points[row] - points[col])
        derivative[row, row] = -np.sum(derivative[row])
    return points, derivative


def derivative_rows():
    _, derivative = cheb_matrix()
    lane = np.arange(NODES)
    return np.concatenate([derivative[lane // 64 % 8].T, derivative[lane // 8 % 8].T, derivative[lane % 8].T], axis=0)


def face_table():
    pick = np.zeros((NODES, FACES))
    for face in range(6):
        for first in range(8):
            for second in range(8):
                coords = [first, second]
                coords.insert(face // 2, 7 * (face % 2))
                node = 64 * coords[0] + 8 * coords[1] + coords[2]
                pick[node, face * 64 + first * 8 + second] = 1.0
    return pick


def spread_table():
    pick = face_table()
    order = np.concatenate([np.arange(64) + 64 * (face ^ 1) for face in range(6)])
    return pick[:, order].T


def basis_tables():
    points, _ = cheb_matrix()
    powers = np.stack([points**power for power in range(DEG + 1)])
    basis = np.zeros((6, 6, 8, 8, 8, 8))
    basis[:, :, :6] = np.einsum("xa,yb,zc->xyzabc", powers, powers, powers)
    basis = basis.reshape(ROWS, NODES).astype(np.float32)
    top = np.asarray(basis.astype(jnp.bfloat16))
    rest = np.asarray((basis - top.astype(np.float32)).astype(jnp.bfloat16))
    return np.concatenate([top, rest], axis=0)


def compact_table():
    table = np.zeros((ROWS, 256), jnp.bfloat16)
    for group in range(36):
        for power in range(6):
            table[group * 8 + power, group * 6 + power] = 1.0 / 512.0
    return table


def box_rows():
    morton = lax.axis_index("morton")
    key_bits = 3 * LMAX - (lax.axis_size("morton").bit_length() - 1)
    base = jnp.full((1, LANES), morton, jnp.int32) << key_bits
    lane = lax.broadcasted_iota(jnp.int32, (1, LANES), 1)
    to_root = (lane >= 3) & (lane < 6)
    sides = [2.0 ** max(0, min(LMAX, (key_bits - offset + 2) // 3)) / 2.0**LMAX for offset in (2, 1, 0)]
    scale = 0.5 * max(sides)
    centers = []
    for side, offset in zip(sides, (2, 1, 0)):
        cell = jnp.zeros_like(base)
        for bit in range(LMAX):
            cell = cell + jnp.left_shift(jnp.bitwise_and(jnp.right_shift(base, 3 * bit + offset), 1), bit)
        centers.append(cell.astype(f32) * (1.0 / 2.0**LMAX) + 0.5 * side)
    shifts = [jnp.where(to_root, (center - 0.5) * 2.0, 0.0) for center in centers]
    ratio = jnp.where(to_root, scale * 2.0, 1.0)
    return jnp.concatenate(shifts + [ratio] + centers + [jnp.full((1, LANES), 1.0 / scale, f32)], axis=0)


def swap(block, axis, apart):
    return lax.ppermute(block, axis, [(at, at ^ apart) for at in range(lax.axis_size(axis))])


def pairs(block, first):
    route = []
    for low in range(first, lax.axis_size("morton") - 1, 2):
        route += [(low, low + 1), (low + 1, low)]
    return lax.ppermute(block, "morton", route)


def dot(left, right):
    return jnp.dot(left, right, preferred_element_type=f32)


def dot_nt(left, right, precision=None):
    return lax.dot_general(
        left, right, (((1,), (1,)), ((), ())), preferred_element_type=f32, precision=precision
    )


def pack_kernel(
    counts_ref, vel_ref, visc_ref, nbrs_ref, levels_ref, keys_ref,
    faces_ref, even_ref, odd_ref, spots_ref, *request_refs,
):
    sib_count = lax.axis_size("sib")
    morton = lax.axis_index("morton")
    sib = lax.axis_index("sib")
    own = morton * sib_count + sib
    leaf_count = faces_ref.shape[0]
    fields = jnp.concatenate([vel_ref[0], vel_ref[1], vel_ref[2], visc_ref[...].astype(bf16)], axis=0)
    lane = lax.broadcasted_iota(jnp.int32, (1, FACES), 1)
    first_at, second_at = jnp.bitwise_and(jnp.right_shift(lane, 3), 7), jnp.bitwise_and(lane, 7)
    end_at = 7 * jnp.bitwise_and(jnp.right_shift(lane, 6), 1)
    taken = jnp.where(
        lane < LANES,
        64 * end_at + 8 * first_at + second_at,
        jnp.where(
            lane < 2 * LANES, 64 * first_at + 8 * end_at + second_at, 64 * first_at + 8 * second_at + end_at
        ),
    )
    node = lax.broadcasted_iota(jnp.int32, (NODES, FACES), 0)
    picked = dot(fields, jnp.where(node == taken, 1.0, 0.0).astype(bf16))
    for dim in range(3):
        block = picked[3 * leaf_count :, dim * LANES : (dim + 1) * LANES]
        block = pltpu.roll(block, LANES // 2, 1).astype(bf16)
        for request_ref in request_refs:
            request_ref[:leaf_count, dim * LANES : (dim + 1) * LANES] = block
    picked = picked[: 3 * leaf_count].astype(bf16)
    for comp in range(3):
        for dim in range(3):
            lane = (dim * 3 + comp) * LANES
            rows = picked[comp * leaf_count : (comp + 1) * leaf_count]
            faces_ref[:, lane : lane + LANES] = rows[:, dim * LANES : (dim + 1) * LANES]
    first = counts_ref[own] - BAND
    row = lax.broadcasted_iota(jnp.int32, (BAND, leaf_count), 0)
    col = lax.broadcasted_iota(jnp.int32, (BAND, leaf_count), 1)
    last_rows = jnp.where(col == row + first, 1.0, 0.0).astype(bf16)
    high = dot(last_rows, faces_ref[...]).astype(bf16)
    low = faces_ref[:BAND, :]
    is_odd = jnp.bitwise_and(morton, 1) == 1
    even_ref[...] = jnp.where(is_odd, low, high)
    odd_ref[...] = jnp.where(is_odd, high, low)

    nbrs = nbrs_ref[...]
    target = jnp.maximum(nbrs, 0)
    owner = target // leaf_count
    slot = target - owner * leaf_count
    owner_morton = owner // sib_count
    owner_sib = owner - owner_morton * sib_count
    step = owner_morton - morton
    below = jnp.maximum(morton - 1, 0) * sib_count
    band_start = jnp.zeros_like(slot)
    for other in range(sib_count):
        band_start = jnp.where(owner_sib == other, counts_ref[below + other] - BAND, band_start)
    below_at = BAND * jnp.bitwise_and(morton, 1)
    in_band = jnp.where(step < 0, slot - band_start + below_at, slot + BAND - below_at)
    box = box_rows()
    shift_bits = 3 * (LMAX - levels_ref[...])
    anchor = jnp.left_shift(jnp.right_shift(keys_ref[...], shift_bits), shift_bits)
    span = jnp.left_shift(jnp.ones_like(shift_bits), LMAX - levels_ref[...]).astype(f32)
    finest = 1.0 / float(2**LMAX)
    places = []
    for dim, offset in enumerate((2, 1, 0)):
        cell = jnp.zeros_like(anchor)
        for bit in range(LMAX):
            picked = jnp.bitwise_and(jnp.right_shift(anchor, 3 * bit + offset), 1)
            cell = cell + jnp.left_shift(picked, bit)
        center = (cell.astype(f32) + 0.5 * span) * finest
        places.append((center - box[4 + dim : 5 + dim, :]) * box[7:8, :])
    places.append(0.5 * span * finest * box[7:8, :])
    places.append(jnp.zeros((4, leaf_count), f32))
    geom = jnp.concatenate(places, axis=0)
    for side in range(sib_count // 2):
        piece = jnp.bitwise_xor(owner_sib, jnp.bitwise_xor(sib, 2 * side))
        spot = jnp.where(step == 0, piece * leaf_count + slot, 2 * leaf_count + piece * (2 * BAND) + in_band)
        spot = jnp.where((nbrs >= 0) & (piece < 2), spot, -1)
        if side == 0:
            spots_ref[...] = jnp.concatenate([spot.astype(f32), jnp.zeros((2, leaf_count), f32), geom[:4], box[:4]], axis=0)
            continue
        whole = jnp.right_shift(spot, 4)
        parts = [whole.astype(f32), (spot - 16 * whole).astype(f32), geom[:4]]
        request_ref = request_refs[side - 1]
        request_ref[leaf_count:, :LANES] = jnp.concatenate(parts, axis=0).astype(bf16)
        request_ref[leaf_count:, LANES:] = jnp.zeros((16, FACES - LANES), bf16)


def gathered(asked, window_refs, start):
    leaf_count = asked[0].shape[1]
    rows = sum(ref.shape[0] for ref in window_refs)
    blank = jnp.full((LANES - 8 * len(asked), leaf_count), -1.0, f32)
    places = jnp.concatenate([spots[:8] for spots in asked] + [blank], axis=0).T.astype(jnp.int32)
    cols = lax.broadcasted_iota(jnp.int32, (leaf_count, rows), 1) + start
    upper = jnp.bitwise_and(lax.broadcasted_iota(jnp.int32, (leaf_count, FACES), 1), 64) > 0
    chosen = [[] for _ in asked]
    for dim in range(3):
        at = dim * FACES
        window = jnp.concatenate([ref[:, at : at + FACES] for ref in window_refs], axis=0)
        faces = [8 * who + face for who in range(len(asked)) for face in (2 * dim, 2 * dim + 1)]
        onehot = [jnp.where(cols == places[:, face : face + 1], 1.0, 0.0).astype(bf16) for face in faces]
        found = dot(jnp.concatenate(onehot, axis=0), window)
        for who in range(len(asked)):
            first, second = (found[(2 * who + side) * leaf_count : (2 * who + side + 1) * leaf_count] for side in (0, 1))
            chosen[who].append(jnp.where(upper, first, second).astype(bf16))
    return chosen


def requested(ref):
    leaf_count = ref.shape[0] - 16
    parts = ref[leaf_count:, :LANES].astype(f32)
    blank = jnp.zeros((2, leaf_count), f32)
    rows = [parts[:6] * 16.0 + parts[6:12], blank, parts[12:], jnp.zeros((4, leaf_count), f32)]
    return jnp.concatenate(rows, axis=0)


def by_comp(chosen):
    comps = [
        jnp.concatenate([block[:, comp * LANES : (comp + 1) * LANES] for block in chosen], axis=1) for comp in range(3)
    ]
    return jnp.concatenate(comps, axis=0)


def fill_tables(rows_ref, dx_ref, dyz_ref):
    row = lax.broadcasted_iota(jnp.int32, (64, NODES), 0)
    col = lax.broadcasted_iota(jnp.int32, (64, NODES), 1)
    same = row == jnp.bitwise_and(col, 63)
    for at in range(8):
        dx_ref[64 * at : 64 * at + 64, :] = jnp.where(same, rows_ref[at : at + 1, :], 0.0).astype(bf16)
    row = lax.broadcasted_iota(jnp.int32, (8, 256), 0)
    col = lax.broadcasted_iota(jnp.int32, (8, 256), 1)
    same = row == jnp.bitwise_and(col, 7)
    group = jnp.right_shift(col, 3)
    for pair in range(16):
        blocks = []
        for at in (2 * pair, 2 * pair + 1):
            here = same & (jnp.right_shift(group, 3) == at // 8)
            along_y = jnp.where(here, rows_ref[8 + at % 8 : 9 + at % 8, :256], 0.0)
            along_z = jnp.where(group == at, rows_ref[16:24, :256], 0.0)
            blocks.append(jnp.concatenate([along_y, along_z], axis=1))
        dyz_ref[16 * pair : 16 * pair + 16, :] = jnp.concatenate(blocks, axis=0).astype(bf16)


def operator_kernel(
    counts_ref, vel_ref, press_ref, visc_ref, rows_ref,
    part_ref, mass_ref, dx_ref, dyz_ref,
):
    sib_count = lax.axis_size("sib")
    own = lax.axis_index("morton") * sib_count + lax.axis_index("sib")
    leaf_count = mass_ref.shape[0]
    live = lax.broadcasted_iota(jnp.int32, (leaf_count, NODES), 0) < counts_ref[own]
    node = lax.broadcasted_iota(jnp.int32, (1, NODES), 1)
    touching = jnp.zeros((1, NODES), f32)
    for shift in (6, 3, 0):
        idx = jnp.bitwise_and(jnp.right_shift(node, shift), 7)
        touching = touching + jnp.where((idx == 0) | (idx == 7), 1.0, 0.0)
    fill_tables(rows_ref, dx_ref, dyz_ref)

    def rows(stack, at):
        return stack[at * leaf_count : (at + 1) * leaf_count]

    visc = visc_ref[...]
    fields = jnp.concatenate([vel_ref[0], vel_ref[1], vel_ref[2], press_ref[...]], axis=0)
    halves = [dot(fields[:, at : at + 256], dyz_ref[...]) for at in (0, 256)]
    grads = [
        dot(fields, dx_ref[...]),
        jnp.concatenate([half[:, :256] for half in halves], axis=1),
        jnp.concatenate([half[:, 256:] for half in halves], axis=1),
    ]
    mass = -(rows(grads[0], 0) + rows(grads[1], 1) + rows(grads[2], 2)) * mass_scale
    mass_ref[...] = jnp.where(live, mass, 0.0)
    stress = {}
    for first in range(3):
        for second in range(first, 3):
            value = (visc * (rows(grads[second], first) + rows(grads[first], second))).astype(bf16)
            stress[first, second] = stress[second, first] = value
    columns = [jnp.concatenate([stress[comp, dim] for comp in range(3)], axis=0) for dim in range(3)]
    rest = [
        dot(columns[1][:, at : at + 256], dyz_ref[:, :256]) + dot(columns[2][:, at : at + 256], dyz_ref[:, 256:])
        for at in (0, 256)
    ]
    div = dot(columns[0], dx_ref[...]) + jnp.concatenate(rest, axis=1)
    for comp in range(3):
        jump = touching * vel_ref[comp].astype(f32)
        part = (penalty * visc * jump - rows(div, comp) + rows(grads[comp], 3)) * out_scale
        part_ref[comp] = jnp.where(live, part, 0.0)


def group_kernel(spots_ref, *refs):
    sides = lax.axis_size("sib") // 2
    request_refs, window_refs, move_ref, out_refs = refs[: sides - 1], refs[sides - 1 : sides + 1], refs[sides + 1], refs[sides + 2 :]
    chosen = gathered([spots_ref[...]] + [requested(ref) for ref in request_refs], window_refs, 0)
    for blocks, out_ref in zip(chosen, out_refs):
        for dim, block in enumerate(blocks):
            out_ref[:, dim * FACES : (dim + 1) * FACES] = block
    box = spots_ref[12:, :]
    move = jnp.ones((256, 256), f32)
    for dim, stride in enumerate((36, 6, 1)):
        col = lax.broadcasted_iota(jnp.int32, (1, 256), 1) // stride % 6
        row = lax.broadcasted_iota(jnp.int32, (256, 1), 0) // stride % 6
        along, scale = box[dim : dim + 1, 3:4], box[3:4, 3:4]
        powers = [jnp.ones((1, 1), f32)]
        for _ in range(DEG):
            powers.append(powers[-1] * along)
        factor = jnp.zeros((256, 256), f32)
        below = jnp.ones((1, 1), f32)
        for low in range(DEG + 1):
            line = jnp.zeros((1, 256), f32)
            for high in range(low, DEG + 1):
                line = jnp.where(col == high, powers[high - low] * below * float(math.comb(high, low)), line)
            factor = jnp.where(row == low, line, factor)
            below = below * scale
        move = move * factor
    move_ref[...] = move


def shifted(tiles, geom):
    width = tiles[0].shape
    scale = jnp.broadcast_to(geom[3:4, :], width)
    level = lax.broadcasted_iota(jnp.int32, width, 0)
    depth = jnp.ones(width, f32)
    for power in range(1, DEG + 1):
        depth = depth * jnp.where(level >= power, scale, 1.0)
    scales = [depth]
    for _ in range(2 * DEG):
        scales.append(scales[-1] * scale)
    tiles = [tile * scales[at // 6 + at % 6] for at, tile in enumerate(tiles)]
    along = [jnp.broadcast_to(geom[dim : dim + 1, :], width) for dim in range(3)]
    for low in range(1, DEG + 1):
        for power in range(DEG, low - 1, -1):
            for other in range(6):
                at = power * 6 + other
                tiles[at] = tiles[at] + along[0] * tiles[at - 6]
            for other in range(6):
                at = other * 6 + power
                tiles[at] = tiles[at] + along[1] * tiles[at - 1]
    steps = [jnp.where(level >= low, along[2], 0.0) for low in range(1, DEG + 1)]
    for step in steps:
        tiles = [tile + step * pltpu.roll(tile, 1, 0) for tile in tiles]
    return tiles


def split(values, parts):
    pieces = []
    for _ in range(parts):
        pieces.append(values.astype(bf16))
        values = values - pieces[-1].astype(f32)
    return pieces


def lane_sums(raw_ref, geoms):
    leaf_count = geoms[0].shape[1]
    geom = jnp.concatenate([leaf for leaf in geoms for _ in range(3)], axis=1)
    tiles = shifted([raw_ref[8 * at : 8 * at + 8, :] for at in range(36)], geom)
    span = 3 * leaf_count
    tiles = [sum(tile[:, span * who : span * (who + 1)] for who in range(len(geoms))) for tile in tiles]
    group = lax.broadcasted_iota(jnp.int32, (span, LANES), 0) // leaf_count
    column = lax.broadcasted_iota(jnp.int32, (span, LANES), 1)
    gather = jnp.where((group == column) | (group + 3 == column), 1.0, 0.0).astype(bf16)
    return sum(dot(piece, gather) for piece in split(jnp.concatenate(tiles, axis=0), 3))


def own_kernel(part_ref, basis_ref, faces_ref, spots_ref, raw_ref):
    leaf_count = part_ref.shape[1]
    high, low = split(part_ref[...].reshape(3 * leaf_count, NODES), 2)
    raw = dot_nt(basis_ref[...], high)
    raw_ref[...] = raw[:ROWS] + raw[ROWS:] + dot_nt(basis_ref[:ROWS, :], low)


def moment_kernel(
    own_ref, face_basis_ref, compact_ref, spots_ref, weights_ref, *refs
):
    sides = lax.axis_size("sib") // 2
    window_refs, request_refs, group_refs = refs[:2], refs[2 : 1 + sides], refs[1 + sides : 1 + 2 * sides]
    near_ref, served_refs, sums_ref, raw_ref = refs[1 + 2 * sides], refs[2 + 2 * sides : -2], refs[-2], refs[-1]
    morton = lax.axis_index("morton")
    leaf_count = spots_ref.shape[1]
    asked = [spots_ref[...]] + [requested(ref) for ref in request_refs]
    chosen = gathered(asked, window_refs, 2 * leaf_count)
    values = []
    for blocks, group_ref, out_ref, ref in zip(
        chosen, group_refs, (near_ref, *served_refs), (weights_ref, *request_refs)
    ):
        for dim in range(3):
            lanes = slice(dim * FACES, (dim + 1) * FACES)
            blocks[dim] = blocks[dim] + group_ref[:, lanes]
            out_ref[:, lanes] = blocks[dim]
        weight = ref[:leaf_count].astype(f32) * (-penalty * out_scale)
        values.append(jnp.concatenate([weight] * 3, axis=0) * by_comp(blocks).astype(f32))
    raw = dot_nt(face_basis_ref[...], jnp.concatenate(values, axis=0).astype(bf16))
    span = 3 * leaf_count
    raw_ref[:, :span] = raw[:, :span] + own_ref[...]
    raw_ref[:, span:] = raw[:, span:]
    summed = lane_sums(raw_ref, [spots[8:] for spots in asked])
    box = spots_ref[12:, :]
    both = shifted([summed[8 * at : 8 * at + 8, :] for at in range(36)], box)
    flat = jnp.concatenate(both, axis=0).T
    sums = sum(dot(piece, compact_ref[...]) for piece in split(flat[:8], 3))
    blank = jnp.zeros((2, LANES), f32)
    to_box = jnp.concatenate([sums[:3, :LANES], sums[:3, LANES:], blank], axis=0)
    to_root = jnp.concatenate([sums[3:6, :LANES], sums[3:6, LANES:], blank], axis=0)
    sib_count = lax.axis_size("sib")
    for other in range(sums_ref.shape[0]):
        sums_ref[other] = jnp.where(morton == other // sib_count, to_box, to_root)


def last_kernel(part_ref, visc_ref, spread_ref, sums_ref, move_ref, near_ref, *refs):
    got_refs, (force_hbm, box_hbm, root_hbm, force_ref, box_ref, root_ref, sems) = refs[:-7], refs[-7:]
    faces = near_ref[...]
    for got_ref in got_refs:
        faces = faces + got_ref[...]
    weight = visc_ref[...] * (penalty * out_scale)
    stores = []
    for comp in range(3):
        lanes = [(dim * 3 + comp) * LANES for dim in range(3)]
        jump = dot(jnp.concatenate([faces[:, at : at + LANES] for at in lanes], axis=1), spread_ref[...])
        force_ref[comp] = part_ref[comp] - weight * jump
        stores.append(pltpu.make_async_copy(force_ref.at[comp], force_hbm.at[comp], sems.at[comp]))
        stores[-1].start()
    sib_count = lax.axis_size("sib")
    morton = lax.axis_index("morton")
    box = jnp.zeros(sums_ref.shape[1:], f32)
    root = jnp.zeros(sums_ref.shape[1:], f32)
    for group in range(sums_ref.shape[0] // sib_count):
        total = jnp.sum(sums_ref[group * sib_count : (group + 1) * sib_count], axis=0)
        box = box + jnp.where(morton == group, total, 0.0)
        root = root + jnp.where(morton == group, 0.0, total)
    box = jnp.concatenate([box[:3], box[3:6]], axis=1)
    root = jnp.concatenate([root[:3], root[3:6]], axis=1)
    box_rows = jnp.concatenate([box, jnp.zeros((5, 2 * LANES), f32)], axis=0)
    pieces = jnp.concatenate([piece.astype(f32) for piece in split(box_rows, 3)], axis=0).astype(bf16)
    moved = sum(dot(pieces, table) for table in split(move_ref[...], 2))
    root = root + (moved[:3] + moved[8:11] + moved[16:19])
    for comp in range(3):
        box_ref[comp] = box[comp : comp + 1, :MOMENTS]
        root_ref[comp] = root[comp : comp + 1, :MOMENTS]
    stores.append(pltpu.make_async_copy(box_ref, box_hbm, sems.at[3]))
    stores.append(pltpu.make_async_copy(root_ref, root_hbm, sems.at[4]))
    for store in stores[3:]:
        store.start()
    for store in stores:
        store.wait()


def call(kernel, shapes, flops, scalars, operands, scratch=(), place=pltpu.VMEM, outs=None, grant=32):
    specs = [pl.BlockSpec(memory_space=pltpu.SMEM)] * len(scalars)
    specs += [pl.BlockSpec(memory_space=place)] * len(operands)
    outs = outs or [pltpu.VMEM] * len(shapes)
    moved = sum(array.size * array.dtype.itemsize for array in operands)
    return pl.pallas_call(
        kernel,
        out_shape=[jax.ShapeDtypeStruct(shape, dtype) for shape, dtype in shapes],
        in_specs=specs,
        out_specs=[pl.BlockSpec(memory_space=out) for out in outs],
        scratch_shapes=list(scratch),
        compiler_params=pltpu.CompilerParams(vmem_limit_bytes=grant * 2**20),
        cost_estimate=pl.CostEstimate(flops=flops, bytes_accessed=moved, transcendentals=0),
    )(*scalars, *operands)


def on_device(velocity, pressure, viscosity, levels, morton_keys, counts, neighbors):
    leaf_count = velocity.shape[0]
    morton_count = lax.axis_size("morton")
    rows = jnp.asarray(derivative_rows().astype(np.float32))
    spread = jnp.asarray(spread_table().astype(np.float32)).astype(bf16)
    basis = basis_tables()
    face_basis = (basis.astype(np.float32) @ spread_table().T.astype(np.float32)).astype(jnp.bfloat16)
    basis, face_basis = jnp.asarray(basis), jnp.asarray(face_basis[:ROWS])
    vel = jnp.transpose(velocity, (1, 0, 2))
    nbrs = jnp.transpose(neighbors, (1, 0))

    width = 3 * FACES
    sib_count = lax.axis_size("sib")
    sides = sib_count // 2
    other_sides = [2 * side for side in range(1, sides)]
    faces, even, odd, spots, *requests = call(
        pack_kernel,
        [
            ((leaf_count, width), bf16),
            ((BAND, width), bf16),
            ((BAND, width), bf16),
            ((16, leaf_count), f32),
        ]
        + [((leaf_count + 16, FACES), bf16)] * (sides - 1),
        4 * 10**8,
        [counts],
        [vel, viscosity, nbrs, levels.reshape(1, -1), morton_keys.reshape(1, -1)],
        grant=60,
    )
    weights = requests[0]
    odd = pairs(odd, 1)
    across = swap(faces, "sib", 1)
    across, requests, even, pressure = lax.optimization_barrier((across, requests, even, pressure))
    requests = [swap(block, "sib", apart) for block, apart in zip(requests, other_sides)]
    even = pairs(even, 0)
    part, continuity = call(
        operator_kernel,
        [((3, leaf_count, NODES), f32), ((leaf_count, NODES), f32)],
        2 * 10**9,
        [counts],
        [vel, pressure, viscosity, rows],
        [pltpu.VMEM((NODES, NODES), bf16), pltpu.VMEM((256, NODES), bf16)],
    )
    (own_raw,) = call(
        own_kernel,
        [((ROWS, 3 * leaf_count), f32)],
        10**9,
        [],
        [part, basis, faces, spots],
    )
    odd, even, own_raw = lax.optimization_barrier((odd, even, own_raw))
    bands = jnp.concatenate([odd, even], axis=0)
    move, *group = call(
        group_kernel,
        [((256, 256), f32)] + [((leaf_count, width), bf16)] * sides,
        10**9,
        [],
        [spots, *requests, faces, across],
    )
    near, *served, sums = call(
        moment_kernel,
        [((leaf_count, width), bf16)] * sides + [((morton_count * sib_count, 8, LANES), f32)],
        2 * 10**9,
        [],
        [
            own_raw, face_basis, jnp.asarray(compact_table()), spots, weights,
            bands, swap(bands, "sib", 1), *requests, *group,
        ],
        [pltpu.VMEM((ROWS, 3 * sides * leaf_count), f32)],
    )
    got = [swap(block, "sib", apart) for block, apart in zip(served, other_sides)]
    every = lax.all_to_all(sums, ("morton", "sib"), 0, 0, tiled=True)
    every, *got = lax.optimization_barrier((every, *got))
    force, box, root = call(
        last_kernel,
        [((3, leaf_count, NODES), f32), ((3, 1, MOMENTS), f32), ((3, 1, MOMENTS), f32)],
        2 * 10**8,
        [],
        [part, viscosity, spread, every, move, near, *got],
        [
            pltpu.VMEM((3, leaf_count, NODES), f32),
            pltpu.VMEM((3, 1, MOMENTS), f32),
            pltpu.VMEM((3, 1, MOMENTS), f32),
            pltpu.SemaphoreType.DMA((5,)),
        ],
        outs=[pltpu.HBM] * 3,
    )
    return (
        jnp.transpose(force, (1, 0, 2)),
        continuity,
        jnp.transpose(box, (1, 0, 2)),
        jnp.transpose(root, (1, 0, 2)),
    )


def solution(mesh):
    spread_all = ("morton", "sib")
    in_specs = (
        P(spread_all, None, None),
        P(spread_all, None),
        P(spread_all, None),
        P(spread_all),
        P(spread_all),
        P(),
        P(spread_all, None),
    )
    out_specs = (
        P(spread_all, None, None),
        P(spread_all, None),
        P("morton", None, None),
        P("morton", None, None),
    )
    return jax.shard_map(
        on_device, mesh=mesh, in_specs=in_specs, out_specs=out_specs, check_vma=False
    )
```

```python
import math

import jax
import jax.numpy as jnp
import numpy as np
from jax import lax
from jax.experimental import pallas as pl
from jax.experimental.pallas import tpu as pltpu
from jax.sharding import PartitionSpec as P

DEG = 5
LMAX = 7
MOMENTS = 216
BAND = 32
NODES = 512
FACES = 384
ROWS = 288
LANES = 128

penalty = 256.0
out_scale = 1.0 / 1024.0
mass_scale = 1.0 / 32.0
highest = lax.Precision.HIGHEST
f32 = jnp.float32
bf16 = jnp.bfloat16


def cheb_matrix():
    points = -np.cos(np.pi * np.arange(8) / 7.0)
    weights = np.array([(-1.0) ** node for node in range(8)])
    weights[0] *= 0.5
    weights[7] *= 0.5
    derivative = np.zeros((8, 8))
    for row in range(8):
        for col in range(8):
            if row != col:
                derivative[row, col] = weights[col] / weights[row] / (points[row] - points[col])
        derivative[row, row] = -np.sum(derivative[row])
    return points, derivative


def derivative_rows():
    _, derivative = cheb_matrix()
    lane = np.arange(NODES)
    return np.concatenate([derivative[lane // 64 % 8].T, derivative[lane // 8 % 8].T, derivative[lane % 8].T], axis=0)


def face_table():
    pick = np.zeros((NODES, FACES))
    for face in range(6):
        for first in range(8):
            for second in range(8):
                coords = [first, second]
                coords.insert(face // 2, 7 * (face % 2))
                node = 64 * coords[0] + 8 * coords[1] + coords[2]
                pick[node, face * 64 + first * 8 + second] = 1.0
    return pick


def spread_table():
    pick = face_table()
    order = np.concatenate([np.arange(64) + 64 * (face ^ 1) for face in range(6)])
    return pick[:, order].T


def basis_tables():
    points, _ = cheb_matrix()
    powers = np.stack([points**power for power in range(DEG + 1)])
    basis = np.zeros((6, 6, 8, 8, 8, 8))
    basis[:, :, :6] = np.einsum("xa,yb,zc->xyzabc", powers, powers, powers)
    basis = basis.reshape(ROWS, NODES).astype(np.float32)
    top = np.asarray(basis.astype(jnp.bfloat16))
    rest = np.asarray((basis - top.astype(np.float32)).astype(jnp.bfloat16))
    return np.concatenate([top, rest], axis=0)


def compact_table():
    table = np.zeros((ROWS, 256), jnp.bfloat16)
    for group in range(36):
        for power in range(6):
            table[group * 8 + power, group * 6 + power] = 1.0 / 512.0
    return table


def box_rows():
    morton = lax.axis_index("morton")
    key_bits = 3 * LMAX - (lax.axis_size("morton").bit_length() - 1)
    base = jnp.full((1, LANES), morton, jnp.int32) << key_bits
    lane = lax.broadcasted_iota(jnp.int32, (1, LANES), 1)
    to_root = (lane >= 3) & (lane < 6)
    sides = [2.0 ** max(0, min(LMAX, (key_bits - offset + 2) // 3)) / 2.0**LMAX for offset in (2, 1, 0)]
    scale = 0.5 * max(sides)
    centers = []
    for side, offset in zip(sides, (2, 1, 0)):
        cell = jnp.zeros_like(base)
        for bit in range(LMAX):
            cell = cell + jnp.left_shift(jnp.bitwise_and(jnp.right_shift(base, 3 * bit + offset), 1), bit)
        centers.append(cell.astype(f32) * (1.0 / 2.0**LMAX) + 0.5 * side)
    shifts = [jnp.where(to_root, (center - 0.5) * 2.0, 0.0) for center in centers]
    ratio = jnp.where(to_root, scale * 2.0, 1.0)
    return jnp.concatenate(shifts + [ratio] + centers + [jnp.full((1, LANES), 1.0 / scale, f32)], axis=0)


def swap(block, axis, apart):
    return lax.ppermute(block, axis, [(at, at ^ apart) for at in range(lax.axis_size(axis))])


def pairs(block, first):
    route = []
    for low in range(first, lax.axis_size("morton") - 1, 2):
        route += [(low, low + 1), (low + 1, low)]
    return lax.ppermute(block, "morton", route)


def dot(left, right):
    return jnp.dot(left, right, preferred_element_type=f32)


def dot_nt(left, right, precision=None):
    return lax.dot_general(
        left, right, (((1,), (1,)), ((), ())), preferred_element_type=f32, precision=precision
    )


def pack_kernel(
    counts_ref, vel_ref, visc_ref, nbrs_ref, levels_ref, keys_ref,
    faces_ref, even_ref, odd_ref, spots_ref, *request_refs,
):
    sib_count = lax.axis_size("sib")
    morton = lax.axis_index("morton")
    sib = lax.axis_index("sib")
    own = morton * sib_count + sib
    leaf_count = faces_ref.shape[0]
    fields = jnp.concatenate([vel_ref[0], vel_ref[1], vel_ref[2], visc_ref[...].astype(bf16)], axis=0)
    lane = lax.broadcasted_iota(jnp.int32, (1, FACES), 1)
    first_at, second_at = jnp.bitwise_and(jnp.right_shift(lane, 3), 7), jnp.bitwise_and(lane, 7)
    end_at = 7 * jnp.bitwise_and(jnp.right_shift(lane, 6), 1)
    taken = jnp.where(
        lane < LANES,
        64 * end_at + 8 * first_at + second_at,
        jnp.where(
            lane < 2 * LANES, 64 * first_at + 8 * end_at + second_at, 64 * first_at + 8 * second_at + end_at
        ),
    )
    node = lax.broadcasted_iota(jnp.int32, (NODES, FACES), 0)
    picked = dot(fields, jnp.where(node == taken, 1.0, 0.0).astype(bf16))
    for dim in range(3):
        block = picked[3 * leaf_count :, dim * LANES : (dim + 1) * LANES]
        block = pltpu.roll(block, LANES // 2, 1).astype(bf16)
        for request_ref in request_refs:
            request_ref[:leaf_count, dim * LANES : (dim + 1) * LANES] = block
    picked = picked[: 3 * leaf_count].astype(bf16)
    for comp in range(3):
        for dim in range(3):
            lane = (dim * 3 + comp) * LANES
            rows = picked[comp * leaf_count : (comp + 1) * leaf_count]
            faces_ref[:, lane : lane + LANES] = rows[:, dim * LANES : (dim + 1) * LANES]
    first = counts_ref[own] - BAND
    row = lax.broadcasted_iota(jnp.int32, (BAND, leaf_count), 0)
    col = lax.broadcasted_iota(jnp.int32, (BAND, leaf_count), 1)
    last_rows = jnp.where(col == row + first, 1.0, 0.0).astype(bf16)
    high = dot(last_rows, faces_ref[...]).astype(bf16)
    low = faces_ref[:BAND, :]
    is_odd = jnp.bitwise_and(morton, 1) == 1
    even_ref[...] = jnp.where(is_odd, low, high)
    odd_ref[...] = jnp.where(is_odd, high, low)

    nbrs = nbrs_ref[...]
    target = jnp.maximum(nbrs, 0)
    owner = target // leaf_count
    slot = target - owner * leaf_count
    owner_morton = owner // sib_count
    owner_sib = owner - owner_morton * sib_count
    step = owner_morton - morton
    below = jnp.maximum(morton - 1, 0) * sib_count
    band_start = jnp.zeros_like(slot)
    for other in range(sib_count):
        band_start = jnp.where(owner_sib == other, counts_ref[below + other] - BAND, band_start)
    below_at = BAND * jnp.bitwise_and(morton, 1)
    in_band = jnp.where(step < 0, slot - band_start + below_at, slot + BAND - below_at)
    box = box_rows()
    shift_bits = 3 * (LMAX - levels_ref[...])
    anchor = jnp.left_shift(jnp.right_shift(keys_ref[...], shift_bits), shift_bits)
    span = jnp.left_shift(jnp.ones_like(shift_bits), LMAX - levels_ref[...]).astype(f32)
    finest = 1.0 / float(2**LMAX)
    places = []
    for dim, offset in enumerate((2, 1, 0)):
        cell = jnp.zeros_like(anchor)
        for bit in range(LMAX):
            picked = jnp.bitwise_and(jnp.right_shift(anchor, 3 * bit + offset), 1)
            cell = cell + jnp.left_shift(picked, bit)
        center = (cell.astype(f32) + 0.5 * span) * finest
        places.append((center - box[4 + dim : 5 + dim, :]) * box[7:8, :])
    places.append(0.5 * span * finest * box[7:8, :])
    places.append(jnp.zeros((4, leaf_count), f32))
    geom = jnp.concatenate(places, axis=0)
    for side in range(sib_count // 2):
        piece = jnp.bitwise_xor(owner_sib, jnp.bitwise_xor(sib, 2 * side))
        spot = jnp.where(step == 0, piece * leaf_count + slot, 2 * leaf_count + piece * (2 * BAND) + in_band)
        spot = jnp.where((nbrs >= 0) & (piece < 2), spot, -1)
        if side == 0:
            spots_ref[...] = jnp.concatenate([spot.astype(f32), jnp.zeros((2, leaf_count), f32), geom[:4], box[:4]], axis=0)
            continue
        whole = jnp.right_shift(spot, 4)
        parts = [whole.astype(f32), (spot - 16 * whole).astype(f32), geom[:4]]
        request_ref = request_refs[side - 1]
        request_ref[leaf_count:, :LANES] = jnp.concatenate(parts, axis=0).astype(bf16)
        request_ref[leaf_count:, LANES:] = jnp.zeros((16, FACES - LANES), bf16)


def gathered(asked, window_refs, start):
    leaf_count = asked[0].shape[1]
    rows = sum(ref.shape[0] for ref in window_refs)
    blank = jnp.full((LANES - 8 * len(asked), leaf_count), -1.0, f32)
    places = jnp.concatenate([spots[:8] for spots in asked] + [blank], axis=0).T.astype(jnp.int32)
    cols = lax.broadcasted_iota(jnp.int32, (leaf_count, rows), 1) + start
    upper = jnp.bitwise_and(lax.broadcasted_iota(jnp.int32, (leaf_count, FACES), 1), 64) > 0
    chosen = [[] for _ in asked]
    for dim in range(3):
        at = dim * FACES
        window = jnp.concatenate([ref[:, at : at + FACES] for ref in window_refs], axis=0)
        faces = [8 * who + face for who in range(len(asked)) for face in (2 * dim, 2 * dim + 1)]
        onehot = [jnp.where(cols == places[:, face : face + 1], 1.0, 0.0).astype(bf16) for face in faces]
        found = dot(jnp.concatenate(onehot, axis=0), window)
        for who in range(len(asked)):
            first, second = (found[(2 * who + side) * leaf_count : (2 * who + side + 1) * leaf_count] for side in (0, 1))
            chosen[who].append(jnp.where(upper, first, second).astype(bf16))
    return chosen


def requested(ref):
    leaf_count = ref.shape[0] - 16
    parts = ref[leaf_count:, :LANES].astype(f32)
    blank = jnp.zeros((2, leaf_count), f32)
    rows = [parts[:6] * 16.0 + parts[6:12], blank, parts[12:], jnp.zeros((4, leaf_count), f32)]
    return jnp.concatenate(rows, axis=0)


def by_comp(chosen):
    comps = [
        jnp.concatenate([block[:, comp * LANES : (comp + 1) * LANES] for block in chosen], axis=1) for comp in range(3)
    ]
    return jnp.concatenate(comps, axis=0)


def fill_tables(rows_ref, dx_ref, dyz_ref):
    row = lax.broadcasted_iota(jnp.int32, (64, NODES), 0)
    col = lax.broadcasted_iota(jnp.int32, (64, NODES), 1)
    same = row == jnp.bitwise_and(col, 63)
    for at in range(8):
        dx_ref[64 * at : 64 * at + 64, :] = jnp.where(same, rows_ref[at : at + 1, :], 0.0).astype(bf16)
    row = lax.broadcasted_iota(jnp.int32, (8, 256), 0)
    col = lax.broadcasted_iota(jnp.int32, (8, 256), 1)
    same = row == jnp.bitwise_and(col, 7)
    group = jnp.right_shift(col, 3)
    for pair in range(16):
        blocks = []
        for at in (2 * pair, 2 * pair + 1):
            here = same & (jnp.right_shift(group, 3) == at // 8)
            along_y = jnp.where(here, rows_ref[8 + at % 8 : 9 + at % 8, :256], 0.0)
            along_z = jnp.where(group == at, rows_ref[16:24, :256], 0.0)
            blocks.append(jnp.concatenate([along_y, along_z], axis=1))
        dyz_ref[16 * pair : 16 * pair + 16, :] = jnp.concatenate(blocks, axis=0).astype(bf16)


def operator_kernel(
    counts_ref, vel_ref, press_ref, visc_ref, rows_ref,
    part_ref, mass_ref, dx_ref, dyz_ref,
):
    sib_count = lax.axis_size("sib")
    own = lax.axis_index("morton") * sib_count + lax.axis_index("sib")
    leaf_count = mass_ref.shape[0]
    live = lax.broadcasted_iota(jnp.int32, (leaf_count, NODES), 0) < counts_ref[own]
    node = lax.broadcasted_iota(jnp.int32, (1, NODES), 1)
    touching = jnp.zeros((1, NODES), f32)
    for shift in (6, 3, 0):
        idx = jnp.bitwise_and(jnp.right_shift(node, shift), 7)
        touching = touching + jnp.where((idx == 0) | (idx == 7), 1.0, 0.0)
    fill_tables(rows_ref, dx_ref, dyz_ref)

    def rows(stack, at):
        return stack[at * leaf_count : (at + 1) * leaf_count]

    visc = visc_ref[...]
    fields = jnp.concatenate([vel_ref[0], vel_ref[1], vel_ref[2], press_ref[...]], axis=0)
    halves = [dot(fields[:, at : at + 256], dyz_ref[...]) for at in (0, 256)]
    grads = [
        dot(fields, dx_ref[...]),
        jnp.concatenate([half[:, :256] for half in halves], axis=1),
        jnp.concatenate([half[:, 256:] for half in halves], axis=1),
    ]
    mass = -(rows(grads[0], 0) + rows(grads[1], 1) + rows(grads[2], 2)) * mass_scale
    mass_ref[...] = jnp.where(live, mass, 0.0)
    stress = {}
    for first in range(3):
        for second in range(first, 3):
            value = (visc * (rows(grads[second], first) + rows(grads[first], second))).astype(bf16)
            stress[first, second] = stress[second, first] = value
    columns = [jnp.concatenate([stress[comp, dim] for comp in range(3)], axis=0) for dim in range(3)]
    rest = [
        dot(columns[1][:, at : at + 256], dyz_ref[:, :256]) + dot(columns[2][:, at : at + 256], dyz_ref[:, 256:])
        for at in (0, 256)
    ]
    div = dot(columns[0], dx_ref[...]) + jnp.concatenate(rest, axis=1)
    for comp in range(3):
        jump = touching * vel_ref[comp].astype(f32)
        part = (penalty * visc * jump - rows(div, comp) + rows(grads[comp], 3)) * out_scale
        part_ref[comp] = jnp.where(live, part, 0.0)


def group_kernel(spots_ref, *refs):
    sides = lax.axis_size("sib") // 2
    request_refs, window_refs, move_ref, out_refs = refs[: sides - 1], refs[sides - 1 : sides + 1], refs[sides + 1], refs[sides + 2 :]
    chosen = gathered([spots_ref[...]] + [requested(ref) for ref in request_refs], window_refs, 0)
    for blocks, out_ref in zip(chosen, out_refs):
        for dim, block in enumerate(blocks):
            out_ref[:, dim * FACES : (dim + 1) * FACES] = block
    box = spots_ref[12:, :]
    move = jnp.ones((256, 256), f32)
    for dim, stride in enumerate((36, 6, 1)):
        col = lax.broadcasted_iota(jnp.int32, (1, 256), 1) // stride % 6
        row = lax.broadcasted_iota(jnp.int32, (256, 1), 0) // stride % 6
        along, scale = box[dim : dim + 1, 3:4], box[3:4, 3:4]
        powers = [jnp.ones((1, 1), f32)]
        for _ in range(DEG):
            powers.append(powers[-1] * along)
        factor = jnp.zeros((256, 256), f32)
        below = jnp.ones((1, 1), f32)
        for low in range(DEG + 1):
            line = jnp.zeros((1, 256), f32)
            for high in range(low, DEG + 1):
                line = jnp.where(col == high, powers[high - low] * below * float(math.comb(high, low)), line)
            factor = jnp.where(row == low, line, factor)
            below = below * scale
        move = move * factor
    move_ref[...] = move


def shifted(tiles, geom):
    width = tiles[0].shape
    scale = jnp.broadcast_to(geom[3:4, :], width)
    level = lax.broadcasted_iota(jnp.int32, width, 0)
    depth = jnp.ones(width, f32)
    for power in range(1, DEG + 1):
        depth = depth * jnp.where(level >= power, scale, 1.0)
    scales = [depth]
    for _ in range(2 * DEG):
        scales.append(scales[-1] * scale)
    tiles = [tile * scales[at // 6 + at % 6] for at, tile in enumerate(tiles)]
    along = [jnp.broadcast_to(geom[dim : dim + 1, :], width) for dim in range(3)]
    for low in range(1, DEG + 1):
        for power in range(DEG, low - 1, -1):
            for other in range(6):
                at = power * 6 + other
                tiles[at] = tiles[at] + along[0] * tiles[at - 6]
            for other in range(6):
                at = other * 6 + power
                tiles[at] = tiles[at] + along[1] * tiles[at - 1]
    steps = [jnp.where(level >= low, along[2], 0.0) for low in range(1, DEG + 1)]
    for step in steps:
        tiles = [tile + step * pltpu.roll(tile, 1, 0) for tile in tiles]
    return tiles


def split(values, parts):
    pieces = []
    for _ in range(parts):
        pieces.append(values.astype(bf16))
        values = values - pieces[-1].astype(f32)
    return pieces


def lane_sums(raw_ref, geoms):
    leaf_count = geoms[0].shape[1]
    geom = jnp.concatenate([leaf for leaf in geoms for _ in range(3)], axis=1)
    tiles = shifted([raw_ref[8 * at : 8 * at + 8, :] for at in range(36)], geom)
    span = 3 * leaf_count
    tiles = [sum(tile[:, span * who : span * (who + 1)] for who in range(len(geoms))) for tile in tiles]
    group = lax.broadcasted_iota(jnp.int32, (span, LANES), 0) // leaf_count
    column = lax.broadcasted_iota(jnp.int32, (span, LANES), 1)
    gather = jnp.where((group == column) | (group + 3 == column), 1.0, 0.0).astype(bf16)
    return sum(dot(piece, gather) for piece in split(jnp.concatenate(tiles, axis=0), 2))


def own_kernel(part_ref, basis_ref, faces_ref, spots_ref, raw_ref):
    leaf_count = part_ref.shape[1]
    high, low = split(part_ref[...].reshape(3 * leaf_count, NODES), 2)
    raw = dot_nt(basis_ref[...], high)
    raw_ref[...] = raw[:ROWS] + raw[ROWS:] + dot_nt(basis_ref[:ROWS, :], low)


def moment_kernel(
    own_ref, face_basis_ref, compact_ref, spots_ref, weights_ref, *refs
):
    sides = lax.axis_size("sib") // 2
    window_refs, request_refs, group_refs = refs[:2], refs[2 : 1 + sides], refs[1 + sides : 1 + 2 * sides]
    near_ref, served_refs, sums_ref, raw_ref = refs[1 + 2 * sides], refs[2 + 2 * sides : -2], refs[-2], refs[-1]
    morton = lax.axis_index("morton")
    leaf_count = spots_ref.shape[1]
    asked = [spots_ref[...]] + [requested(ref) for ref in request_refs]
    chosen = gathered(asked, window_refs, 2 * leaf_count)
    values = []
    for blocks, group_ref, out_ref, ref in zip(
        chosen, group_refs, (near_ref, *served_refs), (weights_ref, *request_refs)
    ):
        for dim in range(3):
            lanes = slice(dim * FACES, (dim + 1) * FACES)
            blocks[dim] = blocks[dim] + group_ref[:, lanes]
            out_ref[:, lanes] = blocks[dim]
        weight = ref[:leaf_count].astype(f32) * (-penalty * out_scale)
        values.append(jnp.concatenate([weight] * 3, axis=0) * by_comp(blocks).astype(f32))
    raw = dot_nt(face_basis_ref[...], jnp.concatenate(values, axis=0).astype(bf16))
    span = 3 * leaf_count
    raw_ref[:, :span] = raw[:, :span] + own_ref[...]
    raw_ref[:, span:] = raw[:, span:]
    summed = lane_sums(raw_ref, [spots[8:] for spots in asked])
    box = spots_ref[12:, :]
    both = shifted([summed[8 * at : 8 * at + 8, :] for at in range(36)], box)
    flat = jnp.concatenate(both, axis=0).T
    sums = sum(dot(piece, compact_ref[...]) for piece in split(flat[:8], 2))
    blank = jnp.zeros((2, LANES), f32)
    to_box = jnp.concatenate([sums[:3, :LANES], sums[:3, LANES:], blank], axis=0)
    to_root = jnp.concatenate([sums[3:6, :LANES], sums[3:6, LANES:], blank], axis=0)
    sib_count = lax.axis_size("sib")
    for other in range(sums_ref.shape[0]):
        sums_ref[other] = jnp.where(morton == other // sib_count, to_box, to_root)


def last_kernel(part_ref, visc_ref, spread_ref, sums_ref, move_ref, near_ref, *refs):
    got_refs, (force_hbm, box_hbm, root_hbm, force_ref, box_ref, root_ref, sems) = refs[:-7], refs[-7:]
    faces = near_ref[...]
    for got_ref in got_refs:
        faces = faces + got_ref[...]
    weight = visc_ref[...] * (penalty * out_scale)
    stores = []
    for comp in range(3):
        lanes = [(dim * 3 + comp) * LANES for dim in range(3)]
        jump = dot(jnp.concatenate([faces[:, at : at + LANES] for at in lanes], axis=1), spread_ref[...])
        force_ref[comp] = part_ref[comp] - weight * jump
        stores.append(pltpu.make_async_copy(force_ref.at[comp], force_hbm.at[comp], sems.at[comp]))
        stores[-1].start()
    sib_count = lax.axis_size("sib")
    morton = lax.axis_index("morton")
    box = jnp.zeros(sums_ref.shape[1:], f32)
    root = jnp.zeros(sums_ref.shape[1:], f32)
    for group in range(sums_ref.shape[0] // sib_count):
        total = jnp.sum(sums_ref[group * sib_count : (group + 1) * sib_count], axis=0)
        box = box + jnp.where(morton == group, total, 0.0)
        root = root + jnp.where(morton == group, 0.0, total)
    box = jnp.concatenate([box[:3], box[3:6]], axis=1)
    root = jnp.concatenate([root[:3], root[3:6]], axis=1)
    box_rows = jnp.concatenate([box, jnp.zeros((5, 2 * LANES), f32)], axis=0)
    pieces = jnp.concatenate([piece.astype(f32) for piece in split(box_rows, 3)], axis=0).astype(bf16)
    moved = sum(dot(pieces, table) for table in split(move_ref[...], 2))
    root = root + (moved[:3] + moved[8:11] + moved[16:19])
    for comp in range(3):
        box_ref[comp] = box[comp : comp + 1, :MOMENTS]
        root_ref[comp] = root[comp : comp + 1, :MOMENTS]
    stores.append(pltpu.make_async_copy(box_ref, box_hbm, sems.at[3]))
    stores.append(pltpu.make_async_copy(root_ref, root_hbm, sems.at[4]))
    for store in stores[3:]:
        store.start()
    for store in stores:
        store.wait()


def call(kernel, shapes, flops, scalars, operands, scratch=(), place=pltpu.VMEM, outs=None, grant=32):
    specs = [pl.BlockSpec(memory_space=pltpu.SMEM)] * len(scalars)
    specs += [pl.BlockSpec(memory_space=place)] * len(operands)
    outs = outs or [pltpu.VMEM] * len(shapes)
    moved = sum(array.size * array.dtype.itemsize for array in operands)
    return pl.pallas_call(
        kernel,
        out_shape=[jax.ShapeDtypeStruct(shape, dtype) for shape, dtype in shapes],
        in_specs=specs,
        out_specs=[pl.BlockSpec(memory_space=out) for out in outs],
        scratch_shapes=list(scratch),
        compiler_params=pltpu.CompilerParams(vmem_limit_bytes=grant * 2**20),
        cost_estimate=pl.CostEstimate(flops=flops, bytes_accessed=moved, transcendentals=0),
    )(*scalars, *operands)


def on_device(velocity, pressure, viscosity, levels, morton_keys, counts, neighbors):
    leaf_count = velocity.shape[0]
    morton_count = lax.axis_size("morton")
    rows = jnp.asarray(derivative_rows().astype(np.float32))
    spread = jnp.asarray(spread_table().astype(np.float32)).astype(bf16)
    basis = basis_tables()
    face_basis = (basis.astype(np.float32) @ spread_table().T.astype(np.float32)).astype(jnp.bfloat16)
    basis, face_basis = jnp.asarray(basis), jnp.asarray(face_basis[:ROWS])
    vel = jnp.transpose(velocity, (1, 0, 2))
    nbrs = jnp.transpose(neighbors, (1, 0))

    width = 3 * FACES
    sib_count = lax.axis_size("sib")
    sides = sib_count // 2
    other_sides = [2 * side for side in range(1, sides)]
    faces, even, odd, spots, *requests = call(
        pack_kernel,
        [
            ((leaf_count, width), bf16),
            ((BAND, width), bf16),
            ((BAND, width), bf16),
            ((16, leaf_count), f32),
        ]
        + [((leaf_count + 16, FACES), bf16)] * (sides - 1),
        4 * 10**8,
        [counts],
        [vel, viscosity, nbrs, levels.reshape(1, -1), morton_keys.reshape(1, -1)],
        grant=60,
    )
    weights = requests[0]
    odd = pairs(odd, 1)
    across = swap(faces, "sib", 1)
    across, requests, even, pressure = lax.optimization_barrier((across, requests, even, pressure))
    requests = [swap(block, "sib", apart) for block, apart in zip(requests, other_sides)]
    even = pairs(even, 0)
    part, continuity = call(
        operator_kernel,
        [((3, leaf_count, NODES), f32), ((leaf_count, NODES), f32)],
        2 * 10**9,
        [counts],
        [vel, pressure, viscosity, rows],
        [pltpu.VMEM((NODES, NODES), bf16), pltpu.VMEM((256, NODES), bf16)],
    )
    (own_raw,) = call(
        own_kernel,
        [((ROWS, 3 * leaf_count), f32)],
        10**9,
        [],
        [part, basis, faces, spots],
    )
    odd, even, own_raw = lax.optimization_barrier((odd, even, own_raw))
    bands = jnp.concatenate([odd, even], axis=0)
    move, *group = call(
        group_kernel,
        [((256, 256), f32)] + [((leaf_count, width), bf16)] * sides,
        10**9,
        [],
        [spots, *requests, faces, across],
    )
    near, *served, sums = call(
        moment_kernel,
        [((leaf_count, width), bf16)] * sides + [((morton_count * sib_count, 8, LANES), f32)],
        2 * 10**9,
        [],
        [
            own_raw, face_basis, jnp.asarray(compact_table()), spots, weights,
            bands, swap(bands, "sib", 1), *requests, *group,
        ],
        [pltpu.VMEM((ROWS, 3 * sides * leaf_count), f32)],
    )
    got = [swap(block, "sib", apart) for block, apart in zip(served, other_sides)]
    every = lax.all_to_all(sums, ("morton", "sib"), 0, 0, tiled=True)
    every, *got = lax.optimization_barrier((every, *got))
    force, box, root = call(
        last_kernel,
        [((3, leaf_count, NODES), f32), ((3, 1, MOMENTS), f32), ((3, 1, MOMENTS), f32)],
        2 * 10**8,
        [],
        [part, viscosity, spread, every, move, near, *got],
        [
            pltpu.VMEM((3, leaf_count, NODES), f32),
            pltpu.VMEM((3, 1, MOMENTS), f32),
            pltpu.VMEM((3, 1, MOMENTS), f32),
            pltpu.SemaphoreType.DMA((5,)),
        ],
        outs=[pltpu.HBM] * 3,
    )
    return (
        jnp.transpose(force, (1, 0, 2)),
        continuity,
        jnp.transpose(box, (1, 0, 2)),
        jnp.transpose(root, (1, 0, 2)),
    )


def solution(mesh):
    spread_all = ("morton", "sib")
    in_specs = (
        P(spread_all, None, None),
        P(spread_all, None),
        P(spread_all, None),
        P(spread_all),
        P(spread_all),
        P(),
        P(spread_all, None),
    )
    out_specs = (
        P(spread_all, None, None),
        P(spread_all, None),
        P("morton", None, None),
        P("morton", None, None),
    )
    return jax.shard_map(
        on_device, mesh=mesh, in_specs=in_specs, out_specs=out_specs, check_vma=False
    )
```
